32 devices in a mesh: section: 2 (over core), dp: 8 (over z, y), mp: 2 (over x).
Axes of the slice: x: 2, y: 2, z: 4, core: 2. Of those that a mesh axis runs over, the one named last changes fastest.
Arguments:
- word_state: bfloat16 [2, 32, 20, 768], P(None, 'dp'), may hold values from -6 to 6
- region_state: bfloat16 [2, 32, 36, 768], P(None, 'dp'), may hold values from -6 to 6
- word_lengths: int32 [2, 32], P(None, 'dp'), may hold values from 5 to 20
- region_counts: int32 [2, 32], P(None, 'dp'), may hold values from 10 to 36
- word_cotangent: bfloat16 [2, 32, 20, 768], P(None, 'dp'), may hold values from -6 to 6
- region_cotangent: bfloat16 [2, 32, 36, 768], P(None, 'dp'), may hold values from -6 to 6
- cross_in: bfloat16 [768, 3, 768], P(None, None, 'mp'), may hold values from -0.21875 to 0.21875
- cross_bias: float32 [2, 768], P(None, 'mp'), may hold values from -1 to 1
- cross_out: bfloat16 [768, 768], P('mp'), may hold values from -0.875 to 0.875
- cross_post: float32 [3, 768], replicated
- attention_in: bfloat16 [2, 2, 768, 3, 768], P('section', None, None, None, 'mp'), may hold values from -0.21875 to 0.21875
- attention_bias: float32 [2, 2, 2, 768], P('section', None, None, 'mp'), may hold values from -1 to 1
- attention_out: bfloat16 [2, 2, 768, 768], P('section', None, 'mp'), may hold values from -0.875 to 0.875
- attention_post: float32 [2, 2, 3, 768], P('section')
- feed_in: bfloat16 [2, 2, 768, 3072], P('section', None, None, 'mp'), may hold values from -0.21875 to 0.21875
- feed_bias: float32 [2, 2, 3072], P('section', None, 'mp'), may hold values from -1 to 1
- feed_out: bfloat16 [2, 2, 3072, 768], P('section', None, 'mp'), may hold values from -0.109375 to 0.109375
- feed_post: float32 [2, 2, 3, 768], P('section')
Outputs:
- word_output: bfloat16 [2, 32, 20, 768], P('section', 'dp')
- region_output: bfloat16 [2, 32, 36, 768], P('section', 'dp')
- word_gradient: bfloat16 [2, 32, 20, 768], P('section', 'dp')
- region_gradient: bfloat16 [2, 32, 36, 768], P('section', 'dp')
- cross_in_gradient: float32 [768, 3, 768], P(('section', 'dp'), None, 'mp')
- cross_bias_gradient: float32 [2, 768], P(None, 'mp')
- cross_out_gradient: float32 [768, 768], P('mp', ('section', 'dp'))
- cross_post_gradient: float32 [3, 768], replicated
- attention_in_gradient: float32 [2, 2, 768, 3, 768], P('section', None, 'dp', None, 'mp')
- attention_bias_gradient: float32 [2, 2, 2, 768], P('section', None, None, 'mp')
- attention_out_gradient: float32 [2, 2, 768, 768], P('section', None, 'mp', 'dp')
- attention_post_gradient: float32 [2, 2, 3, 768], P('section')
- feed_in_gradient: float32 [2, 2, 768, 3072], P('section', None, 'dp', 'mp')
- feed_bias_gradient: float32 [2, 2, 3072], P('section', None, 'mp')
- feed_out_gradient: float32 [2, 2, 3072, 768], P('section', None, 'mp', 'dp')
- feed_post_gradient: float32 [2, 2, 3, 768], P('section')
- branch_scales: float32 [2, 8], P('section')
The draws below stay inside these ranges and needn't reach their ends.
All inputs are finite; a program needn't handle non-finite values.
Results may differ from the reference program's by a relative error of at most 0.039.
Values may be sent and summed in bfloat16 or wider, within the bound.
No kernel may reach another device: no remote copies, remote signals or barrier semaphores. Data moves between devices by JAX's collectives and lax.ppermute only.
A program may use at most 256 MiB of HBM per device.

```python
import jax
import jax.numpy as jnp
from jax import lax

D = 768
HEADS = 12
FF = 3072
HEAD_DIM = 64
WORDS = 20
REGIONS = 36
MICRO = 2
LAYERS = 2
ITEMS_MB = 32


def bounded_counts(key, lowest, highest_value):
    first, second = jax.random.split(key)
    values = jax.random.randint(first, (MICRO * ITEMS_MB,), lowest, highest_value + 1)
    place = jax.random.randint(second, (), 0, MICRO * ITEMS_MB)
    values = jnp.where(jnp.arange(MICRO * ITEMS_MB) == place, highest_value, values)
    return values.reshape(MICRO, ITEMS_MB).astype(jnp.int32)


def post_rows(key, shape):
    first, second, third = jax.random.split(key, 3)
    bias_rows = 0.2 * jax.random.normal(first, shape, jnp.float32)
    gain_rows = jax.random.uniform(second, shape, jnp.float32, 0.7, 1.3)
    shift_rows = 0.2 * jax.random.normal(third, shape, jnp.float32)
    return jnp.stack([bias_rows, gain_rows, shift_rows], axis=-2)


def draw_word_lengths(key, part):
    key = jax.random.fold_in(key, 11)
    return bounded_counts(key, 5, WORDS)


def draw_region_counts(key, part):
    key = jax.random.fold_in(key, 13)
    return bounded_counts(key, 10, REGIONS)


def draw_attention_post(key, part):
    key = jax.random.fold_in(key, 17)
    return post_rows(key, (LAYERS, 2, D))


def draw_feed_post(key, part):
    key = jax.random.fold_in(key, 19)
    return post_rows(key, (LAYERS, 2, D))


def draw_cross_post(key, part):
    key = jax.random.fold_in(key, 23)
    return post_rows(key, (D,))


def block_scale(stream_key, extent, pieces, low, largest):
    def one(position, parts):
        steps = jax.random.uniform(jax.random.fold_in(jax.random.fold_in(stream_key, 6), position), (parts,), jnp.float32, low / len(pieces), largest / len(pieces))
        return jnp.repeat(jnp.exp(steps), extent[position] // parts).reshape((-1,) + (1,) * (len(extent) - position - 1))

    loudness = one(*pieces[0])
    for cut in pieces[1:]:
        loudness = loudness * one(*cut)
    return loudness


def noise(rng, extent, scale, most, cuts=(), dtype=jnp.bfloat16):
    values = jax.random.normal(rng, extent, jnp.float32) * scale
    if len(cuts) > 0:
        values = block_scale(rng, extent, cuts, -0.22, 0.18) * values
    return jnp.clip(values, min=-most, max=most).astype(dtype)


def setup_inputs(seed: int = 0) -> dict:
    key_of = jax.random.split(jax.random.key(seed), 19)
    word_state = noise(key_of[0], (MICRO, ITEMS_MB, WORDS, D), 1.0, 6.0, ((1, 8),))
    region_state = noise(key_of[1], (MICRO, ITEMS_MB, REGIONS, D), 1.0, 6.0, ((1, 8),))
    word_lengths = draw_word_lengths(jax.random.fold_in(key_of[18], 71), 0)
    region_counts = draw_region_counts(jax.random.fold_in(key_of[18], 71), 0)
    word_cotangent = noise(key_of[4], (MICRO, ITEMS_MB, WORDS, D), 1.0, 6.0, ((1, 8),))
    region_cotangent = noise(key_of[5], (MICRO, ITEMS_MB, REGIONS, D), 1.0, 6.0, ((1, 8),))
    cross_in = noise(key_of[6], (D, 3, D), D ** -0.5, 0.21875, ((2, 2),))
    cross_bias = noise(key_of[7], (2, D), 0.2, 1.0, ((1, 2),), jnp.float32)
    cross_out = noise(key_of[8], (D, D), (D // 16) ** -0.5, 0.875, ((0, 2),))
    cross_post = draw_cross_post(jax.random.fold_in(key_of[18], 71), 0)
    attention_in = noise(key_of[10], (LAYERS, 2, D, 3, D), D ** -0.5, 0.21875, ((0, 2), (4, 2)))
    attention_bias = noise(key_of[11], (LAYERS, 2, 2, D), 0.2, 1.0, ((0, 2), (3, 2)), jnp.float32)
    attention_out = noise(key_of[12], (LAYERS, 2, D, D), (D // 16) ** -0.5, 0.875, ((0, 2), (2, 2)))
    attention_post = draw_attention_post(jax.random.fold_in(key_of[18], 71), 0)
    feed_in = noise(key_of[14], (LAYERS, 2, D, FF), D ** -0.5, 0.21875, ((0, 2), (3, 2)))
    feed_bias = noise(key_of[15], (LAYERS, 2, FF), 0.2, 1.0, ((0, 2), (2, 2)), jnp.float32)
    feed_out = noise(key_of[16], (LAYERS, 2, FF, D), FF ** -0.5, 0.109375, ((0, 2), (2, 2)))
    feed_post = draw_feed_post(jax.random.fold_in(key_of[18], 71), 0)
    return {"word_state": word_state, "region_state": region_state, "word_lengths": word_lengths, "region_counts": region_counts, "word_cotangent": word_cotangent, "region_cotangent": region_cotangent, "cross_in": cross_in, "cross_bias": cross_bias, "cross_out": cross_out, "cross_post": cross_post, "attention_in": attention_in, "attention_bias": attention_bias, "attention_out": attention_out, "attention_post": attention_post, "feed_in": feed_in, "feed_bias": feed_bias, "feed_out": feed_out, "feed_post": feed_post}


@jax.custom_vjp
def low(v):
    return lax.optimization_barrier(v.astype(jnp.bfloat16)).astype(jnp.float32)

@jax.custom_vjp
def low_back(v):
    return v

def low_keep(v):
    return (low(v), None)

def low_pass(kept, grad):
    return (grad,)

def back_keep(v):
    return (v, None)

def back_low(kept, grad):
    return (low(grad),)
low.defvjp(low_keep, low_pass)
low_back.defvjp(back_keep, back_low)
epsilon = 1e-06
highest = lax.Precision.HIGHEST

def rounded(value):
    return low(low_back(value))

def normalize(value, gain, shift):
    centred = value - lax.optimization_barrier(jnp.mean(value, axis=-1, keepdims=True))
    spread = lax.optimization_barrier(jnp.mean(centred * centred, axis=-1, keepdims=True))
    return centred * lax.rsqrt(spread + epsilon) * gain + shift

def project(inputs, weight, bias):
    full_bias = jnp.stack([bias[0], jnp.zeros_like(bias[0]), bias[1]])
    return rounded(jnp.einsum('bld,dke->blke', inputs, weight, precision=highest) + full_bias)

def attend(query, keys, values, key_mask):
    batch = query.shape[0]
    rows = query.shape[1]
    query = query.reshape(batch, rows, HEADS, HEAD_DIM)
    keys = keys.reshape(batch, keys.shape[1], HEADS, HEAD_DIM)
    values = values.reshape(batch, values.shape[1], HEADS, HEAD_DIM)
    scores = low_back(jnp.einsum('bqhe,bkhe->bhqk', query, keys, precision=highest) * HEAD_DIM ** (-0.5))
    scores = jnp.where(key_mask[:, None, None, :], scores, -1000000000.0)
    weights = low(jax.nn.softmax(scores, axis=-1))
    context = jnp.einsum('bhqk,bkhe->bqhe', weights, values, precision=highest)
    return rounded(context.reshape(batch, rows, D))

def branch(context, weight, post):
    return low_back(jnp.einsum('bld,de->ble', context, weight, precision=highest) + post[0])

def masked_squares(value, valid):
    return jnp.sum(lax.optimization_barrier(jnp.sum(value * value, axis=-1)) * valid)

def stream_block(mixed, mask, side, weights):
    attention_in, attention_bias, attention_out, attention_post, feed_in, feed_bias, feed_out, feed_post = weights
    own = project(low(mixed), attention_in[side], attention_bias[side])
    context = attend(own[:, :, 0], own[:, :, 1], own[:, :, 2], mask)
    second = branch(context, attention_out[side], attention_post[side])
    settled = normalize(mixed + second, attention_post[side, 1], attention_post[side, 2])
    hidden = low_back(jnp.einsum('bld,df->blf', low(settled), feed_in[side], precision=highest) + feed_bias[side])
    activated = low(jax.nn.gelu(hidden, approximate=False))
    third = low_back(jnp.einsum('blf,fd->bld', activated, feed_out[side], precision=highest) + feed_post[side, 0])
    result = low(normalize(settled + third, feed_post[side, 1], feed_post[side, 2]))
    return (result, second, third)

def layer(word_input, region_input, word_mask, region_mask, word_valid, region_valid, weights, cross_weights, crossing):
    word_input = low_back(word_input)
    region_input = low_back(region_input)
    if crossing:
        cross_in, cross_bias, cross_out, cross_post = cross_weights
        cross_words = project(low(word_input), cross_in, cross_bias)
        cross_regions = project(low(region_input), cross_in, cross_bias)
        context_words = attend(cross_words[:, :, 0], cross_regions[:, :, 1], cross_regions[:, :, 2], region_mask)
        context_regions = attend(cross_regions[:, :, 0], cross_words[:, :, 1], cross_words[:, :, 2], word_mask)
        lead_words = branch(context_words, cross_out, cross_post)
        lead_regions = branch(context_regions, cross_out, cross_post)
        mixed_words = normalize(word_input + lead_words, cross_post[1], cross_post[2])
        mixed_regions = normalize(region_input + lead_regions, cross_post[1], cross_post[2])
    else:
        lead_words, lead_regions = (word_input, region_input)
        mixed_words, mixed_regions = (word_input, region_input)
    out_words, self_words, feed_words = stream_block(mixed_words, word_mask, 0, weights)
    out_regions, self_regions, feed_regions = stream_block(mixed_regions, region_mask, 1, weights)
    word_terms = [masked_squares(value, word_valid) for value in (lead_words, self_words, feed_words, out_words)]
    region_terms = [masked_squares(value, region_valid) for value in (lead_regions, self_regions, feed_regions, out_regions)]
    return (out_words, out_regions, jnp.stack(word_terms + region_terms))

def reference(word_state, region_state, word_lengths, region_counts, word_cotangent, region_cotangent, cross_in, cross_bias, cross_out, cross_post, attention_in, attention_bias, attention_out, attention_post, feed_in, feed_bias, feed_out, feed_post):
    items = MICRO * ITEMS_MB
    word_mask = jnp.arange(WORDS)[None, :] < word_lengths.reshape(items, 1)
    region_mask = jnp.arange(REGIONS)[None, :] < region_counts.reshape(items, 1)
    word_valid = word_mask.astype(jnp.float32)
    region_valid = region_mask.astype(jnp.float32)
    weights = tuple((tensor.astype(jnp.float32) for tensor in (attention_in, attention_bias, attention_out, attention_post, feed_in, feed_bias, feed_out, feed_post)))
    crossing = tuple((tensor.astype(jnp.float32) for tensor in (cross_in, cross_bias, cross_out, cross_post)))

    def forward(first_words, first_regions, layer_weights, cross_weights):
        current_words = first_words
        current_regions = first_regions
        collected = []
        for layer_index in range(LAYERS):
            taken = tuple((tensor[layer_index] for tensor in layer_weights))
            current_words, current_regions, terms = layer(current_words, current_regions, word_mask, region_mask, word_valid, region_valid, taken, cross_weights, layer_index > 0)
            collected.append(terms)
        return ((current_words, current_regions), jnp.stack(collected))
    start_words = word_state.astype(jnp.float32).reshape(items, WORDS, D)
    start_regions = region_state.astype(jnp.float32).reshape(items, REGIONS, D)
    outputs, pull, sums = jax.vjp(forward, start_words, start_regions, weights, crossing, has_aux=True)
    cotangent_words = word_cotangent.astype(jnp.float32).reshape(items, WORDS, D) * word_valid[:, :, None]
    cotangent_regions = region_cotangent.astype(jnp.float32).reshape(items, REGIONS, D) * region_valid[:, :, None]
    grad_words, grad_regions, grad_weights, grad_cross = pull((cotangent_words, cotangent_regions))
    counts = jnp.stack([jnp.sum(word_valid), jnp.sum(region_valid)])
    divisor = jnp.repeat(counts, 4) * D
    scales = jnp.sqrt(sums / divisor[None, :])
    word_shape = (MICRO, ITEMS_MB, WORDS, D)
    region_shape = (MICRO, ITEMS_MB, REGIONS, D)
    return (outputs[0].astype(jnp.bfloat16).reshape(word_shape), outputs[1].astype(jnp.bfloat16).reshape(region_shape), grad_words.astype(jnp.bfloat16).reshape(word_shape), grad_regions.astype(jnp.bfloat16).reshape(region_shape), grad_cross[0], grad_cross[1], grad_cross[2], grad_cross[3], grad_weights[0], grad_weights[1], grad_weights[2], grad_weights[3], grad_weights[4], grad_weights[5], grad_weights[6], grad_weights[7], scales)
```

```python
from functools import partial

import jax
import jax.numpy as jnp
from jax import lax
from jax.experimental import pallas as pl
from jax.experimental.pallas import tpu as pltpu
from jax.sharding import PartitionSpec as P

D = 768
HALF = D // 2
HEAD_DIM = 64
PAIR = 2 * HEAD_DIM
WORDS = 20
REGIONS = 36
EPS = 1e-06
SCALE = HEAD_DIM**-0.5
bf16 = jnp.bfloat16
f32 = jnp.float32

ROW_ATT_BIAS, ROW_ATT_POST, ROW_FEED_BIAS, ROW_FEED_POST, SMALL_ROWS = 0, 1, 4, 6, 16


def mm(a, b):
    return jnp.dot(a, b, preferred_element_type=f32)


def mm_nt(a, b):
    return lax.dot_general(a, b, (((1,), (1,)), ((), ())), preferred_element_type=f32)


def mm_tn(a, b):
    return lax.dot_general(a, b, (((0,), (0,)), ((), ())), preferred_element_type=f32)


def norm_of(value, gain, shift):
    centred = value - jnp.mean(value, axis=-1, keepdims=True)
    spread = jnp.mean(centred * centred, axis=-1, keepdims=True)
    rstd = lax.rsqrt(spread + EPS)
    unit = centred * rstd
    return unit, rstd, unit * gain + shift


def norm_back(unit, rstd, gain, incoming):
    scaled = incoming * gain
    mean = jnp.mean(scaled, axis=-1, keepdims=True)
    along = jnp.mean(scaled * unit, axis=-1, keepdims=True)
    return (scaled - mean - unit * along) * rstd


def summed(own, other):
    return own[...].astype(f32) + other[...].astype(f32)


def column_sum(value):
    return jnp.sum(value, axis=0, keepdims=True)


def square_sum(value, valid):
    rows = jnp.sum(value * value, axis=-1, keepdims=True) * valid
    return jnp.broadcast_to(jnp.sum(rows, axis=0, keepdims=True), (1, 128))


def lengths_of(meta, side, batch, item):
    result = jnp.zeros_like(item)
    for i in range(batch):
        result = jnp.where(item == i, meta[1 + side * batch + i], result)
    return result


def row_valid(meta, side, batch, rows):
    index = lax.broadcasted_iota(jnp.int32, (rows, 1), 0)
    length = lengths_of(meta, side, batch, lax.rem(index, batch))
    return (lax.div(index, batch) < length).astype(f32)


def pair_valid(meta, side, batch, rows, keys):
    index = lax.broadcasted_iota(jnp.int32, (1, keys), 1)
    item = lax.rem(index, batch)
    length = lengths_of(meta, side, batch, item)
    item = jnp.where(lax.div(index, batch) < length, item, -1)
    row_item = lax.rem(lax.broadcasted_iota(jnp.int32, (rows, 1), 0), batch)
    return jnp.broadcast_to(row_item, (rows, keys)) == jnp.broadcast_to(item, (rows, keys))


def head_lanes(head):
    lane = lax.broadcasted_iota(jnp.int32, (1, PAIR), 1)
    return (lane // HEAD_DIM) == head


def attend(query, keys, values, valid, probs_ref, context_ref):
    for pair in range(query.shape[1] // PAIR):
        lanes = slice(pair * PAIR, (pair + 1) * PAIR)
        contexts = []
        for head in range(2):
            chosen = query[:, lanes] * head_lanes(head).astype(bf16)
            scores = mm_nt(chosen, keys[:, lanes]) * SCALE
            scores = jnp.where(valid, scores, -1e9)
            shifted = jnp.exp(scores - jnp.max(scores, axis=-1, keepdims=True))
            total = jnp.sum(shifted, axis=-1, keepdims=True)
            probs = (shifted * (1.0 / total)).astype(bf16)
            probs_ref[2 * pair + head] = probs
            contexts.append(mm(probs, values[:, lanes]))
        context_ref[:, lanes] = jnp.where(head_lanes(0), contexts[0], contexts[1]).astype(bf16)


def attend_back(query, keys, values, probs_ref, grad_context, emit):
    first = head_lanes(0)
    for pair in range(query.shape[1] // PAIR):
        lanes = slice(pair * PAIR, (pair + 1) * PAIR)
        grads = ([], [], [])
        for head in range(2):
            probs = probs_ref[2 * pair + head]
            chosen = grad_context[:, lanes] * head_lanes(head).astype(bf16)
            grad_probs = mm_nt(chosen, values[:, lanes])
            wide = probs.astype(f32)
            product = wide * grad_probs
            grad_scores = product - wide * jnp.sum(product, axis=-1, keepdims=True)
            grad_scores = grad_scores.astype(bf16)
            grads[0].append(mm(grad_scores, keys[:, lanes]) * SCALE)
            grads[1].append(mm_tn(grad_scores, query[:, lanes]) * SCALE)
            grads[2].append(mm_tn(probs, grad_context[:, lanes]))
        for kind in range(3):
            emit(kind, lanes, jnp.where(first, grads[kind][0], grads[kind][1]).astype(bf16))


class Weights:
    def __init__(self, meta, layer, pairs, buffers, sems):
        self.copies = []
        mine = meta[0] == layer
        for slot, ((own, other), buffer) in enumerate(zip(pairs, buffers)):
            if other is None:
                copy = pltpu.make_async_copy(own, buffer, sems.at[slot])
                copy.start()
            else:
                copy = pltpu.make_async_copy(own, buffer, sems.at[slot])
                second = pltpu.make_async_copy(other, buffer, sems.at[slot])
                pl.when(mine)(copy.start)
                pl.when(jnp.logical_not(mine))(second.start)
            self.copies.append((copy, buffer))

    def get(self, slot):
        copy, buffer = self.copies[slot]
        copy.wait()
        return buffer


def call(body, ins, outs, scratch=(), flops=0, name=None):
    spaces = {"v": pltpu.VMEM, "s": pltpu.SMEM, "h": pl.ANY}
    arrays = [array for array, space in ins]
    total = sum(a.size * a.dtype.itemsize for a in arrays)
    return pl.pallas_call(
        body,
        out_shape=[jax.ShapeDtypeStruct(shape, dtype) for shape, dtype in outs],
        in_specs=[pl.BlockSpec(memory_space=spaces[space]) for array, space in ins],
        out_specs=[pl.BlockSpec(memory_space=pltpu.VMEM) for _ in outs],
        scratch_shapes=list(scratch),
        compiler_params=pltpu.CompilerParams(vmem_limit_bytes=40 * 1024 * 1024),
        cost_estimate=pl.CostEstimate(
            flops=int(flops), bytes_accessed=int(total), transcendentals=0
        ),
        name=name,
    )(*arrays)


def select_rows(value, chooser, own_ref, pack_ref):
    moved = mm(value, chooser[...]).astype(bf16)
    own_ref[...] = moved[:, :HALF]
    pack_ref[:, :HALF] = moved[:, HALF:]


def project(low, weights, bias_q, bias_v, qkv_ref):
    qkv_ref[0] = (mm(low, weights[0]) + bias_q).astype(bf16)
    qkv_ref[1] = mm(low, weights[1]).astype(bf16)
    qkv_ref[2] = (mm(low, weights[2]) + bias_v).astype(bf16)


def self_forward(side, layer, batch, meta, state, prior, small, chooser, att_in, att_out):
    rows = state.shape[0]
    width = att_in[0].shape[-1]
    first = prior is None

    def body(meta, state, *refs):
        refs = list(refs)
        if not first:
            own, other, post = refs[:3]
            refs = refs[3:]
        small, chooser, in_own, in_other, out_own, out_other = refs[:6]
        qkv, probs, selected, pack, part, squares = refs[6:12]
        refs = refs[12:]
        if not first:
            mixed_ref, unit_ref, rstd_ref = refs[:3]
            refs = refs[3:]
        in_buffer, out_buffer, sems = refs
        weights = Weights(
            meta,
            layer,
            ((in_own.at[0, side], in_other.at[0, side]), (out_own.at[0, side], out_other.at[0, side])),
            (in_buffer, out_buffer),
            sems,
        )
        valid = row_valid(meta, side, batch, rows)
        if first:
            low = state[...]
            squares[...] = square_sum(low.astype(f32), valid)
        else:
            branch = summed(own, other) + post[0:1]
            squares[...] = square_sum(branch, valid)
            unit, rstd, mixed = norm_of(state[...].astype(f32) + branch, post[1:2], post[2:3])
            unit_ref[...] = unit
            rstd_ref[...] = rstd
            mixed_ref[...] = mixed
            low = mixed.astype(bf16)
        select_rows(low, chooser, selected, pack)
        biases = small[ROW_ATT_BIAS : ROW_ATT_BIAS + 1]
        project(low, weights.get(0), biases[:, :width], biases[:, width : 2 * width], qkv)
        context = pack.at[:, HALF:]
        attend(
            qkv[0], qkv[1], qkv[2], pair_valid(meta, side, batch, rows, rows), probs, context
        )
        part[...] = mm(context[...], weights.get(1)[...]).astype(bf16)

    ins = [(meta, "s"), (state, "v")]
    if not first:
        ins += [(item, "v") for item in prior]
    ins += [(small, "v"), (chooser, "v")] + [(item, "h") for item in att_in + att_out]
    outs = [
        ((3, rows, width), bf16),
        ((width // HEAD_DIM, rows, rows), bf16),
        ((rows, HALF), bf16),
        ((rows, HALF + width), bf16),
        ((rows, D), bf16),
        ((1, 128), f32),
    ]
    if not first:
        outs += [((rows, D), f32), ((rows, D), f32), ((rows, 1), f32)]
    scratch = [
        pltpu.VMEM((3, D, width), bf16),
        pltpu.VMEM((width, D), bf16),
        pltpu.SemaphoreType.DMA((2,)),
    ]
    return call(body, ins, outs, scratch, 2 * rows * D * 5 * width, f"self_forward_{layer}_{side}")


def feed_forward(side, layer, batch, meta, residual, own, other, small, chooser, feed_in, feed_out):
    rows = residual.shape[0]
    units = feed_in[0].shape[-1]
    step = units // 4

    def body(
        meta, residual, own, other, small, chooser, in_own, in_other, out_own, out_other,
        settled_ref, unit_ref, rstd_ref, selected, pack, slope, part, squares,
        in_buffer, out_buffer, sems,
    ):
        weights = Weights(
            meta,
            layer,
            ((in_own.at[0, side], in_other.at[0, side]), (out_own.at[0, side], out_other.at[0, side])),
            (in_buffer, out_buffer),
            sems,
        )
        post = small[ROW_ATT_POST : ROW_ATT_POST + 3]
        branch = summed(own, other) + post[0:1]
        squares[...] = square_sum(branch, row_valid(meta, side, batch, rows))
        unit, rstd, settled = norm_of(residual[...].astype(f32) + branch, post[1:2], post[2:3])
        unit_ref[...] = unit
        rstd_ref[...] = rstd
        settled_ref[...] = settled
        low = settled.astype(bf16)
        select_rows(low, chooser, selected, pack)
        first = weights.get(0)
        for i in range(units // step):
            columns = slice(i * step, (i + 1) * step)
            row = ROW_FEED_BIAS + (i * step) // D
            place = (i * step) % D
            hidden = mm(low, first[:, columns]) + small[row : row + 1, place : place + step]
            below = 0.5 + 0.5 * lax.erf(hidden * (0.5**0.5))
            density = jnp.exp(hidden * hidden * -0.5) * 0.3989422804014327
            pack[:, HALF + i * step : HALF + (i + 1) * step] = (hidden * below).astype(bf16)
            slope[:, columns] = (below + hidden * density).astype(bf16)
        part[...] = mm(pack[:, HALF:], weights.get(1)[...]).astype(bf16)

    ins = [(meta, "s")] + [(a, "v") for a in (residual, own, other, small, chooser)]
    ins += [(item, "h") for item in feed_in + feed_out]
    outs = [
        ((rows, D), f32),
        ((rows, D), f32),
        ((rows, 1), f32),
        ((rows, HALF), bf16),
        ((rows, HALF + units), bf16),
        ((rows, units), bf16),
        ((rows, D), bf16),
        ((1, 128), f32),
    ]
    scratch = [
        pltpu.VMEM((D, units), bf16),
        pltpu.VMEM((units, D), bf16),
        pltpu.SemaphoreType.DMA((2,)),
    ]
    return call(body, ins, outs, scratch, 2 * rows * D * 2 * units, f"feed_forward_{layer}_{side}")


def cross_forward(batch, meta, streams, smalls, chooser, cross_in, cross_bias, cross_out):
    rows = [stream[0].shape[0] for stream in streams]
    width = cross_out.shape[0]
    heads = width // HEAD_DIM

    def body(meta, *refs):
        given = (refs[0:3], refs[3:6])
        small, chooser, in_ref, bias, out_ref = (refs[6:8], *refs[8:12])
        outs = (refs[12:21], refs[21:30])
        in_buffer, out_buffer, sems = refs[30:]
        weights = Weights(meta, 0, ((in_ref, None), (out_ref, None)), (in_buffer, out_buffer), sems)
        lows = []
        for side in (0, 1):
            settled, own, other = given[side]
            state, unit_ref, rstd_ref, squares, selected, pack, qkv, probs, part = outs[side]
            post = small[side][ROW_FEED_POST : ROW_FEED_POST + 3]
            branch = summed(own, other) + post[0:1]
            unit, rstd, result = norm_of(settled[...] + branch, post[1:2], post[2:3])
            unit_ref[...] = unit
            rstd_ref[...] = rstd
            low = result.astype(bf16)
            state[...] = low
            valid = row_valid(meta, side, batch, rows[side])
            squares[0:1] = square_sum(branch, valid)
            squares[1:2] = square_sum(low.astype(f32), valid)
            select_rows(low, chooser, selected, pack)
            lows.append(low)
        entry = weights.get(0)
        for side in (0, 1):
            project(lows[side], entry, bias[0:1], bias[1:2], outs[side][6])
        leave = weights.get(1)
        for side in (0, 1):
            pack, qkv, probs, part = outs[side][5:]
            there = outs[1 - side][6]
            valid = pair_valid(meta, 1 - side, batch, rows[side], rows[1 - side])
            context = pack.at[:, HALF:]
            attend(qkv[0], there[1], there[2], valid, probs, context)
            part[...] = mm(context[...], leave[...]).astype(bf16)

    ins = [(meta, "s")] + [(item, "v") for stream in streams for item in stream]
    ins += [(item, "v") for item in smalls]
    ins += [(chooser, "v"), (cross_in, "h"), (cross_bias, "v"), (cross_out, "h")]
    outs = []
    for side in (0, 1):
        here, there = rows[side], rows[1 - side]
        outs += [
            ((here, D), bf16),
            ((here, D), f32),
            ((here, 1), f32),
            ((2, 128), f32),
            ((here, HALF), bf16),
            ((here, HALF + width), bf16),
            ((3, here, width), bf16),
            ((heads, here, there), bf16),
            ((here, D), bf16),
        ]
    scratch = [
        pltpu.VMEM((3, D, width), bf16),
        pltpu.VMEM((width, D), bf16),
        pltpu.SemaphoreType.DMA((2,)),
    ]
    result = call(
        body, ins, outs, scratch, 2 * sum(rows) * D * 4 * width, "cross_forward"
    )
    return result[:9], result[9:]


def feed_backward(side, layer, batch, meta, top, small, chooser, slope, feed_in, feed_out):
    last = len(top) == 4
    rows, units = slope.shape
    step = units // 4

    def body(meta, *refs):
        given = refs[: len(top)]
        refs = refs[len(top) :]
        small, chooser, slope, in_own, in_other, out_own, out_other = refs[:7]
        grad_ref, selected, pack, part, post_ref, bias_ref = refs[7:13]
        if last:
            result_ref, squares = refs[13:15]
        in_buffer, out_buffer, sems = refs[-3:]
        weights = Weights(
            meta,
            layer,
            ((out_own.at[0, side], out_other.at[0, side]), (in_own.at[0, side], in_other.at[0, side])),
            (out_buffer, in_buffer),
            sems,
        )
        post = small[ROW_FEED_POST : ROW_FEED_POST + 3]
        if last:
            settled, own, other, cotangent = given
            branch = summed(own, other) + post[0:1]
            unit, rstd, result = norm_of(settled[...] + branch, post[1:2], post[2:3])
            low = result.astype(bf16)
            result_ref[...] = low
            valid = row_valid(meta, side, batch, rows)
            squares[0:1] = square_sum(branch, valid)
            squares[1:2] = square_sum(low.astype(f32), valid)
            incoming = cotangent[...].astype(f32) * valid
        else:
            unit_ref, rstd_ref, grad_in, own, other = given
            unit, rstd = unit_ref[...], rstd_ref[...]
            incoming = (grad_in[...] + summed(own, other)).astype(bf16).astype(f32)
        grad = norm_back(unit, rstd, post[1:2], incoming)
        grad_ref[...] = grad
        low = grad.astype(bf16)
        post_ref[0:1] = column_sum(low.astype(f32))
        post_ref[1:2] = column_sum(incoming * unit)
        post_ref[2:3] = column_sum(incoming)
        select_rows(low, chooser, selected, pack)
        leave = weights.get(0)
        for i in range(units // step):
            columns = slice(i * step, (i + 1) * step)
            active = mm_nt(low, leave[columns, :])
            hidden = (active * slope[:, columns].astype(f32)).astype(bf16)
            pack[:, HALF + i * step : HALF + (i + 1) * step] = hidden
            bias_ref[:, columns] = column_sum(hidden.astype(f32))
        part[...] = mm_nt(pack[:, HALF:], weights.get(1)[...]).astype(bf16)

    ins = [(meta, "s")] + [(a, "v") for a in top] + [(a, "v") for a in (small, chooser, slope)]
    ins += [(item, "h") for item in feed_in + feed_out]
    outs = [
        ((rows, D), f32),
        ((rows, HALF), bf16),
        ((rows, HALF + units), bf16),
        ((rows, D), bf16),
        ((3, D), f32),
        ((1, units), f32),
    ]
    if last:
        outs += [((rows, D), bf16), ((2, 128), f32)]
    scratch = [
        pltpu.VMEM((D, units), bf16),
        pltpu.VMEM((units, D), bf16),
        pltpu.SemaphoreType.DMA((2,)),
    ]
    return call(body, ins, outs, scratch, 2 * rows * D * 2 * units, f"feed_backward_{layer}_{side}")


def back_through_norm(top, gain, grad_ref, post_ref):
    unit_ref, rstd_ref, grad_in, own, other = top
    incoming = grad_in[...] + summed(own, other)
    unit = unit_ref[...]
    grad = norm_back(unit, rstd_ref[...], gain, incoming)
    grad_ref[...] = grad
    low = grad.astype(bf16)
    post_ref[0:1] = column_sum(low.astype(f32))
    post_ref[1:2] = column_sum(incoming * unit)
    post_ref[2:3] = column_sum(incoming)
    return low


def emit_into(pack, width):
    def emit(kind, lanes, value):
        start = HALF + kind * width + lanes.start
        pack[:, start : start + PAIR] = value

    return emit


def back_to_input(pack, entry, width):
    grads = [pack[:, HALF + j * width : HALF + (j + 1) * width] for j in range(3)]
    total = mm_nt(grads[0], entry[0]) + mm_nt(grads[1], entry[1]) + mm_nt(grads[2], entry[2])
    return total.astype(bf16)


def self_backward(side, layer, meta, top, small, chooser, qkv, probs, att_in, att_out):
    rows, width = qkv.shape[1:]

    def body(meta, *refs):
        top = refs[:5]
        small, chooser, qkv, probs, in_own, in_other, out_own, out_other = refs[5:13]
        grad_ref, selected, pack, part, post_ref, bias_ref = refs[13:19]
        in_buffer, out_buffer, sems = refs[19:]
        weights = Weights(
            meta,
            layer,
            ((out_own.at[0, side], out_other.at[0, side]), (in_own.at[0, side], in_other.at[0, side])),
            (out_buffer, in_buffer),
            sems,
        )
        low = back_through_norm(top, small[ROW_ATT_POST + 1 : ROW_ATT_POST + 2], grad_ref, post_ref)
        select_rows(low, chooser, selected, pack)
        context = mm_nt(low, weights.get(0)[...]).astype(bf16)
        attend_back(qkv[0], qkv[1], qkv[2], probs, context, emit_into(pack, width))
        bias_ref[0:1] = column_sum(pack[:, HALF : HALF + width].astype(f32))
        bias_ref[1:2] = column_sum(pack[:, HALF + 2 * width :].astype(f32))
        part[...] = back_to_input(pack, weights.get(1), width)

    ins = [(meta, "s")] + [(a, "v") for a in top]
    ins += [(a, "v") for a in (small, chooser, qkv, probs)]
    ins += [(item, "h") for item in att_in + att_out]
    outs = [
        ((rows, D), f32),
        ((rows, HALF), bf16),
        ((rows, HALF + 3 * width), bf16),
        ((rows, D), bf16),
        ((3, D), f32),
        ((2, width), f32),
    ]
    scratch = [
        pltpu.VMEM((3, D, width), bf16),
        pltpu.VMEM((width, D), bf16),
        pltpu.SemaphoreType.DMA((2,)),
    ]
    return call(body, ins, outs, scratch, 2 * rows * D * 6 * width, f"self_backward_{layer}_{side}")


def cross_backward(meta, tops, post, chooser, qkvs, probs, cross_in, cross_out):
    rows = [qkv.shape[1] for qkv in qkvs]
    width = cross_out.shape[0]

    def body(meta, *refs):
        tops = (refs[0:5], refs[5:10])
        post, chooser, qkv_w, qkv_r, probs_w, probs_r, in_ref, out_ref = refs[10:18]
        outs = (refs[18:22], refs[22:26])
        post_out, bias_out, in_buffer, out_buffer, post_each, sems = refs[26:]
        qkvs, probs = (qkv_w, qkv_r), (probs_w, probs_r)
        weights = Weights(meta, 0, ((out_ref, None), (in_ref, None)), (out_buffer, in_buffer), sems)
        lows = []
        for side in (0, 1):
            grad_ref, selected, pack, part = outs[side]
            low = back_through_norm(tops[side], post[1:2], grad_ref, post_each.at[side])
            select_rows(low, chooser, selected, pack)
            lows.append(low)
        post_out[...] = post_each[0] + post_each[1]
        leave = weights.get(0)
        for side in (0, 1):
            here, there = outs[side][2], outs[1 - side][2]
            context = mm_nt(lows[side], leave[...]).astype(bf16)
            to_here, to_there = emit_into(here, width), emit_into(there, width)

            def emit(kind, lanes, value):
                (to_here if kind == 0 else to_there)(kind, lanes, value)

            attend_back(
                qkvs[side][0], qkvs[1 - side][1], qkvs[1 - side][2], probs[side], context, emit
            )
        bias_out[0:1] = sum(
            column_sum(outs[side][2][:, HALF : HALF + width].astype(f32)) for side in (0, 1)
        )
        bias_out[1:2] = sum(
            column_sum(outs[side][2][:, HALF + 2 * width :].astype(f32)) for side in (0, 1)
        )
        entry = weights.get(1)
        for side in (0, 1):
            outs[side][3][...] = back_to_input(outs[side][2], entry, width)

    ins = [(meta, "s")] + [(a, "v") for top in tops for a in top]
    ins += [(post, "v"), (chooser, "v")] + [(a, "v") for a in (*qkvs, *probs)]
    ins += [(cross_in, "h"), (cross_out, "h")]
    outs = []
    for side in (0, 1):
        here = rows[side]
        outs += [
            ((here, D), f32),
            ((here, HALF), bf16),
            ((here, HALF + 3 * width), bf16),
            ((here, D), bf16),
        ]
    outs += [((3, D), f32), ((2, width), f32)]
    scratch = [
        pltpu.VMEM((3, D, width), bf16),
        pltpu.VMEM((width, D), bf16),
        pltpu.VMEM((2, 3, D), f32),
        pltpu.SemaphoreType.DMA((2,)),
    ]
    result = call(body, ins, outs, scratch, 2 * sum(rows) * D * 6 * width, "cross_backward")
    return result[:4], result[4:8], result[8], result[9]


def weight_products(given, names, row_slice=slice(None)):
    in_sel, in_pack, in_got, out_sel, out_pack, out_got = given
    first = mm_tn(in_sel[:, row_slice], out_pack[:, HALF:])
    first += mm_tn(in_got[:, row_slice], out_got[:, HALF:])
    second = mm_tn(out_sel[:, row_slice], in_pack[:, HALF:])
    second += mm_tn(out_got[:, row_slice], in_got[:, HALF:])
    return first, second


def stream_gradients(meta, words, regions, name):
    first = words[4].shape[1] - HALF
    second = words[1].shape[1] - HALF

    def body(meta, *refs):
        streams = (refs[:6], refs[6:12])
        keep, send = refs[12:]
        for side in (0, 1):
            in_sel, in_pack, in_got, out_sel, out_pack, out_got = streams[side]

            def store(target, start, stop, value):
                target[:, start:stop] = value

            for left, right, left_got, right_got, base, size in (
                (in_sel, out_pack, in_got, out_got, 0, first),
                (out_sel, in_pack, out_got, in_got, first, second),
            ):
                step = HALF
                for start in range(0, size, step):
                    columns = slice(HALF + start, HALF + start + step)
                    value = mm_tn(left[...], right[:, columns])
                    value += mm_tn(left_got[:, :HALF], right_got[:, columns])
                    value = value.astype(bf16)
                    begin, end = base + start, base + start + step
                    pl.when(meta[0] == side)(partial(store, keep, begin, end, value))
                    pl.when(meta[0] != side)(partial(store, send, begin, end, value))

    ins = [(meta, "s")] + [(a, "v") for a in (*words, *regions)]
    outs = [((HALF, first + second), bf16)] * 2
    rows = words[0].shape[0] + regions[0].shape[0]
    return call(body, ins, outs, (), 4 * rows * HALF * (first + second), name)


def cross_gradients(words, regions):
    first = words[4].shape[1] - HALF
    second = words[1].shape[1] - HALF
    part = HALF // 2

    def body(*refs):
        streams = (refs[:6], refs[6:12])
        keep, send = refs[12:]
        for start in range(0, first + second, HALF):
            value = 0.0
            for in_sel, in_pack, in_got, out_sel, out_pack, out_got in streams:
                if start < first:
                    left, right, left_got, right_got = in_sel, out_pack, in_got, out_got
                    base = start
                else:
                    left, right, left_got, right_got = out_sel, in_pack, out_got, in_got
                    base = start - first
                columns = slice(HALF + base, HALF + base + HALF)
                value += mm_tn(left[...], right[:, columns])
                value += mm_tn(left_got[:, :HALF], right_got[:, columns])
            value = value.astype(bf16)
            keep[:, start : start + HALF] = value[:part]
            send[:, start : start + HALF] = value[part:]

    ins = [(a, "v") for a in (*words, *regions)]
    outs = [((part, first + second), bf16)] * 2
    rows = words[0].shape[0] + regions[0].shape[0]
    return call(body, ins, outs, (), 4 * rows * HALF * (first + second), "cross_gradients")


def swap(value, axis, distance=1):
    count = lax.axis_size(axis)
    return lax.ppermute(value, axis, [(i, i ^ distance) for i in range(count)])


def on_device(
    word_state,
    region_state,
    word_lengths,
    region_counts,
    word_cotangent,
    region_cotangent,
    cross_in,
    cross_bias,
    cross_out,
    cross_post,
    attention_in,
    attention_bias,
    attention_out,
    attention_post,
    feed_in,
    feed_bias,
    feed_out,
    feed_post,
):
    section = lax.axis_index("section")
    dp_count = lax.axis_size("dp")
    groups = dp_count // 2
    place = lax.axis_index("dp") % 2
    batch = word_state.shape[1]
    width = cross_out.shape[0]
    units = feed_in.shape[-1]
    both = (0, 1)
    chain = [[2 * z + y for z in range(groups)] for y in both]

    def flat(value):
        own = lax.dynamic_index_in_dim(value, section, 0, keepdims=False)
        return own.transpose(1, 0, 2).reshape(-1, D)

    def unflat(value):
        return value.reshape(-1, batch, D).transpose(1, 0, 2)[None]

    def chooser_of(pieces, per_section):
        column = jnp.arange(D)
        half = column // HALF
        inner = column % HALF
        side = jnp.where(half == 0, place, 1 - place)
        size = D // pieces
        if per_section:
            block = inner // (HALF // 2)
            inner = inner % (HALF // 2)
            block = jnp.where(block == 0, section, 1 - section)
            feature = size * (dp_count * block + 2 * (inner // size) + side) + inner % size
        else:
            feature = size * (2 * (inner // size) + side) + inner % size
        return (jnp.arange(D)[:, None] == feature[None, :]).astype(bf16)

    chooser = chooser_of(dp_count, False)
    cross_chooser = chooser_of(2 * dp_count, True)

    small_own = jnp.concatenate(
        [
            attention_bias[0].reshape(2, 1, D),
            attention_post[0],
            feed_bias[0].reshape(2, -1, D),
            feed_post[0],
            jnp.zeros((2, SMALL_ROWS - 9, D), f32),
        ],
        axis=1,
    )
    small_other = swap(small_own, "section")
    smalls = [
        jnp.where(section == layer, small_own, small_other) for layer in both
    ]
    att_in_own = attention_in.transpose(0, 1, 3, 2, 4)
    att_in = (att_in_own, swap(att_in_own, "section"))
    att_out = (attention_out, swap(attention_out, "section"))
    ff_in = (feed_in, swap(feed_in, "section"))
    ff_out = (feed_out, swap(feed_out, "section"))
    cross_entry = cross_in.transpose(1, 0, 2)

    lengths = [
        lax.dynamic_index_in_dim(value, section, 0, keepdims=False)
        for value in (word_lengths, region_counts)
    ]
    meta = jnp.concatenate([section[None].astype(jnp.int32), *lengths])
    states = [flat(word_state), flat(region_state)]
    cotangents = [flat(word_cotangent), flat(region_cotangent)]
    small = [[smalls[layer][side] for side in both] for layer in both]

    self0 = [
        self_forward(side, 0, batch, meta, states[side], None, small[0][side], chooser, att_in, att_out)
        for side in both
    ]
    got = [swap(self0[side][4], "mp") for side in both]
    feed0 = [
        feed_forward(
            side, 0, batch, meta, states[side], self0[side][4], got[side], small[0][side], chooser, ff_in, ff_out
        )
        for side in both
    ]
    got = [swap(feed0[side][6], "mp") for side in both]
    cross = cross_forward(
        batch,
        meta,
        [(feed0[side][0], feed0[side][6], got[side]) for side in both],
        small[0],
        cross_chooser,
        cross_entry,
        cross_bias,
        cross_out,
    )
    got = [swap(cross[side][8], "mp") for side in both]
    self1 = [
        self_forward(
            side,
            1,
            batch,
            meta,
            cross[side][0],
            (cross[side][8], got[side], cross_post),
            small[1][side],
            chooser,
            att_in,
            att_out,
        )
        for side in both
    ]
    got = [swap(self1[side][4], "mp") for side in both]
    feed1 = [
        feed_forward(
            side, 1, batch, meta, self1[side][6], self1[side][4], got[side], small[1][side], chooser, ff_in, ff_out
        )
        for side in both
    ]
    got = [swap(feed1[side][6], "mp") for side in both]
    feed1_there = [swap(feed1[side][4], "dp") for side in both]

    back_feed1 = [
        feed_backward(
            side,
            1,
            batch,
            meta,
            (feed1[side][0], feed1[side][6], got[side], cotangents[side]),
            small[1][side],
            chooser,
            feed1[side][5],
            ff_in,
            ff_out,
        )
        for side in both
    ]
    got = [swap(back_feed1[side][3], "mp") for side in both]
    back_feed1_there = [swap(back_feed1[side][2], "dp") for side in both]

    def gathered(fronts, front_index, there, backs, back_there):
        return [
            (
                fronts[side][front_index],
                fronts[side][front_index + 1],
                there[side],
                backs[side][1],
                backs[side][2],
                back_there[side],
            )
            for side in both
        ]

    def combined(pair):
        keep, send = pair
        return keep.astype(f32) + swap(send, "section").astype(f32)

    def scatter(value):
        return lax.psum_scatter(
            value, "dp", scatter_dimension=0, axis_index_groups=chain, tiled=True
        )

    feed1_total = combined(
        stream_gradients(
            meta, *gathered(feed1, 3, feed1_there, back_feed1, back_feed1_there), "feed_gradients_1"
        )
    ).astype(bf16)
    feed1_share = scatter(feed1_total)

    self1_there = [swap(self1[side][3], "dp") for side in both]
    back_self1 = [
        self_backward(
            side,
            1,
            meta,
            (feed1[side][1], feed1[side][2], back_feed1[side][0], back_feed1[side][3], got[side]),
            small[1][side],
            chooser,
            self1[side][0],
            self1[side][1],
            att_in,
            att_out,
        )
        for side in both
    ]
    got = [swap(back_self1[side][3], "mp") for side in both]
    back_self1_there = [swap(back_self1[side][2], "dp") for side in both]
    self1_total = combined(
        stream_gradients(
            meta, *gathered(self1, 2, self1_there, back_self1, back_self1_there), "self_gradients_1"
        )
    )

    cross_there = [swap(cross[side][5], "dp") for side in both]
    back_cross_w, back_cross_r, cross_post_grad, cross_bias_grad = cross_backward(
        meta,
        [
            (self1[side][7], self1[side][8], back_self1[side][0], back_self1[side][3], got[side])
            for side in both
        ],
        cross_post,
        cross_chooser,
        [cross[side][6] for side in both],
        [cross[side][7] for side in both],
        cross_entry,
        cross_out,
    )
    back_cross = (back_cross_w, back_cross_r)
    got = [swap(back_cross[side][3], "mp") for side in both]
    back_cross_there = [swap(back_cross[side][2], "dp") for side in both]
    cross_total = combined(
        cross_gradients(*gathered(cross, 4, cross_there, back_cross, back_cross_there))
    )
    chunk = D // dp_count
    late1 = jnp.concatenate(
        [
            self1_total.reshape(groups, chunk, 4 * width),
            cross_total.reshape(groups, chunk // 2, 4 * width),
        ],
        axis=1,
    ).astype(bf16)
    late1_share = scatter(late1.reshape(-1, 4 * width))

    feed0_there = [swap(feed0[side][4], "dp") for side in both]
    back_feed0 = [
        feed_backward(
            side,
            0,
            batch,
            meta,
            (cross[side][1], cross[side][2], back_cross[side][0], back_cross[side][3], got[side]),
            small[0][side],
            chooser,
            feed0[side][5],
            ff_in,
            ff_out,
        )
        for side in both
    ]
    got = [swap(back_feed0[side][3], "mp") for side in both]
    back_feed0_there = [swap(back_feed0[side][2], "dp") for side in both]
    feed0_total = combined(
        stream_gradients(
            meta, *gathered(feed0, 3, feed0_there, back_feed0, back_feed0_there), "feed_gradients_0"
        )
    )
    self0_there = [swap(self0[side][3], "dp") for side in both]
    back_self0 = [
        self_backward(
            side,
            0,
            meta,
            (feed0[side][1], feed0[side][2], back_feed0[side][0], back_feed0[side][3], got[side]),
            small[0][side],
            chooser,
            self0[side][0],
            self0[side][1],
            att_in,
            att_out,
        )
        for side in both
    ]
    got = [swap(back_self0[side][3], "mp") for side in both]
    back_self0_there = [swap(back_self0[side][2], "dp") for side in both]
    self0_total = combined(
        stream_gradients(
            meta, *gathered(self0, 2, self0_there, back_self0, back_self0_there), "self_gradients_0"
        )
    )
    layer0_share = scatter(jnp.concatenate([feed0_total, self0_total], axis=1).astype(bf16))

    state_grads = [
        (back_self0[side][0] + (back_self0[side][3].astype(f32) + got[side].astype(f32))).astype(bf16)
        for side in both
    ]

    def packed(back_self, back_feed, squares):
        rows = [
            back_self[side][5].reshape(1, D) for side in both
        ] + [
            back_self[side][4] for side in both
        ] + [
            back_feed[side][5].reshape(-1, D) for side in both
        ] + [back_feed[side][4] for side in both]
        row = jnp.concatenate([value.reshape(1, 128) for value in squares[:6]], axis=1)
        rest = jnp.concatenate([value.reshape(1, 128) for value in squares[6:]], axis=1)
        rest = jnp.concatenate([rest, jnp.zeros((1, D - rest.shape[1]), f32)], axis=1)
        return jnp.concatenate(rows + [row, rest], axis=0)

    def squares_of(lead, second, tail):
        result = []
        for side in both:
            result += [lead[side], second[side], tail[side][0:1], tail[side][1:2]]
        return result

    packs = [
        packed(
            back_self0,
            back_feed0,
            squares_of(
                [self0[side][5] for side in both],
                [feed0[side][7] for side in both],
                [cross[side][3] for side in both],
            ),
        ),
        packed(
            back_self1,
            back_feed1,
            squares_of(
                [self1[side][5] for side in both],
                [feed1[side][7] for side in both],
                [back_feed1[side][7] for side in both],
            ),
        ),
    ]
    counts = jnp.stack([jnp.sum(word_lengths), jnp.sum(region_counts)]).astype(f32)
    counts = jnp.pad(counts, (0, D - 2))[None] * 0.5
    mine = jnp.where(section == 0, packs[0], packs[1])
    theirs = jnp.where(section == 0, packs[1], packs[0])
    shared = [cross_post_grad, cross_bias_grad.reshape(1, D), counts]
    small_rows = packs[0].shape[0]
    total = jnp.concatenate([mine] + shared, axis=0) + swap(
        jnp.concatenate([theirs] + shared, axis=0), "section"
    )
    distance = 1
    while distance < dp_count:
        total = total + swap(total, "dp", distance)
        distance *= 2
    unit_rows = units // D
    at = 0
    att_bias_grad = total[0:2].reshape(1, 2, 2, width)
    at = 2
    att_post_grad = total[at : at + 6].reshape(1, 2, 3, D)
    at += 6
    feed_bias_grad = total[at : at + 2 * unit_rows].reshape(1, 2, units)
    at += 2 * unit_rows
    feed_post_grad = total[at : at + 6].reshape(1, 2, 3, D)
    at += 6
    squares = total[at : at + 2].reshape(-1, 128)[:8, 0]
    at = small_rows
    cross_post_total = total[at : at + 3]
    cross_bias_total = total[at + 3].reshape(2, width)
    valid_counts = total[at + 4, :2]
    scales = jnp.sqrt(squares / (jnp.repeat(valid_counts, 4) * D))[None]

    layer1_share = jnp.concatenate([feed1_share, late1_share[:chunk]], axis=1)
    late_words = lax.ppermute(layer1_share, "section", [(0, 1)])
    late_regions = lax.ppermute(layer0_share, "section", [(1, 0)])
    words_grad = jnp.where(section == 0, layer0_share, late_words)
    regions_grad = jnp.where(section == 0, late_regions, layer1_share)

    def stacked(start, stop):
        return jnp.stack([words_grad[:, start:stop], regions_grad[:, start:stop]]).astype(f32)

    feed_in_grad = stacked(0, units)[None]
    feed_out_grad = stacked(units, 2 * units).transpose(0, 2, 1)[None]
    base = 2 * units
    att_in_grad = stacked(base, base + 3 * width).reshape(2, chunk, 3, width)[None]
    att_out_grad = stacked(base + 3 * width, base + 4 * width).transpose(0, 2, 1)[None]
    cross_share = late1_share[chunk:].astype(f32)
    cross_in_grad = cross_share[:, : 3 * width].reshape(-1, 3, width)
    cross_out_grad = cross_share[:, 3 * width :].T
    return (
        unflat(back_feed1[0][6]),
        unflat(back_feed1[1][6]),
        unflat(state_grads[0]),
        unflat(state_grads[1]),
        cross_in_grad,
        cross_bias_total,
        cross_out_grad,
        cross_post_total,
        att_in_grad,
        att_bias_grad,
        att_out_grad,
        att_post_grad,
        feed_in_grad,
        feed_bias_grad,
        feed_out_grad,
        feed_post_grad,
        scales,
    )


def solution(mesh):
    placed = (
        P(None, "dp", None, None),
        P(None, "dp", None, None),
        P(None, "dp"),
        P(None, "dp"),
        P(None, "dp", None, None),
        P(None, "dp", None, None),
        P(None, None, "mp"),
        P(None, "mp"),
        P("mp", None),
        P(),
        P("section", None, None, None, "mp"),
        P("section", None, None, "mp"),
        P("section", None, "mp", None),
        P("section", None, None, None),
        P("section", None, None, "mp"),
        P("section", None, "mp"),
        P("section", None, "mp", None),
        P("section", None, None, None),
    )
    return jax.shard_map(
        on_device,
        mesh=mesh,
        in_specs=placed,
        out_specs=(
            P("section", "dp", None, None),
            P("section", "dp", None, None),
            P("section", "dp", None, None),
            P("section", "dp", None, None),
            P(("section", "dp"), None, "mp"),
            P(None, "mp"),
            P("mp", ("section", "dp")),
            P(),
            P("section", None, "dp", None, "mp"),
            P("section", None, None, "mp"),
            P("section", None, "mp", "dp"),
            P("section", None, None, None),
            P("section", None, "dp", "mp"),
            P("section", None, "mp"),
            P("section", None, "mp", "dp"),
            P("section", None, None, None),
            P("section", None),
        ),
        check_vma=False,
    )
```

```python
from functools import partial

import jax
import jax.numpy as jnp
from jax import lax
from jax.experimental import pallas as pl
from jax.experimental.pallas import tpu as pltpu
from jax.sharding import PartitionSpec as P

D = 768
HALF = D // 2
HEAD_DIM = 64
PAIR = 2 * HEAD_DIM
WORDS = 20
REGIONS = 36
EPS = 1e-06
SCALE = HEAD_DIM**-0.5
bf16 = jnp.bfloat16
f32 = jnp.float32

ROW_ATT_BIAS, ROW_ATT_POST, ROW_FEED_BIAS, ROW_FEED_POST, SMALL_ROWS = 0, 1, 4, 6, 16


def mm(a, b):
    return jnp.dot(a, b, preferred_element_type=f32)


def mm_nt(a, b):
    return lax.dot_general(a, b, (((1,), (1,)), ((), ())), preferred_element_type=f32)


def mm_tn(a, b):
    return lax.dot_general(a, b, (((0,), (0,)), ((), ())), preferred_element_type=f32)


def norm_of(value, gain, shift):
    centred = value - jnp.mean(value, axis=-1, keepdims=True)
    spread = jnp.mean(centred * centred, axis=-1, keepdims=True)
    rstd = lax.rsqrt(spread + EPS)
    unit = centred * rstd
    return unit, rstd, unit * gain + shift


def norm_back(unit, rstd, gain, incoming):
    scaled = incoming * gain
    mean = jnp.mean(scaled, axis=-1, keepdims=True)
    along = jnp.mean(scaled * unit, axis=-1, keepdims=True)
    return (scaled - mean - unit * along) * rstd


def summed(own, other):
    return own[...].astype(f32) + other[...].astype(f32)


def column_sum(value):
    return jnp.sum(value, axis=0, keepdims=True)


def square_sum(value, valid):
    rows = jnp.sum(value * value, axis=-1, keepdims=True) * valid
    return jnp.broadcast_to(jnp.sum(rows, axis=0, keepdims=True), (1, 128))


def lengths_of(meta, side, batch, item):
    result = jnp.zeros_like(item)
    for i in range(batch):
        result = jnp.where(item == i, meta[1 + side * batch + i], result)
    return result


def row_valid(meta, side, batch, rows):
    index = lax.broadcasted_iota(jnp.int32, (rows, 1), 0)
    length = lengths_of(meta, side, batch, lax.rem(index, batch))
    return (lax.div(index, batch) < length).astype(f32)


def pair_valid(meta, side, batch, rows, keys):
    index = lax.broadcasted_iota(jnp.int32, (1, keys), 1)
    item = lax.rem(index, batch)
    length = lengths_of(meta, side, batch, item)
    item = jnp.where(lax.div(index, batch) < length, item, -1)
    row_item = lax.rem(lax.broadcasted_iota(jnp.int32, (rows, 1), 0), batch)
    return jnp.broadcast_to(row_item, (rows, keys)) == jnp.broadcast_to(item, (rows, keys))


def head_lanes(head):
    lane = lax.broadcasted_iota(jnp.int32, (1, PAIR), 1)
    return (lane // HEAD_DIM) == head


def attend(query, keys, values, valid, probs_ref, context_ref):
    for pair in range(query.shape[1] // PAIR):
        lanes = slice(pair * PAIR, (pair + 1) * PAIR)
        contexts = []
        for head in range(2):
            chosen = query[:, lanes] * head_lanes(head).astype(bf16)
            scores = mm_nt(chosen, keys[:, lanes]) * SCALE
            scores = jnp.where(valid, scores, -1e9)
            shifted = jnp.exp(scores - jnp.max(scores, axis=-1, keepdims=True))
            total = jnp.sum(shifted, axis=-1, keepdims=True)
            probs = (shifted * (1.0 / total)).astype(bf16)
            probs_ref[2 * pair + head] = probs
            contexts.append(mm(probs, values[:, lanes]))
        context_ref[:, lanes] = jnp.where(head_lanes(0), contexts[0], contexts[1]).astype(bf16)


def attend_back(query, keys, values, probs_ref, grad_context, emit):
    first = head_lanes(0)
    for pair in range(query.shape[1] // PAIR):
        lanes = slice(pair * PAIR, (pair + 1) * PAIR)
        grads = ([], [], [])
        for head in range(2):
            probs = probs_ref[2 * pair + head]
            chosen = grad_context[:, lanes] * head_lanes(head).astype(bf16)
            grad_probs = mm_nt(chosen, values[:, lanes])
            wide = probs.astype(f32)
            product = wide * grad_probs
            grad_scores = product - wide * jnp.sum(product, axis=-1, keepdims=True)
            grad_scores = grad_scores.astype(bf16)
            grads[0].append(mm(grad_scores, keys[:, lanes]) * SCALE)
            grads[1].append(mm_tn(grad_scores, query[:, lanes]) * SCALE)
            grads[2].append(mm_tn(probs, grad_context[:, lanes]))
        for kind in range(3):
            emit(kind, lanes, jnp.where(first, grads[kind][0], grads[kind][1]).astype(bf16))


class Fetched:
    def __init__(self, copy, buffer):
        self.copy, self.buffer, self.waited = copy, buffer, False
        self.shape, self.dtype = buffer.shape, buffer.dtype

    def wait(self):
        if not self.waited:
            self.copy.wait()
            self.waited = True
        return self.buffer

    def __getitem__(self, index):
        return self.wait()[index]


class Weights:
    def __init__(self, meta, layer, pairs, buffers, sems):
        self.copies = []
        mine = meta[0] == layer
        at = 0
        for (own, other, pieces), buffer in zip(pairs, buffers):
            copies = []
            for piece in pieces:
                copy = pltpu.make_async_copy(own.at[piece], buffer.at[piece], sems.at[at])
                if other is None:
                    copy.start()
                else:
                    second = pltpu.make_async_copy(
                        other.at[piece], buffer.at[piece], sems.at[at]
                    )
                    pl.when(mine)(copy.start)
                    pl.when(jnp.logical_not(mine))(second.start)
                copies.append(Fetched(copy, buffer))
                at += 1
            self.copies.append(copies)

    def get(self, slot, piece=None):
        copies = self.copies[slot]
        for copy in copies if piece is None else (copies[piece],):
            copy.wait()
        return copies[0].buffer


def maps(own, other, side, pieces=((),)):
    if other is None:
        return own, None, pieces
    return own.at[0, side], other.at[0, side], pieces


ENTRY = ((0,), (1,), (2,))


def column_pieces(size, count):
    return tuple(
        (slice(None), slice(i * size // count, (i + 1) * size // count)) for i in range(count)
    )


def row_pieces(size, count):
    return tuple((slice(i * size // count, (i + 1) * size // count),) for i in range(count))


def call(body, ins, outs, scratch=(), flops=0, name=None, ties=()):
    spaces = {"s": pltpu.SMEM, "v": pltpu.VMEM, "w": pltpu.HBM, "h": pltpu.HBM}
    extra = [(i, out[5]) for i, out in enumerate(outs) if len(out) > 3 and out[5] is not None]
    aliases = {len(ins) + at: i for at, (i, _) in enumerate(extra)}
    ins = list(ins) + [(array, "w") for _, array in extra]
    places = [out[3:5] if len(out) > 3 else None for out in outs]
    fetched = [i for i, (_, kind) in enumerate(ins) if kind == "h"]
    written = [i for i, out in enumerate(outs) if out[2] == "h"]
    n_ins, n_ties, n_outs, n_scratch = len(ins), len(ties), len(outs), len(scratch)

    def whole(*refs):
        given = list(refs[:n_ins])
        results = list(refs[n_ins + n_ties : n_ins + n_ties + n_outs])
        rest = refs[n_ins + n_ties + n_outs :]
        own, rest = rest[:n_scratch], rest[n_scratch:]
        buffers, rest = rest[: len(fetched)], rest[len(fetched) :]
        staged, rest = rest[: len(written)], rest[len(written) :]
        sems = rest[0] if rest else None
        for slot, i in enumerate(fetched):
            copy = pltpu.make_async_copy(given[i], buffers[slot], sems.at[slot])
            copy.start()
            given[i] = Fetched(copy, buffers[slot])
        leaving = {}
        for slot, i in enumerate(written):
            target = results[i]
            if places[i] is not None:
                target = target.at[pl.ds(places[i][1], staged[slot].shape[0])]
            copy = pltpu.make_async_copy(staged[slot], target, sems.at[len(fetched) + slot])
            leaving[id(staged[slot])] = copy
            results[i] = staged[slot]
        started = []

        def flush(*done):
            for ref in done:
                copy = leaving.pop(id(ref), None)
                if copy is not None:
                    copy.start()
                    started.append(copy)

        body(flush, *given[: n_ins - len(extra)], *results, *own)
        flush(*[staged[slot] for slot in range(len(written))])
        for copy in started:
            copy.wait()
        for item in given:
            if isinstance(item, Fetched):
                item.wait()

    arrays = [
        pltpu.with_memory_space_constraint(array, spaces[kind]) if kind in "vwh" else array
        for array, kind in ins
    ]
    total = sum(a.size * a.dtype.itemsize for a in arrays)
    own_scratch = list(scratch)
    own_scratch += [pltpu.VMEM(arrays[i].shape, arrays[i].dtype) for i in fetched]
    own_scratch += [pltpu.VMEM(outs[i][0], outs[i][1]) for i in written]
    if fetched or written:
        own_scratch.append(pltpu.SemaphoreType.DMA((len(fetched) + len(written),)))
    tie_space = [pltpu.HBM if tie.size > 32768 else pl.ANY for tie in ties]
    return pl.pallas_call(
        whole,
        out_shape=[
            spaces[out[2]]((out[3], *out[0][1:]) if len(out) > 3 else out[0], out[1]) for out in outs
        ],
        in_specs=[pl.BlockSpec(memory_space=spaces[kind]) for _, kind in ins]
        + [pl.BlockSpec(memory_space=space) for space in tie_space],
        out_specs=[pl.BlockSpec(memory_space=spaces[out[2]]) for out in outs],
        input_output_aliases=aliases,
        scratch_shapes=own_scratch,
        compiler_params=pltpu.CompilerParams(vmem_limit_bytes=28 * 1024 * 1024),
        cost_estimate=pl.CostEstimate(
            flops=int(flops), bytes_accessed=int(total), transcendentals=0
        ),
        name=name,
    )(*arrays, *ties)


def spans_of(rows):
    return slice(0, rows[0]), slice(rows[0], rows[0] + rows[1])


def select_rows(value, chooser, own_ref, pack_ref):
    moved = mm(value, chooser[...]).astype(bf16)
    own_ref[...] = moved[:, :HALF]
    pack_ref[:, :HALF] = moved[:, HALF:]


def project(low, weights, bias_q, bias_v, qkv_ref):
    qkv_ref[0] = (mm(low, weights.get(0, 0)[0]) + bias_q).astype(bf16)
    qkv_ref[1] = mm(low, weights.get(0, 1)[1]).astype(bf16)
    qkv_ref[2] = (mm(low, weights.get(0, 2)[2]) + bias_v).astype(bf16)


def self_forward(
    side, layer, batch, meta, state, prior, small, chooser, att_in, att_out, place, ties=()
):
    rows = state.shape[0]
    width = att_in[0].shape[-1]
    first = prior is None

    def body(flush, meta, state, *refs):
        refs = list(refs)
        if not first:
            own, other, post = refs[:3]
            refs = refs[3:]
        small, chooser, in_own, in_other, out_own, out_other = refs[:6]
        qkv, probs, selected, pack, part, squares = refs[6:12]
        refs = refs[12:]
        if not first:
            mixed_ref, unit_ref, rstd_ref = refs[:3]
            refs = refs[3:]
        in_buffer, out_buffer, sems = refs
        weights = Weights(
            meta,
            layer,
            (maps(in_own, in_other, side, ENTRY), maps(out_own, out_other, side)),
            (in_buffer, out_buffer),
            sems,
        )
        valid = row_valid(meta, side, batch, rows)
        if first:
            low = state[...]
            squares[...] = square_sum(low.astype(f32), valid)
        else:
            branch = summed(own, other) + post[0:1]
            squares[...] = square_sum(branch, valid)
            unit, rstd, mixed = norm_of(state[...].astype(f32) + branch, post[1:2], post[2:3])
            unit_ref[...] = unit
            rstd_ref[...] = rstd
            mixed_ref[...] = mixed
            low = mixed.astype(bf16)
        select_rows(low, chooser, selected, pack)
        flush(selected)
        biases = small[ROW_ATT_BIAS : ROW_ATT_BIAS + 1]
        project(low, weights, biases[:, :width], biases[:, width : 2 * width], qkv)
        context = pack.at[:, HALF:]
        attend(
            qkv[0], qkv[1], qkv[2], pair_valid(meta, side, batch, rows, rows), probs, context
        )
        flush(qkv, probs, pack)
        part[...] = mm(context[...], weights.get(1)[...]).astype(bf16)

    ins = [(meta, "s"), (state, "v")]
    if not first:
        ins += list(zip(prior, "vvv"))
    ins += [(small, "v"), (chooser, "v")] + [(item, "w") for item in att_in + att_out]
    outs = [
        ((3, rows, width), bf16, "h"),
        ((width // HEAD_DIM, rows, rows), bf16, "h"),
        ((rows, HALF), bf16, "h"),
        ((rows, HALF + width), bf16, "h", *place),
        ((rows, D), bf16, "v"),
        ((1, 128), f32, "h"),
    ]
    if not first:
        outs += [((rows, D), f32, "v"), ((rows, D), f32, "h"), ((rows, 1), f32, "h")]
    scratch = [
        pltpu.VMEM((3, D, width), bf16),
        pltpu.VMEM((width, D), bf16),
        pltpu.SemaphoreType.DMA((6,)),
    ]
    flops = 2 * rows * D * 5 * width
    return call(body, ins, outs, scratch, flops, f"self_forward_{layer}_{side}", ties)


def feed_forward(
    side, layer, batch, meta, residual, own, other, small, chooser, feed_in, feed_out, place, ties=()
):
    rows = residual.shape[0]
    units = feed_in[0].shape[-1]
    step = units // 4

    def body(
        flush, meta, residual, own, other, small, chooser, in_own, in_other, out_own, out_other,
        settled_ref, unit_ref, rstd_ref, selected, pack, slope, part, squares,
        in_buffer, out_buffer, sems,
    ):
        weights = Weights(
            meta,
            layer,
            (
                maps(in_own, in_other, side, column_pieces(units, 4)),
                maps(out_own, out_other, side, row_pieces(units, 2)),
            ),
            (in_buffer, out_buffer),
            sems,
        )
        post = small[ROW_ATT_POST : ROW_ATT_POST + 3]
        branch = summed(own, other) + post[0:1]
        squares[...] = square_sum(branch, row_valid(meta, side, batch, rows))
        unit, rstd, settled = norm_of(residual[...].astype(f32) + branch, post[1:2], post[2:3])
        unit_ref[...] = unit
        rstd_ref[...] = rstd
        settled_ref[...] = settled
        low = settled.astype(bf16)
        select_rows(low, chooser, selected, pack)
        flush(unit_ref, rstd_ref, selected)
        for i in range(units // step):
            first = weights.get(0, i)
            columns = slice(i * step, (i + 1) * step)
            row = ROW_FEED_BIAS + (i * step) // D
            place = (i * step) % D
            hidden = mm(low, first[:, columns]) + small[row : row + 1, place : place + step]
            below = 0.5 + 0.5 * lax.erf(hidden * (0.5**0.5))
            density = jnp.exp(hidden * hidden * -0.5) * 0.3989422804014327
            pack[:, HALF + i * step : HALF + (i + 1) * step] = (hidden * below).astype(bf16)
            slope[:, columns] = (below + hidden * density).astype(bf16)
        flush(pack, slope)
        part[...] = mm(pack[:, HALF:], weights.get(1)[...]).astype(bf16)

    ins = [(meta, "s"), (residual, "v"), (own, "v"), (other, "v")]
    ins += [(small, "v"), (chooser, "v")] + [(item, "w") for item in feed_in + feed_out]
    outs = [
        ((rows, D), f32, "v"),
        ((rows, D), f32, "h"),
        ((rows, 1), f32, "h"),
        ((rows, HALF), bf16, "h"),
        ((rows, HALF + units), bf16, "h", *place),
        ((rows, units), bf16, "h"),
        ((rows, D), bf16, "v"),
        ((1, 128), f32, "h"),
    ]
    scratch = [
        pltpu.VMEM((D, units), bf16),
        pltpu.VMEM((units, D), bf16),
        pltpu.SemaphoreType.DMA((6,)),
    ]
    flops = 2 * rows * D * 2 * units
    return call(body, ins, outs, scratch, flops, f"feed_forward_{layer}_{side}", ties)


def cross_forward(
    batch, meta, streams, smalls, chooser, cross_in, cross_bias, cross_out, ties=()
):
    rows = [stream[0].shape[0] for stream in streams]
    spans = spans_of(rows)
    width = cross_out.shape[0]
    heads = width // HEAD_DIM

    def body(flush, meta, *refs):
        given = (refs[0:3], refs[3:6])
        small, chooser, in_ref, bias, out_ref = (refs[6:8], *refs[8:12])
        all_pack = refs[28]
        outs = [refs[12:20], refs[20:28]]
        for side in (0, 1):
            outs[side] = outs[side][:5] + (all_pack.at[spans[side]],) + outs[side][5:]
        in_buffer, out_buffer, sems = refs[29:]
        weights = Weights(
            meta,
            0,
            (maps(in_ref, None, 0, ENTRY), maps(out_ref, None, 0)),
            (in_buffer, out_buffer),
            sems,
        )
        lows = []
        for side in (0, 1):
            settled, own, other = given[side]
            state, unit_ref, rstd_ref, squares, selected, pack, qkv, probs, part = outs[side]
            post = small[side][ROW_FEED_POST : ROW_FEED_POST + 3]
            branch = summed(own, other) + post[0:1]
            unit, rstd, result = norm_of(settled[...] + branch, post[1:2], post[2:3])
            unit_ref[...] = unit
            rstd_ref[...] = rstd
            low = result.astype(bf16)
            state[...] = low
            valid = row_valid(meta, side, batch, rows[side])
            squares[0:1] = square_sum(branch, valid)
            squares[1:2] = square_sum(low.astype(f32), valid)
            select_rows(low, chooser, selected, pack)
            flush(unit_ref, rstd_ref, selected)
            lows.append(low)
        for side in (0, 1):
            project(lows[side], weights, bias[0:1], bias[1:2], outs[side][6])
        leave = weights.get(1)
        for side in (0, 1):
            pack, qkv, probs, part = outs[side][5:]
            there = outs[1 - side][6]
            valid = pair_valid(meta, 1 - side, batch, rows[side], rows[1 - side])
            context = pack.at[:, HALF:]
            attend(qkv[0], there[1], there[2], valid, probs, context)
            flush(qkv, probs)
            part[...] = mm(context[...], leave[...]).astype(bf16)

    ins = [(meta, "s")] + [(item, "v") for stream in streams for item in stream]
    ins += [(item, "v") for item in smalls]
    ins += [(chooser, "v"), (cross_in, "w"), (cross_bias, "v"), (cross_out, "w")]
    outs = []
    for side in (0, 1):
        here, there = rows[side], rows[1 - side]
        outs += [
            ((here, D), bf16, "v"),
            ((here, D), f32, "h"),
            ((here, 1), f32, "h"),
            ((2, 128), f32, "h"),
            ((here, HALF), bf16, "h"),
            ((3, here, width), bf16, "h"),
            ((heads, here, there), bf16, "h"),
            ((here, D), bf16, "v"),
        ]
    outs.append(((sum(rows), HALF + width), bf16, "h"))
    scratch = [
        pltpu.VMEM((3, D, width), bf16),
        pltpu.VMEM((width, D), bf16),
        pltpu.SemaphoreType.DMA((6,)),
    ]
    flops = 2 * sum(rows) * D * 4 * width
    result = call(body, ins, outs, scratch, flops, "cross_forward", ties)
    return result[:8], result[8:16], result[16]


def feed_backward(
    layer, batch, meta, tops, joint, small, chooser, slopes, feed_in, feed_out, ties=()
):
    last = joint is None
    rows = [slope.shape[0] for slope in slopes]
    units = slopes[0].shape[1]
    spans, total = spans_of(rows), sum(rows)
    step = units // 4
    n_top = len(tops[0])

    def body(flush, meta, *refs):
        given = (refs[:n_top], refs[n_top : 2 * n_top])
        refs = refs[2 * n_top :]
        if not last:
            joint, refs = refs[:3], refs[3:]
        small, chooser, slopes = refs[:2], refs[2], refs[3:5]
        in_own, in_other, out_own, out_other = refs[5:9]
        grad_all, selected_all, pack_all, part_all, post_all, bias_all = refs[9:15]
        if last:
            results, squares_all = refs[15:17], refs[17]
        in_buffer, out_buffer, sems = refs[-3:]
        weights = [
            Weights(
                meta,
                layer,
                (
                    maps(out_own, out_other, side, row_pieces(units, 4)),
                    maps(in_own, in_other, side, column_pieces(units, 2)),
                ),
                (out_buffer.at[side], in_buffer.at[side]),
                sems.at[side],
            )
            for side in (1, 0)
        ][::-1]
        lows = [None, None]
        for side in (1, 0):
            here = spans[side]
            post = small[side][ROW_FEED_POST : ROW_FEED_POST + 3]
            if last:
                settled, own, other, cotangent = given[side]
                branch = summed(own, other) + post[0:1]
                unit, rstd, result = norm_of(settled[...] + branch, post[1:2], post[2:3])
                low = result.astype(bf16)
                results[side][...] = low
                valid = row_valid(meta, side, batch, rows[side])
                squares_all[side, 0:1] = square_sum(branch, valid)
                squares_all[side, 1:2] = square_sum(low.astype(f32), valid)
                incoming = cotangent[...].astype(f32) * valid
            else:
                unit_ref, rstd_ref = given[side]
                unit, rstd = unit_ref[...], rstd_ref[...]
                incoming = (joint[0][here] + summed_rows(joint[1], joint[2], here)).astype(bf16)
                incoming = incoming.astype(f32)
            grad = norm_back(unit, rstd, post[1:2], incoming)
            grad_all[here] = grad
            low = grad.astype(bf16)
            post_all[side, 0:1] = column_sum(low.astype(f32))
            post_all[side, 1:2] = column_sum(incoming * unit)
            post_all[side, 2:3] = column_sum(incoming)
            lows[side] = low
        for side in (1, 0):
            here = spans[side]
            select_rows(lows[side], chooser, selected_all.at[here], pack_all.at[here])
            for i in range(units // step):
                columns = slice(i * step, (i + 1) * step)
                active = mm_nt(lows[side], weights[side].get(0, i)[columns, :])
                hidden = (active * slopes[side][:, columns].astype(f32)).astype(bf16)
                pack_all[here, HALF + i * step : HALF + (i + 1) * step] = hidden
                bias_all[side, :, columns] = column_sum(hidden.astype(f32))
        flush(pack_all, selected_all)
        for side in (1, 0):
            here = spans[side]
            part_all[here] = mm_nt(pack_all[here, HALF:], weights[side].get(1)[...]).astype(bf16)

    ins = [(meta, "s")] + [pair for top in tops for pair in zip(top, "vvvv" if last else "hh")]
    if not last:
        ins += [(item, "v") for item in joint]
    ins += [(item, "v") for item in small] + [(chooser, "v")] + [(item, "h") for item in slopes]
    ins += [(item, "w") for item in feed_in + feed_out]
    outs = [
        ((total, D), f32, "v"),
        ((total, HALF), bf16, "h"),
        ((total, HALF + units), bf16, "h"),
        ((total, D), bf16, "v"),
        ((2, 3, D), f32, "h"),
        ((2, 1, units), f32, "h"),
    ]
    if last:
        outs += [((here, D), bf16, "h") for here in rows] + [((2, 2, 128), f32, "h")]
    scratch = [
        pltpu.VMEM((2, D, units), bf16),
        pltpu.VMEM((2, units, D), bf16),
        pltpu.SemaphoreType.DMA((2, 6)),
    ]
    flops = 2 * total * D * 2 * units
    return call(body, ins, outs, scratch, flops, f"feed_backward_{layer}", ties)


def summed_rows(own, other, here):
    return own[here].astype(f32) + other[here].astype(f32)


def back_through_norm(top, joint, here, gain, grad_all, post_ref):
    unit_ref, rstd_ref = top
    incoming = joint[0][here] + summed_rows(joint[1], joint[2], here)
    unit = unit_ref[...]
    grad = norm_back(unit, rstd_ref[...], gain, incoming)
    grad_all[here] = grad
    low = grad.astype(bf16)
    post_ref[0:1] = column_sum(low.astype(f32))
    post_ref[1:2] = column_sum(incoming * unit)
    post_ref[2:3] = column_sum(incoming)
    return low


def emit_into(pack, width):
    def emit(kind, lanes, value):
        start = HALF + kind * width + lanes.start
        pack[:, start : start + PAIR] = value

    return emit


def back_to_input(pack, weights, slot, width):
    grads = [pack[:, HALF + j * width : HALF + (j + 1) * width] for j in range(3)]
    total = mm_nt(grads[0], weights.get(slot, 0)[0])
    total += mm_nt(grads[1], weights.get(slot, 1)[1])
    total += mm_nt(grads[2], weights.get(slot, 2)[2])
    return total.astype(bf16)


def self_backward(
    layer, meta, tops, joint, small, chooser, qkvs, probs, att_in, att_out, ties=()
):
    rows = [qkv.shape[1] for qkv in qkvs]
    width = qkvs[0].shape[2]
    spans, total = spans_of(rows), sum(rows)

    def body(flush, meta, *refs):
        tops, joint = (refs[:2], refs[2:4]), refs[4:7]
        small, chooser, qkvs, probs = refs[7:9], refs[9], refs[10:12], refs[12:14]
        in_own, in_other, out_own, out_other = refs[14:18]
        grad_all, selected_all, pack_all, part_all, post_all, bias_all = refs[18:24]
        in_buffer, out_buffer, sems = refs[24:]
        weights = [
            Weights(
                meta,
                layer,
                (maps(out_own, out_other, side), maps(in_own, in_other, side, ENTRY)),
                (out_buffer.at[side], in_buffer.at[side]),
                sems.at[side],
            )
            for side in (1, 0)
        ][::-1]
        for side in (1, 0):
            here = spans[side]
            pack = pack_all.at[here]
            gain = small[side][ROW_ATT_POST + 1 : ROW_ATT_POST + 2]
            low = back_through_norm(tops[side], joint, here, gain, grad_all, post_all.at[side])
            select_rows(low, chooser, selected_all.at[here], pack)
            context = mm_nt(low, weights[side].get(0)[...]).astype(bf16)
            qkv = qkvs[side]
            attend_back(qkv[0], qkv[1], qkv[2], probs[side], context, emit_into(pack, width))
            bias_all[side, 0:1] = column_sum(pack[:, HALF : HALF + width].astype(f32))
            bias_all[side, 1:2] = column_sum(pack[:, HALF + 2 * width :].astype(f32))
        flush(pack_all, selected_all)
        for side in (1, 0):
            here = spans[side]
            part_all[here] = back_to_input(pack_all.at[here], weights[side], 1, width)

    ins = [(meta, "s")] + [(item, "h") for top in tops for item in top]
    ins += [(item, "v") for item in joint]
    ins += [(item, "v") for item in small] + [(chooser, "v")]
    ins += [(item, "h") for item in (*qkvs, *probs)]
    ins += [(item, "w") for item in att_in + att_out]
    outs = [
        ((total, D), f32, "v"),
        ((total, HALF), bf16, "h"),
        ((total, HALF + 3 * width), bf16, "h"),
        ((total, D), bf16, "v"),
        ((2, 3, D), f32, "h"),
        ((2, 2, width), f32, "h"),
    ]
    scratch = [
        pltpu.VMEM((2, 3, D, width), bf16),
        pltpu.VMEM((2, width, D), bf16),
        pltpu.SemaphoreType.DMA((2, 6)),
    ]
    flops = 2 * total * D * 6 * width
    return call(body, ins, outs, scratch, flops, f"self_backward_{layer}", ties)


def cross_backward(meta, tops, joint, post, chooser, qkvs, probs, cross_in, cross_out, ties=()):
    rows = [qkv.shape[1] for qkv in qkvs]
    width = cross_out.shape[0]
    spans, total = spans_of(rows), sum(rows)

    def body(flush, meta, *refs):
        tops, joint = (refs[:2], refs[2:4]), refs[4:7]
        post, chooser, qkvs, probs = refs[7], refs[8], refs[9:11], refs[11:13]
        in_ref, out_ref = refs[13:15]
        grad_all, selected_all, pack_all, part_all, post_out, bias_out = refs[15:21]
        in_buffer, out_buffer, post_each, sems = refs[21:]
        weights = Weights(
            meta,
            0,
            (maps(out_ref, None, 0), maps(in_ref, None, 0, ENTRY)),
            (out_buffer, in_buffer),
            sems,
        )
        packs = [pack_all.at[here] for here in spans]
        lows = []
        for side in (0, 1):
            here = spans[side]
            low = back_through_norm(
                tops[side], joint, here, post[1:2], grad_all, post_each.at[side]
            )
            select_rows(low, chooser, selected_all.at[here], packs[side])
            lows.append(low)
        post_out[...] = post_each[0] + post_each[1]
        leave = weights.get(0)
        for side in (0, 1):
            context = mm_nt(lows[side], leave[...]).astype(bf16)
            to_here, to_there = emit_into(packs[side], width), emit_into(packs[1 - side], width)

            def emit(kind, lanes, value):
                (to_here if kind == 0 else to_there)(kind, lanes, value)

            attend_back(
                qkvs[side][0], qkvs[1 - side][1], qkvs[1 - side][2], probs[side], context, emit
            )
        bias_out[0:1] = column_sum(pack_all[:, HALF : HALF + width].astype(f32))
        bias_out[1:2] = column_sum(pack_all[:, HALF + 2 * width :].astype(f32))
        flush(pack_all, selected_all)
        part_all[...] = back_to_input(pack_all, weights, 1, width)

    ins = [(meta, "s")] + [(item, "h") for top in tops for item in top]
    ins += [(item, "v") for item in joint]
    ins += [(post, "v"), (chooser, "v")] + [(a, "h") for a in (*qkvs, *probs)]
    ins += [(cross_in, "w"), (cross_out, "w")]
    outs = [
        ((total, D), f32, "v"),
        ((total, HALF), bf16, "h"),
        ((total, HALF + 3 * width), bf16, "h"),
        ((total, D), bf16, "v"),
        ((3, D), f32, "h"),
        ((2, width), f32, "h"),
    ]
    scratch = [
        pltpu.VMEM((3, D, width), bf16),
        pltpu.VMEM((width, D), bf16),
        pltpu.VMEM((2, 3, D), f32),
        pltpu.SemaphoreType.DMA((6,)),
    ]
    flops = 2 * total * D * 6 * width
    return call(body, ins, outs, scratch, flops, "cross_backward", ties)


class Block:
    def __init__(self, in_selected, in_packs, in_gots, out_selected, out_pack, out_got):
        self.parts = [*in_selected, *in_packs, *in_gots, out_selected, out_pack, out_got]
        self.joined = len(in_packs) == 1
        self.sizes = (out_pack.shape[1] - HALF, in_packs[0].shape[1] - HALF)
        self.rows = [array.shape[0] for array in in_selected]

    def buffers(self):
        return [
            pltpu.VMEM((2 * rows, HALF + size), bf16)
            for rows in self.rows
            for size in (self.sizes[1], self.sizes[0])
        ]

    def fetch(self, refs, buffers, sems, at):
        spans = spans_of(self.rows)
        in_selected, rest = refs[:2], refs[2:]
        if self.joined:
            pack, got, rest = [rest[0]] * 2, [rest[1]] * 2, rest[2:]
        else:
            pack, got, rest = rest[:2], rest[2:4], rest[4:]
        out_selected, out_pack, out_got = rest
        result = []
        for side in (0, 1):
            here, count = spans[side], self.rows[side]
            inner = here if self.joined else slice(0, count)
            per_side = []
            for kind, (selected, own, other, span) in enumerate(
                (
                    (in_selected[side], pack[side].at[inner], got[side].at[inner], None),
                    (out_selected.at[here], out_pack.at[here], out_got.at[here], here),
                )
            ):
                buffer = buffers[2 * side + kind]
                size = buffer.shape[1] - HALF
                mine = slice(0, count)
                copies = [
                    pltpu.make_async_copy(
                        selected, buffer.at[mine, pl.ds(0, HALF)], sems.at[at]
                    ),
                    pltpu.make_async_copy(
                        own.at[:, pl.ds(HALF, size)], buffer.at[mine, pl.ds(HALF, size)], sems.at[at + 1]
                    ),
                    pltpu.make_async_copy(
                        other, buffer.at[slice(count, 2 * count)], sems.at[at + 2]
                    ),
                ]
                at += 3
                for copy in copies:
                    copy.start()
                per_side.append((buffer, copies))
            result.append(per_side)
        return result, at


def gradients(meta, blocks, cross, name, ties=()):
    width = sum(sum(block.sizes) for block in blocks)
    every = blocks + ([cross] if cross else [])
    part = HALF // 2
    n_in = sum(len(block.parts) for block in every)
    n_out = 4 if cross else 2
    n_sems = 12 * len(every) + 8 * len(every)

    def body(flush, meta, *refs):
        inputs, outputs, rest = refs[:n_in], refs[n_in : n_in + n_out], list(refs[n_in + n_out :])
        if cross:
            cross_stage = rest.pop()
        stage, sems = rest.pop(), rest.pop()
        at = 0
        fetched = []
        for block in every:
            taken, inputs = inputs[: len(block.parts)], inputs[len(block.parts) :]
            own, rest = rest[:4], rest[4:]
            copies, at = block.fetch(taken, own, sems, at)
            fetched.append(copies)
        waited, leaving = set(), []

        def ready(item):
            buffer, copies = item
            if id(buffer) not in waited:
                waited.add(id(buffer))
                for copy in copies:
                    copy.wait()
            return buffer

        base = 0
        for block, copies in zip(blocks, fetched):
            for side in (0, 1):
                start = base
                for left, right in ((0, 1), (1, 0)):
                    left, right = ready(copies[side][left]), ready(copies[side][right])
                    turned = left[:, :HALF].T
                    size = right.shape[1] - HALF
                    for step in range(0, size, HALF):
                        value = mm(turned, right[:, HALF + step : HALF + step + HALF])
                        stage[side, :, start + step : start + step + HALF] = value.astype(bf16)
                    columns = pl.ds(start, size)
                    source = stage.at[side, :, columns]
                    kept = pltpu.make_async_copy(source, outputs[0].at[:, columns], sems.at[at])
                    sent = pltpu.make_async_copy(source, outputs[1].at[:, columns], sems.at[at])
                    pl.when(meta[0] == side)(kept.start)
                    pl.when(meta[0] != side)(sent.start)
                    leaving.append(kept)
                    at += 1
                    start += size
            base += sum(block.sizes)
        if cross:
            copies = fetched[-1]
            start = 0
            for left, right in ((0, 1), (1, 0)):
                lefts = [ready(copies[side][left])[:, :HALF].T for side in (0, 1)]
                rights = [ready(copies[side][right]) for side in (0, 1)]
                size = rights[0].shape[1] - HALF
                for step in range(0, size, HALF):
                    columns = slice(HALF + step, HALF + step + HALF)
                    value = mm(lefts[0], rights[0][:, columns]) + mm(lefts[1], rights[1][:, columns])
                    cross_stage[:, start + step : start + step + HALF] = value.astype(bf16)
                start += size
            for half in (0, 1):
                copy = pltpu.make_async_copy(
                    cross_stage.at[pl.ds(half * part, part)], outputs[2 + half], sems.at[at]
                )
                copy.start()
                leaving.append(copy)
                at += 1
        for copy in leaving:
            copy.wait()

    ins = [(meta, "s")] + [(array, "w") for block in every for array in block.parts]
    outs = [((HALF, width), bf16, "w")] * 2
    scratch = [buffer for block in every for buffer in block.buffers()]
    if cross:
        outs += [((part, sum(cross.sizes)), bf16, "w")] * 2
        scratch += [
            pltpu.SemaphoreType.DMA((n_sems,)),
            pltpu.VMEM((2, HALF, width), bf16),
            pltpu.VMEM((HALF, sum(cross.sizes)), bf16),
        ]
    else:
        scratch += [pltpu.SemaphoreType.DMA((n_sems,)), pltpu.VMEM((2, HALF, width), bf16)]
    flops = 8 * sum(sum(block.rows) * HALF * sum(block.sizes) for block in every)
    return call(body, ins, outs, scratch, flops, name, ties)


def swap(value, axis, distance=1):
    count = lax.axis_size(axis)
    return lax.ppermute(value, axis, [(i, i ^ distance) for i in range(count)])


def on_device(
    word_state,
    region_state,
    word_lengths,
    region_counts,
    word_cotangent,
    region_cotangent,
    cross_in,
    cross_bias,
    cross_out,
    cross_post,
    attention_in,
    attention_bias,
    attention_out,
    attention_post,
    feed_in,
    feed_bias,
    feed_out,
    feed_post,
):
    section = lax.axis_index("section")
    dp_count = lax.axis_size("dp")
    groups = dp_count // 2
    place = lax.axis_index("dp") % 2
    batch = word_state.shape[1]
    width = cross_out.shape[0]
    units = feed_in.shape[-1]
    both = (0, 1)
    chain = [[2 * z + y for z in range(groups)] for y in both]

    def flat(value):
        own = lax.dynamic_index_in_dim(value, section, 0, keepdims=False)
        return own.transpose(1, 0, 2).reshape(-1, D)

    def unflat(value):
        return value.reshape(-1, batch, D).transpose(1, 0, 2)[None]

    def chooser_of(pieces, per_section):
        column = jnp.arange(D)
        half = column // HALF
        inner = column % HALF
        side = jnp.where(half == 0, place, 1 - place)
        size = D // pieces
        if per_section:
            block = inner // (HALF // 2)
            inner = inner % (HALF // 2)
            block = jnp.where(block == 0, section, 1 - section)
            feature = size * (dp_count * block + 2 * (inner // size) + side) + inner % size
        else:
            feature = size * (2 * (inner // size) + side) + inner % size
        return (jnp.arange(D)[:, None] == feature[None, :]).astype(bf16)

    chooser = chooser_of(dp_count, False)
    cross_chooser = chooser_of(2 * dp_count, True)

    small_own = jnp.concatenate(
        [
            attention_bias[0].reshape(2, 1, D),
            attention_post[0],
            feed_bias[0].reshape(2, -1, D),
            feed_post[0],
            jnp.zeros((2, SMALL_ROWS - 9, D), f32),
        ],
        axis=1,
    )
    small_other = swap(small_own, "section")
    smalls = [jnp.where(section == layer, small_own, small_other) for layer in both]
    small = [[smalls[layer][side] for side in both] for layer in both]
    att_in_own = attention_in.transpose(0, 1, 3, 2, 4)
    att_in = (att_in_own, swap(att_in_own, "section"))
    att_out = (attention_out, swap(attention_out, "section"))
    states = [flat(word_state), flat(region_state)]
    feed_in_later, feed_out_later, *_ = lax.optimization_barrier(
        (feed_in, feed_out, att_in[1], att_out[1], smalls[0], chooser, *states)
    )
    ff_in = (feed_in, swap(feed_in_later, "section"))
    ff_out = (feed_out, swap(feed_out_later, "section"))
    cross_entry = cross_in.transpose(1, 0, 2)

    lengths = [
        lax.dynamic_index_in_dim(value, section, 0, keepdims=False)
        for value in (word_lengths, region_counts)
    ]
    meta = jnp.concatenate([section[None].astype(jnp.int32), *lengths])
    cotangents = [flat(word_cotangent), flat(region_cotangent)]
    rows = [state.shape[0] for state in states]
    total_rows = sum(rows)

    def in_order(step, pack_index, tie=None, joined=True):
        results = [None, None]
        given = None
        for side in (1, 0):
            ties = () if tie is None else (tie,)
            place = (total_rows, rows[0] * side, given) if joined else ()
            results[side] = step(side, place, ties)
            tie, given = results[side][-1], results[side][pack_index]
        return results

    def over_mp(results, index):
        return [swap(results[side][index], "mp") for side in both]

    self0 = in_order(
        lambda side, place, ties: self_forward(
            side, 0, batch, meta, states[side], None, small[0][side], chooser, att_in, att_out,
            place, ties,
        ),
        3,
    )
    got = over_mp(self0, 4)
    feed0 = in_order(
        lambda side, place, ties: feed_forward(
            side, 0, batch, meta, states[side], self0[side][4], got[side], small[0][side], chooser,
            ff_in, ff_out, place, ties,
        ),
        4,
        self0[0][5],
    )
    got = over_mp(feed0, 6)
    self0_there = swap(self0[0][3], "dp")
    cross_w, cross_r, cross_pack = cross_forward(
        batch,
        meta,
        [(feed0[side][0], feed0[side][6], got[side]) for side in both],
        small[0],
        cross_chooser,
        cross_entry,
        cross_bias,
        cross_out,
    )
    cross = (cross_w, cross_r)
    got = over_mp(cross, 7)
    feed0_there = swap(feed0[0][4], "dp")
    self1 = in_order(
        lambda side, place, ties: self_forward(
            side, 1, batch, meta, cross[side][0], (cross[side][7], got[side], cross_post),
            small[1][side], chooser, att_in, att_out, place, ties,
        ),
        3,
    )
    got = over_mp(self1, 4)
    cross_there = swap(cross_pack, "dp")
    feed1 = in_order(
        lambda side, place, ties: feed_forward(
            side, 1, batch, meta, self1[side][6], self1[side][4], got[side], small[1][side], chooser,
            ff_in, ff_out, place, ties + (self0_there,),
        ),
        4,
        self1[0][5],
        False,
    )
    got = over_mp(feed1, 6)
    feed1_there = [swap(feed1[side][4], "dp") for side in both]

    back_feed1 = feed_backward(
        1,
        batch,
        meta,
        [(feed1[side][0], feed1[side][6], got[side], cotangents[side]) for side in both],
        None,
        small[1],
        chooser,
        [feed1[side][5] for side in both],
        ff_in,
        ff_out,
        (feed0_there, feed1_there[1]),
    )
    got = swap(back_feed1[3], "mp")
    back_feed1_there = swap(back_feed1[2], "dp")

    def combined(keep, send):
        return keep.astype(f32) + swap(send, "section").astype(f32)

    def scatter(value):
        return lax.psum_scatter(
            value, "dp", scatter_dimension=0, axis_index_groups=chain, tiled=True
        )

    back_self1 = self_backward(
        1,
        meta,
        [feed1[side][1:3] for side in both],
        (back_feed1[0], back_feed1[3], got),
        small[1],
        chooser,
        [self1[side][0] for side in both],
        [self1[side][1] for side in both],
        att_in,
        att_out,
    )
    got = swap(back_self1[3], "mp")
    feed1_pair = gradients(
        meta,
        [
            Block(
                [feed1[side][3] for side in both],
                [feed1[side][4] for side in both],
                feed1_there,
                *back_feed1[1:3],
                back_feed1_there,
            )
        ],
        None,
        "feed_gradients_1",
        (back_self1[5],),
    )
    self1_there = swap(self1[0][3], "dp")
    back_self1_there = swap(back_self1[2], "dp")
    back_cross = cross_backward(
        meta,
        [self1[side][7:9] for side in both],
        (back_self1[0], back_self1[3], got),
        cross_post,
        cross_chooser,
        [cross[side][5] for side in both],
        [cross[side][6] for side in both],
        cross_entry,
        cross_out,
        (feed1_pair[0],),
    )
    cross_post_grad, cross_bias_grad = back_cross[4:6]
    got = swap(back_cross[3], "mp")
    back_cross_there = swap(back_cross[2], "dp")
    feed1_total = combined(*feed1_pair).astype(bf16)
    feed1_share = scatter(feed1_total)

    back_feed0 = feed_backward(
        0,
        batch,
        meta,
        [cross[side][1:3] for side in both],
        (back_cross[0], back_cross[3], got),
        small[0],
        chooser,
        [feed0[side][5] for side in both],
        ff_in,
        ff_out,
        (feed1_total,),
    )
    got = swap(back_feed0[3], "mp")
    back_feed0_there = swap(back_feed0[2], "dp")
    late1_pairs = gradients(
        meta,
        [
            Block(
                [self1[side][2] for side in both],
                [self1[0][3]],
                [self1_there],
                *back_self1[1:3],
                back_self1_there,
            )
        ],
        Block(
            [cross[side][4] for side in both],
            [cross_pack],
            [cross_there],
            *back_cross[1:3],
            back_cross_there,
        ),
        "late_gradients_1",
        (back_feed0[5],),
    )
    chunk = D // dp_count
    late1 = jnp.concatenate(
        [
            combined(*late1_pairs[:2]).reshape(groups, chunk, 4 * width),
            combined(*late1_pairs[2:]).reshape(groups, chunk // 2, 4 * width),
        ],
        axis=1,
    ).astype(bf16)
    late1 = late1.reshape(-1, 4 * width)
    late1_share = scatter(late1)

    back_self0 = self_backward(
        0,
        meta,
        [feed0[side][1:3] for side in both],
        (back_feed0[0], back_feed0[3], got),
        small[0],
        chooser,
        [self0[side][0] for side in both],
        [self0[side][1] for side in both],
        att_in,
        att_out,
        (late1_pairs[0],),
    )
    got = swap(back_self0[3], "mp")
    back_self0_there = swap(back_self0[2], "dp")
    layer0_pair = gradients(
        meta,
        [
            Block(
                [feed0[side][3] for side in both],
                [feed0[0][4]],
                [feed0_there],
                *back_feed0[1:3],
                back_feed0_there,
            ),
            Block(
                [self0[side][2] for side in both],
                [self0[0][3]],
                [self0_there],
                *back_self0[1:3],
                back_self0_there,
            ),
        ],
        None,
        "gradients_0",
        (late1, feed1_share),
    )
    layer0 = combined(*layer0_pair).astype(bf16)
    layer0, late1_share = lax.optimization_barrier((layer0, late1_share))
    layer0_share = scatter(layer0)

    state_grad = (back_self0[0] + (back_self0[3].astype(f32) + got.astype(f32))).astype(bf16)
    spans = spans_of(rows)

    def packed(back_self, back_feed, squares):
        rows = [
            back_self[5].reshape(2, D),
            back_self[4].reshape(6, D),
            back_feed[5].reshape(-1, D),
            back_feed[4].reshape(6, D),
        ]
        row = jnp.concatenate([value.reshape(1, 128) for value in squares[:6]], axis=1)
        rest = jnp.concatenate([value.reshape(1, 128) for value in squares[6:]], axis=1)
        rest = jnp.concatenate([rest, jnp.zeros((1, D - rest.shape[1]), f32)], axis=1)
        return jnp.concatenate(rows + [row, rest], axis=0)

    def squares_of(lead, second, tail):
        result = []
        for side in both:
            result += [lead[side], second[side], tail[side][0:1], tail[side][1:2]]
        return result

    packs = [
        packed(
            back_self0,
            back_feed0,
            squares_of(
                [self0[side][5] for side in both],
                [feed0[side][7] for side in both],
                [cross[side][3] for side in both],
            ),
        ),
        packed(
            back_self1,
            back_feed1,
            squares_of(
                [self1[side][5] for side in both],
                [feed1[side][7] for side in both],
                [back_feed1[8][side] for side in both],
            ),
        ),
    ]
    counts = jnp.stack([jnp.sum(word_lengths), jnp.sum(region_counts)]).astype(f32)
    counts = jnp.pad(counts, (0, D - 2))[None] * 0.5
    mine = jnp.where(section == 0, packs[0], packs[1])
    theirs = jnp.where(section == 0, packs[1], packs[0])
    shared = [cross_post_grad, cross_bias_grad.reshape(1, D), counts]
    small_rows = packs[0].shape[0]
    total = jnp.concatenate([mine] + shared, axis=0) + swap(
        jnp.concatenate([theirs] + shared, axis=0), "section"
    )
    distance = 1
    while distance < dp_count:
        total = total + swap(total, "dp", distance)
        distance *= 2
    unit_rows = units // D
    at = 0
    att_bias_grad = total[0:2].reshape(1, 2, 2, width)
    at = 2
    att_post_grad = total[at : at + 6].reshape(1, 2, 3, D)
    at += 6
    feed_bias_grad = total[at : at + 2 * unit_rows].reshape(1, 2, units)
    at += 2 * unit_rows
    feed_post_grad = total[at : at + 6].reshape(1, 2, 3, D)
    at += 6
    squares = total[at : at + 2].reshape(-1, 128)[:8, 0]
    at = small_rows
    cross_post_total = total[at : at + 3]
    cross_bias_total = total[at + 3].reshape(2, width)
    valid_counts = total[at + 4, :2]
    scales = jnp.sqrt(squares / (jnp.repeat(valid_counts, 4) * D))[None]

    layer1_share = jnp.concatenate([feed1_share, late1_share[:chunk]], axis=1)
    late_words = lax.ppermute(layer1_share, "section", [(0, 1)])
    late_regions = lax.ppermute(layer0_share, "section", [(1, 0)])
    words_grad = jnp.where(section == 0, layer0_share, late_words)
    regions_grad = jnp.where(section == 0, late_regions, layer1_share)

    def stacked(start, stop):
        return jnp.stack([words_grad[:, start:stop], regions_grad[:, start:stop]]).astype(f32)

    feed_in_grad = stacked(0, units)[None]
    feed_out_grad = stacked(units, 2 * units).transpose(0, 2, 1)[None]
    base = 2 * units
    att_in_grad = stacked(base, base + 3 * width).reshape(2, chunk, 3, width)[None]
    att_out_grad = stacked(base + 3 * width, base + 4 * width).transpose(0, 2, 1)[None]
    cross_share = late1_share[chunk:].astype(f32)
    cross_in_grad = cross_share[:, : 3 * width].reshape(-1, 3, width)
    cross_out_grad = cross_share[:, 3 * width :].T
    return (
        unflat(back_feed1[6]),
        unflat(back_feed1[7]),
        unflat(state_grad[spans[0]]),
        unflat(state_grad[spans[1]]),
        cross_in_grad,
        cross_bias_total,
        cross_out_grad,
        cross_post_total,
        att_in_grad,
        att_bias_grad,
        att_out_grad,
        att_post_grad,
        feed_in_grad,
        feed_bias_grad,
        feed_out_grad,
        feed_post_grad,
        scales,
    )


def solution(mesh):
    placed = (
        P(None, "dp", None, None),
        P(None, "dp", None, None),
        P(None, "dp"),
        P(None, "dp"),
        P(None, "dp", None, None),
        P(None, "dp", None, None),
        P(None, None, "mp"),
        P(None, "mp"),
        P("mp", None),
        P(),
        P("section", None, None, None, "mp"),
        P("section", None, None, "mp"),
        P("section", None, "mp", None),
        P("section", None, None, None),
        P("section", None, None, "mp"),
        P("section", None, "mp"),
        P("section", None, "mp", None),
        P("section", None, None, None),
    )
    return jax.shard_map(
        on_device,
        mesh=mesh,
        in_specs=placed,
        out_specs=(
            P("section", "dp", None, None),
            P("section", "dp", None, None),
            P("section", "dp", None, None),
            P("section", "dp", None, None),
            P(("section", "dp"), None, "mp"),
            P(None, "mp"),
            P("mp", ("section", "dp")),
            P(),
            P("section", None, "dp", None, "mp"),
            P("section", None, None, "mp"),
            P("section", None, "mp", "dp"),
            P("section", None, None, None),
            P("section", None, "dp", "mp"),
            P("section", None, "mp"),
            P("section", None, "mp", "dp"),
            P("section", None, None, None),
            P("section", None),
        ),
        check_vma=False,
    )
```

```python
from functools import partial

import jax
import jax.numpy as jnp
from jax import lax
from jax.experimental import pallas as pl
from jax.experimental.pallas import tpu as pltpu
from jax.sharding import PartitionSpec as P

D = 768
HALF = D // 2
HEAD_DIM = 64
PAIR = 2 * HEAD_DIM
WORDS = 20
REGIONS = 36
EPS = 1e-06
SCALE = HEAD_DIM**-0.5
COST_SCALE = 0.5
bf16 = jnp.bfloat16
f32 = jnp.float32

ROW_ATT_BIAS, ROW_ATT_POST, ROW_FEED_BIAS, ROW_FEED_POST, SMALL_ROWS = 0, 1, 4, 6, 16


def mm(a, b):
    return jnp.dot(a, b, preferred_element_type=f32)


def mm_nt(a, b):
    return lax.dot_general(a, b, (((1,), (1,)), ((), ())), preferred_element_type=f32)


def mm_tn(a, b):
    return lax.dot_general(a, b, (((0,), (0,)), ((), ())), preferred_element_type=f32)


def norm_of(value, gain, shift):
    centred = value - jnp.mean(value, axis=-1, keepdims=True)
    spread = jnp.mean(centred * centred, axis=-1, keepdims=True)
    rstd = lax.rsqrt(spread + EPS)
    unit = centred * rstd
    return unit, rstd, unit * gain + shift


def norm_back(unit, rstd, gain, incoming):
    scaled = incoming * gain
    mean = jnp.mean(scaled, axis=-1, keepdims=True)
    along = jnp.mean(scaled * unit, axis=-1, keepdims=True)
    return (scaled - mean - unit * along) * rstd


def summed(own, other):
    return own[...].astype(f32) + other[...].astype(f32)


def column_sum(value):
    return jnp.sum(value, axis=0, keepdims=True)


def square_sum(value, valid):
    rows = jnp.sum(value * value, axis=-1, keepdims=True) * valid
    return jnp.broadcast_to(jnp.sum(rows, axis=0, keepdims=True), (1, 128))


def lengths_of(meta, side, batch, item):
    result = jnp.zeros_like(item)
    for i in range(batch):
        result = jnp.where(item == i, meta[1 + side * batch + i], result)
    return result


def row_valid(meta, side, batch, rows):
    index = lax.broadcasted_iota(jnp.int32, (rows, 1), 0)
    length = lengths_of(meta, side, batch, lax.rem(index, batch))
    return (lax.div(index, batch) < length).astype(f32)


def pair_valid(meta, side, batch, rows, keys):
    index = lax.broadcasted_iota(jnp.int32, (1, keys), 1)
    item = lax.rem(index, batch)
    length = lengths_of(meta, side, batch, item)
    item = jnp.where(lax.div(index, batch) < length, item, -1)
    row_item = lax.rem(lax.broadcasted_iota(jnp.int32, (rows, 1), 0), batch)
    return jnp.broadcast_to(row_item, (rows, keys)) == jnp.broadcast_to(item, (rows, keys))


def head_lanes(head):
    lane = lax.broadcasted_iota(jnp.int32, (1, PAIR), 1)
    return (lane // HEAD_DIM) == head


def attend(query, keys, values, valid, probs_ref, context_ref):
    for pair in range(query.shape[1] // PAIR):
        lanes = slice(pair * PAIR, (pair + 1) * PAIR)
        contexts = []
        for head in range(2):
            chosen = query[:, lanes] * head_lanes(head).astype(bf16)
            scores = mm_nt(chosen, keys[:, lanes]) * SCALE
            scores = jnp.where(valid, scores, -1e9)
            shifted = jnp.exp(scores - jnp.max(scores, axis=-1, keepdims=True))
            total = jnp.sum(shifted, axis=-1, keepdims=True)
            probs = (shifted * (1.0 / total)).astype(bf16)
            probs_ref[2 * pair + head] = probs
            contexts.append(mm(probs, values[:, lanes]))
        context_ref[:, lanes] = jnp.where(head_lanes(0), contexts[0], contexts[1]).astype(bf16)


def attend_back(query, keys, values, probs_ref, grad_context, emit):
    first = head_lanes(0)
    for pair in range(query.shape[1] // PAIR):
        lanes = slice(pair * PAIR, (pair + 1) * PAIR)
        grads = ([], [], [])
        for head in range(2):
            probs = probs_ref[2 * pair + head]
            chosen = grad_context[:, lanes] * head_lanes(head).astype(bf16)
            grad_probs = mm_nt(chosen, values[:, lanes])
            wide = probs.astype(f32)
            product = wide * grad_probs
            grad_scores = product - wide * jnp.sum(product, axis=-1, keepdims=True)
            grad_scores = grad_scores.astype(bf16)
            grads[0].append(mm(grad_scores, keys[:, lanes]) * SCALE)
            grads[1].append(mm_tn(grad_scores, query[:, lanes]) * SCALE)
            grads[2].append(mm_tn(probs, grad_context[:, lanes]))
        for kind in range(3):
            emit(kind, lanes, jnp.where(first, grads[kind][0], grads[kind][1]).astype(bf16))


class Fetched:
    def __init__(self, copy, buffer):
        self.copy, self.buffer, self.waited = copy, buffer, False
        self.shape, self.dtype = buffer.shape, buffer.dtype

    def wait(self):
        if not self.waited:
            self.copy.wait()
            self.waited = True
        return self.buffer

    def __getitem__(self, index):
        return self.wait()[index]


class Weights:
    def __init__(self, meta, layer, pairs, buffers, sems):
        self.copies = []
        mine = meta[0] == layer
        at = 0
        for (own, other, pieces), buffer in zip(pairs, buffers):
            copies = []
            for piece in pieces:
                copy = pltpu.make_async_copy(own.at[piece], buffer.at[piece], sems.at[at])
                if other is None:
                    copy.start()
                else:
                    second = pltpu.make_async_copy(
                        other.at[piece], buffer.at[piece], sems.at[at]
                    )
                    pl.when(mine)(copy.start)
                    pl.when(jnp.logical_not(mine))(second.start)
                copies.append(Fetched(copy, buffer))
                at += 1
            self.copies.append(copies)

    def get(self, slot, piece=None):
        copies = self.copies[slot]
        for copy in copies if piece is None else (copies[piece],):
            copy.wait()
        return copies[0].buffer


def maps(own, other, side, pieces=((),)):
    if other is None:
        return own, None, pieces
    return own.at[0, side], other.at[0, side], pieces


ENTRY = ((0,), (1,), (2,))


def column_pieces(size, count):
    return tuple(
        (slice(None), slice(i * size // count, (i + 1) * size // count)) for i in range(count)
    )


def row_pieces(size, count):
    return tuple((slice(i * size // count, (i + 1) * size // count),) for i in range(count))


def call(body, ins, outs, scratch=(), cost=0.0, name=None, ties=(), mib=14):
    spaces = {
        "s": pltpu.SMEM, "v": pltpu.VMEM, "w": pltpu.HBM, "h": pltpu.HBM, "a": pl.ANY, "f": pl.ANY
    }
    ties = [tie if isinstance(tie, tuple) else (tie, "w") for tie in ties]
    extra = [(i, out[5]) for i, out in enumerate(outs) if len(out) > 3 and out[5] is not None]
    aliases = {len(ins) + at: i for at, (i, _) in enumerate(extra)}
    ins = list(ins) + [(array, "w") for _, array in extra]
    places = [out[3:5] if len(out) > 3 else None for out in outs]
    fetched = [i for i, (_, kind) in enumerate(ins) if kind in "hf"]
    written = [i for i, out in enumerate(outs) if out[2] == "h"]
    n_ins, n_ties, n_outs, n_scratch = len(ins), len(ties), len(outs), len(scratch)

    def whole(*refs):
        given = list(refs[:n_ins])
        results = list(refs[n_ins + n_ties : n_ins + n_ties + n_outs])
        rest = refs[n_ins + n_ties + n_outs :]
        own, rest = rest[:n_scratch], rest[n_scratch:]
        buffers, rest = rest[: len(fetched)], rest[len(fetched) :]
        staged, rest = rest[: len(written)], rest[len(written) :]
        sems = rest[0] if rest else None
        for slot, i in enumerate(fetched):
            copy = pltpu.make_async_copy(given[i], buffers[slot], sems.at[slot])
            copy.start()
            given[i] = Fetched(copy, buffers[slot])
        leaving = {}
        for slot, i in enumerate(written):
            target = results[i]
            if places[i] is not None:
                target = target.at[pl.ds(places[i][1], staged[slot].shape[0])]
            copy = pltpu.make_async_copy(staged[slot], target, sems.at[len(fetched) + slot])
            leaving[id(staged[slot])] = copy
            results[i] = staged[slot]
        started = []

        def flush(*done):
            for ref in done:
                copy = leaving.pop(id(ref), None)
                if copy is not None:
                    copy.start()
                    started.append(copy)

        body(flush, *given[: n_ins - len(extra)], *results, *own)
        flush(*[staged[slot] for slot in range(len(written))])
        for copy in started:
            copy.wait()
        for item in given:
            if isinstance(item, Fetched):
                item.wait()

    arrays = [
        pltpu.with_memory_space_constraint(array, spaces[kind]) if kind in "vwh" else array
        for array, kind in [*ins, *ties]
    ]
    own_scratch = list(scratch)
    own_scratch += [pltpu.VMEM(arrays[i].shape, arrays[i].dtype) for i in fetched]
    own_scratch += [pltpu.VMEM(outs[i][0], outs[i][1]) for i in written]
    if fetched or written:
        own_scratch.append(pltpu.SemaphoreType.DMA((len(fetched) + len(written),)))
    return pl.pallas_call(
        whole,
        out_shape=[
            spaces[out[2]]((out[3], *out[0][1:]) if len(out) > 3 else out[0], out[1]) for out in outs
        ],
        in_specs=[pl.BlockSpec(memory_space=spaces[kind]) for _, kind in [*ins, *ties]],
        out_specs=[pl.BlockSpec(memory_space=spaces[out[2]]) for out in outs],
        input_output_aliases=aliases,
        scratch_shapes=own_scratch,
        compiler_params=pltpu.CompilerParams(vmem_limit_bytes=mib * 1024 * 1024),
        cost_estimate=pl.CostEstimate(
            flops=int(cost * COST_SCALE * 1.15e9), bytes_accessed=0, transcendentals=0
        ),
        name=name,
    )(*arrays)


def spans_of(rows):
    return slice(0, rows[0]), slice(rows[0], rows[0] + rows[1])


def select_rows(value, chooser, own_ref, pack_ref):
    moved = mm(value, chooser[...]).astype(bf16)
    own_ref[...] = moved[:, :HALF]
    pack_ref[:, :HALF] = moved[:, HALF:]


def project(low, weights, bias_q, bias_v, qkv_ref):
    qkv_ref[0] = (mm(low, weights.get(0, 0)[0]) + bias_q).astype(bf16)
    qkv_ref[1] = mm(low, weights.get(0, 1)[1]).astype(bf16)
    qkv_ref[2] = (mm(low, weights.get(0, 2)[2]) + bias_v).astype(bf16)


def self_forward(
    side, layer, batch, meta, state, prior, small, chooser, att_in, att_out, place, ties=()
):
    rows = state.shape[0]
    width = att_in[0].shape[-1]
    first = prior is None

    def body(flush, meta, state, *refs):
        refs = list(refs)
        if not first:
            own, other, post = refs[:3]
            refs = refs[3:]
        small, chooser, in_own, in_other, out_own, out_other = refs[:6]
        qkv, probs, selected, pack, part, squares = refs[6:12]
        refs = refs[12:]
        if not first:
            mixed_ref, unit_ref, rstd_ref = refs[:3]
            refs = refs[3:]
        in_buffer, out_buffer, sems = refs
        weights = Weights(
            meta,
            layer,
            (maps(in_own, in_other, side, ENTRY), maps(out_own, out_other, side)),
            (in_buffer, out_buffer),
            sems,
        )
        valid = row_valid(meta, side, batch, rows)
        if first:
            low = state[...]
            squares[...] = square_sum(low.astype(f32), valid)
        else:
            branch = summed(own, other) + post[0:1]
            squares[...] = square_sum(branch, valid)
            unit, rstd, mixed = norm_of(state[...].astype(f32) + branch, post[1:2], post[2:3])
            unit_ref[...] = unit
            rstd_ref[...] = rstd
            mixed_ref[...] = mixed
            low = mixed.astype(bf16)
        select_rows(low, chooser, selected, pack)
        flush(selected)
        biases = small[ROW_ATT_BIAS : ROW_ATT_BIAS + 1]
        project(low, weights, biases[:, :width], biases[:, width : 2 * width], qkv)
        context = pack.at[:, HALF:]
        attend(
            qkv[0], qkv[1], qkv[2], pair_valid(meta, side, batch, rows, rows), probs, context
        )
        flush(qkv, probs, pack)
        part[...] = mm(context[...], weights.get(1)[...]).astype(bf16)

    ins = [(meta, "s"), (state, "v")]
    if not first:
        ins += list(zip(prior, "vvv"))
    ins += [(small, "v"), (chooser, "v")] + list(zip(att_in + att_out, "wawa"))
    outs = [
        ((3, rows, width), bf16, "h"),
        ((width // HEAD_DIM, rows, rows), bf16, "h"),
        ((rows, HALF), bf16, "h"),
        ((rows, HALF + width), bf16, "h", *place),
        ((rows, D), bf16, "v"),
        ((1, 128), f32, "h"),
    ]
    if not first:
        outs += [((rows, D), f32, "v"), ((rows, D), f32, "h"), ((rows, 1), f32, "h")]
    scratch = [
        pltpu.VMEM((3, D, width), bf16),
        pltpu.VMEM((width, D), bf16),
        pltpu.SemaphoreType.DMA((6,)),
    ]
    return call(body, ins, outs, scratch, 4.0, f"self_forward_{layer}_{side}", ties)


def feed_forward(
    side, layer, batch, meta, residual, own, other, small, chooser, feed_in, feed_out, place, ties=()
):
    rows = residual.shape[0]
    units = feed_in[0].shape[-1]
    step = units // 4

    def body(
        flush, meta, residual, own, other, small, chooser, in_own, in_other, out_own, out_other,
        settled_ref, unit_ref, rstd_ref, selected, pack, slope, part, squares,
        in_buffer, out_buffer, sems,
    ):
        weights = Weights(
            meta,
            layer,
            (
                maps(in_own, in_other, side, column_pieces(units, 4)),
                maps(out_own, out_other, side, row_pieces(units, 2)),
            ),
            (in_buffer, out_buffer),
            sems,
        )
        post = small[ROW_ATT_POST : ROW_ATT_POST + 3]
        branch = summed(own, other) + post[0:1]
        squares[...] = square_sum(branch, row_valid(meta, side, batch, rows))
        unit, rstd, settled = norm_of(residual[...].astype(f32) + branch, post[1:2], post[2:3])
        unit_ref[...] = unit
        rstd_ref[...] = rstd
        settled_ref[...] = settled
        low = settled.astype(bf16)
        select_rows(low, chooser, selected, pack)
        flush(unit_ref, rstd_ref, selected)
        for i in range(units // step):
            first = weights.get(0, i)
            columns = slice(i * step, (i + 1) * step)
            row = ROW_FEED_BIAS + (i * step) // D
            place = (i * step) % D
            hidden = mm(low, first[:, columns]) + small[row : row + 1, place : place + step]
            below = 0.5 + 0.5 * lax.erf(hidden * (0.5**0.5))
            density = jnp.exp(hidden * hidden * -0.5) * 0.3989422804014327
            pack[:, HALF + i * step : HALF + (i + 1) * step] = (hidden * below).astype(bf16)
            slope[:, columns] = (below + hidden * density).astype(bf16)
        flush(pack, slope)
        part[...] = mm(pack[:, HALF:], weights.get(1)[...]).astype(bf16)

    ins = [(meta, "s"), (residual, "v"), (own, "v"), (other, "v")]
    ins += [(small, "v"), (chooser, "v")] + list(zip(feed_in + feed_out, "wawa"))
    outs = [
        ((rows, D), f32, "h"),
        ((rows, D), f32, "h"),
        ((rows, 1), f32, "h"),
        ((rows, HALF), bf16, "h"),
        ((rows, HALF + units), bf16, "h", *place),
        ((rows, units), bf16, "h"),
        ((rows, D), bf16, "v"),
        ((1, 128), f32, "h"),
    ]
    scratch = [
        pltpu.VMEM((D, units), bf16),
        pltpu.VMEM((units, D), bf16),
        pltpu.SemaphoreType.DMA((6,)),
    ]
    return call(body, ins, outs, scratch, 4.3, f"feed_forward_{layer}_{side}", ties)


def cross_forward(
    batch, meta, streams, smalls, chooser, cross_in, cross_bias, cross_out, ties=()
):
    rows = [stream[0].shape[0] for stream in streams]
    spans = spans_of(rows)
    width = cross_out.shape[0]
    heads = width // HEAD_DIM

    def body(flush, meta, *refs):
        given = (refs[0:3], refs[3:6])
        small, chooser, in_ref, bias, out_ref = (refs[6:8], *refs[8:12])
        all_pack = refs[28]
        outs = [refs[12:20], refs[20:28]]
        for side in (0, 1):
            outs[side] = outs[side][:5] + (all_pack.at[spans[side]],) + outs[side][5:]
        in_buffer, out_buffer, sems = refs[29:]
        weights = Weights(
            meta,
            0,
            (maps(in_ref, None, 0, ENTRY), maps(out_ref, None, 0)),
            (in_buffer, out_buffer),
            sems,
        )
        lows = []
        for side in (0, 1):
            settled, own, other = given[side]
            state, unit_ref, rstd_ref, squares, selected, pack, qkv, probs, part = outs[side]
            post = small[side][ROW_FEED_POST : ROW_FEED_POST + 3]
            branch = summed(own, other) + post[0:1]
            unit, rstd, result = norm_of(settled[...] + branch, post[1:2], post[2:3])
            unit_ref[...] = unit
            rstd_ref[...] = rstd
            low = result.astype(bf16)
            state[...] = low
            valid = row_valid(meta, side, batch, rows[side])
            squares[0:1] = square_sum(branch, valid)
            squares[1:2] = square_sum(low.astype(f32), valid)
            select_rows(low, chooser, selected, pack)
            flush(unit_ref, rstd_ref, selected)
            lows.append(low)
        for side in (0, 1):
            project(lows[side], weights, bias[0:1], bias[1:2], outs[side][6])
        leave = weights.get(1)
        for side in (0, 1):
            pack, qkv, probs, part = outs[side][5:]
            there = outs[1 - side][6]
            valid = pair_valid(meta, 1 - side, batch, rows[side], rows[1 - side])
            context = pack.at[:, HALF:]
            attend(qkv[0], there[1], there[2], valid, probs, context)
            flush(qkv, probs)
            part[...] = mm(context[...], leave[...]).astype(bf16)

    ins = [(meta, "s")] + [pair for stream in streams for pair in zip(stream, "hvv")]
    ins += [(item, "v") for item in smalls]
    ins += [(chooser, "v"), (cross_in, "w"), (cross_bias, "v"), (cross_out, "w")]
    outs = []
    for side in (0, 1):
        here, there = rows[side], rows[1 - side]
        outs += [
            ((here, D), bf16, "v"),
            ((here, D), f32, "h"),
            ((here, 1), f32, "h"),
            ((2, 128), f32, "h"),
            ((here, HALF), bf16, "h"),
            ((3, here, width), bf16, "h"),
            ((heads, here, there), bf16, "h"),
            ((here, D), bf16, "v"),
        ]
    outs.append(((sum(rows), HALF + width), bf16, "h"))
    scratch = [
        pltpu.VMEM((3, D, width), bf16),
        pltpu.VMEM((width, D), bf16),
        pltpu.SemaphoreType.DMA((6,)),
    ]
    result = call(body, ins, outs, scratch, 6.8, "cross_forward", ties)
    return result[:8], result[8:16], result[16]


def feed_backward(
    layer, batch, meta, tops, joint, small, chooser, slopes, feed_in, feed_out, ties=()
):
    last = joint is None
    rows = [slope.shape[0] for slope in slopes]
    units = slopes[0].shape[1]
    spans, total = spans_of(rows), sum(rows)
    step = units // 4
    n_top = len(tops[0])

    def body(flush, meta, *refs):
        given = (refs[:n_top], refs[n_top : 2 * n_top])
        refs = refs[2 * n_top :]
        if not last:
            joint, refs = refs[:3], refs[3:]
        small, chooser, slopes = refs[:2], refs[2], refs[3:5]
        in_own, in_other, out_own, out_other = refs[5:9]
        grad_all, selected_all, pack_all, part_all, post_all, bias_all = refs[9:15]
        if last:
            results, squares_all = refs[15:17], refs[17]
        in_buffer, out_buffer, sems = refs[-3:]
        weights = [
            Weights(
                meta,
                layer,
                (
                    maps(out_own, out_other, side, row_pieces(units, 4)),
                    maps(in_own, in_other, side, column_pieces(units, 2)),
                ),
                (out_buffer.at[side], in_buffer.at[side]),
                sems.at[side],
            )
            for side in (1, 0)
        ][::-1]
        lows = [None, None]
        for side in (1, 0):
            here = spans[side]
            post = small[side][ROW_FEED_POST : ROW_FEED_POST + 3]
            if last:
                settled, own, other, cotangent = given[side]
                branch = summed(own, other) + post[0:1]
                unit, rstd, result = norm_of(settled[...] + branch, post[1:2], post[2:3])
                low = result.astype(bf16)
                results[side][...] = low
                valid = row_valid(meta, side, batch, rows[side])
                squares_all[side, 0:1] = square_sum(branch, valid)
                squares_all[side, 1:2] = square_sum(low.astype(f32), valid)
                incoming = cotangent[...].astype(f32) * valid
            else:
                unit_ref, rstd_ref = given[side]
                unit, rstd = unit_ref[...], rstd_ref[...]
                incoming = (joint[0][here] + summed_rows(joint[1], joint[2], here)).astype(bf16)
                incoming = incoming.astype(f32)
            grad = norm_back(unit, rstd, post[1:2], incoming)
            grad_all[here] = grad
            low = grad.astype(bf16)
            post_all[side, 0:1] = column_sum(low.astype(f32))
            post_all[side, 1:2] = column_sum(incoming * unit)
            post_all[side, 2:3] = column_sum(incoming)
            lows[side] = low
        for side in (1, 0):
            here = spans[side]
            select_rows(lows[side], chooser, selected_all.at[here], pack_all.at[here])
            for i in range(units // step):
                columns = slice(i * step, (i + 1) * step)
                active = mm_nt(lows[side], weights[side].get(0, i)[columns, :])
                hidden = (active * slopes[side][:, columns].astype(f32)).astype(bf16)
                pack_all[here, HALF + i * step : HALF + (i + 1) * step] = hidden
                bias_all[side, :, columns] = column_sum(hidden.astype(f32))
        flush(pack_all, selected_all)
        for side in (1, 0):
            here = spans[side]
            part_all[here] = mm_nt(pack_all[here, HALF:], weights[side].get(1)[...]).astype(bf16)

    ins = [(meta, "s")] + [pair for top in tops for pair in zip(top, "hfff" if last else "hh")]
    if not last:
        ins += list(zip(joint, "hhf"))
    ins += [(item, "f") for item in small] + [(chooser, "f")] + [(item, "h") for item in slopes]
    ins += list(zip(feed_in + feed_out, "wawa"))
    outs = [
        ((total, D), f32, "h"),
        ((total, HALF), bf16, "h"),
        ((total, HALF + units), bf16, "h"),
        ((total, D), bf16, "h"),
        ((2, 3, D), f32, "h"),
        ((2, 1, units), f32, "h"),
    ]
    if last:
        outs += [((here, D), bf16, "h") for here in rows] + [((2, 2, 128), f32, "h")]
    scratch = [
        pltpu.VMEM((2, D, units), bf16),
        pltpu.VMEM((2, units, D), bf16),
        pltpu.SemaphoreType.DMA((2, 6)),
    ]
    return call(body, ins, outs, scratch, 11.0, f"feed_backward_{layer}", ties, 24)


def summed_rows(own, other, here):
    return own[here].astype(f32) + other[here].astype(f32)


def back_through_norm(top, joint, here, gain, grad_all, post_ref):
    unit_ref, rstd_ref = top
    incoming = joint[0][here] + summed_rows(joint[1], joint[2], here)
    unit = unit_ref[...]
    grad = norm_back(unit, rstd_ref[...], gain, incoming)
    grad_all[here] = grad
    low = grad.astype(bf16)
    post_ref[0:1] = column_sum(low.astype(f32))
    post_ref[1:2] = column_sum(incoming * unit)
    post_ref[2:3] = column_sum(incoming)
    return low


def emit_into(pack, width):
    def emit(kind, lanes, value):
        start = HALF + kind * width + lanes.start
        pack[:, start : start + PAIR] = value

    return emit


def back_to_input(pack, weights, slot, width):
    grads = [pack[:, HALF + j * width : HALF + (j + 1) * width] for j in range(3)]
    total = mm_nt(grads[0], weights.get(slot, 0)[0])
    total += mm_nt(grads[1], weights.get(slot, 1)[1])
    total += mm_nt(grads[2], weights.get(slot, 2)[2])
    return total.astype(bf16)


def self_backward(
    layer, meta, tops, joint, small, chooser, qkvs, probs, att_in, att_out, ties=()
):
    rows = [qkv.shape[1] for qkv in qkvs]
    width = qkvs[0].shape[2]
    spans, total = spans_of(rows), sum(rows)

    def body(flush, meta, *refs):
        tops, joint = (refs[:2], refs[2:4]), refs[4:7]
        small, chooser, qkvs, probs = refs[7:9], refs[9], refs[10:12], refs[12:14]
        in_own, in_other, out_own, out_other = refs[14:18]
        grad_all, selected_all, pack_all, part_all, post_all, bias_all = refs[18:24]
        in_buffer, out_buffer, sems = refs[24:]
        weights = [
            Weights(
                meta,
                layer,
                (maps(out_own, out_other, side), maps(in_own, in_other, side, ENTRY)),
                (out_buffer.at[side], in_buffer.at[side]),
                sems.at[side],
            )
            for side in (1, 0)
        ][::-1]
        for side in (1, 0):
            here = spans[side]
            pack = pack_all.at[here]
            gain = small[side][ROW_ATT_POST + 1 : ROW_ATT_POST + 2]
            low = back_through_norm(tops[side], joint, here, gain, grad_all, post_all.at[side])
            select_rows(low, chooser, selected_all.at[here], pack)
            context = mm_nt(low, weights[side].get(0)[...]).astype(bf16)
            qkv = qkvs[side]
            attend_back(qkv[0], qkv[1], qkv[2], probs[side], context, emit_into(pack, width))
            bias_all[side, 0:1] = column_sum(pack[:, HALF : HALF + width].astype(f32))
            bias_all[side, 1:2] = column_sum(pack[:, HALF + 2 * width :].astype(f32))
        flush(pack_all, selected_all)
        for side in (1, 0):
            here = spans[side]
            part_all[here] = back_to_input(pack_all.at[here], weights[side], 1, width)

    ins = [(meta, "s")] + [(item, "h") for top in tops for item in top]
    ins += list(zip(joint, "hhf"))
    ins += [(item, "f") for item in small] + [(chooser, "f")]
    ins += [(item, "h") for item in (*qkvs, *probs)]
    ins += list(zip(att_in + att_out, "wawa"))
    outs = [
        ((total, D), f32, "h"),
        ((total, HALF), bf16, "h"),
        ((total, HALF + 3 * width), bf16, "h"),
        ((total, D), bf16, "h"),
        ((2, 3, D), f32, "h"),
        ((2, 2, width), f32, "h"),
    ]
    scratch = [
        pltpu.VMEM((2, 3, D, width), bf16),
        pltpu.VMEM((2, width, D), bf16),
        pltpu.SemaphoreType.DMA((2, 6)),
    ]
    return call(body, ins, outs, scratch, 12.0, f"self_backward_{layer}", ties, 18)


def cross_backward(meta, tops, joint, post, chooser, qkvs, probs, cross_in, cross_out, ties=()):
    rows = [qkv.shape[1] for qkv in qkvs]
    width = cross_out.shape[0]
    spans, total = spans_of(rows), sum(rows)

    def body(flush, meta, *refs):
        tops, joint = (refs[:2], refs[2:4]), refs[4:7]
        post, chooser, qkvs, probs = refs[7], refs[8], refs[9:11], refs[11:13]
        in_ref, out_ref = refs[13:15]
        grad_all, selected_all, pack_all, part_all, post_out, bias_out = refs[15:21]
        in_buffer, out_buffer, post_each, sems = refs[21:]
        weights = Weights(
            meta,
            0,
            (maps(out_ref, None, 0), maps(in_ref, None, 0, ENTRY)),
            (out_buffer, in_buffer),
            sems,
        )
        packs = [pack_all.at[here] for here in spans]
        lows = []
        for side in (0, 1):
            here = spans[side]
            low = back_through_norm(
                tops[side], joint, here, post[1:2], grad_all, post_each.at[side]
            )
            select_rows(low, chooser, selected_all.at[here], packs[side])
            lows.append(low)
        post_out[...] = post_each[0] + post_each[1]
        leave = weights.get(0)
        for side in (0, 1):
            context = mm_nt(lows[side], leave[...]).astype(bf16)
            to_here, to_there = emit_into(packs[side], width), emit_into(packs[1 - side], width)

            def emit(kind, lanes, value):
                (to_here if kind == 0 else to_there)(kind, lanes, value)

            attend_back(
                qkvs[side][0], qkvs[1 - side][1], qkvs[1 - side][2], probs[side], context, emit
            )
        bias_out[0:1] = column_sum(pack_all[:, HALF : HALF + width].astype(f32))
        bias_out[1:2] = column_sum(pack_all[:, HALF + 2 * width :].astype(f32))
        flush(pack_all, selected_all)
        part_all[...] = back_to_input(pack_all, weights, 1, width)

    ins = [(meta, "s")] + [(item, "h") for top in tops for item in top]
    ins += list(zip(joint, "hhf"))
    ins += [(post, "f"), (chooser, "f")] + [(a, "h") for a in (*qkvs, *probs)]
    ins += [(cross_in, "w"), (cross_out, "w")]
    outs = [
        ((total, D), f32, "h"),
        ((total, HALF), bf16, "h"),
        ((total, HALF + 3 * width), bf16, "h"),
        ((total, D), bf16, "h"),
        ((3, D), f32, "h"),
        ((2, width), f32, "h"),
    ]
    scratch = [
        pltpu.VMEM((3, D, width), bf16),
        pltpu.VMEM((width, D), bf16),
        pltpu.VMEM((2, 3, D), f32),
        pltpu.SemaphoreType.DMA((6,)),
    ]
    return call(body, ins, outs, scratch, 10.0, "cross_backward", ties, 16)


class Block:
    def __init__(self, in_selected, in_packs, in_gots, out_selected, out_pack, out_got):
        self.parts = [*in_selected, *in_packs, *in_gots, out_selected, out_pack, out_got]
        self.joined = len(in_packs) == 1
        self.kinds = "w" * len(self.parts)
        self.sizes = (out_pack.shape[1] - HALF, in_packs[0].shape[1] - HALF)
        self.rows = [array.shape[0] for array in in_selected]

    def buffers(self):
        return [
            pltpu.VMEM((2 * rows, HALF + size), bf16)
            for rows in self.rows
            for size in (self.sizes[1], self.sizes[0])
        ]

    def fetch(self, refs, buffers, sems, at):
        spans = spans_of(self.rows)
        in_selected, rest = refs[:2], refs[2:]
        if self.joined:
            pack, got, rest = [rest[0]] * 2, [rest[1]] * 2, rest[2:]
        else:
            pack, got, rest = rest[:2], rest[2:4], rest[4:]
        out_selected, out_pack, out_got = rest
        result = []
        for side in (0, 1):
            here, count = spans[side], self.rows[side]
            inner = here if self.joined else slice(0, count)
            per_side = []
            for kind, (selected, own, other, span) in enumerate(
                (
                    (in_selected[side], pack[side].at[inner], got[side].at[inner], None),
                    (out_selected.at[here], out_pack.at[here], out_got.at[here], here),
                )
            ):
                buffer = buffers[2 * side + kind]
                size = buffer.shape[1] - HALF
                mine = slice(0, count)
                copies = [
                    pltpu.make_async_copy(
                        selected, buffer.at[mine, pl.ds(0, HALF)], sems.at[at]
                    ),
                    pltpu.make_async_copy(
                        own.at[:, pl.ds(HALF, size)], buffer.at[mine, pl.ds(HALF, size)], sems.at[at + 1]
                    ),
                    pltpu.make_async_copy(
                        other, buffer.at[slice(count, 2 * count)], sems.at[at + 2]
                    ),
                ]
                at += 3
                for copy in copies:
                    copy.start()
                per_side.append((buffer, copies))
            result.append(per_side)
        return result, at


def chunk_order(groups):
    return [(s, z) for z in range(groups) for s in ((0, 1) if z % 2 == 0 else (1, 0))]


def gradients(blocks, cross, groups, name, ties=()):
    chunk = HALF // groups
    half = chunk // 2
    size = chunk + half if cross else chunk
    order = chunk_order(groups)
    aligned = half % 16 == 0
    width = sum(sum(block.sizes) for block in blocks)
    every = blocks + ([cross] if cross else [])
    n_in = sum(len(block.parts) for block in every)
    n_out = 1 if aligned else 3 if cross else 2
    n_sems = 12 * len(every) + 4 * len(every)

    def body(flush, *refs):
        inputs, outputs, rest = refs[:n_in], refs[n_in : n_in + n_out], list(refs[n_in + n_out :])
        if cross:
            cross_stage = rest.pop()
        stage, sems = rest.pop(), rest.pop()
        at = 0
        fetched = []
        for block in every:
            taken, inputs = inputs[: len(block.parts)], inputs[len(block.parts) :]
            own, rest = rest[:4], rest[4:]
            copies, at = block.fetch(taken, own, sems, at)
            fetched.append(copies)
        waited, leaving = set(), []

        def leave(source, side, columns, at):
            if not aligned:
                copies = [(source, outputs[side].at[:, columns])]
            elif side < 2:
                copies = [
                    (source.at[pl.ds(z * chunk, chunk)], outputs[0].at[pl.ds(k * size, chunk), columns])
                    for k, (s, z) in enumerate(order)
                    if s == side
                ]
            else:
                copies = [
                    (
                        source.at[pl.ds((s * groups + z) * half, half)],
                        outputs[0].at[pl.ds(k * size + chunk, half), columns],
                    )
                    for k, (s, z) in enumerate(order)
                ]
            for one, target in copies:
                copy = pltpu.make_async_copy(one, target, sems.at[at])
                copy.start()
                leaving.append(copy)

        def ready(item):
            buffer, copies = item
            if id(buffer) not in waited:
                waited.add(id(buffer))
                for copy in copies:
                    copy.wait()
            return buffer

        base = 0
        for block, copies in zip(blocks, fetched):
            for side in (0, 1):
                start = base
                for left, right in ((0, 1), (1, 0)):
                    left, right = ready(copies[side][left]), ready(copies[side][right])
                    turned = left[:, :HALF].T
                    span = right.shape[1] - HALF
                    for step in range(0, span, HALF):
                        value = mm(turned, right[:, HALF + step : HALF + step + HALF])
                        stage[side, :, start + step : start + step + HALF] = value.astype(bf16)
                    columns = pl.ds(start, span)
                    leave(stage.at[side, :, columns], side, columns, at)
                    at += 1
                    start += span
            base += sum(block.sizes)
        if cross:
            copies = fetched[-1]
            start = 0
            for left, right in ((0, 1), (1, 0)):
                lefts = [ready(copies[side][left])[:, :HALF].T for side in (0, 1)]
                rights = [ready(copies[side][right]) for side in (0, 1)]
                span = rights[0].shape[1] - HALF
                for step in range(0, span, HALF):
                    columns = slice(HALF + step, HALF + step + HALF)
                    value = mm(lefts[0], rights[0][:, columns]) + mm(lefts[1], rights[1][:, columns])
                    cross_stage[:, start + step : start + step + HALF] = value.astype(bf16)
                columns = pl.ds(start, span)
                leave(cross_stage.at[:, columns], 2, columns, at)
                at += 1
                start += span
        for copy in leaving:
            copy.wait()

    ins = [pair for block in every for pair in zip(block.parts, block.kinds)]
    if aligned:
        outs = [((2 * groups * size, width), bf16, "w")]
    else:
        outs = [((HALF, width), bf16, "w")] * n_out
    scratch = [buffer for block in every for buffer in block.buffers()]
    if cross:
        scratch += [
            pltpu.SemaphoreType.DMA((n_sems,)),
            pltpu.VMEM((2, HALF, width), bf16),
            pltpu.VMEM((HALF, sum(cross.sizes)), bf16),
        ]
    else:
        scratch += [pltpu.SemaphoreType.DMA((n_sems,)), pltpu.VMEM((2, HALF, width), bf16)]
    result = call(body, ins, outs, scratch, 6.0, name, ties, 20)
    if aligned:
        return result[0]
    chunks = [result[side].reshape(groups, chunk, width) for side in (0, 1)]
    pieces = [chunks[s][z] for s, z in order]
    if cross:
        extra = result[2].reshape(2, groups, half, width)
        pieces = [jnp.concatenate([one, extra[s, z]]) for one, (s, z) in zip(pieces, order)]
    return jnp.concatenate(pieces)


def placed_gradients(
    meta, feed1, late1, late_words, layer0, late_regions, chunk, width, units
):
    def body(flush, meta, feed1, late1, words_feed, words_late, layer0, regions, *outs):
        feed_in, feed_out, att_in, att_out, cross_in, cross_out = outs

        def store(side, feed, feed_base, late, late_base):
            feed_in[side] = feed[:, feed_base : feed_base + units].astype(f32)
            feed_out[side] = feed[:, feed_base + units : feed_base + 2 * units].astype(f32)
            for j in range(3):
                start = late_base + j * width
                att_in[side, j] = late[:chunk, start : start + width].astype(f32)
            att_out[side] = late[:chunk, late_base + 3 * width : late_base + 4 * width].astype(f32)

        items = [item.wait() for item in (feed1, late1, words_feed, words_late, layer0, regions)]
        feed1, late1, words_feed, words_late, layer0, regions = items

        @pl.when(meta[0] == 0)
        def _():
            store(0, layer0, 0, layer0, 2 * units)
            store(1, regions, 0, regions, 2 * units)

        @pl.when(meta[0] != 0)
        def _():
            store(0, words_feed, 0, words_late, 0)
            store(1, feed1, 0, late1, 0)

        for j in range(3):
            cross_in[j] = late1[chunk:, j * width : (j + 1) * width].astype(f32)
        cross_out[...] = late1[chunk:, 3 * width :].astype(f32)

    ins = [(meta, "s")]
    ins += [(item, "f") for item in (feed1, late1, *late_words, layer0, late_regions)]
    half = chunk // 2
    outs = [
        ((2, chunk, units), f32, "h"),
        ((2, chunk, units), f32, "h"),
        ((2, 3, chunk, width), f32, "h"),
        ((2, chunk, width), f32, "h"),
        ((3, half, width), f32, "h"),
        ((half, width), f32, "h"),
    ]
    return call(body, ins, outs, (), 4.0, "placed_gradients")


def swap(value, axis, distance=1):
    count = lax.axis_size(axis)
    return lax.ppermute(value, axis, [(i, i ^ distance) for i in range(count)])


def on_device(
    word_state,
    region_state,
    word_lengths,
    region_counts,
    word_cotangent,
    region_cotangent,
    cross_in,
    cross_bias,
    cross_out,
    cross_post,
    attention_in,
    attention_bias,
    attention_out,
    attention_post,
    feed_in,
    feed_bias,
    feed_out,
    feed_post,
):
    section = lax.axis_index("section")
    dp_count = lax.axis_size("dp")
    groups = dp_count // 2
    place = lax.axis_index("dp") % 2
    batch = word_state.shape[1]
    width = cross_out.shape[0]
    units = feed_in.shape[-1]
    both = (0, 1)
    chains = [[s * dp_count + 2 * z + y for s, z in chunk_order(groups)] for y in both]

    def flat(value):
        own = lax.dynamic_index_in_dim(value, section, 0, keepdims=False)
        return own.transpose(1, 0, 2).reshape(-1, D)

    def unflat(value):
        return value.reshape(-1, batch, D).transpose(1, 0, 2)[None]

    def chooser_of(pieces, per_section):
        column = jnp.arange(D)
        half = column // HALF
        inner = column % HALF
        side = jnp.where(half == 0, place, 1 - place)
        size = D // pieces
        if per_section:
            block = inner // (HALF // 2)
            inner = inner % (HALF // 2)
            feature = size * (dp_count * block + 2 * (inner // size) + side) + inner % size
        else:
            feature = size * (2 * (inner // size) + side) + inner % size
        return (jnp.arange(D)[:, None] == feature[None, :]).astype(bf16)

    chooser = chooser_of(dp_count, False)
    cross_chooser = chooser_of(2 * dp_count, True)

    small_own = jnp.concatenate(
        [
            attention_bias[0].reshape(2, 1, D),
            attention_post[0],
            feed_bias[0].reshape(2, -1, D),
            feed_post[0],
            jnp.zeros((2, SMALL_ROWS - 9, D), f32),
        ],
        axis=1,
    )
    small_other = swap(small_own, "section")
    smalls = [jnp.where(section == layer, small_own, small_other) for layer in both]
    small = [[smalls[layer][side] for side in both] for layer in both]
    att_in_own = attention_in.transpose(0, 1, 3, 2, 4)
    att_in = (att_in_own, swap(att_in_own, "section"))
    att_out = (attention_out, swap(attention_out, "section"))
    states = [flat(word_state), flat(region_state)]
    feed_in_later, feed_out_later, *_ = lax.optimization_barrier(
        (feed_in, feed_out, att_in[1], att_out[1], smalls[0], chooser, *states)
    )
    ff_in = (feed_in, swap(feed_in_later, "section"))
    ff_out = (feed_out, swap(feed_out_later, "section"))
    cross_entry = cross_in.transpose(1, 0, 2)

    lengths = [
        lax.dynamic_index_in_dim(value, section, 0, keepdims=False)
        for value in (word_lengths, region_counts)
    ]
    meta = jnp.concatenate([section[None].astype(jnp.int32), *lengths])
    cotangents = [flat(word_cotangent), flat(region_cotangent)]
    rows = [state.shape[0] for state in states]
    total_rows = sum(rows)

    def in_order(step, pack_index, tie=None, joined=True):
        results = [None, None]
        given = None
        for side in (1, 0):
            ties = () if tie is None else (tie,)
            place = (total_rows, rows[0] * side, given) if joined else ()
            results[side] = step(side, place, ties)
            tie, given = results[side][-1], results[side][pack_index]
        return results

    def over_mp(results, index):
        return [swap(results[side][index], "mp") for side in both]

    self0 = in_order(
        lambda side, place, ties: self_forward(
            side, 0, batch, meta, states[side], None, small[0][side], chooser, att_in, att_out,
            place, ties,
        ),
        3,
    )
    got = over_mp(self0, 4)
    feed0 = in_order(
        lambda side, place, ties: feed_forward(
            side, 0, batch, meta, states[side], self0[side][4], got[side], small[0][side], chooser,
            ff_in, ff_out, place, ties,
        ),
        4,
        self0[0][5],
    )
    got = over_mp(feed0, 6)
    self0_there = swap(self0[0][3], "dp")
    cross_w, cross_r, cross_pack = cross_forward(
        batch,
        meta,
        [(feed0[side][0], feed0[side][6], got[side]) for side in both],
        small[0],
        cross_chooser,
        cross_entry,
        cross_bias,
        cross_out,
        [(value, "a") for value in cotangents],
    )
    cross = (cross_w, cross_r)
    got = over_mp(cross, 7)
    feed0_there = swap(feed0[0][4], "dp")
    self1 = in_order(
        lambda side, place, ties: self_forward(
            side, 1, batch, meta, cross[side][0], (cross[side][7], got[side], cross_post),
            small[1][side], chooser, att_in, att_out, place, ties + (self0_there,),
        ),
        3,
    )
    got = over_mp(self1, 4)
    cross_there = swap(cross_pack, "dp")
    feed1 = in_order(
        lambda side, place, ties: feed_forward(
            side, 1, batch, meta, self1[side][6], self1[side][4], got[side], small[1][side], chooser,
            ff_in, ff_out, place, ties + (cross_there if side == 0 else feed0_there,),
        ),
        4,
        self1[0][5],
        False,
    )
    got = over_mp(feed1, 6)
    self1_there = swap(self1[0][3], "dp")
    feed1_there = [swap(feed1[side][4], "dp") for side in both]

    back_feed1 = feed_backward(
        1,
        batch,
        meta,
        [(feed1[side][0], feed1[side][6], got[side], cotangents[side]) for side in both],
        None,
        small[1],
        chooser,
        [feed1[side][5] for side in both],
        ff_in,
        ff_out,
        feed1_there[1:],
    )
    got = swap(back_feed1[3], "mp")
    back_feed1_there = swap(back_feed1[2], "dp")

    def scatter(value):
        return lax.psum_scatter(
            value, ("section", "dp"), scatter_dimension=0, axis_index_groups=chains, tiled=True
        )

    back_self1 = self_backward(
        1,
        meta,
        [feed1[side][1:3] for side in both],
        (back_feed1[0], back_feed1[3], got),
        small[1],
        chooser,
        [self1[side][0] for side in both],
        [self1[side][1] for side in both],
        att_in,
        att_out,
    )
    got = swap(back_self1[3], "mp")
    feed1_grads = gradients(
        [
            Block(
                [feed1[side][3] for side in both],
                [feed1[side][4] for side in both],
                feed1_there,
                *back_feed1[1:3],
                back_feed1_there,
            )
        ],
        None,
        groups,
        "feed_gradients_1",
        (back_self1[5],),
    )
    back_self1_there = swap(back_self1[2], "dp")
    back_cross = cross_backward(
        meta,
        [self1[side][7:9] for side in both],
        (back_self1[0], back_self1[3], got),
        cross_post,
        cross_chooser,
        [cross[side][5] for side in both],
        [cross[side][6] for side in both],
        cross_entry,
        cross_out,
        (feed1_grads, (self1_there, "w")),
    )
    cross_post_grad, cross_bias_grad = back_cross[4:6]
    got = swap(back_cross[3], "mp")
    back_cross_there = swap(back_cross[2], "dp")
    feed1_share = scatter(feed1_grads)

    back_feed0 = feed_backward(
        0,
        batch,
        meta,
        [cross[side][1:3] for side in both],
        (back_cross[0], back_cross[3], got),
        small[0],
        chooser,
        [feed0[side][5] for side in both],
        ff_in,
        ff_out,
        ((back_self1_there, "w"),),
    )
    got = swap(back_feed0[3], "mp")
    back_feed0_there = swap(back_feed0[2], "dp")
    late1_grads = gradients(
        [
            Block(
                [self1[side][2] for side in both],
                [self1[0][3]],
                [self1_there],
                *back_self1[1:3],
                back_self1_there,
            )
        ],
        Block(
            [cross[side][4] for side in both],
            [cross_pack],
            [cross_there],
            *back_cross[1:3],
            back_cross_there,
        ),
        groups,
        "late_gradients_1",
        (back_feed0[5],),
    )
    back_self0 = self_backward(
        0,
        meta,
        [feed0[side][1:3] for side in both],
        (back_feed0[0], back_feed0[3], got),
        small[0],
        chooser,
        [self0[side][0] for side in both],
        [self0[side][1] for side in both],
        att_in,
        att_out,
        (late1_grads,),
    )
    got = swap(back_self0[3], "mp")
    back_self0_there = swap(back_self0[2], "dp")
    late1_grads, feed1_share, back_feed0_there, _ = lax.optimization_barrier(
        (late1_grads, feed1_share, back_feed0_there, back_self0[5])
    )
    late1_share = scatter(late1_grads)
    layer0_grads = gradients(
        [
            Block(
                [feed0[side][3] for side in both],
                [feed0[0][4]],
                [feed0_there],
                *back_feed0[1:3],
                back_feed0_there,
            ),
            Block(
                [self0[side][2] for side in both],
                [self0[0][3]],
                [self0_there],
                *back_self0[1:3],
                back_self0_there,
            ),
        ],
        None,
        groups,
        "gradients_0",
        (back_self0[5],),
    )
    layer0_grads, late1_share = lax.optimization_barrier((layer0_grads, late1_share))
    layer0_share = scatter(layer0_grads)
    chunk = D // dp_count

    state_grad = (back_self0[0] + (back_self0[3].astype(f32) + got.astype(f32))).astype(bf16)
    spans = spans_of(rows)

    def packed(back_self, back_feed, squares):
        rows = [
            back_self[5].reshape(2, D),
            back_self[4].reshape(6, D),
            back_feed[5].reshape(-1, D),
            back_feed[4].reshape(6, D),
        ]
        row = jnp.concatenate([value.reshape(1, 128) for value in squares[:6]], axis=1)
        rest = jnp.concatenate([value.reshape(1, 128) for value in squares[6:]], axis=1)
        rest = jnp.concatenate([rest, jnp.zeros((1, D - rest.shape[1]), f32)], axis=1)
        return jnp.concatenate(rows + [row, rest], axis=0)

    def squares_of(lead, second, tail):
        result = []
        for side in both:
            result += [lead[side], second[side], tail[side][0:1], tail[side][1:2]]
        return result

    packs = [
        packed(
            back_self0,
            back_feed0,
            squares_of(
                [self0[side][5] for side in both],
                [feed0[side][7] for side in both],
                [cross[side][3] for side in both],
            ),
        ),
        packed(
            back_self1,
            back_feed1,
            squares_of(
                [self1[side][5] for side in both],
                [feed1[side][7] for side in both],
                [back_feed1[8][side] for side in both],
            ),
        ),
    ]
    counts = jnp.stack([jnp.sum(word_lengths), jnp.sum(region_counts)]).astype(f32)
    counts = jnp.pad(counts, (0, D - 2))[None] * 0.5
    mine = jnp.where(section == 0, packs[0], packs[1])
    theirs = jnp.where(section == 0, packs[1], packs[0])
    shared = [cross_post_grad, cross_bias_grad.reshape(1, D), counts]
    small_rows = packs[0].shape[0]
    total = jnp.concatenate([mine] + shared, axis=0) + swap(
        jnp.concatenate([theirs] + shared, axis=0), "section"
    )
    distance = 1
    while distance < dp_count:
        total = total + swap(total, "dp", distance)
        distance *= 2
    unit_rows = units // D
    at = 0
    att_bias_grad = total[0:2].reshape(1, 2, 2, width)
    at = 2
    att_post_grad = total[at : at + 6].reshape(1, 2, 3, D)
    at += 6
    feed_bias_grad = total[at : at + 2 * unit_rows].reshape(1, 2, units)
    at += 2 * unit_rows
    feed_post_grad = total[at : at + 6].reshape(1, 2, 3, D)
    at += 6
    squares = total[at : at + 2].reshape(-1, 128)[:8, 0]
    at = small_rows
    cross_post_total = total[at : at + 3]
    cross_bias_total = total[at + 3].reshape(2, width)
    valid_counts = total[at + 4, :2]
    scales = jnp.sqrt(squares / (jnp.repeat(valid_counts, 4) * D))[None]

    late_words = [
        lax.ppermute(value, "section", [(0, 1)]) for value in (feed1_share, late1_share[:chunk])
    ]
    outputs = (
        unflat(back_feed1[6]),
        unflat(back_feed1[7]),
        unflat(state_grad[spans[0]]),
        unflat(state_grad[spans[1]]),
        cross_bias_total,
        cross_post_total,
        att_bias_grad,
        att_post_grad,
        feed_bias_grad,
        feed_post_grad,
        scales,
    )
    layer0_share, late_words, outputs = lax.optimization_barrier((layer0_share, late_words, outputs))
    late_regions = lax.ppermute(layer0_share, "section", [(1, 0)])
    feed_in_grad, feed_out_grad, att_in_grad, att_out_grad, cross_in_grad, cross_out_grad = (
        placed_gradients(
            meta, feed1_share, late1_share, late_words, layer0_share, late_regions, chunk, width, units
        )
    )
    feed_in_grad = feed_in_grad[None]
    feed_out_grad = feed_out_grad.transpose(0, 2, 1)[None]
    att_in_grad = att_in_grad.transpose(0, 2, 1, 3)[None]
    att_out_grad = att_out_grad.transpose(0, 2, 1)[None]
    cross_in_grad = cross_in_grad.transpose(1, 0, 2)
    cross_out_grad = cross_out_grad.T
    return (
        *outputs[:4],
        cross_in_grad,
        outputs[4],
        cross_out_grad,
        outputs[5],
        att_in_grad,
        outputs[6],
        att_out_grad,
        outputs[7],
        feed_in_grad,
        outputs[8],
        feed_out_grad,
        outputs[9],
        outputs[10],
    )


def solution(mesh):
    placed = (
        P(None, "dp", None, None),
        P(None, "dp", None, None),
        P(None, "dp"),
        P(None, "dp"),
        P(None, "dp", None, None),
        P(None, "dp", None, None),
        P(None, None, "mp"),
        P(None, "mp"),
        P("mp", None),
        P(),
        P("section", None, None, None, "mp"),
        P("section", None, None, "mp"),
        P("section", None, "mp", None),
        P("section", None, None, None),
        P("section", None, None, "mp"),
        P("section", None, "mp"),
        P("section", None, "mp", None),
        P("section", None, None, None),
    )
    return jax.shard_map(
        on_device,
        mesh=mesh,
        in_specs=placed,
        out_specs=(
            P("section", "dp", None, None),
            P("section", "dp", None, None),
            P("section", "dp", None, None),
            P("section", "dp", None, None),
            P(("section", "dp"), None, "mp"),
            P(None, "mp"),
            P("mp", ("section", "dp")),
            P(),
            P("section", None, "dp", None, "mp"),
            P("section", None, None, "mp"),
            P("section", None, "mp", "dp"),
            P("section", None, None, None),
            P("section", None, "dp", "mp"),
            P("section", None, "mp"),
            P("section", None, "mp", "dp"),
            P("section", None, None, None),
            P("section", None),
        ),
        check_vma=False,
    )
```

```python
from functools import partial

import jax
import jax.numpy as jnp
from jax import lax
from jax.experimental import pallas as pl
from jax.experimental.pallas import tpu as pltpu
from jax.sharding import PartitionSpec as P

D = 768
HALF = D // 2
HEAD_DIM = 64
PAIR = 2 * HEAD_DIM
WORDS = 20
REGIONS = 36
EPS = 1e-06
SCALE = HEAD_DIM**-0.5
COST_SCALE = 0.5
bf16 = jnp.bfloat16
f32 = jnp.float32

ROW_ATT_BIAS, ROW_ATT_POST, ROW_FEED_BIAS, ROW_FEED_POST, SMALL_ROWS = 0, 1, 4, 6, 16


def mm(a, b):
    return jnp.dot(a, b, preferred_element_type=f32)


def mm_nt(a, b):
    return lax.dot_general(a, b, (((1,), (1,)), ((), ())), preferred_element_type=f32)


def mm_tn(a, b):
    return lax.dot_general(a, b, (((0,), (0,)), ((), ())), preferred_element_type=f32)


def norm_of(value, gain, shift):
    centred = value - jnp.mean(value, axis=-1, keepdims=True)
    spread = jnp.mean(centred * centred, axis=-1, keepdims=True)
    rstd = lax.rsqrt(spread + EPS)
    unit = centred * rstd
    return unit, rstd, unit * gain + shift


def norm_back(unit, rstd, gain, incoming):
    scaled = incoming * gain
    mean = jnp.mean(scaled, axis=-1, keepdims=True)
    along = jnp.mean(scaled * unit, axis=-1, keepdims=True)
    return (scaled - mean - unit * along) * rstd


def summed(own, other):
    return own[...].astype(f32) + other[...].astype(f32)


def column_sum(value):
    return jnp.sum(value, axis=0, keepdims=True)


def square_sum(value, valid):
    rows = jnp.sum(value * value, axis=-1, keepdims=True) * valid
    return jnp.broadcast_to(jnp.sum(rows, axis=0, keepdims=True), (1, 128))


def lengths_of(meta, side, batch, item):
    result = jnp.zeros_like(item)
    for i in range(batch):
        result = jnp.where(item == i, meta[1 + side * batch + i], result)
    return result


def row_valid(meta, side, batch, rows):
    index = lax.broadcasted_iota(jnp.int32, (rows, 1), 0)
    length = lengths_of(meta, side, batch, lax.rem(index, batch))
    return (lax.div(index, batch) < length).astype(f32)


def pair_valid(meta, side, batch, rows, keys):
    index = lax.broadcasted_iota(jnp.int32, (1, keys), 1)
    item = lax.rem(index, batch)
    length = lengths_of(meta, side, batch, item)
    item = jnp.where(lax.div(index, batch) < length, item, -1)
    row_item = lax.rem(lax.broadcasted_iota(jnp.int32, (rows, 1), 0), batch)
    return jnp.broadcast_to(row_item, (rows, keys)) == jnp.broadcast_to(item, (rows, keys))


def head_lanes(head):
    lane = lax.broadcasted_iota(jnp.int32, (1, PAIR), 1)
    return (lane // HEAD_DIM) == head


def attend(query, keys, values, valid, probs_ref, context_ref):
    for pair in range(query.shape[1] // PAIR):
        lanes = slice(pair * PAIR, (pair + 1) * PAIR)
        contexts = []
        for head in range(2):
            chosen = query[:, lanes] * head_lanes(head).astype(bf16)
            scores = mm_nt(chosen, keys[:, lanes]) * SCALE
            scores = jnp.where(valid, scores, -1e9)
            shifted = jnp.exp(scores - jnp.max(scores, axis=-1, keepdims=True))
            total = jnp.sum(shifted, axis=-1, keepdims=True)
            probs = (shifted * (1.0 / total)).astype(bf16)
            probs_ref[2 * pair + head] = probs
            contexts.append(mm(probs, values[:, lanes]))
        context_ref[:, lanes] = jnp.where(head_lanes(0), contexts[0], contexts[1]).astype(bf16)


def attend_back(query, keys, values, probs_ref, grad_context, emit):
    first = head_lanes(0)
    for pair in range(query.shape[1] // PAIR):
        lanes = slice(pair * PAIR, (pair + 1) * PAIR)
        grads = ([], [], [])
        for head in range(2):
            probs = probs_ref[2 * pair + head]
            chosen = grad_context[:, lanes] * head_lanes(head).astype(bf16)
            grad_probs = mm_nt(chosen, values[:, lanes])
            wide = probs.astype(f32)
            product = wide * grad_probs
            grad_scores = product - wide * jnp.sum(product, axis=-1, keepdims=True)
            grad_scores = grad_scores.astype(bf16)
            grads[0].append(mm(grad_scores, keys[:, lanes]) * SCALE)
            grads[1].append(mm_tn(grad_scores, query[:, lanes]) * SCALE)
            grads[2].append(mm_tn(probs, grad_context[:, lanes]))
        for kind in range(3):
            emit(kind, lanes, jnp.where(first, grads[kind][0], grads[kind][1]).astype(bf16))


class Fetched:
    def __init__(self, copy, buffer):
        self.copy, self.buffer, self.waited = copy, buffer, False
        self.shape, self.dtype = buffer.shape, buffer.dtype

    def wait(self):
        if not self.waited:
            self.copy.wait()
            self.waited = True
        return self.buffer

    def __getitem__(self, index):
        return self.wait()[index]


class Weights:
    def __init__(self, meta, layer, pairs, buffers, sems):
        self.copies = []
        mine = meta[0] == layer
        at = 0
        for (own, other, pieces), buffer in zip(pairs, buffers):
            copies = []
            for piece in pieces:
                copy = pltpu.make_async_copy(own.at[piece], buffer.at[piece], sems.at[at])
                if other is None:
                    copy.start()
                else:
                    second = pltpu.make_async_copy(
                        other.at[piece], buffer.at[piece], sems.at[at]
                    )
                    pl.when(mine)(copy.start)
                    pl.when(jnp.logical_not(mine))(second.start)
                copies.append(Fetched(copy, buffer))
                at += 1
            self.copies.append(copies)

    def get(self, slot, piece=None):
        copies = self.copies[slot]
        for copy in copies if piece is None else (copies[piece],):
            copy.wait()
        return copies[0].buffer


def maps(own, other, side, pieces=((),)):
    if other is None:
        return own, None, pieces
    return own.at[0, side], other.at[0, side], pieces


ENTRY = ((0,), (1,), (2,))


def column_pieces(size, count):
    return tuple(
        (slice(None), slice(i * size // count, (i + 1) * size // count)) for i in range(count)
    )


def row_pieces(size, count):
    return tuple((slice(i * size // count, (i + 1) * size // count),) for i in range(count))


def call(body, ins, outs, scratch=(), cost=0.0, name=None, ties=(), mib=14):
    spaces = {
        "s": pltpu.SMEM, "v": pltpu.VMEM, "w": pltpu.HBM, "h": pltpu.HBM, "a": pl.ANY, "f": pl.ANY
    }
    ties = [tie if isinstance(tie, tuple) else (tie, "w") for tie in ties]
    extra = [(i, out[5]) for i, out in enumerate(outs) if len(out) > 3 and out[5] is not None]
    aliases = {len(ins) + at: i for at, (i, _) in enumerate(extra)}
    ins = list(ins) + [(array, "w") for _, array in extra]
    places = [out[3:5] if len(out) > 3 else None for out in outs]
    fetched = [i for i, (_, kind) in enumerate(ins) if kind in "hf"]
    written = [i for i, out in enumerate(outs) if out[2] == "h"]
    n_ins, n_ties, n_outs, n_scratch = len(ins), len(ties), len(outs), len(scratch)

    def whole(*refs):
        given = list(refs[:n_ins])
        results = list(refs[n_ins + n_ties : n_ins + n_ties + n_outs])
        rest = refs[n_ins + n_ties + n_outs :]
        own, rest = rest[:n_scratch], rest[n_scratch:]
        buffers, rest = rest[: len(fetched)], rest[len(fetched) :]
        staged, rest = rest[: len(written)], rest[len(written) :]
        sems = rest[0] if rest else None
        for slot, i in enumerate(fetched):
            copy = pltpu.make_async_copy(given[i], buffers[slot], sems.at[slot])
            copy.start()
            given[i] = Fetched(copy, buffers[slot])
        leaving = {}
        for slot, i in enumerate(written):
            target = results[i]
            if places[i] is not None:
                target = target.at[pl.ds(places[i][1], staged[slot].shape[0])]
            copy = pltpu.make_async_copy(staged[slot], target, sems.at[len(fetched) + slot])
            leaving[id(staged[slot])] = copy
            results[i] = staged[slot]
        started = []

        def flush(*done):
            for ref in done:
                copy = leaving.pop(id(ref), None)
                if copy is not None:
                    copy.start()
                    started.append(copy)

        body(flush, *given[: n_ins - len(extra)], *results, *own)
        flush(*[staged[slot] for slot in range(len(written))])
        for copy in started:
            copy.wait()
        for item in given:
            if isinstance(item, Fetched):
                item.wait()

    arrays = [
        pltpu.with_memory_space_constraint(array, spaces[kind]) if kind in "vwh" else array
        for array, kind in [*ins, *ties]
    ]
    own_scratch = list(scratch)
    own_scratch += [pltpu.VMEM(arrays[i].shape, arrays[i].dtype) for i in fetched]
    own_scratch += [pltpu.VMEM(outs[i][0], outs[i][1]) for i in written]
    if fetched or written:
        own_scratch.append(pltpu.SemaphoreType.DMA((len(fetched) + len(written),)))
    return pl.pallas_call(
        whole,
        out_shape=[
            spaces[out[2]]((out[3], *out[0][1:]) if len(out) > 3 else out[0], out[1]) for out in outs
        ],
        in_specs=[pl.BlockSpec(memory_space=spaces[kind]) for _, kind in [*ins, *ties]],
        out_specs=[pl.BlockSpec(memory_space=spaces[out[2]]) for out in outs],
        input_output_aliases=aliases,
        scratch_shapes=own_scratch,
        compiler_params=pltpu.CompilerParams(vmem_limit_bytes=mib * 1024 * 1024),
        cost_estimate=pl.CostEstimate(
            flops=int(cost * COST_SCALE * 1.15e9), bytes_accessed=0, transcendentals=0
        ),
        name=name,
    )(*arrays)


def spans_of(rows):
    return slice(0, rows[0]), slice(rows[0], rows[0] + rows[1])


def select_rows(value, chooser, own_ref, pack_ref):
    moved = mm(value, chooser[...]).astype(bf16)
    own_ref[...] = moved[:, :HALF]
    pack_ref[:, :HALF] = moved[:, HALF:]


def project(low, weights, bias_q, bias_v, qkv_ref):
    qkv_ref[0] = (mm(low, weights.get(0, 0)[0]) + bias_q).astype(bf16)
    qkv_ref[1] = mm(low, weights.get(0, 1)[1]).astype(bf16)
    qkv_ref[2] = (mm(low, weights.get(0, 2)[2]) + bias_v).astype(bf16)


def self_forward(
    side, layer, batch, meta, state, prior, small, chooser, att_in, att_out, place, ties=()
):
    rows = state.shape[0]
    width = att_in[0].shape[-1]
    first = prior is None

    def body(flush, meta, state, *refs):
        refs = list(refs)
        if not first:
            own, other, post = refs[:3]
            refs = refs[3:]
        small, chooser, in_own, in_other, out_own, out_other = refs[:6]
        qkv, probs, selected, pack, part, squares = refs[6:12]
        refs = refs[12:]
        if not first:
            mixed_ref, unit_ref, rstd_ref = refs[:3]
            refs = refs[3:]
        in_buffer, out_buffer, sems = refs
        weights = Weights(
            meta,
            layer,
            (maps(in_own, in_other, side, ENTRY), maps(out_own, out_other, side)),
            (in_buffer, out_buffer),
            sems,
        )
        valid = row_valid(meta, side, batch, rows)
        if first:
            low = state[...]
            squares[...] = square_sum(low.astype(f32), valid)
        else:
            branch = summed(own, other) + post[0:1]
            squares[...] = square_sum(branch, valid)
            unit, rstd, mixed = norm_of(state[...].astype(f32) + branch, post[1:2], post[2:3])
            unit_ref[...] = unit
            rstd_ref[...] = rstd
            mixed_ref[...] = mixed
            low = mixed.astype(bf16)
        select_rows(low, chooser, selected, pack)
        flush(selected)
        biases = small[ROW_ATT_BIAS : ROW_ATT_BIAS + 1]
        project(low, weights, biases[:, :width], biases[:, width : 2 * width], qkv)
        context = pack.at[:, HALF:]
        attend(
            qkv[0], qkv[1], qkv[2], pair_valid(meta, side, batch, rows, rows), probs, context
        )
        flush(qkv, probs, pack)
        part[...] = mm(context[...], weights.get(1)[...]).astype(bf16)

    ins = [(meta, "s"), (state, "v")]
    if not first:
        ins += list(zip(prior, "vvv"))
    ins += [(small, "v"), (chooser, "v")]
    ins += list(zip(att_in + att_out, "wawa" if layer == 0 else "wwww"))
    outs = [
        ((3, rows, width), bf16, "h"),
        ((width // HEAD_DIM, rows, rows), bf16, "h"),
        ((rows, HALF), bf16, "h"),
        ((rows, HALF + width), bf16, "h", *place),
        ((rows, D), bf16, "v"),
        ((1, 128), f32, "h"),
    ]
    if not first:
        outs += [((rows, D), f32, "v"), ((rows, D), f32, "h"), ((rows, 1), f32, "h")]
    scratch = [
        pltpu.VMEM((3, D, width), bf16),
        pltpu.VMEM((width, D), bf16),
        pltpu.SemaphoreType.DMA((6,)),
    ]
    return call(body, ins, outs, scratch, 4.0, f"self_forward_{layer}_{side}", ties)


def feed_forward(
    side, layer, batch, meta, residual, own, other, small, chooser, feed_in, feed_out, place, ties=()
):
    rows = residual.shape[0]
    units = feed_in[0].shape[-1]
    step = units // 4

    def body(
        flush, meta, residual, own, other, small, chooser, in_own, in_other, out_own, out_other,
        settled_ref, unit_ref, rstd_ref, selected, pack, slope, part, squares,
        in_buffer, out_buffer, sems,
    ):
        weights = Weights(
            meta,
            layer,
            (
                maps(in_own, in_other, side, column_pieces(units, 4)),
                maps(out_own, out_other, side, row_pieces(units, 2)),
            ),
            (in_buffer, out_buffer),
            sems,
        )
        post = small[ROW_ATT_POST : ROW_ATT_POST + 3]
        branch = summed(own, other) + post[0:1]
        squares[...] = square_sum(branch, row_valid(meta, side, batch, rows))
        unit, rstd, settled = norm_of(residual[...].astype(f32) + branch, post[1:2], post[2:3])
        unit_ref[...] = unit
        rstd_ref[...] = rstd
        settled_ref[...] = settled
        low = settled.astype(bf16)
        select_rows(low, chooser, selected, pack)
        flush(unit_ref, rstd_ref, selected)
        for i in range(units // step):
            first = weights.get(0, i)
            columns = slice(i * step, (i + 1) * step)
            row = ROW_FEED_BIAS + (i * step) // D
            place = (i * step) % D
            hidden = mm(low, first[:, columns]) + small[row : row + 1, place : place + step]
            below = 0.5 + 0.5 * lax.erf(hidden * (0.5**0.5))
            density = jnp.exp(hidden * hidden * -0.5) * 0.3989422804014327
            pack[:, HALF + i * step : HALF + (i + 1) * step] = (hidden * below).astype(bf16)
            slope[:, columns] = (below + hidden * density).astype(bf16)
        flush(pack, slope)
        part[...] = mm(pack[:, HALF:], weights.get(1)[...]).astype(bf16)

    ins = [(meta, "s"), (residual, "v"), (own, "v"), (other, "v")]
    ins += [(small, "v"), (chooser, "v")]
    ins += list(zip(feed_in + feed_out, "wawa" if layer == 0 else "wwww"))
    outs = [
        ((rows, D), f32, "v"),
        ((rows, D), f32, "h"),
        ((rows, 1), f32, "h"),
        ((rows, HALF), bf16, "h"),
        ((rows, HALF + units), bf16, "h", *place),
        ((rows, units), bf16, "h"),
        ((rows, D), bf16, "v"),
        ((1, 128), f32, "h"),
    ]
    scratch = [
        pltpu.VMEM((D, units), bf16),
        pltpu.VMEM((units, D), bf16),
        pltpu.SemaphoreType.DMA((6,)),
    ]
    return call(body, ins, outs, scratch, 4.3, f"feed_forward_{layer}_{side}", ties)


def cross_forward(
    batch, meta, streams, smalls, chooser, cross_in, cross_bias, cross_out, ties=()
):
    rows = [stream[0].shape[0] for stream in streams]
    spans = spans_of(rows)
    width = cross_out.shape[0]
    heads = width // HEAD_DIM

    def body(flush, meta, *refs):
        given = (refs[0:3], refs[3:6])
        small, chooser, in_ref, bias, out_ref = (refs[6:8], *refs[8:12])
        all_pack = refs[28]
        outs = [refs[12:20], refs[20:28]]
        for side in (0, 1):
            outs[side] = outs[side][:5] + (all_pack.at[spans[side]],) + outs[side][5:]
        in_buffer, out_buffer, sems = refs[29:]
        weights = Weights(
            meta,
            0,
            (maps(in_ref, None, 0, ENTRY), maps(out_ref, None, 0)),
            (in_buffer, out_buffer),
            sems,
        )
        lows = []
        for side in (0, 1):
            settled, own, other = given[side]
            state, unit_ref, rstd_ref, squares, selected, pack, qkv, probs, part = outs[side]
            post = small[side][ROW_FEED_POST : ROW_FEED_POST + 3]
            branch = summed(own, other) + post[0:1]
            unit, rstd, result = norm_of(settled[...] + branch, post[1:2], post[2:3])
            unit_ref[...] = unit
            rstd_ref[...] = rstd
            low = result.astype(bf16)
            state[...] = low
            valid = row_valid(meta, side, batch, rows[side])
            squares[0:1] = square_sum(branch, valid)
            squares[1:2] = square_sum(low.astype(f32), valid)
            select_rows(low, chooser, selected, pack)
            flush(unit_ref, rstd_ref, selected)
            lows.append(low)
        for side in (0, 1):
            project(lows[side], weights, bias[0:1], bias[1:2], outs[side][6])
        leave = weights.get(1)
        for side in (0, 1):
            pack, qkv, probs, part = outs[side][5:]
            there = outs[1 - side][6]
            valid = pair_valid(meta, 1 - side, batch, rows[side], rows[1 - side])
            context = pack.at[:, HALF:]
            attend(qkv[0], there[1], there[2], valid, probs, context)
            flush(qkv, probs)
            part[...] = mm(context[...], leave[...]).astype(bf16)

    ins = [(meta, "s")] + [pair for stream in streams for pair in zip(stream, "vvv")]
    ins += [(item, "v") for item in smalls]
    ins += [(chooser, "v"), (cross_in, "w"), (cross_bias, "v"), (cross_out, "w")]
    outs = []
    for side in (0, 1):
        here, there = rows[side], rows[1 - side]
        outs += [
            ((here, D), bf16, "v"),
            ((here, D), f32, "h"),
            ((here, 1), f32, "h"),
            ((2, 128), f32, "h"),
            ((here, HALF), bf16, "h"),
            ((3, here, width), bf16, "h"),
            ((heads, here, there), bf16, "h"),
            ((here, D), bf16, "v"),
        ]
    outs.append(((sum(rows), HALF + width), bf16, "h"))
    scratch = [
        pltpu.VMEM((3, D, width), bf16),
        pltpu.VMEM((width, D), bf16),
        pltpu.SemaphoreType.DMA((6,)),
    ]
    result = call(body, ins, outs, scratch, 6.8, "cross_forward", ties)
    return result[:8], result[8:16], result[16]


class Layout:
    def __init__(self, sides, rows, given):
        self.sides, self.total, self.spans = sides, sum(rows), spans_of(rows)
        self.single = len(sides) == 1
        self.side = sides[0]
        self.count = rows[self.side] if self.single else self.total
        self.given = given

    def here(self, side):
        return slice(0, self.count) if self.single else self.spans[side]

    def index(self, side):
        return 0 if self.single else side

    def rows(self, width, dtype, at):
        if not self.single:
            return (self.total, width), dtype, "h"
        given = self.given[at] if self.given else None
        return (self.count, width), dtype, "h", self.total, self.spans[self.side].start, given

    def each(self, shape, at):
        if not self.single:
            return (2, *shape), f32, "h"
        given = self.given[at] if self.given else None
        return (1, *shape), f32, "h", 2, self.side, given


def feed_backward(
    layer, sides, rows, batch, meta, tops, joint, small, chooser, slopes, feed_in, feed_out, ties=(),
    given=None,
):
    last = joint is None
    layout = Layout(sides, rows, given)
    units = slopes[0].shape[1]
    step = units // 4
    n_top = len(tops[0])
    n = len(sides)

    def body(flush, meta, *refs):
        tops = {}
        for side in sides:
            tops[side], refs = refs[:n_top], refs[n_top:]
        if not last:
            joint, refs = refs[:3], refs[3:]
        small, refs = dict(zip(sides, refs[:n])), refs[n:]
        chooser, slopes, refs = refs[0], dict(zip(sides, refs[1 : 1 + n])), refs[1 + n :]
        in_own, in_other, out_own, out_other = refs[:4]
        grad_all, selected_all, pack_all, part_all, post_all, bias_all = refs[4:10]
        if last:
            squares_all, results = refs[10], dict(zip(sides, refs[11 : 11 + n]))
        in_buffer, out_buffer, sems = refs[-3:]
        weights = {}
        for i, side in enumerate(sides):
            weights[side] = Weights(
                meta,
                layer,
                (
                    maps(out_own, out_other, side, row_pieces(units, 4)),
                    maps(in_own, in_other, side, column_pieces(units, 2)),
                ),
                (out_buffer.at[i], in_buffer.at[i]),
                sems.at[i],
            )
        lows = {}
        for side in sides:
            here, at = layout.here(side), layout.index(side)
            post = small[side][ROW_FEED_POST : ROW_FEED_POST + 3]
            if last:
                settled, own, other, cotangent = tops[side]
                branch = summed(own, other) + post[0:1]
                unit, rstd, result = norm_of(settled[...] + branch, post[1:2], post[2:3])
                low = result.astype(bf16)
                results[side][...] = low
                valid = row_valid(meta, side, batch, rows[side])
                squares_all[at, 0:1] = square_sum(branch, valid)
                squares_all[at, 1:2] = square_sum(low.astype(f32), valid)
                incoming = cotangent[...].astype(f32) * valid
            else:
                unit_ref, rstd_ref = tops[side]
                unit, rstd = unit_ref[...], rstd_ref[...]
                incoming = (joint[0][here] + summed_rows(joint[1], joint[2], here)).astype(bf16)
                incoming = incoming.astype(f32)
            grad = norm_back(unit, rstd, post[1:2], incoming)
            grad_all[here] = grad
            low = grad.astype(bf16)
            post_all[at, 0:1] = column_sum(low.astype(f32))
            post_all[at, 1:2] = column_sum(incoming * unit)
            post_all[at, 2:3] = column_sum(incoming)
            lows[side] = low
        flush(grad_all, post_all)
        for side in sides:
            here, at = layout.here(side), layout.index(side)
            for i in range(units // step):
                columns = slice(i * step, (i + 1) * step)
                active = mm_nt(lows[side], weights[side].get(0, i)[columns, :])
                hidden = (active * slopes[side][:, columns].astype(f32)).astype(bf16)
                pack_all[here, HALF + i * step : HALF + (i + 1) * step] = hidden
                bias_all[at, :, columns] = column_sum(hidden.astype(f32))
            select_rows(lows[side], chooser, selected_all.at[here], pack_all.at[here])
        flush(pack_all, selected_all)
        for side in sides:
            here = layout.here(side)
            part_all[here] = mm_nt(pack_all[here, HALF:], weights[side].get(1)[...]).astype(bf16)

    ins = [(meta, "s")] + [pair for top in tops for pair in zip(top, "vvvv" if last else "vv")]
    if not last:
        ins += [(item, "v") for item in joint]
    ins += [(item, "v") for item in (*small, chooser, *slopes)]
    ins += list(zip(feed_in + feed_out, "wwww"))
    count = layout.count
    outs = [
        ((count, D), f32, "v" if last else "h"),
        layout.rows(HALF, bf16, 1),
        ((count, HALF + units), bf16, "h"),
        ((count, D), bf16, "v" if last else "h"),
        layout.each((3, D), 4),
        layout.each((1, units), 5),
    ]
    if last:
        outs += [layout.each((2, 128), 6)] + [((rows[side], D), bf16, "h") for side in sides]
    scratch = [
        pltpu.VMEM((n, D, units), bf16),
        pltpu.VMEM((n, units, D), bf16),
        pltpu.SemaphoreType.DMA((n, 6)),
    ]
    name = f"feed_backward_{layer}_" + "".join(map(str, sides))
    return call(body, ins, outs, scratch, 11.0 * count / layout.total, name, ties, 24)


def summed_rows(own, other, here):
    return own[here].astype(f32) + other[here].astype(f32)


def back_through_norm(top, grad_in, branch, gain, grad_ref, post_ref):
    unit_ref, rstd_ref = top
    incoming = grad_in + branch
    unit = unit_ref[...]
    grad = norm_back(unit, rstd_ref[...], gain, incoming)
    grad_ref[...] = grad
    low = grad.astype(bf16)
    post_ref[0:1] = column_sum(low.astype(f32))
    post_ref[1:2] = column_sum(incoming * unit)
    post_ref[2:3] = column_sum(incoming)
    return low


def emit_into(pack, width):
    def emit(kind, lanes, value):
        start = HALF + kind * width + lanes.start
        pack[:, start : start + PAIR] = value

    return emit


def back_to_input(pack, weights, slot, width):
    grads = [pack[:, HALF + j * width : HALF + (j + 1) * width] for j in range(3)]
    total = mm_nt(grads[0], weights.get(slot, 0)[0])
    total += mm_nt(grads[1], weights.get(slot, 1)[1])
    total += mm_nt(grads[2], weights.get(slot, 2)[2])
    return total.astype(bf16)


def self_backward(
    layer, sides, rows, meta, tops, joint, small, chooser, qkvs, probs, att_in, att_out, ties=(),
    given=None,
):
    layout = Layout(sides, rows, given)
    width = qkvs[0].shape[2]
    n = len(sides)

    def body(flush, meta, *refs):
        tops = {side: refs[2 * i : 2 * i + 2] for i, side in enumerate(sides)}
        joint, refs = refs[2 * n : 2 * n + 3], refs[2 * n + 3 :]
        small, chooser, refs = dict(zip(sides, refs[:n])), refs[n], refs[n + 1 :]
        qkvs, probs, refs = dict(zip(sides, refs[:n])), dict(zip(sides, refs[n : 2 * n])), refs[2 * n :]
        in_own, in_other, out_own, out_other = refs[:4]
        grad_all, selected_all, pack_all, part_all, post_all, bias_all = refs[4:10]
        in_buffer, out_buffer, sems = refs[10:]
        weights = {}
        for i, side in enumerate(sides):
            weights[side] = Weights(
                meta,
                layer,
                (maps(out_own, out_other, side), maps(in_own, in_other, side, ENTRY)),
                (out_buffer.at[i], in_buffer.at[i]),
                sems.at[i],
            )
        for side in sides:
            here, at = layout.here(side), layout.index(side)
            pack = pack_all.at[here]
            gain = small[side][ROW_ATT_POST + 1 : ROW_ATT_POST + 2]
            low = back_through_norm(
                tops[side],
                joint[0][here],
                summed_rows(joint[1], joint[2], here),
                gain,
                grad_all.at[here],
                post_all.at[at],
            )
            context = mm_nt(low, weights[side].get(0)[...]).astype(bf16)
            qkv = qkvs[side]
            attend_back(qkv[0], qkv[1], qkv[2], probs[side], context, emit_into(pack, width))
            bias_all[at, 0:1] = column_sum(pack[:, HALF : HALF + width].astype(f32))
            bias_all[at, 1:2] = column_sum(pack[:, HALF + 2 * width :].astype(f32))
            select_rows(low, chooser, selected_all.at[here], pack)
        flush(pack_all, selected_all, grad_all, post_all, bias_all)
        for side in sides:
            here = layout.here(side)
            part_all[here] = back_to_input(pack_all.at[here], weights[side], 1, width)

    near = "v" if layer == 1 else "h"
    ins = [(meta, "s")] + [(item, near) for top in tops for item in top]
    ins += [*zip(joint, "vvv" if layer == 1 else "hhf")] + [(item, near) for item in small]
    ins += [(item, near) for item in (chooser, *qkvs, *probs)]
    ins += list(zip(att_in + att_out, "wwww"))
    outs = [
        ((layout.count, D), f32, "h"),
        layout.rows(HALF, bf16, 1),
        layout.rows(HALF + 3 * width, bf16, 2),
        ((layout.count, D), bf16, "h"),
        layout.each((3, D), 4),
        layout.each((2, width), 5),
    ]
    scratch = [
        pltpu.VMEM((n, 3, D, width), bf16),
        pltpu.VMEM((n, width, D), bf16),
        pltpu.SemaphoreType.DMA((n, 6)),
    ]
    name = f"self_backward_{layer}_" + "".join(map(str, sides))
    return call(body, ins, outs, scratch, 12.0 * layout.count / layout.total, name, ties, 18)


def cross_backward(meta, tops, grads, owns, others, post, chooser, qkvs, probs, cross_in, cross_out, ties=()):
    rows = [qkv.shape[1] for qkv in qkvs]
    width = cross_out.shape[0]
    spans, total = spans_of(rows), sum(rows)

    def body(flush, meta, *refs):
        tops, grads, owns, others = (refs[:2], refs[2:4]), refs[4:6], refs[6:8], refs[8:10]
        post, chooser, qkvs, probs = refs[10], refs[11], refs[12:14], refs[14:16]
        in_ref, out_ref = refs[16:18]
        grad_all, selected_all, pack_all, part_all, post_out, bias_out = refs[18:24]
        in_buffer, out_buffer, post_each, sems = refs[24:]
        weights = Weights(
            meta,
            0,
            (maps(out_ref, None, 0), maps(in_ref, None, 0, ENTRY)),
            (out_buffer, in_buffer),
            sems,
        )
        packs = [pack_all.at[here] for here in spans]
        lows = []
        for side in (0, 1):
            here = spans[side]
            low = back_through_norm(
                tops[side],
                grads[side][...],
                summed(owns[side], others[side]),
                post[1:2],
                grad_all.at[here],
                post_each.at[side],
            )
            lows.append(low)
        post_out[...] = post_each[0] + post_each[1]
        leave = weights.get(0)
        for side in (0, 1):
            context = mm_nt(lows[side], leave[...]).astype(bf16)
            to_here, to_there = emit_into(packs[side], width), emit_into(packs[1 - side], width)

            def emit(kind, lanes, value):
                (to_here if kind == 0 else to_there)(kind, lanes, value)

            attend_back(
                qkvs[side][0], qkvs[1 - side][1], qkvs[1 - side][2], probs[side], context, emit
            )
        for side in (0, 1):
            select_rows(lows[side], chooser, selected_all.at[spans[side]], packs[side])
        bias_out[0:1] = column_sum(pack_all[:, HALF : HALF + width].astype(f32))
        bias_out[1:2] = column_sum(pack_all[:, HALF + 2 * width :].astype(f32))
        flush(pack_all, selected_all)
        part_all[...] = back_to_input(pack_all, weights, 1, width)

    ins = [(meta, "s")] + [(item, "h") for top in tops for item in top]
    ins += [(item, "h") for item in (*grads, *owns)] + [(item, "f") for item in others]
    ins += [(item, "h") for item in (post, chooser, *qkvs, *probs)]
    ins += [(cross_in, "w"), (cross_out, "w")]
    outs = [
        ((total, D), f32, "v"),
        ((total, HALF), bf16, "h"),
        ((total, HALF + 3 * width), bf16, "h"),
        ((total, D), bf16, "v"),
        ((3, D), f32, "h"),
        ((2, width), f32, "h"),
    ]
    scratch = [
        pltpu.VMEM((3, D, width), bf16),
        pltpu.VMEM((width, D), bf16),
        pltpu.VMEM((2, 3, D), f32),
        pltpu.SemaphoreType.DMA((6,)),
    ]
    return call(body, ins, outs, scratch, 10.0, "cross_backward", ties, 16)


class Block:
    def __init__(self, in_selected, in_packs, in_gots, out_selected, out_packs, out_gots):
        self.parts = [*in_selected, *in_packs, *in_gots, out_selected, *out_packs, *out_gots]
        self.counts = (len(in_packs), len(out_packs))
        self.kinds = "w" * len(self.parts)
        self.sizes = (out_packs[0].shape[1] - HALF, in_packs[0].shape[1] - HALF)
        self.rows = [array.shape[0] for array in in_selected]

    def buffers(self):
        return [
            pltpu.VMEM((2 * rows, HALF + size), bf16)
            for rows in self.rows
            for size in (self.sizes[1], self.sizes[0])
        ]

    def fetch(self, refs, buffers, sems, at):
        spans = spans_of(self.rows)
        in_selected, rest = refs[:2], refs[2:]
        n_in, n_out = self.counts
        pack, got, rest = rest[:n_in], rest[n_in : 2 * n_in], rest[2 * n_in :]
        out_selected, out_pack, out_got = rest[0], rest[1 : 1 + n_out], rest[1 + n_out :]

        def rows_of(items, side):
            return items[0].at[spans[side]] if len(items) == 1 else items[side]

        result = []
        for side in (0, 1):
            count = self.rows[side]
            per_side = []
            for kind, (selected, own, other) in enumerate(
                (
                    (in_selected[side], rows_of(pack, side), rows_of(got, side)),
                    (out_selected.at[spans[side]], rows_of(out_pack, side), rows_of(out_got, side)),
                )
            ):
                buffer = buffers[2 * side + kind]
                size = buffer.shape[1] - HALF
                mine = slice(0, count)
                copies = [
                    pltpu.make_async_copy(
                        selected, buffer.at[mine, pl.ds(0, HALF)], sems.at[at]
                    ),
                    pltpu.make_async_copy(
                        own.at[:, pl.ds(HALF, size)], buffer.at[mine, pl.ds(HALF, size)], sems.at[at + 1]
                    ),
                    pltpu.make_async_copy(
                        other, buffer.at[slice(count, 2 * count)], sems.at[at + 2]
                    ),
                ]
                at += 3
                for copy in copies:
                    copy.start()
                per_side.append((buffer, copies))
            result.append(per_side)
        return result, at


def chunk_order(groups):
    return [(s, z) for z in range(groups) for s in ((0, 1) if z % 2 == 0 else (1, 0))]


def gradients(meta, blocks, cross, groups, name, ties=(), split=False):
    chunk = HALF // groups
    half = chunk // 2
    size = chunk + half if cross else chunk
    order = chunk_order(groups)
    aligned = half % 16 == 0
    width = sum(sum(block.sizes) for block in blocks)
    every = blocks + ([cross] if cross else [])
    n_in = sum(len(block.parts) for block in every)
    n_out = 2 if split else 1 if aligned else 3 if cross else 2
    n_sems = 12 * len(every) + 4 * len(every)

    def body(flush, meta, *refs):
        inputs, outputs, rest = refs[:n_in], refs[n_in : n_in + n_out], list(refs[n_in + n_out :])
        if cross:
            cross_stage = rest.pop()
        stage, sems = rest.pop(), rest.pop()
        at = 0
        fetched = []
        for block in every:
            taken, inputs = inputs[: len(block.parts)], inputs[len(block.parts) :]
            own, rest = rest[:4], rest[4:]
            copies, at = block.fetch(taken, own, sems, at)
            fetched.append(copies)
        waited, leaving = set(), []

        def leave(source, side, columns, at):
            if split:
                kept = pltpu.make_async_copy(source, outputs[0].at[:, columns], sems.at[at])
                sent = pltpu.make_async_copy(source, outputs[1].at[:, columns], sems.at[at])
                pl.when(meta[0] == side)(kept.start)
                pl.when(meta[0] != side)(sent.start)
                leaving.append(kept)
                return
            if not aligned:
                copies = [(source, outputs[side].at[:, columns])]
            elif side < 2:
                copies = [
                    (source.at[pl.ds(z * chunk, chunk)], outputs[0].at[pl.ds(k * size, chunk), columns])
                    for k, (s, z) in enumerate(order)
                    if s == side
                ]
            else:
                copies = [
                    (
                        source.at[pl.ds((s * groups + z) * half, half)],
                        outputs[0].at[pl.ds(k * size + chunk, half), columns],
                    )
                    for k, (s, z) in enumerate(order)
                ]
            for one, target in copies:
                copy = pltpu.make_async_copy(one, target, sems.at[at])
                copy.start()
                leaving.append(copy)

        def ready(item):
            buffer, copies = item
            if id(buffer) not in waited:
                waited.add(id(buffer))
                for copy in copies:
                    copy.wait()
            return buffer

        base = 0
        for block, copies in zip(blocks, fetched):
            for side in (0, 1):
                start = base
                for left, right in ((0, 1), (1, 0)):
                    left, right = ready(copies[side][left]), ready(copies[side][right])
                    turned = left[:, :HALF].T
                    span = right.shape[1] - HALF
                    for step in range(0, span, HALF):
                        value = mm(turned, right[:, HALF + step : HALF + step + HALF])
                        stage[side, :, start + step : start + step + HALF] = value.astype(bf16)
                    columns = pl.ds(start, span)
                    leave(stage.at[side, :, columns], side, columns, at)
                    at += 1
                    start += span
            base += sum(block.sizes)
        if cross:
            copies = fetched[-1]
            start = 0
            for left, right in ((0, 1), (1, 0)):
                lefts = [ready(copies[side][left])[:, :HALF].T for side in (0, 1)]
                rights = [ready(copies[side][right]) for side in (0, 1)]
                span = rights[0].shape[1] - HALF
                for step in range(0, span, HALF):
                    columns = slice(HALF + step, HALF + step + HALF)
                    value = mm(lefts[0], rights[0][:, columns]) + mm(lefts[1], rights[1][:, columns])
                    cross_stage[:, start + step : start + step + HALF] = value.astype(bf16)
                columns = pl.ds(start, span)
                leave(cross_stage.at[:, columns], 2, columns, at)
                at += 1
                start += span
        for copy in leaving:
            copy.wait()

    ins = [(meta, "s")] + [pair for block in every for pair in zip(block.parts, block.kinds)]
    if aligned and not split:
        outs = [((2 * groups * size, width), bf16, "w")]
    else:
        outs = [((HALF, width), bf16, "w")] * n_out
    scratch = [buffer for block in every for buffer in block.buffers()]
    if cross:
        scratch += [
            pltpu.SemaphoreType.DMA((n_sems,)),
            pltpu.VMEM((2, HALF, width), bf16),
            pltpu.VMEM((HALF, sum(cross.sizes)), bf16),
        ]
    else:
        scratch += [pltpu.SemaphoreType.DMA((n_sems,)), pltpu.VMEM((2, HALF, width), bf16)]
    result = call(body, ins, outs, scratch, 6.0, name, ties, 20)
    if split:
        return result
    if aligned:
        return result[0]
    chunks = [result[side].reshape(groups, chunk, width) for side in (0, 1)]
    pieces = [chunks[s][z] for s, z in order]
    if cross:
        extra = result[2].reshape(2, groups, half, width)
        pieces = [jnp.concatenate([one, extra[s, z]]) for one, (s, z) in zip(pieces, order)]
    return jnp.concatenate(pieces)


def placed_gradients(
    meta, feed1, late1, late_words, layer0, late_regions, chunk, width, units
):
    def body(flush, meta, feed1, late1, words_feed, words_late, layer0, regions, *outs):
        feed_in, feed_out, att_in, att_out, cross_in, cross_out = outs

        def store(side, feed, feed_base, late, late_base):
            feed_in[side] = feed[:, feed_base : feed_base + units].astype(f32)
            feed_out[side] = feed[:, feed_base + units : feed_base + 2 * units].astype(f32)
            for j in range(3):
                start = late_base + j * width
                att_in[side, j] = late[:chunk, start : start + width].astype(f32)
            att_out[side] = late[:chunk, late_base + 3 * width : late_base + 4 * width].astype(f32)

        items = [item.wait() for item in (feed1, late1, words_feed, words_late, layer0, regions)]
        feed1, late1, words_feed, words_late, layer0, regions = items

        @pl.when(meta[0] == 0)
        def _():
            store(0, layer0, 0, layer0, 2 * units)
            store(1, regions, 0, regions, 2 * units)

        @pl.when(meta[0] != 0)
        def _():
            store(0, words_feed, 0, words_late, 0)
            store(1, feed1, 0, late1, 0)

        for j in range(3):
            cross_in[j] = late1[chunk:, j * width : (j + 1) * width].astype(f32)
        cross_out[...] = late1[chunk:, 3 * width :].astype(f32)

    ins = [(meta, "s")]
    ins += [(item, "f") for item in (feed1, late1, *late_words, layer0, late_regions)]
    half = chunk // 2
    outs = [
        ((2, chunk, units), f32, "h"),
        ((2, chunk, units), f32, "h"),
        ((2, 3, chunk, width), f32, "h"),
        ((2, chunk, width), f32, "h"),
        ((3, half, width), f32, "h"),
        ((half, width), f32, "h"),
    ]
    return call(body, ins, outs, (), 4.0, "placed_gradients")


def swap(value, axis, distance=1):
    count = lax.axis_size(axis)
    return lax.ppermute(value, axis, [(i, i ^ distance) for i in range(count)])


def on_device(
    word_state,
    region_state,
    word_lengths,
    region_counts,
    word_cotangent,
    region_cotangent,
    cross_in,
    cross_bias,
    cross_out,
    cross_post,
    attention_in,
    attention_bias,
    attention_out,
    attention_post,
    feed_in,
    feed_bias,
    feed_out,
    feed_post,
):
    section = lax.axis_index("section")
    dp_count = lax.axis_size("dp")
    groups = dp_count // 2
    place = lax.axis_index("dp") % 2
    batch = word_state.shape[1]
    width = cross_out.shape[0]
    units = feed_in.shape[-1]
    both = (0, 1)
    chains = [[s * dp_count + 2 * z + y for s, z in chunk_order(groups)] for y in both]

    def flat(value):
        own = lax.dynamic_index_in_dim(value, section, 0, keepdims=False)
        return own.transpose(1, 0, 2).reshape(-1, D)

    def unflat(value):
        return value.reshape(-1, batch, D).transpose(1, 0, 2)[None]

    def chooser_of(pieces, per_section):
        column = jnp.arange(D)
        half = column // HALF
        inner = column % HALF
        side = jnp.where(half == 0, place, 1 - place)
        size = D // pieces
        if per_section:
            block = inner // (HALF // 2)
            inner = inner % (HALF // 2)
            feature = size * (dp_count * block + 2 * (inner // size) + side) + inner % size
        else:
            feature = size * (2 * (inner // size) + side) + inner % size
        return (jnp.arange(D)[:, None] == feature[None, :]).astype(bf16)

    chooser = chooser_of(dp_count, False)
    cross_chooser = chooser_of(2 * dp_count, True)

    small_own = jnp.concatenate(
        [
            attention_bias[0].reshape(2, 1, D),
            attention_post[0],
            feed_bias[0].reshape(2, -1, D),
            feed_post[0],
            jnp.zeros((2, SMALL_ROWS - 9, D), f32),
        ],
        axis=1,
    )
    small_other = swap(small_own, "section")
    smalls = [jnp.where(section == layer, small_own, small_other) for layer in both]
    small = [[smalls[layer][side] for side in both] for layer in both]
    att_in_own = attention_in.transpose(0, 1, 3, 2, 4)
    att_in = (att_in_own, swap(att_in_own, "section"))
    att_out = (attention_out, swap(attention_out, "section"))
    states = [flat(word_state), flat(region_state)]
    feed_in_later, feed_out_later, *_ = lax.optimization_barrier(
        (feed_in, feed_out, att_in[1], att_out[1], smalls[0], chooser, cross_chooser, *states)
    )
    ff_in = (feed_in, swap(feed_in_later, "section"))
    ff_out = (feed_out, swap(feed_out_later, "section"))
    cross_entry = cross_in.transpose(1, 0, 2)

    lengths = [
        lax.dynamic_index_in_dim(value, section, 0, keepdims=False)
        for value in (word_lengths, region_counts)
    ]
    meta = jnp.concatenate([section[None].astype(jnp.int32), *lengths])
    cotangents = [flat(word_cotangent), flat(region_cotangent)]
    rows = [state.shape[0] for state in states]
    total_rows = sum(rows)

    def in_order(step, pack_index, tie=None, joined=True):
        results = [None, None]
        given = None
        for side in (1, 0):
            ties = () if tie is None else (tie,)
            place = (total_rows, rows[0] * side, given) if joined else ()
            results[side] = step(side, place, ties)
            tie, given = results[side][-1], results[side][pack_index]
        return results

    def over_mp(results, index):
        return [swap(results[side][index], "mp") for side in both]

    self0 = in_order(
        lambda side, place, ties: self_forward(
            side, 0, batch, meta, states[side], None, small[0][side], chooser, att_in, att_out,
            place, ties,
        ),
        3,
    )
    got = over_mp(self0, 4)
    feed0 = in_order(
        lambda side, place, ties: feed_forward(
            side, 0, batch, meta, states[side], self0[side][4], got[side], small[0][side], chooser,
            ff_in, ff_out, place, ties,
        ),
        4,
        self0[0][5],
    )
    got = over_mp(feed0, 6)
    self0_there = swap(self0[0][3], "dp")
    cross_w, cross_r, cross_pack = cross_forward(
        batch,
        meta,
        [(feed0[side][0], feed0[side][6], got[side]) for side in both],
        small[0],
        cross_chooser,
        cross_entry,
        cross_bias,
        cross_out,
    )
    cross = (cross_w, cross_r)
    got = over_mp(cross, 7)
    feed0_there = swap(feed0[0][4], "dp")
    self1 = in_order(
        lambda side, place, ties: self_forward(
            side, 1, batch, meta, cross[side][0], (cross[side][7], got[side], cross_post),
            small[1][side], chooser, att_in, att_out, place, ties + ((self0_there, "a"), (cotangents[side], "w")),
        ),
        3,
    )
    got = over_mp(self1, 4)
    cross_there = swap(cross_pack, "dp")
    feed1 = in_order(
        lambda side, place, ties: feed_forward(
            side, 1, batch, meta, self1[side][6], self1[side][4], got[side], small[1][side], chooser,
            ff_in, ff_out, place, ties + ((cross_there if side == 0 else feed0_there, "a"),),
        ),
        4,
        self1[0][5],
        False,
    )
    got = over_mp(feed1, 6)
    self1_there = swap(self1[0][3], "dp")
    feed1_there = [swap(feed1[side][4], "dp") for side in both]

    given, back_feed1 = None, [None, None]
    for side in (1, 0):
        given = feed_backward(
            1,
            (side,),
            rows,
            batch,
            meta,
            [(feed1[side][0], feed1[side][6], got[side], cotangents[side])],
            None,
            [small[1][side]],
            chooser,
            [feed1[side][5]],
            ff_in,
            ff_out,
            ((feed1_there[side], "a"),),
            given,
        )
        back_feed1[side] = given
    got = over_mp(back_feed1, 3)
    back_feed1_there = [swap(back_feed1[side][2], "dp") for side in both]

    def scatter(value):
        return lax.psum_scatter(
            value, ("section", "dp"), scatter_dimension=0, axis_index_groups=chains, tiled=True
        )

    given, back_self1 = None, [None, None]
    for side in (1, 0):
        given = self_backward(
            1,
            (side,),
            rows,
            meta,
            [feed1[side][1:3]],
            (back_feed1[side][0], back_feed1[side][3], got[side]),
            [small[1][side]],
            chooser,
            [self1[side][0]],
            [self1[side][1]],
            att_in,
            att_out,
            (),
            given,
        )
        back_self1[side] = given
    got = over_mp(back_self1, 3)
    feed1_grads = gradients(
        meta,
        [
            Block(
                [feed1[side][3] for side in both],
                [feed1[side][4] for side in both],
                feed1_there,
                back_feed1[0][1],
                [back_feed1[side][2] for side in both],
                back_feed1_there,
            )
        ],
        None,
        groups,
        "feed_gradients_1",
        (back_self1[0][5],),
    )
    back_self1_there = swap(back_self1[0][2], "dp")
    back_cross = cross_backward(
        meta,
        [self1[side][7:9] for side in both],
        [back_self1[side][0] for side in both],
        [back_self1[side][3] for side in both],
        got,
        cross_post,
        cross_chooser,
        [cross[side][5] for side in both],
        [cross[side][6] for side in both],
        cross_entry,
        cross_out,
        (feed1_grads, (self1_there, "a")),
    )
    cross_post_grad, cross_bias_grad = back_cross[4:6]
    got = swap(back_cross[3], "mp")
    back_cross_there = swap(back_cross[2], "dp")
    feed1_share = scatter(feed1_grads)

    back_feed0 = feed_backward(
        0,
        (1, 0),
        rows,
        batch,
        meta,
        [cross[side][1:3] for side in (1, 0)],
        (back_cross[0], back_cross[3], got),
        small[0][::-1],
        chooser,
        [feed0[side][5] for side in (1, 0)],
        ff_in,
        ff_out,
        ((back_self1_there, "a"),),
    )
    got = swap(back_feed0[3], "mp")
    back_feed0_there = swap(back_feed0[2], "dp")
    late1_grads = gradients(
        meta,
        [
            Block(
                [self1[side][2] for side in both],
                [self1[0][3]],
                [self1_there],
                back_self1[0][1],
                [back_self1[0][2]],
                [back_self1_there],
            )
        ],
        Block(
            [cross[side][4] for side in both],
            [cross_pack],
            [cross_there],
            back_cross[1],
            [back_cross[2]],
            [back_cross_there],
        ),
        groups,
        "late_gradients_1",
        (back_feed0[5],),
    )
    back_self0 = self_backward(
        0,
        (1, 0),
        rows,
        meta,
        [feed0[side][1:3] for side in (1, 0)],
        (back_feed0[0], back_feed0[3], got),
        small[0][::-1],
        chooser,
        [self0[side][0] for side in (1, 0)],
        [self0[side][1] for side in (1, 0)],
        att_in,
        att_out,
        (late1_grads,),
    )
    got = swap(back_self0[3], "mp")
    back_self0_there = swap(back_self0[2], "dp")
    late1_share = scatter(late1_grads)
    layer0_grads = gradients(
        meta,
        [
            Block(
                [feed0[side][3] for side in both],
                [feed0[0][4]],
                [feed0_there],
                back_feed0[1],
                [back_feed0[2]],
                [back_feed0_there],
            ),
            Block(
                [self0[side][2] for side in both],
                [self0[0][3]],
                [self0_there],
                back_self0[1],
                [back_self0[2]],
                [back_self0_there],
            ),
        ],
        None,
        groups,
        "gradients_0",
        (back_self0[5], feed1_share),
        True,
    )
    layer0_kept, layer0_sent = layer0_grads
    layer0_total = layer0_kept.astype(f32) + swap(layer0_sent, "section").astype(f32)
    layer0_total, late1_share = lax.optimization_barrier((layer0_total.astype(bf16), late1_share))
    layer0_share = lax.psum_scatter(
        layer0_total,
        "dp",
        scatter_dimension=0,
        axis_index_groups=[[2 * z + y for z in range(groups)] for y in both],
        tiled=True,
    )
    chunk = D // dp_count

    state_grad = (back_self0[0] + (back_self0[3].astype(f32) + got.astype(f32))).astype(bf16)
    spans = spans_of(rows)

    def packed(back_self, back_feed, squares):
        rows = [
            back_self[5].reshape(2, D),
            back_self[4].reshape(6, D),
            back_feed[5].reshape(-1, D),
            back_feed[4].reshape(6, D),
        ]
        row = jnp.concatenate([value.reshape(1, 128) for value in squares[:6]], axis=1)
        rest = jnp.concatenate([value.reshape(1, 128) for value in squares[6:]], axis=1)
        rest = jnp.concatenate([rest, jnp.zeros((1, D - rest.shape[1]), f32)], axis=1)
        return jnp.concatenate(rows + [row, rest], axis=0)

    def squares_of(lead, second, tail):
        result = []
        for side in both:
            result += [lead[side], second[side], tail[side][0:1], tail[side][1:2]]
        return result

    packs = [
        packed(
            back_self0,
            back_feed0,
            squares_of(
                [self0[side][5] for side in both],
                [feed0[side][7] for side in both],
                [cross[side][3] for side in both],
            ),
        ),
        packed(
            back_self1[0],
            back_feed1[0],
            squares_of(
                [self1[side][5] for side in both],
                [feed1[side][7] for side in both],
                [back_feed1[0][6][side] for side in both],
            ),
        ),
    ]
    counts = jnp.stack([jnp.sum(word_lengths), jnp.sum(region_counts)]).astype(f32)
    counts = jnp.pad(counts, (0, D - 2))[None] * 0.5
    mine = jnp.where(section == 0, packs[0], packs[1])
    theirs = jnp.where(section == 0, packs[1], packs[0])
    shared = [cross_post_grad, cross_bias_grad.reshape(1, D), counts]
    small_rows = packs[0].shape[0]
    total = jnp.concatenate([mine] + shared, axis=0) + swap(
        jnp.concatenate([theirs] + shared, axis=0), "section"
    )
    distance = 1
    while distance < dp_count:
        total = total + swap(total, "dp", distance)
        distance *= 2
    unit_rows = units // D
    at = 0
    att_bias_grad = total[0:2].reshape(1, 2, 2, width)
    at = 2
    att_post_grad = total[at : at + 6].reshape(1, 2, 3, D)
    at += 6
    feed_bias_grad = total[at : at + 2 * unit_rows].reshape(1, 2, units)
    at += 2 * unit_rows
    feed_post_grad = total[at : at + 6].reshape(1, 2, 3, D)
    at += 6
    squares = total[at : at + 2].reshape(-1, 128)[:8, 0]
    at = small_rows
    cross_post_total = total[at : at + 3]
    cross_bias_total = total[at + 3].reshape(2, width)
    valid_counts = total[at + 4, :2]
    scales = jnp.sqrt(squares / (jnp.repeat(valid_counts, 4) * D))[None]

    late_words = [
        lax.ppermute(value, "section", [(0, 1)]) for value in (feed1_share, late1_share[:chunk])
    ]
    outputs = (
        unflat(back_feed1[0][7]),
        unflat(back_feed1[1][7]),
        unflat(state_grad[spans[0]]),
        unflat(state_grad[spans[1]]),
        cross_bias_total,
        cross_post_total,
        att_bias_grad,
        att_post_grad,
        feed_bias_grad,
        feed_post_grad,
        scales,
    )
    layer0_share, late_words, outputs = lax.optimization_barrier((layer0_share, late_words, outputs))
    late_regions = lax.ppermute(layer0_share, "section", [(1, 0)])
    feed_in_grad, feed_out_grad, att_in_grad, att_out_grad, cross_in_grad, cross_out_grad = (
        placed_gradients(
            meta, feed1_share, late1_share, late_words, layer0_share, late_regions, chunk, width, units
        )
    )
    feed_in_grad = feed_in_grad[None]
    feed_out_grad = feed_out_grad.transpose(0, 2, 1)[None]
    att_in_grad = att_in_grad.transpose(0, 2, 1, 3)[None]
    att_out_grad = att_out_grad.transpose(0, 2, 1)[None]
    cross_in_grad = cross_in_grad.transpose(1, 0, 2)
    cross_out_grad = cross_out_grad.T
    return (
        *outputs[:4],
        cross_in_grad,
        outputs[4],
        cross_out_grad,
        outputs[5],
        att_in_grad,
        outputs[6],
        att_out_grad,
        outputs[7],
        feed_in_grad,
        outputs[8],
        feed_out_grad,
        outputs[9],
        outputs[10],
    )


def solution(mesh):
    placed = (
        P(None, "dp", None, None),
        P(None, "dp", None, None),
        P(None, "dp"),
        P(None, "dp"),
        P(None, "dp", None, None),
        P(None, "dp", None, None),
        P(None, None, "mp"),
        P(None, "mp"),
        P("mp", None),
        P(),
        P("section", None, None, None, "mp"),
        P("section", None, None, "mp"),
        P("section", None, "mp", None),
        P("section", None, None, None),
        P("section", None, None, "mp"),
        P("section", None, "mp"),
        P("section", None, "mp", None),
        P("section", None, None, None),
    )
    return jax.shard_map(
        on_device,
        mesh=mesh,
        in_specs=placed,
        out_specs=(
            P("section", "dp", None, None),
            P("section", "dp", None, None),
            P("section", "dp", None, None),
            P("section", "dp", None, None),
            P(("section", "dp"), None, "mp"),
            P(None, "mp"),
            P("mp", ("section", "dp")),
            P(),
            P("section", None, "dp", None, "mp"),
            P("section", None, None, "mp"),
            P("section", None, "mp", "dp"),
            P("section", None, None, None),
            P("section", None, "dp", "mp"),
            P("section", None, "mp"),
            P("section", None, "mp", "dp"),
            P("section", None, None, None),
            P("section", None),
        ),
        check_vma=False,
    )
```

```python
from functools import partial

import jax
import jax.numpy as jnp
from jax import lax
from jax.experimental import pallas as pl
from jax.experimental.pallas import tpu as pltpu
from jax.sharding import PartitionSpec as P

D = 768
HALF = D // 2
HEAD_DIM = 64
PAIR = 2 * HEAD_DIM
WORDS = 20
REGIONS = 36
EPS = 1e-06
SCALE = HEAD_DIM**-0.5
COST_SCALE = 0.5
ORDER = (1, 0)
bf16 = jnp.bfloat16
f32 = jnp.float32

ROW_ATT_BIAS, ROW_ATT_POST, ROW_FEED_BIAS, ROW_FEED_POST, SMALL_ROWS = 0, 1, 4, 6, 16


def mm(a, b):
    return jnp.dot(a, b, preferred_element_type=f32)


def mm_nt(a, b):
    return lax.dot_general(a, b, (((1,), (1,)), ((), ())), preferred_element_type=f32)


def mm_tn(a, b):
    return lax.dot_general(a, b, (((0,), (0,)), ((), ())), preferred_element_type=f32)


def norm_of(value, gain, shift):
    centred = value - jnp.mean(value, axis=-1, keepdims=True)
    spread = jnp.mean(centred * centred, axis=-1, keepdims=True)
    rstd = lax.rsqrt(spread + EPS)
    unit = centred * rstd
    return unit, rstd, unit * gain + shift


def norm_back(unit, rstd, gain, incoming):
    scaled = incoming * gain
    mean = jnp.mean(scaled, axis=-1, keepdims=True)
    along = jnp.mean(scaled * unit, axis=-1, keepdims=True)
    return (scaled - mean - unit * along) * rstd


def summed(own, other):
    return own[...].astype(f32) + other[...].astype(f32)


def column_sum(value):
    return jnp.sum(value, axis=0, keepdims=True)


def square_sum(value, valid):
    rows = jnp.sum(value * value, axis=-1, keepdims=True) * valid
    return jnp.broadcast_to(jnp.sum(rows, axis=0, keepdims=True), (1, 128))


def lengths_of(meta, side, batch, item):
    result = jnp.zeros_like(item)
    for i in range(batch):
        result = jnp.where(item == i, meta[1 + side * batch + i], result)
    return result


def row_valid(meta, side, batch, rows):
    index = lax.broadcasted_iota(jnp.int32, (rows, 1), 0)
    length = lengths_of(meta, side, batch, lax.rem(index, batch))
    return (lax.div(index, batch) < length).astype(f32)


def pair_valid(meta, side, batch, rows, keys):
    index = lax.broadcasted_iota(jnp.int32, (1, keys), 1)
    item = lax.rem(index, batch)
    length = lengths_of(meta, side, batch, item)
    item = jnp.where(lax.div(index, batch) < length, item, -1)
    row_item = lax.rem(lax.broadcasted_iota(jnp.int32, (rows, 1), 0), batch)
    return jnp.broadcast_to(row_item, (rows, keys)) == jnp.broadcast_to(item, (rows, keys))


def head_lanes(head):
    lane = lax.broadcasted_iota(jnp.int32, (1, PAIR), 1)
    return (lane // HEAD_DIM) == head


def attend(query, keys, values, valid, probs_ref, context_ref):
    for pair in range(query.shape[1] // PAIR):
        lanes = slice(pair * PAIR, (pair + 1) * PAIR)
        contexts = []
        for head in range(2):
            chosen = query[:, lanes] * head_lanes(head).astype(bf16)
            scores = mm_nt(chosen, keys[:, lanes]) * SCALE
            scores = jnp.where(valid, scores, -1e9)
            shifted = jnp.exp(scores - jnp.max(scores, axis=-1, keepdims=True))
            total = jnp.sum(shifted, axis=-1, keepdims=True)
            probs = (shifted * (1.0 / total)).astype(bf16)
            probs_ref[2 * pair + head] = probs
            contexts.append(mm(probs, values[:, lanes]))
        context_ref[:, lanes] = jnp.where(head_lanes(0), contexts[0], contexts[1]).astype(bf16)


def attend_back(query, keys, values, probs_ref, grad_context, emit):
    first = head_lanes(0)
    for pair in range(query.shape[1] // PAIR):
        lanes = slice(pair * PAIR, (pair + 1) * PAIR)
        grads = ([], [], [])
        for head in range(2):
            probs = probs_ref[2 * pair + head]
            chosen = grad_context[:, lanes] * head_lanes(head).astype(bf16)
            grad_probs = mm_nt(chosen, values[:, lanes])
            wide = probs.astype(f32)
            product = wide * grad_probs
            grad_scores = product - wide * jnp.sum(product, axis=-1, keepdims=True)
            grad_scores = grad_scores.astype(bf16)
            grads[0].append(mm(grad_scores, keys[:, lanes]) * SCALE)
            grads[1].append(mm_tn(grad_scores, query[:, lanes]) * SCALE)
            grads[2].append(mm_tn(probs, grad_context[:, lanes]))
        for kind in range(3):
            emit(kind, lanes, jnp.where(first, grads[kind][0], grads[kind][1]).astype(bf16))


def small_of(meta, layer, side, own, other):
    return jnp.where(meta[0] == layer, own[side], other[side])


class Fetched:
    def __init__(self, copy, buffer):
        self.copy, self.buffer, self.waited = copy, buffer, False
        self.shape, self.dtype = buffer.shape, buffer.dtype

    def wait(self):
        if not self.waited:
            self.copy.wait()
            self.waited = True
        return self.buffer

    def __getitem__(self, index):
        return self.wait()[index]


class Weights:
    def __init__(self, meta, layer, pairs, buffers, sems):
        self.copies = []
        mine = meta[0] == layer
        at = 0
        for (own, other, pieces), buffer in zip(pairs, buffers):
            copies = []
            for piece in pieces:
                copy = pltpu.make_async_copy(own.at[piece], buffer.at[piece], sems.at[at])
                if other is None:
                    copy.start()
                else:
                    second = pltpu.make_async_copy(
                        other.at[piece], buffer.at[piece], sems.at[at]
                    )
                    pl.when(mine)(copy.start)
                    pl.when(jnp.logical_not(mine))(second.start)
                copies.append(Fetched(copy, buffer))
                at += 1
            self.copies.append(copies)

    def get(self, slot, piece=None):
        copies = self.copies[slot]
        for copy in copies if piece is None else (copies[piece],):
            copy.wait()
        return copies[0].buffer


class Held:
    def __init__(self, *refs):
        self.refs = refs

    def get(self, slot, piece=None):
        return self.refs[slot]


def weight_inputs(entry, leave, kinds="wwww"):
    if len(entry) == 1:
        return [(entry[0], "v"), (leave[0], "v")]
    return list(zip(entry + leave, kinds))


def pass_on(meta, layer, offered, taken, sems):
    copies = []
    for i, target in enumerate(taken):
        own = pltpu.make_async_copy(offered[2 * i].at[0], target, sems.at[i])
        other = pltpu.make_async_copy(offered[2 * i + 1].at[0], target, sems.at[i])
        pl.when(meta[0] == layer)(own.start)
        pl.when(meta[0] != layer)(other.start)
        copies.append(own)
    return copies


def items_of(meta, source, raw, rows_ref, sem, batch):
    copy = pltpu.make_async_copy(source.at[meta[0]], raw, sem)
    copy.start()
    copy.wait()
    for slot in range(raw.shape[0]):
        rows_ref[slot * batch : (slot + 1) * batch] = raw[slot].astype(f32)


def maps(own, other, side, pieces=((),)):
    if other is None:
        return own, None, pieces
    return own.at[0, side], other.at[0, side], pieces


ENTRY = ((0,), (1,), (2,))


def column_pieces(size, count):
    return tuple(
        (slice(None), slice(i * size // count, (i + 1) * size // count)) for i in range(count)
    )


def row_pieces(size, count):
    return tuple((slice(i * size // count, (i + 1) * size // count),) for i in range(count))


def call(body, ins, outs, scratch=(), cost=0.0, name=None, ties=(), mib=14):
    spaces = {
        "s": pltpu.SMEM, "v": pltpu.VMEM, "w": pltpu.HBM, "h": pltpu.HBM, "a": pl.ANY, "f": pl.ANY
    }
    ties = [tie if isinstance(tie, tuple) else (tie, "w") for tie in ties]
    extra = [(i, out[5]) for i, out in enumerate(outs) if len(out) > 3 and out[5] is not None]
    aliases = {len(ins) + at: i for at, (i, _) in enumerate(extra)}
    ins = list(ins) + [(array, "w") for _, array in extra]
    places = [out[3:5] if len(out) > 3 else None for out in outs]
    fetched = [i for i, (_, kind) in enumerate(ins) if kind in "hf"]
    written = [i for i, out in enumerate(outs) if out[2] == "h"]
    n_ins, n_ties, n_outs, n_scratch = len(ins), len(ties), len(outs), len(scratch)

    def whole(*refs):
        given = list(refs[:n_ins])
        results = list(refs[n_ins + n_ties : n_ins + n_ties + n_outs])
        rest = refs[n_ins + n_ties + n_outs :]
        own, rest = rest[:n_scratch], rest[n_scratch:]
        buffers, rest = rest[: len(fetched)], rest[len(fetched) :]
        staged, rest = rest[: len(written)], rest[len(written) :]
        sems = rest[0] if rest else None
        for slot, i in enumerate(fetched):
            copy = pltpu.make_async_copy(given[i], buffers[slot], sems.at[slot])
            copy.start()
            given[i] = Fetched(copy, buffers[slot])
        leaving = {}
        for slot, i in enumerate(written):
            target = results[i]
            if places[i] is not None:
                target = target.at[pl.ds(places[i][1], staged[slot].shape[0])]
            copy = pltpu.make_async_copy(staged[slot], target, sems.at[len(fetched) + slot])
            leaving[id(staged[slot])] = copy
            results[i] = staged[slot]
        started = []

        def flush(*done):
            for ref in done:
                copy = leaving.pop(id(ref), None)
                if copy is not None:
                    copy.start()
                    started.append(copy)

        body(flush, *given[: n_ins - len(extra)], *results, *own)
        flush(*[staged[slot] for slot in range(len(written))])
        for copy in started:
            copy.wait()
        for item in given:
            if isinstance(item, Fetched):
                item.wait()

    arrays = [
        pltpu.with_memory_space_constraint(array, spaces[kind]) if kind in "vwh" else array
        for array, kind in [*ins, *ties]
    ]
    own_scratch = list(scratch)
    own_scratch += [pltpu.VMEM(arrays[i].shape, arrays[i].dtype) for i in fetched]
    own_scratch += [pltpu.VMEM(outs[i][0], outs[i][1]) for i in written]
    if fetched or written:
        own_scratch.append(pltpu.SemaphoreType.DMA((len(fetched) + len(written),)))
    return pl.pallas_call(
        whole,
        out_shape=[
            spaces[out[2]]((out[3], *out[0][1:]) if len(out) > 3 else out[0], out[1]) for out in outs
        ],
        in_specs=[pl.BlockSpec(memory_space=spaces[kind]) for _, kind in [*ins, *ties]],
        out_specs=[pl.BlockSpec(memory_space=spaces[out[2]]) for out in outs],
        input_output_aliases=aliases,
        scratch_shapes=own_scratch,
        compiler_params=pltpu.CompilerParams(vmem_limit_bytes=mib * 1024 * 1024),
        cost_estimate=pl.CostEstimate(
            flops=int(cost * COST_SCALE * 1.15e9), bytes_accessed=0, transcendentals=0
        ),
        name=name,
    )(*arrays)


def spans_of(rows):
    return slice(0, rows[0]), slice(rows[0], rows[0] + rows[1])


def select_rows(value, chooser, own_ref, pack_ref):
    moved = mm(value, chooser[...]).astype(bf16)
    own_ref[...] = moved[:, :HALF]
    pack_ref[:, :HALF] = moved[:, HALF:]


def project(low, weights, bias_q, bias_v, qkv_ref):
    qkv_ref[0] = (mm(low, weights.get(0, 0)[0]) + bias_q).astype(bf16)
    qkv_ref[1] = mm(low, weights.get(0, 1)[1]).astype(bf16)
    qkv_ref[2] = (mm(low, weights.get(0, 2)[2]) + bias_v).astype(bf16)


def self_forward(
    side, layer, batch, meta, state, prior, small, chooser, att_in, att_out, place, ties=(), later=()
):
    rows = state.shape[1] * batch if prior is None else state.shape[0]
    width = att_in[0].shape[-1]
    first = prior is None
    held, n_maps = len(att_in) == 1, len(att_in + att_out)

    def body(flush, meta, state, *refs):
        refs = list(refs)
        if not first:
            own, other, post = refs[:3]
            refs = refs[3:]
        small = small_of(meta, layer, side, refs[0], refs[1])
        chooser, refs = refs[2], refs[3:]
        given, refs = refs[:n_maps], refs[n_maps:]
        offered, refs = refs[: 2 * len(later)], refs[2 * len(later) :]
        qkv, probs, selected, pack, part, squares = refs[:6]
        refs = refs[6:]
        if not first:
            mixed_ref, unit_ref, rstd_ref = refs[:3]
            taken, refs = refs[3 : 3 + len(later)], refs[3 + len(later) :]
            passing = pass_on(meta, layer, offered, taken, refs[-1]) if later else []
        else:
            low_ref, refs = refs[0], refs[1:]
            raw, rows_ref, raw_sem = refs[-3:]
            refs = refs[:-3]
        if held:
            weights = Held(given[0].at[side], given[1].at[side])
        else:
            in_buffer, out_buffer, sems = refs
            weights = Weights(
                meta,
                layer,
                (maps(*given[:2], side, ENTRY), maps(*given[2:], side)),
                (in_buffer, out_buffer),
                sems,
            )
        valid = row_valid(meta, side, batch, rows)
        if first:
            items_of(meta, state, raw, rows_ref, raw_sem, batch)
            squares[...] = square_sum(rows_ref[...], valid)
            low = rows_ref[...].astype(bf16)
            low_ref[...] = low
        else:
            branch = summed(own, other) + post[0:1]
            squares[...] = square_sum(branch, valid)
            unit, rstd, mixed = norm_of(state[...].astype(f32) + branch, post[1:2], post[2:3])
            unit_ref[...] = unit
            rstd_ref[...] = rstd
            mixed_ref[...] = mixed
            low = mixed.astype(bf16)
        select_rows(low, chooser, selected, pack)
        flush(selected)
        biases = small[ROW_ATT_BIAS : ROW_ATT_BIAS + 1]
        project(low, weights, biases[:, :width], biases[:, width : 2 * width], qkv)
        context = pack.at[:, HALF:]
        attend(
            qkv[0], qkv[1], qkv[2], pair_valid(meta, side, batch, rows, rows), probs, context
        )
        flush(qkv, probs, pack)
        part[...] = mm(context[...], weights.get(1)[...]).astype(bf16)
        if not first:
            for copy in passing:
                copy.wait()

    ins = [(meta, "s"), (state, "w" if first else "v")]
    if not first:
        ins += list(zip(prior, "vvv"))
    ins += [(item, "v") for item in (*small, chooser)]
    ins += weight_inputs(att_in, att_out, "wawa")
    ins += [(item, "w") for pair in later for item in pair]
    outs = [
        ((3, rows, width), bf16, "h"),
        ((width // HEAD_DIM, rows, rows), bf16, "h"),
        ((rows, HALF), bf16, "h"),
        ((rows, HALF + width), bf16, "h", *place),
        ((rows, D), bf16, "v"),
        ((1, 128), f32, "h"),
    ]
    if not first:
        outs += [((rows, D), f32, "v"), ((rows, D), f32, "h"), ((rows, 1), f32, "h")]
        outs += [(pair[0].shape[1:], bf16, "v") for pair in later]
    else:
        outs.append(((rows, D), bf16, "v"))
    scratch = [
        pltpu.VMEM((3, D, width), bf16),
        pltpu.VMEM((width, D), bf16),
        pltpu.SemaphoreType.DMA((6,)),
    ]
    scratch = [] if held else scratch
    if first:
        scratch += [
            pltpu.VMEM(state.shape[1:], bf16),
            pltpu.VMEM((rows, D), f32),
            pltpu.SemaphoreType.DMA,
        ]
    if later:
        scratch.append(pltpu.SemaphoreType.DMA((len(later),)))
    return call(body, ins, outs, scratch, 4.0, f"self_forward_{layer}_{side}", ties, 12)


def hand_over(low_ref, kept, sent, sems):
    copies = []
    for slot, target in enumerate((kept, sent)):
        copies.append(
            pltpu.make_async_copy(low_ref, target.at[:, pl.ds(0, D)], sems.at[slot])
        )
        copies[-1].start()
    return copies


def hand_halves(meta, batch, wide_ref, kept, sent, sems):
    count = wide_ref.shape[1] // 2
    copies = []
    for half in (0, 1):
        source = wide_ref.at[:, pl.ds(half * count, count)]
        to_kept, to_sent = (
            pltpu.make_async_copy(source, target.at[:, pl.ds(D, count)], sems.at[2 + half])
            for target in (kept, sent)
        )
        mine = meta[1 + 2 * batch] == half
        pl.when(mine)(to_kept.start)
        pl.when(jnp.logical_not(mine))(to_sent.start)
        copies.append(to_kept)
    return copies


def hand_scratch(rows, units):
    return [
        pltpu.VMEM((rows, D), bf16),
        pltpu.VMEM((rows, units), bf16),
        pltpu.SemaphoreType.DMA((4,)),
    ]


def feed_forward(
    side, layer, batch, meta, residual, own, other, small, chooser, feed_in, feed_out, place, ties=()
):
    rows = residual.shape[0]
    units = feed_in[0].shape[-1]
    step = units // 4

    held, n_maps = len(feed_in) == 1, len(feed_in + feed_out)

    def body(flush, meta, residual, own, other, small_own, small_other, *refs):
        small = small_of(meta, layer, side, small_own, small_other)
        if not held:
            chooser, refs = refs[0], refs[1:]
        given, refs = refs[:n_maps], refs[n_maps:]
        settled_ref, unit_ref, rstd_ref, selected, pack, slope, part, squares = refs[:8]
        if held:
            weights = Held(given[0].at[side], given[1].at[side])
            low_ref, active_ref, sems = refs[8:]
        else:
            in_buffer, out_buffer, sems = refs[8:]
            weights = Weights(
                meta,
                layer,
                (
                    maps(*given[:2], side, column_pieces(units, 4)),
                    maps(*given[2:], side, row_pieces(units, 2)),
                ),
                (in_buffer, out_buffer),
                sems,
            )
        post = small[ROW_ATT_POST : ROW_ATT_POST + 3]
        branch = summed(own, other) + post[0:1]
        squares[...] = square_sum(branch, row_valid(meta, side, batch, rows))
        unit, rstd, settled = norm_of(residual[...].astype(f32) + branch, post[1:2], post[2:3])
        unit_ref[...] = unit
        rstd_ref[...] = rstd
        settled_ref[...] = settled
        low = settled.astype(bf16)
        if held:
            low_ref[...] = low
            copies = hand_over(low_ref, selected, pack, sems)
            flush(unit_ref, rstd_ref)
        else:
            select_rows(low, chooser, selected, pack)
            active_ref = pack.at[:, HALF:]
            flush(unit_ref, rstd_ref, selected)
        for i in range(units // step):
            first = weights.get(0, i)
            columns = slice(i * step, (i + 1) * step)
            row = ROW_FEED_BIAS + (i * step) // D
            place = (i * step) % D
            hidden = mm(low, first[:, columns]) + small[row : row + 1, place : place + step]
            below = 0.5 + 0.5 * lax.erf(hidden * (0.5**0.5))
            density = jnp.exp(hidden * hidden * -0.5) * 0.3989422804014327
            active_ref[:, columns] = (hidden * below).astype(bf16)
            slope[:, columns] = (below + hidden * density).astype(bf16)
        flush(pack, slope)
        if held:
            copies += hand_halves(meta, batch, active_ref, selected, pack, sems)
        part[...] = mm(active_ref[...], weights.get(1)[...]).astype(bf16)
        if held:
            for copy in copies:
                copy.wait()

    ins = [(meta, "s"), (residual, "v"), (own, "v"), (other, "v")]
    ins += [(item, "v") for item in ((*small,) if held else (*small, chooser))]
    ins += weight_inputs(feed_in, feed_out, "wawa")
    outs = [
        ((rows, D), f32, "v"),
        ((rows, D), f32, "h"),
        ((rows, 1), f32, "h"),
        *(
            [((rows, D + units // 2), bf16, "w")] * 2
            if held
            else [((rows, HALF), bf16, "h"), ((rows, HALF + units), bf16, "h", *place)]
        ),
        ((rows, units), bf16, "h"),
        ((rows, D), bf16, "v"),
        ((1, 128), f32, "h"),
    ]
    scratch = [
        pltpu.VMEM((D, units), bf16),
        pltpu.VMEM((units, D), bf16),
        pltpu.SemaphoreType.DMA((6,)),
    ]
    if held:
        scratch = hand_scratch(rows, units)
    return call(body, ins, outs, scratch, 4.3, f"feed_forward_{layer}_{side}", ties, 12 if held else 14)


def cross_forward(
    batch, meta, streams, smalls, chooser, cross_in, cross_bias, cross_out, later, ties=()
):
    rows = [stream[0].shape[0] for stream in streams]
    spans = spans_of(rows)
    width = cross_out.shape[0]
    heads = width // HEAD_DIM

    def body(flush, meta, *refs):
        given = (refs[0:3], refs[3:6])
        small = [small_of(meta, 0, side, refs[6], refs[7]) for side in (0, 1)]
        chooser, in_ref, bias, out_ref = refs[8:12]
        offered, refs = refs[12 : 12 + 2 * len(later)], refs[:12] + refs[12 + 2 * len(later) :]
        taken, refs = refs[29 : 29 + len(later)], refs[:29] + refs[29 + len(later) :]
        all_pack = refs[28]
        outs = [refs[12:20], refs[20:28]]
        for side in (0, 1):
            outs[side] = outs[side][:5] + (all_pack.at[spans[side]],) + outs[side][5:]
        in_buffer, out_buffer, sems, later_sems = refs[29:]
        weights = Weights(
            meta,
            0,
            (maps(in_ref, None, 0, ENTRY), maps(out_ref, None, 0)),
            (in_buffer, out_buffer),
            sems,
        )
        passing = pass_on(meta, 1, offered, taken, later_sems)
        lows = []
        for side in (0, 1):
            settled, own, other = given[side]
            state, unit_ref, rstd_ref, squares, selected, pack, qkv, probs, part = outs[side]
            post = small[side][ROW_FEED_POST : ROW_FEED_POST + 3]
            branch = summed(own, other) + post[0:1]
            unit, rstd, result = norm_of(settled[...] + branch, post[1:2], post[2:3])
            unit_ref[...] = unit
            rstd_ref[...] = rstd
            low = result.astype(bf16)
            state[...] = low
            valid = row_valid(meta, side, batch, rows[side])
            squares[0:1] = square_sum(branch, valid)
            squares[1:2] = square_sum(low.astype(f32), valid)
            select_rows(low, chooser, selected, pack)
            flush(unit_ref, rstd_ref, selected)
            lows.append(low)
        for side in (0, 1):
            project(lows[side], weights, bias[0:1], bias[1:2], outs[side][6])
        leave = weights.get(1)
        for side in (0, 1):
            pack, qkv, probs, part = outs[side][5:]
            there = outs[1 - side][6]
            valid = pair_valid(meta, 1 - side, batch, rows[side], rows[1 - side])
            context = pack.at[:, HALF:]
            attend(qkv[0], there[1], there[2], valid, probs, context)
            flush(qkv, probs)
            part[...] = mm(context[...], leave[...]).astype(bf16)
        for copy in passing:
            copy.wait()

    ins = [(meta, "s")] + [pair for stream in streams for pair in zip(stream, "vvv")]
    ins += [(item, "v") for item in smalls]
    ins += [(chooser, "v"), (cross_in, "w"), (cross_bias, "v"), (cross_out, "w")]
    ins += [(item, "w") for pair in later for item in pair]
    outs = []
    for side in (0, 1):
        here, there = rows[side], rows[1 - side]
        outs += [
            ((here, D), bf16, "v"),
            ((here, D), f32, "h"),
            ((here, 1), f32, "h"),
            ((2, 128), f32, "h"),
            ((here, HALF), bf16, "h"),
            ((3, here, width), bf16, "h"),
            ((heads, here, there), bf16, "h"),
            ((here, D), bf16, "v"),
        ]
    outs.append(((sum(rows), HALF + width), bf16, "h"))
    outs += [(pair[0].shape[1:], bf16, "v") for pair in later]
    scratch = [
        pltpu.VMEM((3, D, width), bf16),
        pltpu.VMEM((width, D), bf16),
        pltpu.SemaphoreType.DMA((6,)),
        pltpu.SemaphoreType.DMA((len(later),)),
    ]
    result = call(body, ins, outs, scratch, 6.8, "cross_forward", ties)
    return result[:8], result[8:16], result[16], result[17:]


class Layout:
    def __init__(self, sides, rows, given):
        self.sides, self.total, self.spans = sides, sum(rows), spans_of(rows)
        self.single = len(sides) == 1
        self.side = sides[0]
        self.count = rows[self.side] if self.single else self.total
        self.given = given

    def here(self, side):
        return slice(0, self.count) if self.single else self.spans[side]

    def index(self, side):
        return 0 if self.single else side

    def rows(self, width, dtype, at):
        if not self.single:
            return (self.total, width), dtype, "h"
        given = self.given[at] if self.given else None
        return (self.count, width), dtype, "h", self.total, self.spans[self.side].start, given

    def each(self, shape, at):
        if not self.single:
            return (2, *shape), f32, "h"
        given = self.given[at] if self.given else None
        return (1, *shape), f32, "h", 2, self.side, given


def feed_backward(
    layer, sides, rows, batch, meta, tops, joint, small, chooser, slopes, feed_in, feed_out, ties=(),
    given=None,
):
    last = joint is None
    layout = Layout(sides, rows, given)
    units = slopes[0].shape[1]
    step = units // 4
    n_top = len(tops[0])
    n = len(sides)
    held, n_maps = len(feed_in) == 1, len(feed_in + feed_out)

    def body(flush, meta, *refs):
        tops = {}
        for side in sides:
            tops[side], refs = refs[:n_top], refs[n_top:]
        if not last:
            joint, refs = refs[:3], refs[3:]
        small = {side: small_of(meta, layer, side, refs[0], refs[1]) for side in sides}
        refs = refs[2:]
        if not held:
            chooser, refs = refs[0], refs[1:]
        slopes, refs = dict(zip(sides, refs[:n])), refs[n:]
        given, refs = refs[:n_maps], refs[n_maps:]
        grad_all, selected_all, pack_all, part_all, post_all, bias_all = refs[:6]
        if last:
            squares_all, results = refs[6], dict(zip(sides, refs[7 : 7 + n]))
            low_ref, hidden_ref, hand_sems, raw, rows_ref, raw_sem = refs[-6:]
        weights = {}
        for i, side in enumerate(sides):
            if held:
                weights[side] = Held(given[1].at[side], given[0].at[side])
                continue
            in_buffer, out_buffer, sems = refs[-3:]
            weights[side] = Weights(
                meta,
                layer,
                (
                    maps(*given[2:], side, row_pieces(units, 4)),
                    maps(*given[:2], side, column_pieces(units, 2)),
                ),
                (out_buffer.at[i], in_buffer.at[i]),
                sems.at[i],
            )
        lows = {}
        for side in sides:
            here, at = layout.here(side), layout.index(side)
            post = small[side][ROW_FEED_POST : ROW_FEED_POST + 3]
            if last:
                settled, own, other, cotangent = tops[side]
                branch = summed(own, other) + post[0:1]
                unit, rstd, result = norm_of(settled[...] + branch, post[1:2], post[2:3])
                low = result.astype(bf16)
                results[side][...] = low
                valid = row_valid(meta, side, batch, rows[side])
                squares_all[at, 0:1] = square_sum(branch, valid)
                squares_all[at, 1:2] = square_sum(low.astype(f32), valid)
                items_of(meta, cotangent, raw, rows_ref, raw_sem, batch)
                incoming = rows_ref[...] * valid
            else:
                unit_ref, rstd_ref = tops[side]
                unit, rstd = unit_ref[...], rstd_ref[...]
                incoming = (joint[0][here] + summed_rows(joint[1], joint[2], here)).astype(bf16)
                incoming = incoming.astype(f32)
            grad = norm_back(unit, rstd, post[1:2], incoming)
            grad_all[here] = grad
            low = grad.astype(bf16)
            post_all[at, 0:1] = column_sum(low.astype(f32))
            post_all[at, 1:2] = column_sum(incoming * unit)
            post_all[at, 2:3] = column_sum(incoming)
            lows[side] = low
        flush(grad_all, post_all)
        if held:
            low_ref[...] = lows[sides[0]]
            copies = hand_over(low_ref, selected_all, pack_all, hand_sems)
        else:
            hidden_ref = pack_all.at[:, HALF:]
        for side in sides:
            here, at = layout.here(side), layout.index(side)
            for i in range(units // step):
                columns = slice(i * step, (i + 1) * step)
                active = mm_nt(lows[side], weights[side].get(0, i)[columns, :])
                hidden = (active * slopes[side][:, columns].astype(f32)).astype(bf16)
                hidden_ref[here, columns] = hidden
                bias_all[at, :, columns] = column_sum(hidden.astype(f32))
            if not held:
                select_rows(lows[side], chooser, selected_all.at[here], pack_all.at[here])
        flush(pack_all, selected_all)
        if held:
            copies += hand_halves(meta, batch, hidden_ref, selected_all, pack_all, hand_sems)
        for side in sides:
            here = layout.here(side)
            part_all[here] = mm_nt(hidden_ref[here], weights[side].get(1)[...]).astype(bf16)
        if held:
            for copy in copies:
                copy.wait()

    ins = [(meta, "s")] + [pair for top in tops for pair in zip(top, "vvvw" if last else "vv")]
    if not last:
        ins += [(item, "v") for item in joint]
    ins += [(item, "v") for item in ((*small, *slopes) if held else (*small, chooser, *slopes))]
    ins += weight_inputs(feed_in, feed_out)
    count = layout.count
    outs = [
        ((count, D), f32, "v" if last else "h"),
        *(
            [((count, D + units // 2), bf16, "w")] * 2
            if held
            else [layout.rows(HALF, bf16, 1), ((count, HALF + units), bf16, "h")]
        ),
        ((count, D), bf16, "v" if last else "h"),
        layout.each((3, D), 4),
        layout.each((1, units), 5),
    ]
    if last:
        outs += [layout.each((2, 128), 6)] + [((rows[side], D), bf16, "h") for side in sides]
    scratch = [
        pltpu.VMEM((n, D, units), bf16),
        pltpu.VMEM((n, units, D), bf16),
        pltpu.SemaphoreType.DMA((n, 6)),
    ]
    if last:
        side = sides[0]
        scratch = hand_scratch(rows[side], units) + [
            pltpu.VMEM(tops[0][3].shape[1:], bf16),
            pltpu.VMEM((rows[side], D), f32),
            pltpu.SemaphoreType.DMA,
        ]
    name = f"feed_backward_{layer}_" + "".join(map(str, sides))
    return call(body, ins, outs, scratch, 11.0 * count / layout.total, name, ties, 12 if held else 24)


def summed_rows(own, other, here):
    return own[here].astype(f32) + other[here].astype(f32)


def back_through_norm(top, grad_in, branch, gain, grad_ref, post_ref):
    unit_ref, rstd_ref = top
    incoming = grad_in + branch
    unit = unit_ref[...]
    grad = norm_back(unit, rstd_ref[...], gain, incoming)
    grad_ref[...] = grad
    low = grad.astype(bf16)
    post_ref[0:1] = column_sum(low.astype(f32))
    post_ref[1:2] = column_sum(incoming * unit)
    post_ref[2:3] = column_sum(incoming)
    return low


def emit_into(pack, width):
    def emit(kind, lanes, value):
        start = HALF + kind * width + lanes.start
        pack[:, start : start + PAIR] = value

    return emit


def back_to_input(pack, weights, slot, width):
    grads = [pack[:, HALF + j * width : HALF + (j + 1) * width] for j in range(3)]
    total = mm_nt(grads[0], weights.get(slot, 0)[0])
    total += mm_nt(grads[1], weights.get(slot, 1)[1])
    total += mm_nt(grads[2], weights.get(slot, 2)[2])
    return total.astype(bf16)


def self_backward(
    layer, sides, rows, meta, tops, joint, small, chooser, qkvs, probs, att_in, att_out, ties=(),
    given=None,
):
    layout = Layout(sides, rows, given)
    width = qkvs[0].shape[2]
    n = len(sides)
    held, n_maps = len(att_in) == 1, len(att_in + att_out)

    def body(flush, meta, *refs):
        tops = {side: refs[2 * i : 2 * i + 2] for i, side in enumerate(sides)}
        joint, refs = refs[2 * n : 2 * n + 3], refs[2 * n + 3 :]
        small = {side: small_of(meta, layer, side, refs[0], refs[1]) for side in sides}
        chooser, refs = refs[2], refs[3:]
        qkvs, probs, refs = dict(zip(sides, refs[:n])), dict(zip(sides, refs[n : 2 * n])), refs[2 * n :]
        given, refs = refs[:n_maps], refs[n_maps:]
        grad_all, selected_all, pack_all, part_all, post_all, bias_all = refs[:6]
        weights = {}
        for i, side in enumerate(sides):
            if held:
                weights[side] = Held(given[1].at[side], given[0].at[side])
                continue
            in_buffer, out_buffer, sems = refs[6:]
            weights[side] = Weights(
                meta,
                layer,
                (maps(*given[2:], side), maps(*given[:2], side, ENTRY)),
                (out_buffer.at[i], in_buffer.at[i]),
                sems.at[i],
            )
        for side in sides:
            here, at = layout.here(side), layout.index(side)
            pack = pack_all.at[here]
            gain = small[side][ROW_ATT_POST + 1 : ROW_ATT_POST + 2]
            low = back_through_norm(
                tops[side],
                joint[0][here],
                summed_rows(joint[1], joint[2], here),
                gain,
                grad_all.at[here],
                post_all.at[at],
            )
            context = mm_nt(low, weights[side].get(0)[...]).astype(bf16)
            qkv = qkvs[side]
            attend_back(qkv[0], qkv[1], qkv[2], probs[side], context, emit_into(pack, width))
            bias_all[at, 0:1] = column_sum(pack[:, HALF : HALF + width].astype(f32))
            bias_all[at, 1:2] = column_sum(pack[:, HALF + 2 * width :].astype(f32))
            select_rows(low, chooser, selected_all.at[here], pack)
        flush(pack_all, selected_all, grad_all, post_all, bias_all)
        for side in sides:
            here = layout.here(side)
            part_all[here] = back_to_input(pack_all.at[here], weights[side], 1, width)

    near = "v" if layer == 1 else "h"
    ins = [(meta, "s")] + [(item, near) for top in tops for item in top]
    ins += [*zip(joint, "vvv" if layer == 1 else "hhf")] + [(item, near) for item in small]
    ins += [(item, near) for item in (chooser, *qkvs, *probs)]
    ins += weight_inputs(att_in, att_out)
    outs = [
        ((layout.count, D), f32, "h"),
        layout.rows(HALF, bf16, 1),
        layout.rows(HALF + 3 * width, bf16, 2),
        ((layout.count, D), bf16, "h"),
        layout.each((3, D), 4),
        layout.each((2, width), 5),
    ]
    scratch = [
        pltpu.VMEM((n, 3, D, width), bf16),
        pltpu.VMEM((n, width, D), bf16),
        pltpu.SemaphoreType.DMA((n, 6)),
    ]
    scratch = [] if held else scratch
    name = f"self_backward_{layer}_" + "".join(map(str, sides))
    return call(body, ins, outs, scratch, 12.0 * layout.count / layout.total, name, ties, 12 if held else 18)


def cross_backward(meta, tops, grads, owns, others, post, chooser, qkvs, probs, cross_in, cross_out, ties=()):
    rows = [qkv.shape[1] for qkv in qkvs]
    width = cross_out.shape[0]
    spans, total = spans_of(rows), sum(rows)

    def body(flush, meta, *refs):
        tops, grads, owns, others = (refs[:2], refs[2:4]), refs[4:6], refs[6:8], refs[8:10]
        post, chooser, qkvs, probs = refs[10], refs[11], refs[12:14], refs[14:16]
        in_ref, out_ref = refs[16:18]
        grad_all, selected_all, pack_all, part_all, post_out, bias_out = refs[18:24]
        in_buffer, out_buffer, post_each, sems = refs[24:]
        weights = Weights(
            meta,
            0,
            (maps(out_ref, None, 0), maps(in_ref, None, 0, ENTRY)),
            (out_buffer, in_buffer),
            sems,
        )
        packs = [pack_all.at[here] for here in spans]
        lows = []
        for side in (0, 1):
            here = spans[side]
            low = back_through_norm(
                tops[side],
                grads[side][...],
                summed(owns[side], others[side]),
                post[1:2],
                grad_all.at[here],
                post_each.at[side],
            )
            lows.append(low)
        post_out[...] = post_each[0] + post_each[1]
        leave = weights.get(0)
        for side in (0, 1):
            context = mm_nt(lows[side], leave[...]).astype(bf16)
            to_here, to_there = emit_into(packs[side], width), emit_into(packs[1 - side], width)

            def emit(kind, lanes, value):
                (to_here if kind == 0 else to_there)(kind, lanes, value)

            attend_back(
                qkvs[side][0], qkvs[1 - side][1], qkvs[1 - side][2], probs[side], context, emit
            )
        for side in (0, 1):
            select_rows(lows[side], chooser, selected_all.at[spans[side]], packs[side])
        bias_out[0:1] = column_sum(pack_all[:, HALF : HALF + width].astype(f32))
        bias_out[1:2] = column_sum(pack_all[:, HALF + 2 * width :].astype(f32))
        flush(pack_all, selected_all)
        part_all[...] = back_to_input(pack_all, weights, 1, width)

    ins = [(meta, "s")] + [(item, "h") for top in tops for item in top]
    ins += [(item, "h") for item in (*grads, *owns)] + [(item, "f") for item in others]
    ins += [(item, "h") for item in (post, chooser, *qkvs, *probs)]
    ins += [(cross_in, "w"), (cross_out, "w")]
    outs = [
        ((total, D), f32, "v"),
        ((total, HALF), bf16, "h"),
        ((total, HALF + 3 * width), bf16, "h"),
        ((total, D), bf16, "v"),
        ((3, D), f32, "h"),
        ((2, width), f32, "h"),
    ]
    scratch = [
        pltpu.VMEM((3, D, width), bf16),
        pltpu.VMEM((width, D), bf16),
        pltpu.VMEM((2, 3, D), f32),
        pltpu.SemaphoreType.DMA((6,)),
    ]
    return call(body, ins, outs, scratch, 10.0, "cross_backward", ties, 16)


class Block:
    def __init__(self, in_selected, in_packs, in_gots, out_selected, out_packs, out_gots):
        self.parts = [*in_selected, *in_packs, *in_gots, out_selected, *out_packs, *out_gots]
        self.counts = (len(in_packs), len(out_packs))
        self.lead = HALF
        self.kinds = "w" * len(self.parts)
        self.sizes = (out_packs[0].shape[1] - HALF, in_packs[0].shape[1] - HALF)
        self.rows = [array.shape[0] for array in in_selected]

    def buffers(self):
        return [
            pltpu.VMEM((2 * rows, HALF + size), bf16)
            for rows in self.rows
            for size in (self.sizes[1], self.sizes[0])
        ]

    def fetch(self, refs, buffers, sems, at):
        spans = spans_of(self.rows)
        in_selected, rest = refs[:2], refs[2:]
        n_in, n_out = self.counts
        pack, got, rest = rest[:n_in], rest[n_in : 2 * n_in], rest[2 * n_in :]
        out_selected, out_pack, out_got = rest[0], rest[1 : 1 + n_out], rest[1 + n_out :]

        def rows_of(items, side):
            return items[0].at[spans[side]] if len(items) == 1 else items[side]

        result = []
        for side in (0, 1):
            count = self.rows[side]
            per_side = []
            for kind, (selected, own, other) in enumerate(
                (
                    (in_selected[side], rows_of(pack, side), rows_of(got, side)),
                    (out_selected.at[spans[side]], rows_of(out_pack, side), rows_of(out_got, side)),
                )
            ):
                buffer = buffers[2 * side + kind]
                size = buffer.shape[1] - HALF
                mine = slice(0, count)
                copies = [
                    pltpu.make_async_copy(
                        selected, buffer.at[mine, pl.ds(0, HALF)], sems.at[at]
                    ),
                    pltpu.make_async_copy(
                        own.at[:, pl.ds(HALF, size)], buffer.at[mine, pl.ds(HALF, size)], sems.at[at + 1]
                    ),
                    pltpu.make_async_copy(
                        other, buffer.at[slice(count, 2 * count)], sems.at[at + 2]
                    ),
                ]
                at += 3
                for copy in copies:
                    copy.start()
                per_side.append((buffer, copies))
            result.append(per_side)
        return result, at


class Halves:
    def __init__(self, in_kept, in_gots, out_kept, out_gots):
        self.parts = [*in_kept, *in_gots, *out_kept, *out_gots]
        self.kinds = "w" * len(self.parts)
        self.lead = D
        self.sizes = (out_kept[0].shape[1] - D, in_kept[0].shape[1] - D)
        self.rows = [array.shape[0] for array in in_kept]

    def buffers(self):
        return [
            pltpu.VMEM((2 * rows, D + size), bf16)
            for rows in self.rows
            for size in (self.sizes[1], self.sizes[0])
        ]

    def fetch(self, refs, buffers, sems, at):
        result = []
        for side in (0, 1):
            count = self.rows[side]
            per_side = []
            for kind in (0, 1):
                buffer = buffers[2 * side + kind]
                copies = []
                for part in (0, 1):
                    target = buffer.at[slice(part * count, (part + 1) * count)]
                    source = refs[4 * kind + 2 * part + side]
                    copies.append(pltpu.make_async_copy(source, target, sems.at[at]))
                    copies[-1].start()
                    at += 1
                per_side.append((buffer, copies))
            result.append(per_side)
        return result, at


def chunk_order(groups):
    return [(s, z) for z in range(groups) for s in ((0, 1) if z % 2 == 0 else (1, 0))]


def gradients(meta, blocks, cross, groups, name, ties=(), split=False):
    lead = blocks[0].lead
    chunk = lead // groups
    half = chunk // 2
    size = chunk + half if cross else chunk
    order = chunk_order(groups)
    aligned = half % 16 == 0
    width = sum(sum(block.sizes) for block in blocks)
    every = blocks + ([cross] if cross else [])
    n_in = sum(len(block.parts) for block in every)
    n_out = 2 if split else 1 if aligned else 3 if cross else 2
    n_sems = 12 * len(every) + 4 * len(every)

    def body(flush, meta, *refs):
        inputs, outputs, rest = refs[:n_in], refs[n_in : n_in + n_out], list(refs[n_in + n_out :])
        if cross:
            cross_stage = rest.pop()
        stage, sems = rest.pop(), rest.pop()
        at = 0
        fetched = []
        for block in every:
            taken, inputs = inputs[: len(block.parts)], inputs[len(block.parts) :]
            own, rest = rest[:4], rest[4:]
            copies, at = block.fetch(taken, own, sems, at)
            fetched.append(copies)
        waited, leaving = set(), []

        def leave(source, side, columns, at):
            if split:
                kept = pltpu.make_async_copy(source, outputs[0].at[:, columns], sems.at[at])
                sent = pltpu.make_async_copy(source, outputs[1].at[:, columns], sems.at[at])
                pl.when(meta[0] == side)(kept.start)
                pl.when(meta[0] != side)(sent.start)
                leaving.append(kept)
                return
            if not aligned:
                copies = [(source, outputs[side].at[:, columns])]
            elif side < 2:
                copies = [
                    (source.at[pl.ds(z * chunk, chunk)], outputs[0].at[pl.ds(k * size, chunk), columns])
                    for k, (s, z) in enumerate(order)
                    if s == side
                ]
            else:
                copies = [
                    (
                        source.at[pl.ds((s * groups + z) * half, half)],
                        outputs[0].at[pl.ds(k * size + chunk, half), columns],
                    )
                    for k, (s, z) in enumerate(order)
                ]
            for one, target in copies:
                copy = pltpu.make_async_copy(one, target, sems.at[at])
                copy.start()
                leaving.append(copy)

        def ready(item):
            buffer, copies = item
            if id(buffer) not in waited:
                waited.add(id(buffer))
                for copy in copies:
                    copy.wait()
            return buffer

        base = 0
        for block, copies in zip(blocks, fetched):
            for side in (0, 1):
                start = base
                for left, right in ((0, 1), (1, 0)):
                    left, right = ready(copies[side][left]), ready(copies[side][right])
                    turned = left[:, :lead].T
                    span = right.shape[1] - lead
                    for step in range(0, span, HALF):
                        value = mm(turned, right[:, lead + step : lead + step + HALF])
                        stage[side, :, start + step : start + step + HALF] = value.astype(bf16)
                    columns = pl.ds(start, span)
                    leave(stage.at[side, :, columns], side, columns, at)
                    at += 1
                    start += span
            base += sum(block.sizes)
        if cross:
            copies = fetched[-1]
            start = 0
            for left, right in ((0, 1), (1, 0)):
                lefts = [ready(copies[side][left])[:, :HALF].T for side in (0, 1)]
                rights = [ready(copies[side][right]) for side in (0, 1)]
                span = rights[0].shape[1] - HALF
                for step in range(0, span, HALF):
                    columns = slice(HALF + step, HALF + step + HALF)
                    value = mm(lefts[0], rights[0][:, columns]) + mm(lefts[1], rights[1][:, columns])
                    cross_stage[:, start + step : start + step + HALF] = value.astype(bf16)
                columns = pl.ds(start, span)
                leave(cross_stage.at[:, columns], 2, columns, at)
                at += 1
                start += span
        for copy in leaving:
            copy.wait()

    ins = [(meta, "s")] + [pair for block in every for pair in zip(block.parts, block.kinds)]
    if aligned and not split:
        outs = [((2 * groups * size, width), bf16, "w")]
    else:
        outs = [((lead, width), bf16, "w")] * n_out
    scratch = [buffer for block in every for buffer in block.buffers()]
    if cross:
        scratch += [
            pltpu.SemaphoreType.DMA((n_sems,)),
            pltpu.VMEM((2, lead, width), bf16),
            pltpu.VMEM((HALF, sum(cross.sizes)), bf16),
        ]
    else:
        scratch += [pltpu.SemaphoreType.DMA((n_sems,)), pltpu.VMEM((2, lead, width), bf16)]
    result = call(body, ins, outs, scratch, 6.0, name, ties, 20)
    if split:
        return result
    if aligned:
        return result[0]
    chunks = [result[side].reshape(groups, chunk, width) for side in (0, 1)]
    pieces = [chunks[s][z] for s, z in order]
    if cross:
        extra = result[2].reshape(2, groups, half, width)
        pieces = [jnp.concatenate([one, extra[s, z]]) for one, (s, z) in zip(pieces, order)]
    return jnp.concatenate(pieces)


def placed_gradients(
    meta, feed1, late1, late_words, layer0, late_regions, chunk, width, units
):
    def body(flush, meta, feed1, late1, words_feed, words_late, layer0, regions, *outs):
        feed_in, feed_out, att_in, att_out, cross_in, cross_out = outs

        def store(side, feed, feed_base, late, late_base):
            feed_in[side] = feed[:, feed_base : feed_base + units].astype(f32)
            feed_out[side] = feed[:, feed_base + units : feed_base + 2 * units].astype(f32)
            for j in range(3):
                start = late_base + j * width
                att_in[side, j] = late[:chunk, start : start + width].astype(f32)
            att_out[side] = late[:chunk, late_base + 3 * width : late_base + 4 * width].astype(f32)

        items = [item.wait() for item in (feed1, late1, words_feed, words_late, layer0, regions)]
        feed1, late1, words_feed, words_late, layer0, regions = items

        @pl.when(meta[0] == 0)
        def _():
            store(0, layer0, 0, layer0, 2 * units)
            store(1, regions, 0, regions, 2 * units)

        @pl.when(meta[0] != 0)
        def _():
            store(0, words_feed, 0, words_late, 0)
            store(1, feed1, 0, late1, 0)

        for j in range(3):
            cross_in[j] = late1[chunk:, j * width : (j + 1) * width].astype(f32)
        cross_out[...] = late1[chunk:, 3 * width :].astype(f32)

    ins = [(meta, "s")]
    ins += [(item, "h") for item in (feed1, late1, *late_words, layer0, late_regions)]
    half = chunk // 2
    outs = [
        ((2, chunk, units), f32, "h"),
        ((2, chunk, units), f32, "h"),
        ((2, 3, chunk, width), f32, "h"),
        ((2, chunk, width), f32, "h"),
        ((3, half, width), f32, "h"),
        ((half, width), f32, "h"),
    ]
    return call(body, ins, outs, (), 4.0, "placed_gradients")


def prepared(ids, lengths, att_bias, att_post, feed_bias, feed_post):
    batch = lengths[0].shape[1]
    n_feed = feed_bias.shape[2] // D

    def body(flush, ids, words, regions, att_bias, att_post, feed_bias, feed_post, small, meta):
        meta[0] = ids[0]
        meta[1 + 2 * batch] = ids[1]
        for side, counts in enumerate((words, regions)):
            for i in range(batch):
                meta[1 + side * batch + i] = counts[ids[0], i]
        half = att_bias.shape[3]
        for side in (0, 1):
            for j in (0, 1):
                small[side, ROW_ATT_BIAS : ROW_ATT_BIAS + 1, j * half : (j + 1) * half] = att_bias[
                    0, side, j : j + 1
                ]
            small[side, ROW_ATT_POST : ROW_ATT_POST + 3] = att_post[0, side]
            for j in range(n_feed):
                row = ROW_FEED_BIAS + j
                small[side, row : row + 1] = feed_bias[0, side : side + 1, j * D : (j + 1) * D]
            small[side, ROW_FEED_POST : ROW_FEED_POST + 3] = feed_post[0, side]
            end = ROW_FEED_POST + 3
            small[side, end:] = jnp.zeros((SMALL_ROWS - end, D), f32)

    ins = [(ids, "s"), (lengths[0], "s"), (lengths[1], "s")]
    ins += [(item, "f") for item in (att_bias, att_post, feed_bias, feed_post)]
    outs = [((2, SMALL_ROWS, D), f32, "h"), ((2 + 2 * batch,), jnp.int32, "s")]
    return call(body, ins, outs, (), 1.0, "prepared")


def swap(value, axis, distance=1):
    count = lax.axis_size(axis)
    return lax.ppermute(value, axis, [(i, i ^ distance) for i in range(count)])


def on_device(
    word_state,
    region_state,
    word_lengths,
    region_counts,
    word_cotangent,
    region_cotangent,
    cross_in,
    cross_bias,
    cross_out,
    cross_post,
    attention_in,
    attention_bias,
    attention_out,
    attention_post,
    feed_in,
    feed_bias,
    feed_out,
    feed_post,
):
    section = lax.axis_index("section")
    dp_count = lax.axis_size("dp")
    groups = dp_count // 2
    place = lax.axis_index("dp") % 2
    batch = word_state.shape[1]
    width = cross_out.shape[0]
    units = feed_in.shape[-1]
    both = (0, 1)
    chains = [[s * dp_count + 2 * z + y for s, z in chunk_order(groups)] for y in both]

    def unflat(value):
        return value.reshape(-1, batch, D).transpose(1, 0, 2)[None]

    def chooser_of(pieces, per_section):
        column = jnp.arange(D)
        half = column // HALF
        inner = column % HALF
        side = jnp.where(half == 0, place, 1 - place)
        size = D // pieces
        if per_section:
            block = inner // (HALF // 2)
            inner = inner % (HALF // 2)
            feature = size * (dp_count * block + 2 * (inner // size) + side) + inner % size
        else:
            feature = size * (2 * (inner // size) + side) + inner % size
        return (jnp.arange(D)[:, None] == feature[None, :]).astype(bf16)

    chooser = chooser_of(dp_count, False)
    cross_chooser = chooser_of(2 * dp_count, True)

    ids = jnp.stack([section, place]).astype(jnp.int32)
    small_own, meta = prepared(
        ids,
        (word_lengths, region_counts),
        attention_bias,
        attention_post,
        feed_bias,
        feed_post,
    )
    small = (small_own, swap(small_own, "section"))
    att_in_own = attention_in.transpose(0, 1, 3, 2, 4)
    att_in = (att_in_own, swap(att_in_own, "section"))
    att_out = (attention_out, swap(attention_out, "section"))
    states = [value.transpose(0, 2, 1, 3) for value in (word_state, region_state)]
    feed_in_later, feed_out_later, *_ = lax.optimization_barrier(
        (feed_in, feed_out, att_in[1], att_out[1], small[1], chooser, cross_chooser)
    )
    ff_in = (feed_in, swap(feed_in_later, "section"))
    ff_out = (feed_out, swap(feed_out_later, "section"))
    cross_entry = cross_in.transpose(1, 0, 2)

    cotangents = [value.transpose(0, 2, 1, 3) for value in (word_cotangent, region_cotangent)]
    rows = [state.shape[1] * batch for state in states]
    total_rows = sum(rows)

    def in_order(step, pack_index, tie=None, joined=True, order=(1, 0)):
        results = [None, None]
        given = None
        for side in order:
            ties = () if tie is None else (tie,)
            place = (total_rows, rows[0] * side, given) if joined else ()
            results[side] = step(side, place, ties)
            tie, given = results[side][pack_index + 2], results[side][pack_index]
        return results

    def over_mp(results, index):
        return [swap(results[side][index], "mp") for side in both]

    self0 = in_order(
        lambda side, place, ties: self_forward(
            side, 0, batch, meta, states[side], None, small, chooser, att_in, att_out,
            place, ties,
        ),
        3,
    )
    got = over_mp(self0, 4)
    feed0 = in_order(
        lambda side, place, ties: feed_forward(
            side, 0, batch, meta, self0[side][6], self0[side][4], got[side], small, chooser,
            ff_in, ff_out, place, ties,
        ),
        4,
        self0[0][5],
    )
    got = over_mp(feed0, 6)
    self0_there = swap(self0[0][3], "dp")
    cross_w, cross_r, cross_pack, held = cross_forward(
        batch,
        meta,
        [(feed0[side][0], feed0[side][6], got[side]) for side in both],
        small,
        cross_chooser,
        cross_entry,
        cross_bias,
        cross_out,
        (att_in, att_out),
    )
    att_in1, att_out1 = [(item,) for item in held]
    cross = (cross_w, cross_r)
    got = over_mp(cross, 7)
    feed0_there = swap(feed0[0][4], "dp")
    self1 = in_order(
        lambda side, place, ties: self_forward(
            side, 1, batch, meta, cross[side][0], (cross[side][7], got[side], cross_post),
            small, chooser, att_in1, att_out1, place, ties + ((self0_there, "a"),),
            (ff_in if side == ORDER[0] else ff_out,),
        ),
        3,
        None,
        True,
        ORDER,
    )
    ff_in1, ff_out1 = [(self1[side][9],) for side in ORDER]
    got = over_mp(self1, 4)
    cross_there = swap(cross_pack, "dp")
    feed1 = in_order(
        lambda side, place, ties: feed_forward(
            side, 1, batch, meta, self1[side][6], self1[side][4], got[side], small, chooser,
            ff_in1, ff_out1, place, ties + ((cross_there if side == ORDER[-1] else feed0_there, "a"),),
        ),
        4,
        self1[ORDER[-1]][5],
        False,
        ORDER,
    )
    got = over_mp(feed1, 6)
    self1_there = swap(self1[0][3], "dp")
    feed1_there = [swap(feed1[side][4], "dp") for side in both]

    given, back_feed1 = None, [None, None]
    for side in ORDER:
        given = feed_backward(
            1,
            (side,),
            rows,
            batch,
            meta,
            [(feed1[side][0], feed1[side][6], got[side], cotangents[side])],
            None,
            small,
            chooser,
            [feed1[side][5]],
            ff_in1,
            ff_out1,
            ((feed1_there[side], "a"),),
            given,
        )
        back_feed1[side] = given
    got = over_mp(back_feed1, 3)
    back_feed1_there = [swap(back_feed1[side][2], "dp") for side in both]

    def scatter(value):
        return lax.psum_scatter(
            value, ("section", "dp"), scatter_dimension=0, axis_index_groups=chains, tiled=True
        )

    given, back_self1 = None, [None, None]
    for side in ORDER:
        given = self_backward(
            1,
            (side,),
            rows,
            meta,
            [feed1[side][1:3]],
            (back_feed1[side][0], back_feed1[side][3], got[side]),
            small,
            chooser,
            [self1[side][0]],
            [self1[side][1]],
            att_in1,
            att_out1,
            (),
            given,
        )
        back_self1[side] = given
    got = over_mp(back_self1, 3)
    feed1_grads = gradients(
        meta,
        [
            Halves(
                [feed1[side][3] for side in both],
                feed1_there,
                [back_feed1[side][1] for side in both],
                back_feed1_there,
            )
        ],
        None,
        groups,
        "feed_gradients_1",
        (back_self1[ORDER[-1]][5],),
    )
    back_self1_there = swap(back_self1[ORDER[-1]][2], "dp")
    back_cross = cross_backward(
        meta,
        [self1[side][7:9] for side in both],
        [back_self1[side][0] for side in both],
        [back_self1[side][3] for side in both],
        got,
        cross_post,
        cross_chooser,
        [cross[side][5] for side in both],
        [cross[side][6] for side in both],
        cross_entry,
        cross_out,
        (feed1_grads, (self1_there, "a")),
    )
    cross_post_grad, cross_bias_grad = back_cross[4:6]
    got = swap(back_cross[3], "mp")
    back_cross_there = swap(back_cross[2], "dp")
    feed1_pair = scatter(feed1_grads).reshape(2, D // dp_count, -1)
    feed1_own = lax.dynamic_index_in_dim(feed1_pair, place, 0, keepdims=False)
    feed1_other = swap(lax.dynamic_index_in_dim(feed1_pair, 1 - place, 0, keepdims=False), "dp")
    halves = (
        jnp.where(place == 0, feed1_own, feed1_other),
        jnp.where(place == 0, feed1_other, feed1_own),
    )
    count = units // 2
    feed1_share = jnp.concatenate(
        [half[:, j * count : (j + 1) * count] for j in both for half in halves], axis=1
    )

    back_feed0 = feed_backward(
        0,
        (1, 0),
        rows,
        batch,
        meta,
        [cross[side][1:3] for side in (1, 0)],
        (back_cross[0], back_cross[3], got),
        small,
        chooser,
        [feed0[side][5] for side in (1, 0)],
        ff_in,
        ff_out,
        ((back_self1_there, "a"),),
    )
    got = swap(back_feed0[3], "mp")
    back_feed0_there = swap(back_feed0[2], "dp")
    late1_grads = gradients(
        meta,
        [
            Block(
                [self1[side][2] for side in both],
                [self1[0][3]],
                [self1_there],
                back_self1[ORDER[-1]][1],
                [back_self1[ORDER[-1]][2]],
                [back_self1_there],
            )
        ],
        Block(
            [cross[side][4] for side in both],
            [cross_pack],
            [cross_there],
            back_cross[1],
            [back_cross[2]],
            [back_cross_there],
        ),
        groups,
        "late_gradients_1",
        (back_feed0[5],),
    )
    back_self0 = self_backward(
        0,
        (1, 0),
        rows,
        meta,
        [feed0[side][1:3] for side in (1, 0)],
        (back_feed0[0], back_feed0[3], got),
        small,
        chooser,
        [self0[side][0] for side in (1, 0)],
        [self0[side][1] for side in (1, 0)],
        att_in,
        att_out,
        (late1_grads,),
    )
    got = swap(back_self0[3], "mp")
    back_self0_there = swap(back_self0[2], "dp")
    late1_share = scatter(late1_grads)
    layer0_grads = gradients(
        meta,
        [
            Block(
                [feed0[side][3] for side in both],
                [feed0[0][4]],
                [feed0_there],
                back_feed0[1],
                [back_feed0[2]],
                [back_feed0_there],
            ),
            Block(
                [self0[side][2] for side in both],
                [self0[0][3]],
                [self0_there],
                back_self0[1],
                [back_self0[2]],
                [back_self0_there],
            ),
        ],
        None,
        groups,
        "gradients_0",
        (back_self0[5], feed1_pair),
        True,
    )
    layer0_kept, layer0_sent = layer0_grads
    layer0_total = layer0_kept.astype(f32) + swap(layer0_sent, "section").astype(f32)
    layer0_total, late1_share = lax.optimization_barrier((layer0_total.astype(bf16), late1_share))
    layer0_share = lax.psum_scatter(
        layer0_total,
        "dp",
        scatter_dimension=0,
        axis_index_groups=[[2 * z + y for z in range(groups)] for y in both],
        tiled=True,
    )
    chunk = D // dp_count

    state_grad = (back_self0[0] + (back_self0[3].astype(f32) + got.astype(f32))).astype(bf16)
    spans = spans_of(rows)

    def packed(back_self, back_feed, squares):
        rows = [
            back_self[5].reshape(2, D),
            back_self[4].reshape(6, D),
            back_feed[5].reshape(-1, D),
            back_feed[4].reshape(6, D),
        ]
        row = jnp.concatenate([value.reshape(1, 128) for value in squares[:6]], axis=1)
        rest = jnp.concatenate([value.reshape(1, 128) for value in squares[6:]], axis=1)
        rest = jnp.concatenate([rest, jnp.zeros((1, D - rest.shape[1]), f32)], axis=1)
        return jnp.concatenate(rows + [row, rest], axis=0)

    def squares_of(lead, second, tail):
        result = []
        for side in both:
            result += [lead[side], second[side], tail[side][0:1], tail[side][1:2]]
        return result

    packs = [
        packed(
            back_self0,
            back_feed0,
            squares_of(
                [self0[side][5] for side in both],
                [feed0[side][7] for side in both],
                [cross[side][3] for side in both],
            ),
        ),
        packed(
            back_self1[ORDER[-1]],
            back_feed1[ORDER[-1]],
            squares_of(
                [self1[side][5] for side in both],
                [feed1[side][7] for side in both],
                [back_feed1[ORDER[-1]][6][side] for side in both],
            ),
        ),
    ]
    counts = jnp.stack([jnp.sum(word_lengths), jnp.sum(region_counts)]).astype(f32)
    counts = jnp.pad(counts, (0, D - 2))[None] * 0.5
    mine = jnp.where(section == 0, packs[0], packs[1])
    theirs = jnp.where(section == 0, packs[1], packs[0])
    shared = [cross_post_grad, cross_bias_grad.reshape(1, D), counts]
    small_rows = packs[0].shape[0]
    total = jnp.concatenate([mine] + shared, axis=0) + swap(
        jnp.concatenate([theirs] + shared, axis=0), "section"
    )
    distance = 1
    while distance < dp_count:
        total = total + swap(total, "dp", distance)
        distance *= 2
    unit_rows = units // D
    at = 0
    att_bias_grad = total[0:2].reshape(1, 2, 2, width)
    at = 2
    att_post_grad = total[at : at + 6].reshape(1, 2, 3, D)
    at += 6
    feed_bias_grad = total[at : at + 2 * unit_rows].reshape(1, 2, units)
    at += 2 * unit_rows
    feed_post_grad = total[at : at + 6].reshape(1, 2, 3, D)
    at += 6
    squares = total[at : at + 2].reshape(-1, 128)[:8, 0]
    at = small_rows
    cross_post_total = total[at : at + 3]
    cross_bias_total = total[at + 3].reshape(2, width)
    valid_counts = total[at + 4, :2]
    scales = jnp.sqrt(squares / (jnp.repeat(valid_counts, 4) * D))[None]

    late_words = [
        lax.ppermute(value, "section", [(0, 1)]) for value in (feed1_share, late1_share[:chunk])
    ]
    outputs = (
        unflat(back_feed1[0][7]),
        unflat(back_feed1[1][7]),
        unflat(state_grad[spans[0]]),
        unflat(state_grad[spans[1]]),
        cross_bias_total,
        cross_post_total,
        att_bias_grad,
        att_post_grad,
        feed_bias_grad,
        feed_post_grad,
        scales,
    )
    layer0_share, late_words, outputs = lax.optimization_barrier((layer0_share, late_words, outputs))
    late_regions = lax.ppermute(layer0_share, "section", [(1, 0)])
    feed_in_grad, feed_out_grad, att_in_grad, att_out_grad, cross_in_grad, cross_out_grad = (
        placed_gradients(
            meta, feed1_share, late1_share, late_words, layer0_share, late_regions, chunk, width, units
        )
    )
    feed_in_grad = feed_in_grad[None]
    feed_out_grad = feed_out_grad.transpose(0, 2, 1)[None]
    att_in_grad = att_in_grad.transpose(0, 2, 1, 3)[None]
    att_out_grad = att_out_grad.transpose(0, 2, 1)[None]
    cross_in_grad = cross_in_grad.transpose(1, 0, 2)
    cross_out_grad = cross_out_grad.T
    return (
        *outputs[:4],
        cross_in_grad,
        outputs[4],
        cross_out_grad,
        outputs[5],
        att_in_grad,
        outputs[6],
        att_out_grad,
        outputs[7],
        feed_in_grad,
        outputs[8],
        feed_out_grad,
        outputs[9],
        outputs[10],
    )


def solution(mesh):
    placed = (
        P(None, "dp", None, None),
        P(None, "dp", None, None),
        P(None, "dp"),
        P(None, "dp"),
        P(None, "dp", None, None),
        P(None, "dp", None, None),
        P(None, None, "mp"),
        P(None, "mp"),
        P("mp", None),
        P(),
        P("section", None, None, None, "mp"),
        P("section", None, None, "mp"),
        P("section", None, "mp", None),
        P("section", None, None, None),
        P("section", None, None, "mp"),
        P("section", None, "mp"),
        P("section", None, "mp", None),
        P("section", None, None, None),
    )
    return jax.shard_map(
        on_device,
        mesh=mesh,
        in_specs=placed,
        out_specs=(
            P("section", "dp", None, None),
            P("section", "dp", None, None),
            P("section", "dp", None, None),
            P("section", "dp", None, None),
            P(("section", "dp"), None, "mp"),
            P(None, "mp"),
            P("mp", ("section", "dp")),
            P(),
            P("section", None, "dp", None, "mp"),
            P("section", None, None, "mp"),
            P("section", None, "mp", "dp"),
            P("section", None, None, None),
            P("section", None, "dp", "mp"),
            P("section", None, "mp"),
            P("section", None, "mp", "dp"),
            P("section", None, None, None),
            P("section", None),
        ),
        check_vma=False,
    )
```

```python
from functools import partial

import jax
import jax.numpy as jnp
from jax import lax
from jax.experimental import pallas as pl
from jax.experimental.pallas import tpu as pltpu
from jax.sharding import PartitionSpec as P

D = 768
HALF = D // 2
HEAD_DIM = 64
PAIR = 2 * HEAD_DIM
WORDS = 20
REGIONS = 36
EPS = 1e-06
SCALE = HEAD_DIM**-0.5
COST_SCALE = 0.5
ORDER = (0, 1)
bf16 = jnp.bfloat16
f32 = jnp.float32

ROW_ATT_BIAS, ROW_ATT_POST, ROW_FEED_BIAS, ROW_FEED_POST, SMALL_ROWS = 0, 1, 4, 6, 16


def mm(a, b):
    return jnp.dot(a, b, preferred_element_type=f32)


def mm_nt(a, b):
    return lax.dot_general(a, b, (((1,), (1,)), ((), ())), preferred_element_type=f32)


def mm_tn(a, b):
    return lax.dot_general(a, b, (((0,), (0,)), ((), ())), preferred_element_type=f32)


def norm_of(value, gain, shift):
    centred = value - jnp.mean(value, axis=-1, keepdims=True)
    spread = jnp.mean(centred * centred, axis=-1, keepdims=True)
    rstd = lax.rsqrt(spread + EPS)
    unit = centred * rstd
    return unit, rstd, unit * gain + shift


def norm_back(unit, rstd, gain, incoming):
    scaled = incoming * gain
    mean = jnp.mean(scaled, axis=-1, keepdims=True)
    along = jnp.mean(scaled * unit, axis=-1, keepdims=True)
    return (scaled - mean - unit * along) * rstd


def summed(own, other):
    return own[...].astype(f32) + other[...].astype(f32)


def column_sum(value):
    return jnp.sum(value, axis=0, keepdims=True)


def square_sum(value, valid):
    rows = jnp.sum(value * value, axis=-1, keepdims=True) * valid
    return jnp.broadcast_to(jnp.sum(rows, axis=0, keepdims=True), (1, 128))


def lengths_of(meta, side, batch, item):
    result = jnp.zeros_like(item)
    for i in range(batch):
        result = jnp.where(item == i, meta[1 + side * batch + i], result)
    return result


def row_valid(meta, side, batch, rows):
    index = lax.broadcasted_iota(jnp.int32, (rows, 1), 0)
    length = lengths_of(meta, side, batch, lax.rem(index, batch))
    return (lax.div(index, batch) < length).astype(f32)


def pair_valid(meta, side, batch, rows, keys):
    index = lax.broadcasted_iota(jnp.int32, (1, keys), 1)
    item = lax.rem(index, batch)
    length = lengths_of(meta, side, batch, item)
    item = jnp.where(lax.div(index, batch) < length, item, -1)
    row_item = lax.rem(lax.broadcasted_iota(jnp.int32, (rows, 1), 0), batch)
    return jnp.broadcast_to(row_item, (rows, keys)) == jnp.broadcast_to(item, (rows, keys))


def head_lanes(head):
    lane = lax.broadcasted_iota(jnp.int32, (1, PAIR), 1)
    return (lane // HEAD_DIM) == head


def attend(query, keys, values, valid, probs_ref, context_ref):
    for pair in range(query.shape[1] // PAIR):
        lanes = slice(pair * PAIR, (pair + 1) * PAIR)
        contexts = []
        for head in range(2):
            chosen = query[:, lanes] * head_lanes(head).astype(bf16)
            scores = mm_nt(chosen, keys[:, lanes]) * SCALE
            scores = jnp.where(valid, scores, -1e9)
            shifted = jnp.exp(scores - jnp.max(scores, axis=-1, keepdims=True))
            total = jnp.sum(shifted, axis=-1, keepdims=True)
            probs = (shifted * (1.0 / total)).astype(bf16)
            probs_ref[2 * pair + head] = probs
            contexts.append(mm(probs, values[:, lanes]))
        context_ref[:, lanes] = jnp.where(head_lanes(0), contexts[0], contexts[1]).astype(bf16)


def attend_back(query, keys, values, probs_ref, grad_context, emit):
    first = head_lanes(0)
    for pair in range(query.shape[1] // PAIR):
        lanes = slice(pair * PAIR, (pair + 1) * PAIR)
        grads = ([], [], [])
        for head in range(2):
            probs = probs_ref[2 * pair + head]
            chosen = grad_context[:, lanes] * head_lanes(head).astype(bf16)
            grad_probs = mm_nt(chosen, values[:, lanes])
            wide = probs.astype(f32)
            product = wide * grad_probs
            grad_scores = product - wide * jnp.sum(product, axis=-1, keepdims=True)
            grad_scores = grad_scores.astype(bf16)
            grads[0].append(mm(grad_scores, keys[:, lanes]) * SCALE)
            grads[1].append(mm_tn(grad_scores, query[:, lanes]) * SCALE)
            grads[2].append(mm_tn(probs, grad_context[:, lanes]))
        for kind in range(3):
            emit(kind, lanes, jnp.where(first, grads[kind][0], grads[kind][1]).astype(bf16))


def small_of(meta, layer, side, own, other):
    return jnp.where(meta[0] == layer, own[side], other[side])


class Fetched:
    def __init__(self, copy, buffer):
        self.copy, self.buffer, self.waited = copy, buffer, False
        self.shape, self.dtype = buffer.shape, buffer.dtype

    def wait(self):
        if not self.waited:
            self.copy.wait()
            self.waited = True
        return self.buffer

    def __getitem__(self, index):
        return self.wait()[index]


class Weights:
    def __init__(self, meta, layer, pairs, buffers, sems):
        self.copies = []
        mine = meta[0] == layer
        at = 0
        for (own, other, pieces), buffer in zip(pairs, buffers):
            copies = []
            for piece in pieces:
                copy = pltpu.make_async_copy(own.at[piece], buffer.at[piece], sems.at[at])
                if other is None:
                    copy.start()
                else:
                    second = pltpu.make_async_copy(
                        other.at[piece], buffer.at[piece], sems.at[at]
                    )
                    pl.when(mine)(copy.start)
                    pl.when(jnp.logical_not(mine))(second.start)
                copies.append(Fetched(copy, buffer))
                at += 1
            self.copies.append(copies)

    def get(self, slot, piece=None):
        copies = self.copies[slot]
        for copy in copies if piece is None else (copies[piece],):
            copy.wait()
        return copies[0].buffer


class Held:
    def __init__(self, *refs):
        self.refs = refs

    def get(self, slot, piece=None):
        return self.refs[slot]


def weight_inputs(entry, leave, kinds="wwww"):
    if len(entry) == 1:
        return [(entry[0], "v"), (leave[0], "v")]
    return list(zip(entry + leave, kinds))


def pass_on(meta, layer, offered, taken, sems):
    copies = []
    for i, target in enumerate(taken):
        own = pltpu.make_async_copy(offered[2 * i].at[0], target, sems.at[i])
        other = pltpu.make_async_copy(offered[2 * i + 1].at[0], target, sems.at[i])
        pl.when(meta[0] == layer)(own.start)
        pl.when(meta[0] != layer)(other.start)
        copies.append(own)
    return copies


def items_of(meta, source, raw, rows_ref, sem, batch):
    copy = pltpu.make_async_copy(source.at[meta[0]], raw, sem)
    copy.start()
    copy.wait()
    for slot in range(raw.shape[0]):
        rows_ref[slot * batch : (slot + 1) * batch] = raw[slot].astype(f32)


def maps(own, other, side, pieces=((),)):
    if other is None:
        return own, None, pieces
    return own.at[0, side], other.at[0, side], pieces


ENTRY = ((0,), (1,), (2,))


def column_pieces(size, count):
    return tuple(
        (slice(None), slice(i * size // count, (i + 1) * size // count)) for i in range(count)
    )


def row_pieces(size, count):
    return tuple((slice(i * size // count, (i + 1) * size // count),) for i in range(count))


def call(body, ins, outs, scratch=(), cost=0.0, name=None, ties=(), mib=14):
    spaces = {
        "s": pltpu.SMEM, "v": pltpu.VMEM, "w": pltpu.HBM, "h": pltpu.HBM, "a": pl.ANY, "f": pl.ANY
    }
    ties = [tie if isinstance(tie, tuple) else (tie, "w") for tie in ties]
    extra = [(i, out[5]) for i, out in enumerate(outs) if len(out) > 3 and out[5] is not None]
    aliases = {len(ins) + at: i for at, (i, _) in enumerate(extra)}
    ins = list(ins) + [(array, "w") for _, array in extra]
    places = [out[3:5] if len(out) > 3 else None for out in outs]
    fetched = [i for i, (_, kind) in enumerate(ins) if kind in "hf"]
    written = [i for i, out in enumerate(outs) if out[2] == "h"]
    n_ins, n_ties, n_outs, n_scratch = len(ins), len(ties), len(outs), len(scratch)

    def whole(*refs):
        given = list(refs[:n_ins])
        results = list(refs[n_ins + n_ties : n_ins + n_ties + n_outs])
        rest = refs[n_ins + n_ties + n_outs :]
        own, rest = rest[:n_scratch], rest[n_scratch:]
        buffers, rest = rest[: len(fetched)], rest[len(fetched) :]
        staged, rest = rest[: len(written)], rest[len(written) :]
        sems = rest[0] if rest else None
        for slot, i in enumerate(fetched):
            copy = pltpu.make_async_copy(given[i], buffers[slot], sems.at[slot])
            copy.start()
            given[i] = Fetched(copy, buffers[slot])
        leaving = {}
        for slot, i in enumerate(written):
            target = results[i]
            if places[i] is not None:
                target = target.at[pl.ds(places[i][1], staged[slot].shape[0])]
            copy = pltpu.make_async_copy(staged[slot], target, sems.at[len(fetched) + slot])
            leaving[id(staged[slot])] = copy
            results[i] = staged[slot]
        started = []

        def flush(*done):
            for ref in done:
                copy = leaving.pop(id(ref), None)
                if copy is not None:
                    copy.start()
                    started.append(copy)

        body(flush, *given[: n_ins - len(extra)], *results, *own)
        flush(*[staged[slot] for slot in range(len(written))])
        for copy in started:
            copy.wait()
        for item in given:
            if isinstance(item, Fetched):
                item.wait()

    arrays = [
        pltpu.with_memory_space_constraint(array, spaces[kind]) if kind in "vwh" else array
        for array, kind in [*ins, *ties]
    ]
    own_scratch = list(scratch)
    own_scratch += [pltpu.VMEM(arrays[i].shape, arrays[i].dtype) for i in fetched]
    own_scratch += [pltpu.VMEM(outs[i][0], outs[i][1]) for i in written]
    if fetched or written:
        own_scratch.append(pltpu.SemaphoreType.DMA((len(fetched) + len(written),)))
    return pl.pallas_call(
        whole,
        out_shape=[
            spaces[out[2]]((out[3], *out[0][1:]) if len(out) > 3 else out[0], out[1]) for out in outs
        ],
        in_specs=[pl.BlockSpec(memory_space=spaces[kind]) for _, kind in [*ins, *ties]],
        out_specs=[pl.BlockSpec(memory_space=spaces[out[2]]) for out in outs],
        input_output_aliases=aliases,
        scratch_shapes=own_scratch,
        compiler_params=pltpu.CompilerParams(vmem_limit_bytes=mib * 1024 * 1024),
        cost_estimate=pl.CostEstimate(
            flops=int(cost * COST_SCALE * 1.15e9), bytes_accessed=0, transcendentals=0
        ),
        name=name,
    )(*arrays)


def spans_of(rows):
    return slice(0, rows[0]), slice(rows[0], rows[0] + rows[1])


def select_rows(value, chooser, own_ref, pack_ref):
    moved = mm(value, chooser[...]).astype(bf16)
    own_ref[...] = moved[:, :HALF]
    pack_ref[:, :HALF] = moved[:, HALF:]


def project(low, weights, bias_q, bias_v, qkv_ref):
    qkv_ref[0] = (mm(low, weights.get(0, 0)[0]) + bias_q).astype(bf16)
    qkv_ref[1] = mm(low, weights.get(0, 1)[1]).astype(bf16)
    qkv_ref[2] = (mm(low, weights.get(0, 2)[2]) + bias_v).astype(bf16)


def self_forward(
    side, layer, batch, meta, state, prior, small, chooser, att_in, att_out, place, ties=(), later=()
):
    rows = state.shape[1] * batch if prior is None else state.shape[0]
    width = att_in[0].shape[-1]
    first = prior is None
    held, n_maps = len(att_in) == 1, len(att_in + att_out)

    def body(flush, meta, state, *refs):
        refs = list(refs)
        if not first:
            own, other, post = refs[:3]
            refs = refs[3:]
        small = small_of(meta, layer, side, refs[0], refs[1])
        chooser, refs = refs[2], refs[3:]
        given, refs = refs[:n_maps], refs[n_maps:]
        offered, refs = refs[: 2 * len(later)], refs[2 * len(later) :]
        qkv, probs, selected, pack, part, squares = refs[:6]
        refs = refs[6:]
        if not first:
            mixed_ref, unit_ref, rstd_ref = refs[:3]
            taken, refs = refs[3 : 3 + len(later)], refs[3 + len(later) :]
            passing = pass_on(meta, layer, offered, taken, refs[-1]) if later else []
        else:
            low_ref, refs = refs[0], refs[1:]
            raw, rows_ref, raw_sem = refs[-3:]
            refs = refs[:-3]
        if held:
            weights = Held(given[0].at[side], given[1].at[side])
        else:
            in_buffer, out_buffer, sems = refs
            weights = Weights(
                meta,
                layer,
                (maps(*given[:2], side, ENTRY), maps(*given[2:], side)),
                (in_buffer, out_buffer),
                sems,
            )
        valid = row_valid(meta, side, batch, rows)
        if first:
            items_of(meta, state, raw, rows_ref, raw_sem, batch)
            squares[...] = square_sum(rows_ref[...], valid)
            low = rows_ref[...].astype(bf16)
            low_ref[...] = low
        else:
            branch = summed(own, other) + post[0:1]
            squares[...] = square_sum(branch, valid)
            unit, rstd, mixed = norm_of(state[...].astype(f32) + branch, post[1:2], post[2:3])
            unit_ref[...] = unit
            rstd_ref[...] = rstd
            mixed_ref[...] = mixed
            low = mixed.astype(bf16)
        select_rows(low, chooser, selected, pack)
        flush(selected)
        biases = small[ROW_ATT_BIAS : ROW_ATT_BIAS + 1]
        project(low, weights, biases[:, :width], biases[:, width : 2 * width], qkv)
        context = pack.at[:, HALF:]
        attend(
            qkv[0], qkv[1], qkv[2], pair_valid(meta, side, batch, rows, rows), probs, context
        )
        flush(qkv, probs, pack)
        part[...] = mm(context[...], weights.get(1)[...]).astype(bf16)
        if not first:
            for copy in passing:
                copy.wait()

    ins = [(meta, "s"), (state, "w" if first else "v")]
    if not first:
        ins += list(zip(prior, "vvv"))
    ins += [(item, "v") for item in (*small, chooser)]
    ins += weight_inputs(att_in, att_out, "wawa")
    ins += [(item, "w") for pair in later for item in pair]
    outs = [
        ((3, rows, width), bf16, "h"),
        ((width // HEAD_DIM, rows, rows), bf16, "h"),
        ((rows, HALF), bf16, "h"),
        ((rows, HALF + width), bf16, "h", *place),
        ((rows, D), bf16, "v"),
        ((1, 128), f32, "h"),
    ]
    if not first:
        outs += [((rows, D), f32, "v"), ((rows, D), f32, "h"), ((rows, 1), f32, "h")]
        outs += [(pair[0].shape[1:], bf16, "v") for pair in later]
    else:
        outs.append(((rows, D), bf16, "v"))
    scratch = [
        pltpu.VMEM((3, D, width), bf16),
        pltpu.VMEM((width, D), bf16),
        pltpu.SemaphoreType.DMA((6,)),
    ]
    scratch = [] if held else scratch
    if first:
        scratch += [
            pltpu.VMEM(state.shape[1:], bf16),
            pltpu.VMEM((rows, D), f32),
            pltpu.SemaphoreType.DMA,
        ]
    if later:
        scratch.append(pltpu.SemaphoreType.DMA((len(later),)))
    return call(body, ins, outs, scratch, 4.0, f"self_forward_{layer}_{side}", ties, 12)


def hand_over(low_ref, kept, sent, sems):
    copies = []
    for slot, target in enumerate((kept, sent)):
        copies.append(
            pltpu.make_async_copy(low_ref, target.at[:, pl.ds(0, D)], sems.at[slot])
        )
        copies[-1].start()
    return copies


def hand_halves(meta, batch, wide_ref, kept, sent, sems):
    count = wide_ref.shape[1] // 2
    copies = []
    for half in (0, 1):
        source = wide_ref.at[:, pl.ds(half * count, count)]
        to_kept, to_sent = (
            pltpu.make_async_copy(source, target.at[:, pl.ds(D, count)], sems.at[2 + half])
            for target in (kept, sent)
        )
        mine = meta[1 + 2 * batch] == half
        pl.when(mine)(to_kept.start)
        pl.when(jnp.logical_not(mine))(to_sent.start)
        copies.append(to_kept)
    return copies


def hand_scratch(rows, units):
    return [
        pltpu.VMEM((rows, D), bf16),
        pltpu.VMEM((rows, units), bf16),
        pltpu.SemaphoreType.DMA((4,)),
    ]


def feed_forward(
    side, layer, batch, meta, residual, own, other, small, chooser, feed_in, feed_out, place, ties=()
):
    rows = residual.shape[0]
    units = feed_in[0].shape[-1]
    step = units // 4

    held, n_maps = len(feed_in) == 1, len(feed_in + feed_out)

    def body(flush, meta, residual, own, other, small_own, small_other, *refs):
        small = small_of(meta, layer, side, small_own, small_other)
        if not held:
            chooser, refs = refs[0], refs[1:]
        given, refs = refs[:n_maps], refs[n_maps:]
        settled_ref, unit_ref, rstd_ref, selected, pack, slope, part, squares = refs[:8]
        if held:
            weights = Held(given[0].at[side], given[1].at[side])
            low_ref, active_ref, sems = refs[8:]
        else:
            in_buffer, out_buffer, sems = refs[8:]
            weights = Weights(
                meta,
                layer,
                (
                    maps(*given[:2], side, column_pieces(units, 4)),
                    maps(*given[2:], side, row_pieces(units, 2)),
                ),
                (in_buffer, out_buffer),
                sems,
            )
        post = small[ROW_ATT_POST : ROW_ATT_POST + 3]
        branch = summed(own, other) + post[0:1]
        squares[...] = square_sum(branch, row_valid(meta, side, batch, rows))
        unit, rstd, settled = norm_of(residual[...].astype(f32) + branch, post[1:2], post[2:3])
        unit_ref[...] = unit
        rstd_ref[...] = rstd
        settled_ref[...] = settled
        low = settled.astype(bf16)
        if held:
            low_ref[...] = low
            copies = hand_over(low_ref, selected, pack, sems)
            flush(unit_ref, rstd_ref)
        else:
            select_rows(low, chooser, selected, pack)
            active_ref = pack.at[:, HALF:]
            flush(unit_ref, rstd_ref, selected)
        for i in range(units // step):
            first = weights.get(0, i)
            columns = slice(i * step, (i + 1) * step)
            row = ROW_FEED_BIAS + (i * step) // D
            place = (i * step) % D
            hidden = mm(low, first[:, columns]) + small[row : row + 1, place : place + step]
            below = 0.5 + 0.5 * lax.erf(hidden * (0.5**0.5))
            density = jnp.exp(hidden * hidden * -0.5) * 0.3989422804014327
            active_ref[:, columns] = (hidden * below).astype(bf16)
            slope[:, columns] = (below + hidden * density).astype(bf16)
        flush(pack, slope)
        if held:
            copies += hand_halves(meta, batch, active_ref, selected, pack, sems)
        part[...] = mm(active_ref[...], weights.get(1)[...]).astype(bf16)
        if held:
            for copy in copies:
                copy.wait()

    ins = [(meta, "s"), (residual, "v"), (own, "v"), (other, "v")]
    ins += [(item, "v") for item in ((*small,) if held else (*small, chooser))]
    ins += weight_inputs(feed_in, feed_out, "wawa")
    outs = [
        ((rows, D), f32, "v"),
        ((rows, D), f32, "h"),
        ((rows, 1), f32, "h"),
        *(
            [((rows, D + units // 2), bf16, "w")] * 2
            if held
            else [((rows, HALF), bf16, "h"), ((rows, HALF + units), bf16, "h", *place)]
        ),
        ((rows, units), bf16, "h"),
        ((rows, D), bf16, "v"),
        ((1, 128), f32, "h"),
    ]
    scratch = [
        pltpu.VMEM((D, units), bf16),
        pltpu.VMEM((units, D), bf16),
        pltpu.SemaphoreType.DMA((6,)),
    ]
    if held:
        scratch = hand_scratch(rows, units)
    cost = 12.0 if held and side == ORDER[-1] else 4.3
    return call(body, ins, outs, scratch, cost, f"feed_forward_{layer}_{side}", ties, 12 if held else 14)


def cross_forward(
    batch, meta, streams, smalls, chooser, cross_in, cross_bias, cross_out, later, ties=()
):
    rows = [stream[0].shape[0] for stream in streams]
    spans = spans_of(rows)
    width = cross_out.shape[0]
    heads = width // HEAD_DIM

    def body(flush, meta, *refs):
        given = (refs[0:3], refs[3:6])
        small = [small_of(meta, 0, side, refs[6], refs[7]) for side in (0, 1)]
        chooser, in_ref, bias, out_ref = refs[8:12]
        offered, refs = refs[12 : 12 + 2 * len(later)], refs[:12] + refs[12 + 2 * len(later) :]
        taken, refs = refs[29 : 29 + len(later)], refs[:29] + refs[29 + len(later) :]
        all_pack = refs[28]
        outs = [refs[12:20], refs[20:28]]
        for side in (0, 1):
            outs[side] = outs[side][:5] + (all_pack.at[spans[side]],) + outs[side][5:]
        in_buffer, out_buffer, sems, later_sems = refs[29:]
        weights = Weights(
            meta,
            0,
            (maps(in_ref, None, 0, ENTRY), maps(out_ref, None, 0)),
            (in_buffer, out_buffer),
            sems,
        )
        passing = pass_on(meta, 1, offered, taken, later_sems)
        lows = []
        for side in (0, 1):
            settled, own, other = given[side]
            state, unit_ref, rstd_ref, squares, selected, pack, qkv, probs, part = outs[side]
            post = small[side][ROW_FEED_POST : ROW_FEED_POST + 3]
            branch = summed(own, other) + post[0:1]
            unit, rstd, result = norm_of(settled[...] + branch, post[1:2], post[2:3])
            unit_ref[...] = unit
            rstd_ref[...] = rstd
            low = result.astype(bf16)
            state[...] = low
            valid = row_valid(meta, side, batch, rows[side])
            squares[0:1] = square_sum(branch, valid)
            squares[1:2] = square_sum(low.astype(f32), valid)
            select_rows(low, chooser, selected, pack)
            flush(unit_ref, rstd_ref, selected)
            lows.append(low)
        for side in (0, 1):
            project(lows[side], weights, bias[0:1], bias[1:2], outs[side][6])
        leave = weights.get(1)
        for side in (0, 1):
            pack, qkv, probs, part = outs[side][5:]
            there = outs[1 - side][6]
            valid = pair_valid(meta, 1 - side, batch, rows[side], rows[1 - side])
            context = pack.at[:, HALF:]
            attend(qkv[0], there[1], there[2], valid, probs, context)
            flush(qkv, probs)
            part[...] = mm(context[...], leave[...]).astype(bf16)
        for copy in passing:
            copy.wait()

    ins = [(meta, "s")] + [pair for stream in streams for pair in zip(stream, "vvv")]
    ins += [(item, "v") for item in smalls]
    ins += [(chooser, "v"), (cross_in, "w"), (cross_bias, "v"), (cross_out, "w")]
    ins += [(item, "w") for pair in later for item in pair]
    outs = []
    for side in (0, 1):
        here, there = rows[side], rows[1 - side]
        outs += [
            ((here, D), bf16, "v"),
            ((here, D), f32, "h"),
            ((here, 1), f32, "h"),
            ((2, 128), f32, "h"),
            ((here, HALF), bf16, "h"),
            ((3, here, width), bf16, "h"),
            ((heads, here, there), bf16, "h"),
            ((here, D), bf16, "v"),
        ]
    outs.append(((sum(rows), HALF + width), bf16, "h"))
    outs += [(pair[0].shape[1:], bf16, "v") for pair in later]
    scratch = [
        pltpu.VMEM((3, D, width), bf16),
        pltpu.VMEM((width, D), bf16),
        pltpu.SemaphoreType.DMA((6,)),
        pltpu.SemaphoreType.DMA((len(later),)),
    ]
    result = call(body, ins, outs, scratch, 6.8, "cross_forward", ties)
    return result[:8], result[8:16], result[16], result[17:]


class Layout:
    def __init__(self, sides, rows, given):
        self.sides, self.total, self.spans = sides, sum(rows), spans_of(rows)
        self.single = len(sides) == 1
        self.side = sides[0]
        self.count = rows[self.side] if self.single else self.total
        self.given = given

    def here(self, side):
        return slice(0, self.count) if self.single else self.spans[side]

    def index(self, side):
        return 0 if self.single else side

    def rows(self, width, dtype, at):
        if not self.single:
            return (self.total, width), dtype, "h"
        given = self.given[at] if self.given else None
        return (self.count, width), dtype, "h", self.total, self.spans[self.side].start, given

    def each(self, shape, at):
        if not self.single:
            return (2, *shape), f32, "h"
        given = self.given[at] if self.given else None
        return (1, *shape), f32, "h", 2, self.side, given


def feed_backward(
    layer, sides, rows, batch, meta, tops, joint, small, chooser, slopes, feed_in, feed_out, ties=(),
    given=None,
):
    last = joint is None
    layout = Layout(sides, rows, given)
    units = slopes[0].shape[1]
    step = units // 4
    n_top = len(tops[0])
    n = len(sides)
    held, n_maps = len(feed_in) == 1, len(feed_in + feed_out)

    def body(flush, meta, *refs):
        tops = {}
        for side in sides:
            tops[side], refs = refs[:n_top], refs[n_top:]
        if not last:
            joint, refs = refs[:3], refs[3:]
        small = {side: small_of(meta, layer, side, refs[0], refs[1]) for side in sides}
        refs = refs[2:]
        if not held:
            chooser, refs = refs[0], refs[1:]
        slopes, refs = dict(zip(sides, refs[:n])), refs[n:]
        given, refs = refs[:n_maps], refs[n_maps:]
        grad_all, selected_all, pack_all, part_all, post_all, bias_all = refs[:6]
        if last:
            squares_all, results = refs[6], dict(zip(sides, refs[7 : 7 + n]))
            low_ref, hidden_ref, hand_sems, raw, rows_ref, raw_sem = refs[-6:]
        weights = {}
        for i, side in enumerate(sides):
            if held:
                weights[side] = Held(given[1].at[side], given[0].at[side])
                continue
            in_buffer, out_buffer, sems = refs[-3:]
            weights[side] = Weights(
                meta,
                layer,
                (
                    maps(*given[2:], side, row_pieces(units, 4)),
                    maps(*given[:2], side, column_pieces(units, 2)),
                ),
                (out_buffer.at[i], in_buffer.at[i]),
                sems.at[i],
            )
        lows = {}
        for side in sides:
            here, at = layout.here(side), layout.index(side)
            post = small[side][ROW_FEED_POST : ROW_FEED_POST + 3]
            if last:
                settled, own, other, cotangent = tops[side]
                branch = summed(own, other) + post[0:1]
                unit, rstd, result = norm_of(settled[...] + branch, post[1:2], post[2:3])
                low = result.astype(bf16)
                results[side][...] = low
                valid = row_valid(meta, side, batch, rows[side])
                squares_all[at, 0:1] = square_sum(branch, valid)
                squares_all[at, 1:2] = square_sum(low.astype(f32), valid)
                items_of(meta, cotangent, raw, rows_ref, raw_sem, batch)
                incoming = rows_ref[...] * valid
            else:
                unit_ref, rstd_ref = tops[side]
                unit, rstd = unit_ref[...], rstd_ref[...]
                incoming = (joint[0][here] + summed_rows(joint[1], joint[2], here)).astype(bf16)
                incoming = incoming.astype(f32)
            grad = norm_back(unit, rstd, post[1:2], incoming)
            grad_all[here] = grad
            low = grad.astype(bf16)
            post_all[at, 0:1] = column_sum(low.astype(f32))
            post_all[at, 1:2] = column_sum(incoming * unit)
            post_all[at, 2:3] = column_sum(incoming)
            lows[side] = low
        flush(grad_all, post_all)
        if held:
            low_ref[...] = lows[sides[0]]
            copies = hand_over(low_ref, selected_all, pack_all, hand_sems)
        else:
            hidden_ref = pack_all.at[:, HALF:]
        for side in sides:
            here, at = layout.here(side), layout.index(side)
            for i in range(units // step):
                columns = slice(i * step, (i + 1) * step)
                active = mm_nt(lows[side], weights[side].get(0, i)[columns, :])
                hidden = (active * slopes[side][:, columns].astype(f32)).astype(bf16)
                hidden_ref[here, columns] = hidden
                bias_all[at, :, columns] = column_sum(hidden.astype(f32))
            if not held:
                select_rows(lows[side], chooser, selected_all.at[here], pack_all.at[here])
        flush(pack_all, selected_all)
        if held:
            copies += hand_halves(meta, batch, hidden_ref, selected_all, pack_all, hand_sems)
        for side in sides:
            here = layout.here(side)
            part_all[here] = mm_nt(hidden_ref[here], weights[side].get(1)[...]).astype(bf16)
        if held:
            for copy in copies:
                copy.wait()

    ins = [(meta, "s")] + [pair for top in tops for pair in zip(top, "vvvw" if last else "vv")]
    if not last:
        ins += [(item, "v") for item in joint]
    ins += [(item, "v") for item in ((*small, *slopes) if held else (*small, chooser, *slopes))]
    ins += weight_inputs(feed_in, feed_out)
    count = layout.count
    outs = [
        ((count, D), f32, "v" if last else "h"),
        *(
            [((count, D + units // 2), bf16, "w")] * 2
            if held
            else [layout.rows(HALF, bf16, 1), ((count, HALF + units), bf16, "h")]
        ),
        ((count, D), bf16, "v" if last else "h"),
        layout.each((3, D), 4),
        layout.each((1, units), 5),
    ]
    if last:
        outs += [layout.each((2, 128), 6)] + [((rows[side], D), bf16, "h") for side in sides]
    scratch = [
        pltpu.VMEM((n, D, units), bf16),
        pltpu.VMEM((n, units, D), bf16),
        pltpu.SemaphoreType.DMA((n, 6)),
    ]
    if last:
        side = sides[0]
        scratch = hand_scratch(rows[side], units) + [
            pltpu.VMEM(tops[0][3].shape[1:], bf16),
            pltpu.VMEM((rows[side], D), f32),
            pltpu.SemaphoreType.DMA,
        ]
    name = f"feed_backward_{layer}_" + "".join(map(str, sides))
    cost = 12.0 if sides == ORDER[:1] else 11.0 * count / layout.total
    return call(body, ins, outs, scratch, cost, name, ties, 12 if held else 24)


def summed_rows(own, other, here):
    return own[here].astype(f32) + other[here].astype(f32)


def back_through_norm(top, grad_in, branch, gain, grad_ref, post_ref):
    unit_ref, rstd_ref = top
    incoming = grad_in + branch
    unit = unit_ref[...]
    grad = norm_back(unit, rstd_ref[...], gain, incoming)
    grad_ref[...] = grad
    low = grad.astype(bf16)
    post_ref[0:1] = column_sum(low.astype(f32))
    post_ref[1:2] = column_sum(incoming * unit)
    post_ref[2:3] = column_sum(incoming)
    return low


def emit_into(pack, width):
    def emit(kind, lanes, value):
        start = HALF + kind * width + lanes.start
        pack[:, start : start + PAIR] = value

    return emit


def back_to_input(pack, weights, slot, width):
    grads = [pack[:, HALF + j * width : HALF + (j + 1) * width] for j in range(3)]
    total = mm_nt(grads[0], weights.get(slot, 0)[0])
    total += mm_nt(grads[1], weights.get(slot, 1)[1])
    total += mm_nt(grads[2], weights.get(slot, 2)[2])
    return total.astype(bf16)


def self_backward(
    layer, sides, rows, meta, tops, joint, small, chooser, qkvs, probs, att_in, att_out, ties=(),
    given=None,
):
    layout = Layout(sides, rows, given)
    width = qkvs[0].shape[2]
    n = len(sides)
    held, n_maps = len(att_in) == 1, len(att_in + att_out)

    def body(flush, meta, *refs):
        tops = {side: refs[2 * i : 2 * i + 2] for i, side in enumerate(sides)}
        joint, refs = refs[2 * n : 2 * n + 3], refs[2 * n + 3 :]
        small = {side: small_of(meta, layer, side, refs[0], refs[1]) for side in sides}
        chooser, refs = refs[2], refs[3:]
        qkvs, probs, refs = dict(zip(sides, refs[:n])), dict(zip(sides, refs[n : 2 * n])), refs[2 * n :]
        given, refs = refs[:n_maps], refs[n_maps:]
        grad_all, selected_all, pack_all, part_all, post_all, bias_all = refs[:6]
        weights = {}
        for i, side in enumerate(sides):
            if held:
                weights[side] = Held(given[1].at[side], given[0].at[side])
                continue
            in_buffer, out_buffer, sems = refs[6:]
            weights[side] = Weights(
                meta,
                layer,
                (maps(*given[2:], side), maps(*given[:2], side, ENTRY)),
                (out_buffer.at[i], in_buffer.at[i]),
                sems.at[i],
            )
        for side in sides:
            here, at = layout.here(side), layout.index(side)
            pack = pack_all.at[here]
            gain = small[side][ROW_ATT_POST + 1 : ROW_ATT_POST + 2]
            low = back_through_norm(
                tops[side],
                joint[0][here],
                summed_rows(joint[1], joint[2], here),
                gain,
                grad_all.at[here],
                post_all.at[at],
            )
            context = mm_nt(low, weights[side].get(0)[...]).astype(bf16)
            qkv = qkvs[side]
            attend_back(qkv[0], qkv[1], qkv[2], probs[side], context, emit_into(pack, width))
            bias_all[at, 0:1] = column_sum(pack[:, HALF : HALF + width].astype(f32))
            bias_all[at, 1:2] = column_sum(pack[:, HALF + 2 * width :].astype(f32))
            select_rows(low, chooser, selected_all.at[here], pack)
        flush(pack_all, selected_all, grad_all, post_all, bias_all)
        for side in sides:
            here = layout.here(side)
            part_all[here] = back_to_input(pack_all.at[here], weights[side], 1, width)

    near = "v" if layer == 1 else "h"
    ins = [(meta, "s")] + [(item, near) for top in tops for item in top]
    ins += [*zip(joint, "vvv" if layer == 1 else "hhf")] + [(item, near) for item in small]
    ins += [(item, near) for item in (chooser, *qkvs, *probs)]
    ins += weight_inputs(att_in, att_out)
    outs = [
        ((layout.count, D), f32, "h"),
        layout.rows(HALF, bf16, 1),
        layout.rows(HALF + 3 * width, bf16, 2),
        ((layout.count, D), bf16, "h"),
        layout.each((3, D), 4),
        layout.each((2, width), 5),
    ]
    scratch = [
        pltpu.VMEM((n, 3, D, width), bf16),
        pltpu.VMEM((n, width, D), bf16),
        pltpu.SemaphoreType.DMA((n, 6)),
    ]
    scratch = [] if held else scratch
    name = f"self_backward_{layer}_" + "".join(map(str, sides))
    cost = 12.0 * layout.count / layout.total
    return call(body, ins, outs, scratch, cost, name, ties, 12 if held else 18)


def cross_backward(meta, tops, grads, owns, others, post, chooser, qkvs, probs, cross_in, cross_out, ties=()):
    rows = [qkv.shape[1] for qkv in qkvs]
    width = cross_out.shape[0]
    spans, total = spans_of(rows), sum(rows)

    def body(flush, meta, *refs):
        tops, grads, owns, others = (refs[:2], refs[2:4]), refs[4:6], refs[6:8], refs[8:10]
        post, chooser, qkvs, probs = refs[10], refs[11], refs[12:14], refs[14:16]
        in_ref, out_ref = refs[16:18]
        grad_all, selected_all, pack_all, part_all, post_out, bias_out = refs[18:24]
        in_buffer, out_buffer, post_each, sems = refs[24:]
        weights = Weights(
            meta,
            0,
            (maps(out_ref, None, 0), maps(in_ref, None, 0, ENTRY)),
            (out_buffer, in_buffer),
            sems,
        )
        packs = [pack_all.at[here] for here in spans]
        lows = []
        for side in (0, 1):
            here = spans[side]
            low = back_through_norm(
                tops[side],
                grads[side][...],
                summed(owns[side], others[side]),
                post[1:2],
                grad_all.at[here],
                post_each.at[side],
            )
            lows.append(low)
        post_out[...] = post_each[0] + post_each[1]
        leave = weights.get(0)
        for side in (0, 1):
            context = mm_nt(lows[side], leave[...]).astype(bf16)
            to_here, to_there = emit_into(packs[side], width), emit_into(packs[1 - side], width)

            def emit(kind, lanes, value):
                (to_here if kind == 0 else to_there)(kind, lanes, value)

            attend_back(
                qkvs[side][0], qkvs[1 - side][1], qkvs[1 - side][2], probs[side], context, emit
            )
        for side in (0, 1):
            select_rows(lows[side], chooser, selected_all.at[spans[side]], packs[side])
        bias_out[0:1] = column_sum(pack_all[:, HALF : HALF + width].astype(f32))
        bias_out[1:2] = column_sum(pack_all[:, HALF + 2 * width :].astype(f32))
        flush(pack_all, selected_all)
        part_all[...] = back_to_input(pack_all, weights, 1, width)

    ins = [(meta, "s")] + [(item, "h") for top in tops for item in top]
    ins += [(item, "h") for item in (*grads, *owns)] + [(item, "f") for item in others]
    ins += [(item, "h") for item in (post, chooser, *qkvs, *probs)]
    ins += [(cross_in, "w"), (cross_out, "w")]
    outs = [
        ((total, D), f32, "v"),
        ((total, HALF), bf16, "h"),
        ((total, HALF + 3 * width), bf16, "h"),
        ((total, D), bf16, "v"),
        ((3, D), f32, "h"),
        ((2, width), f32, "h"),
    ]
    scratch = [
        pltpu.VMEM((3, D, width), bf16),
        pltpu.VMEM((width, D), bf16),
        pltpu.VMEM((2, 3, D), f32),
        pltpu.SemaphoreType.DMA((6,)),
    ]
    return call(body, ins, outs, scratch, 10.0, "cross_backward", ties, 16)


class Block:
    def __init__(self, in_selected, in_packs, in_gots, out_selected, out_packs, out_gots):
        self.parts = [*in_selected, *in_packs, *in_gots, out_selected, *out_packs, *out_gots]
        self.counts = (len(in_packs), len(out_packs))
        self.lead = HALF
        self.kinds = "w" * len(self.parts)
        self.sizes = (out_packs[0].shape[1] - HALF, in_packs[0].shape[1] - HALF)
        self.rows = [array.shape[0] for array in in_selected]

    def buffers(self):
        return [
            pltpu.VMEM((2 * rows, HALF + size), bf16)
            for rows in self.rows
            for size in (self.sizes[1], self.sizes[0])
        ]

    def fetch(self, refs, buffers, sems, at):
        spans = spans_of(self.rows)
        in_selected, rest = refs[:2], refs[2:]
        n_in, n_out = self.counts
        pack, got, rest = rest[:n_in], rest[n_in : 2 * n_in], rest[2 * n_in :]
        out_selected, out_pack, out_got = rest[0], rest[1 : 1 + n_out], rest[1 + n_out :]

        def rows_of(items, side):
            return items[0].at[spans[side]] if len(items) == 1 else items[side]

        result = []
        for side in (0, 1):
            count = self.rows[side]
            per_side = []
            for kind, (selected, own, other) in enumerate(
                (
                    (in_selected[side], rows_of(pack, side), rows_of(got, side)),
                    (out_selected.at[spans[side]], rows_of(out_pack, side), rows_of(out_got, side)),
                )
            ):
                buffer = buffers[2 * side + kind]
                size = buffer.shape[1] - HALF
                mine = slice(0, count)
                copies = [
                    pltpu.make_async_copy(
                        selected, buffer.at[mine, pl.ds(0, HALF)], sems.at[at]
                    ),
                    pltpu.make_async_copy(
                        own.at[:, pl.ds(HALF, size)], buffer.at[mine, pl.ds(HALF, size)], sems.at[at + 1]
                    ),
                    pltpu.make_async_copy(
                        other, buffer.at[slice(count, 2 * count)], sems.at[at + 2]
                    ),
                ]
                at += 3
                for copy in copies:
                    copy.start()
                per_side.append((buffer, copies))
            result.append(per_side)
        return result, at


class Halves:
    def __init__(self, in_kept, in_gots, out_kept, out_gots):
        self.parts = [*in_kept, *in_gots, *out_kept, *out_gots]
        self.kinds = "w" * len(self.parts)
        self.lead = D
        self.sizes = (out_kept[0].shape[1] - D, in_kept[0].shape[1] - D)
        self.rows = [array.shape[0] for array in in_kept]

    def buffers(self):
        return [
            pltpu.VMEM((2 * rows, D + size), bf16)
            for rows in self.rows
            for size in (self.sizes[1], self.sizes[0])
        ]

    def fetch(self, refs, buffers, sems, at):
        result = []
        for side in (0, 1):
            count = self.rows[side]
            per_side = []
            for kind in (0, 1):
                buffer = buffers[2 * side + kind]
                copies = []
                for part in (0, 1):
                    target = buffer.at[slice(part * count, (part + 1) * count)]
                    source = refs[4 * kind + 2 * part + side]
                    copies.append(pltpu.make_async_copy(source, target, sems.at[at]))
                    copies[-1].start()
                    at += 1
                per_side.append((buffer, copies))
            result.append(per_side)
        return result, at


def chunk_order(groups):
    return [(s, z) for z in range(groups) for s in ((0, 1) if z % 2 == 0 else (1, 0))]


def places_chunks(groups):
    return (D // (2 * groups) // 2) % 16 == 0


def gradients(meta, blocks, cross, groups, name, ties=(), mode="ring"):
    lead = blocks[0].lead
    chunk = lead // groups
    half = chunk // 2
    size = chunk + half if cross else chunk
    order = chunk_order(groups)
    aligned = places_chunks(groups)
    width = sum(sum(block.sizes) for block in blocks)
    every = blocks + ([cross] if cross else [])
    n_in = sum(len(block.parts) for block in every)
    pair = mode == "split"
    n_out = 2 if pair else 1 if aligned else 3 if cross else 2
    n_sems = 12 * len(every) + 4 * len(every)

    def body(flush, meta, *refs):
        inputs, outputs, rest = refs[:n_in], refs[n_in : n_in + n_out], list(refs[n_in + n_out :])
        if cross:
            cross_stage = rest.pop()
        stage, sems = rest.pop(), rest.pop()
        at = 0
        fetched = []
        for block in every:
            taken, inputs = inputs[: len(block.parts)], inputs[len(block.parts) :]
            own, rest = rest[:4], rest[4:]
            copies, at = block.fetch(taken, own, sems, at)
            fetched.append(copies)
        waited, leaving = set(), []

        def leave(source, side, columns, at):
            if pair and not cross:
                kept, sent = (
                    pltpu.make_async_copy(source, target.at[:, columns], sems.at[at])
                    for target in outputs
                )
                pl.when(meta[0] == side)(kept.start)
                pl.when(meta[0] != side)(sent.start)
                leaving.append(kept)
                return
            if not aligned:
                copy = pltpu.make_async_copy(source, outputs[side].at[:, columns], sems.at[at])
                copy.start()
                leaving.append(copy)
                return
            if mode == "ring":
                for k, (s, z) in enumerate(order):
                    if side == 2:
                        start, count, place = (s * groups + z) * half, half, k * size + chunk
                    elif s == side:
                        start, count, place = z * chunk, chunk, k * size
                    else:
                        continue
                    copy = pltpu.make_async_copy(
                        source.at[pl.ds(start, count)],
                        outputs[0].at[pl.ds(place, count), columns],
                        sems.at[at],
                    )
                    copy.start()
                    leaving.append(copy)
                return
            for section in (0, 1) if side == 2 else (side,):
                for z in range(groups):
                    if side == 2:
                        start, count, place = (section * groups + z) * half, half, z * size + chunk
                    else:
                        start, count, place = z * chunk, chunk, z * size
                    kept, sent = (
                        pltpu.make_async_copy(
                            source.at[pl.ds(start, count)],
                            target.at[pl.ds(place, count), columns],
                            sems.at[at],
                        )
                        for target in outputs
                    )
                    pl.when(meta[0] == section)(kept.start)
                    pl.when(meta[0] != section)(sent.start)
                    leaving.append(kept)

        def ready(item):
            buffer, copies = item
            if id(buffer) not in waited:
                waited.add(id(buffer))
                for copy in copies:
                    copy.wait()
            return buffer

        base = 0
        for block, copies in zip(blocks, fetched):
            for side in (0, 1):
                start = base
                for left, right in ((0, 1), (1, 0)):
                    left, right = ready(copies[side][left]), ready(copies[side][right])
                    turned = left[:, :lead].T
                    span = right.shape[1] - lead
                    for step in range(0, span, HALF):
                        value = mm(turned, right[:, lead + step : lead + step + HALF])
                        stage[side, :, start + step : start + step + HALF] = value.astype(bf16)
                    columns = pl.ds(start, span)
                    leave(stage.at[side, :, columns], side, columns, at)
                    at += 1
                    start += span
            base += sum(block.sizes)
        if cross:
            copies = fetched[-1]
            start = 0
            for left, right in ((0, 1), (1, 0)):
                lefts = [ready(copies[side][left])[:, :HALF].T for side in (0, 1)]
                rights = [ready(copies[side][right]) for side in (0, 1)]
                span = rights[0].shape[1] - HALF
                for step in range(0, span, HALF):
                    columns = slice(HALF + step, HALF + step + HALF)
                    value = mm(lefts[0], rights[0][:, columns]) + mm(lefts[1], rights[1][:, columns])
                    cross_stage[:, start + step : start + step + HALF] = value.astype(bf16)
                columns = pl.ds(start, span)
                leave(cross_stage.at[:, columns], 2, columns, at)
                at += 1
                start += span
        for copy in leaving:
            copy.wait()

    ins = [(meta, "s")] + [pair for block in every for pair in zip(block.parts, block.kinds)]
    if pair:
        outs = [((groups * size, width), bf16, "w")] * 2
    elif aligned:
        outs = [((2 * groups * size, width), bf16, "w")]
    else:
        outs = [((lead, width), bf16, "w")] * n_out
    scratch = [buffer for block in every for buffer in block.buffers()]
    if cross:
        scratch += [
            pltpu.SemaphoreType.DMA((n_sems,)),
            pltpu.VMEM((2, lead, width), bf16),
            pltpu.VMEM((HALF, sum(cross.sizes)), bf16),
        ]
    else:
        scratch += [pltpu.SemaphoreType.DMA((n_sems,)), pltpu.VMEM((2, lead, width), bf16)]
    result = call(body, ins, outs, scratch, 6.0, name, ties, 20)
    if pair:
        return result
    if aligned:
        return result[0]
    chunks = [result[side].reshape(groups, chunk, width) for side in (0, 1)]
    pieces = [chunks[s][z] for s, z in order]
    if cross:
        extra = result[2].reshape(2, groups, half, width)
        pieces = [jnp.concatenate([one, extra[s, z]]) for one, (s, z) in zip(pieces, order)]
    return jnp.concatenate(pieces)


def placed_gradients(meta, first, second, chunk, width, units):
    def body(flush, meta, *refs):
        words0, regions0, feed_words, late_words, feed_regions, late_regions = refs[:6]
        feed_in, feed_out, att_in, att_out, cross_in, cross_out = refs[6:]
        for item in refs[:6]:
            item.wait()

        def store(side, feed, late, base):
            feed_in[side] = feed[:, :units].astype(f32)
            feed_out[side] = feed[:, units : 2 * units].astype(f32)
            for j in range(3):
                start = base + j * width
                att_in[side, j] = late[:chunk, start : start + width].astype(f32)
            att_out[side] = late[:chunk, base + 3 * width : base + 4 * width].astype(f32)

        @pl.when(meta[0] == 0)
        def _():
            store(0, words0, words0, 2 * units)
            store(1, regions0, regions0, 2 * units)

        @pl.when(meta[0] != 0)
        def _():
            store(0, feed_words, late_words, 0)
            store(1, feed_regions, late_regions, 0)

        for j in range(3):
            cross_in[j] = late_regions[chunk:, j * width : (j + 1) * width].astype(f32)
        cross_out[...] = late_regions[chunk:, 3 * width :].astype(f32)

    ins = [(meta, "s")] + [(item, "h") for item in (*first, *second)]
    half = chunk // 2
    outs = [
        ((2, chunk, units), f32, "h"),
        ((2, chunk, units), f32, "h"),
        ((2, 3, chunk, width), f32, "h"),
        ((2, chunk, width), f32, "h"),
        ((3, half, width), f32, "h"),
        ((half, width), f32, "h"),
    ]
    return call(body, ins, outs, (), 4.0, "placed_gradients")


def prepared(ids, lengths, att_bias, att_post, feed_bias, feed_post):
    batch = lengths[0].shape[1]
    n_feed = feed_bias.shape[2] // D
    n_ids = ids.shape[0]

    def body(flush, ids, words, regions, att_bias, att_post, feed_bias, feed_post, small, meta):
        meta[0] = ids[0]
        for i in range(1, n_ids):
            meta[2 * batch + i] = ids[i]
        for side, counts in enumerate((words, regions)):
            for i in range(batch):
                meta[1 + side * batch + i] = counts[ids[0], i]
        half = att_bias.shape[3]
        for side in (0, 1):
            for j in (0, 1):
                small[side, ROW_ATT_BIAS : ROW_ATT_BIAS + 1, j * half : (j + 1) * half] = att_bias[
                    0, side, j : j + 1
                ]
            for j in range(3):
                for row, post in ((ROW_ATT_POST, att_post), (ROW_FEED_POST, feed_post)):
                    small[side, row + j : row + j + 1] = post[0, j, side : side + 1]
            for j in range(n_feed):
                row = ROW_FEED_BIAS + j
                small[side, row : row + 1] = feed_bias[0, side : side + 1, j * D : (j + 1) * D]
            end = ROW_FEED_POST + 3
            small[side, end:] = jnp.zeros((SMALL_ROWS - end, D), f32)

    ins = [(ids, "s"), (lengths[0], "s"), (lengths[1], "s")]
    ins += [(item, "h") for item in (att_bias, att_post, feed_bias, feed_post)]
    outs = [((2, SMALL_ROWS, D), f32, "h"), ((n_ids + 2 * batch,), jnp.int32, "s")]
    return call(body, ins, outs, (), 1.0, "prepared")


def swap(value, axis, distance=1):
    count = lax.axis_size(axis)
    return lax.ppermute(value, axis, [(i, i ^ distance) for i in range(count)])


def total_of(parts):
    return sum(part.astype(f32) for part in parts).astype(bf16)


def behind(values, after):
    return lax.optimization_barrier((values, after))[0] if after else values


def on_device(
    word_state,
    region_state,
    word_lengths,
    region_counts,
    word_cotangent,
    region_cotangent,
    cross_in,
    cross_bias,
    cross_out,
    cross_post,
    attention_in,
    attention_bias,
    attention_out,
    attention_post,
    feed_in,
    feed_bias,
    feed_out,
    feed_post,
):
    section = lax.axis_index("section")
    dp_count = lax.axis_size("dp")
    groups = dp_count // 2
    place = lax.axis_index("dp") % 2
    batch = word_state.shape[1]
    width = cross_out.shape[0]
    units = feed_in.shape[-1]
    both = (0, 1)
    chains = [[s * dp_count + 2 * z + y for s, z in chunk_order(groups)] for y in both]

    def unflat(value):
        return value.reshape(-1, batch, D).transpose(1, 0, 2)[None]

    def chooser_of(pieces, per_section):
        column = jnp.arange(D)
        half = column // HALF
        inner = column % HALF
        side = jnp.where(half == 0, place, 1 - place)
        size = D // pieces
        if per_section:
            block = inner // (HALF // 2)
            inner = inner % (HALF // 2)
            feature = size * (dp_count * block + 2 * (inner // size) + side) + inner % size
        else:
            feature = size * (2 * (inner // size) + side) + inner % size
        return (jnp.arange(D)[:, None] == feature[None, :]).astype(bf16)

    chooser = chooser_of(dp_count, False)
    cross_chooser = chooser_of(2 * dp_count, True)

    ids = jnp.stack([section, place]).astype(jnp.int32)
    small_own, meta = prepared(
        ids,
        (word_lengths, region_counts),
        attention_bias,
        attention_post.transpose(0, 2, 1, 3),
        feed_bias,
        feed_post.transpose(0, 2, 1, 3),
    )
    small = (small_own, swap(small_own, "section"))
    att_in_own = attention_in.transpose(0, 1, 3, 2, 4)
    att_in = (att_in_own, swap(att_in_own, "section"))
    att_out = (attention_out, swap(attention_out, "section"))
    states = [value.transpose(0, 2, 1, 3) for value in (word_state, region_state)]
    feed_in_later, feed_out_later, *_ = lax.optimization_barrier(
        (feed_in, feed_out, att_in[1], att_out[1], small[1], chooser, cross_chooser)
    )
    ff_in = (feed_in, swap(feed_in_later, "section"))
    ff_out = (feed_out, swap(feed_out_later, "section"))
    cross_entry = cross_in.transpose(1, 0, 2)

    cotangents = [value.transpose(0, 2, 1, 3) for value in (word_cotangent, region_cotangent)]
    rows = [state.shape[1] * batch for state in states]
    total_rows = sum(rows)

    def in_order(step, pack_index, tie=None, joined=True, order=(1, 0)):
        results = [None, None]
        given = None
        for side in order:
            ties = () if tie is None else (tie,)
            place = (total_rows, rows[0] * side, given) if joined else ()
            results[side] = step(side, place, ties)
            tie, given = results[side][pack_index + 2], results[side][pack_index]
        return results

    def over_mp(results, index):
        return [swap(results[side][index], "mp") for side in both]

    self0 = in_order(
        lambda side, place, ties: self_forward(
            side, 0, batch, meta, states[side], None, small, chooser, att_in, att_out,
            place, ties,
        ),
        3,
    )
    got = over_mp(self0, 4)
    feed0 = in_order(
        lambda side, place, ties: feed_forward(
            side, 0, batch, meta, self0[side][6], self0[side][4], got[side], small, chooser,
            ff_in, ff_out, place, ties,
        ),
        4,
        self0[0][5],
    )
    got = over_mp(feed0, 6)
    self0_there = swap(self0[0][3], "dp")
    cross_w, cross_r, cross_pack, held = cross_forward(
        batch,
        meta,
        [(feed0[side][0], feed0[side][6], got[side]) for side in both],
        small,
        cross_chooser,
        cross_entry,
        cross_bias,
        cross_out,
        (att_in, att_out, ff_in),
    )
    att_in1, att_out1, ff_in1 = [(item,) for item in held]
    cross = (cross_w, cross_r)
    got = over_mp(cross, 7)
    feed0_there = swap(feed0[0][4], "dp")
    self1 = in_order(
        lambda side, place, ties: self_forward(
            side, 1, batch, meta, cross[side][0], (cross[side][7], got[side], cross_post),
            small, chooser, att_in1, att_out1, place, ties + ((self0_there, "a"),),
            (ff_out,) if side == ORDER[0] else (),
        ),
        3,
        None,
        True,
        ORDER,
    )
    ff_out1 = (self1[ORDER[0]][9],)
    got = over_mp(self1, 4)
    cross_there = swap(cross_pack, "dp")
    feed1 = in_order(
        lambda side, place, ties: feed_forward(
            side, 1, batch, meta, self1[side][6], self1[side][4], got[side], small, chooser,
            ff_in1, ff_out1, place, ties + (((feed0_there, "a"),) if side == ORDER[0] else ()),
        ),
        4,
        self1[ORDER[-1]][5],
        False,
        ORDER,
    )
    got = over_mp(feed1, 6)
    self1_there = swap(self1[ORDER[-1]][3], "dp")
    feed1_there = [swap(feed1[side][4], "dp") for side in both]

    def over_sections_and_groups(value):
        return lax.psum_scatter(
            value, ("section", "dp"), scatter_dimension=0, axis_index_groups=chains, tiled=True
        )

    def over_groups(value):
        pairs = [[2 * z + y for z in range(groups)] for y in both]
        return lax.psum_scatter(
            value, "dp", scatter_dimension=0, axis_index_groups=pairs, tiled=True
        )

    given, back_feed1 = None, [None, None]
    for side in ORDER:
        given = feed_backward(
            1,
            (side,),
            rows,
            batch,
            meta,
            [(feed1[side][0], feed1[side][6], got[side], cotangents[side])],
            None,
            small,
            chooser,
            [feed1[side][5]],
            ff_in1,
            ff_out1,
            ((feed1_there[side], "a"), (cross_there, "a")) if side == ORDER[0] else (),
            given,
        )
        back_feed1[side] = given
    got = over_mp(back_feed1, 3)
    back_feed1_there = [swap(back_feed1[side][2], "dp") for side in both]

    given, back_self1 = None, [None, None]
    for side in ORDER:
        given = self_backward(
            1,
            (side,),
            rows,
            meta,
            [feed1[side][1:3]],
            (back_feed1[side][0], back_feed1[side][3], got[side]),
            small,
            chooser,
            [self1[side][0]],
            [self1[side][1]],
            att_in1,
            att_out1,
            (
                ((feed1_there[ORDER[-1]], "a"), (back_feed1_there[ORDER[0]], "a"))
                if side == ORDER[0]
                else ()
            ),
            given,
        )
        back_self1[side] = given
    got = over_mp(back_self1, 3)
    feed1_grads = gradients(
        meta,
        [
            Halves(
                [feed1[side][3] for side in both],
                feed1_there,
                [back_feed1[side][1] for side in both],
                back_feed1_there,
            )
        ],
        None,
        groups,
        "feed_gradients_1",
        (back_self1[ORDER[-1]][5],),
    )
    feed1_pair = over_sections_and_groups(feed1_grads).reshape(2, D // dp_count, -1)
    back_self1_there = swap(back_self1[ORDER[-1]][2], "dp")
    back_cross = cross_backward(
        meta,
        [self1[side][7:9] for side in both],
        [back_self1[side][0] for side in both],
        [back_self1[side][3] for side in both],
        got,
        cross_post,
        cross_chooser,
        [cross[side][5] for side in both],
        [cross[side][6] for side in both],
        cross_entry,
        cross_out,
        (feed1_grads,),
    )
    cross_post_grad, cross_bias_grad = back_cross[4:6]
    got = swap(back_cross[3], "mp")
    back_cross_there = swap(back_cross[2], "dp")
    feed1_own = lax.dynamic_index_in_dim(feed1_pair, place, 0, keepdims=False)
    feed1_other = swap(lax.dynamic_index_in_dim(feed1_pair, 1 - place, 0, keepdims=False), "dp")
    halves = (
        jnp.where(place == 0, feed1_own, feed1_other),
        jnp.where(place == 0, feed1_other, feed1_own),
    )
    count = units // 2
    feed1_share = jnp.concatenate(
        [half[:, j * count : (j + 1) * count] for j in both for half in halves], axis=1
    )

    back_feed0 = feed_backward(
        0,
        (1, 0),
        rows,
        batch,
        meta,
        [cross[side][1:3] for side in (1, 0)],
        (back_cross[0], back_cross[3], got),
        small,
        chooser,
        [feed0[side][5] for side in (1, 0)],
        ff_in,
        ff_out,
        ((back_self1_there, "a"),),
    )
    got = swap(back_feed0[3], "mp")
    back_feed0_there = swap(back_feed0[2], "dp")
    late1_grads = gradients(
        meta,
        [
            Block(
                [self1[side][2] for side in both],
                [self1[ORDER[-1]][3]],
                [self1_there],
                back_self1[ORDER[-1]][1],
                [back_self1[ORDER[-1]][2]],
                [back_self1_there],
            )
        ],
        Block(
            [cross[side][4] for side in both],
            [cross_pack],
            [cross_there],
            back_cross[1],
            [back_cross[2]],
            [back_cross_there],
        ),
        groups,
        "late_gradients_1",
        (back_feed0[5],),
    )
    late1_share = over_sections_and_groups(late1_grads)
    back_self0 = self_backward(
        0,
        (1, 0),
        rows,
        meta,
        [feed0[side][1:3] for side in (1, 0)],
        (back_feed0[0], back_feed0[3], got),
        small,
        chooser,
        [self0[side][0] for side in (1, 0)],
        [self0[side][1] for side in (1, 0)],
        att_in,
        att_out,
        (late1_grads,),
    )
    got = swap(back_self0[3], "mp")
    back_self0_there = swap(back_self0[2], "dp")
    feed0_grads = gradients(
        meta,
        [
            Block(
                [feed0[side][3] for side in both],
                [feed0[0][4]],
                [feed0_there],
                back_feed0[1],
                [back_feed0[2]],
                [back_feed0_there],
            )
        ],
        None,
        groups,
        "feed_gradients_0",
        (back_self0[5], feed1_pair),
        "split",
    )
    self0_grads = gradients(
        meta,
        [
            Block(
                [self0[side][2] for side in both],
                [self0[0][3]],
                [self0_there],
                back_self0[1],
                [back_self0[2]],
                [back_self0_there],
            )
        ],
        None,
        groups,
        "self_gradients_0",
        (feed0_grads[0],),
        "split",
    )
    layer0_total = jnp.concatenate(
        [
            kept.astype(f32) + swap(sent, "section").astype(f32)
            for kept, sent in (feed0_grads, self0_grads)
        ],
        axis=1,
    ).astype(bf16)
    layer0_total, late1_share = lax.optimization_barrier((layer0_total, late1_share))
    layer0_share = over_groups(layer0_total)
    chunk = D // dp_count
    left = dict(
        self0=back_self0[4:6],
        feed0=back_feed0[4:6],
        self1=back_self1[ORDER[-1]][4:6],
        feed1=back_feed1[ORDER[-1]][4:7],
        squares=[
            [self0[side][5] for side in both],
            [feed0[side][7] for side in both],
            [cross[side][3] for side in both],
            [self1[side][5] for side in both],
            [feed1[side][7] for side in both],
        ],
        cross=(cross_post_grad, cross_bias_grad),
        results=[back_feed1[side][7] for side in both],
        back=(back_self0[0], back_self0[3], got),
    )
    left = behind(left, (layer0_total,))
    cross_post_grad, cross_bias_grad = left["cross"]
    grad, part, got = left["back"]

    state_grad = (grad + (part.astype(f32) + got.astype(f32))).astype(bf16)
    spans = spans_of(rows)

    def packed(back_self, back_feed, squares):
        rows = [
            back_self[1].reshape(2, D),
            back_self[0].reshape(6, D),
            back_feed[1].reshape(-1, D),
            back_feed[0].reshape(6, D),
        ]
        row = jnp.concatenate([value.reshape(1, 128) for value in squares[:6]], axis=1)
        rest = jnp.concatenate([value.reshape(1, 128) for value in squares[6:]], axis=1)
        rest = jnp.concatenate([rest, jnp.zeros((1, D - rest.shape[1]), f32)], axis=1)
        return jnp.concatenate(rows + [row, rest], axis=0)

    def squares_of(lead, second, tail):
        result = []
        for side in both:
            result += [lead[side], second[side], tail[side][0:1], tail[side][1:2]]
        return result

    squares = left["squares"]
    packs = [
        packed(left["self0"], left["feed0"], squares_of(*squares[:3])),
        packed(left["self1"], left["feed1"], squares_of(*squares[3:], left["feed1"][2])),
    ]
    counts = jnp.stack([jnp.sum(word_lengths), jnp.sum(region_counts)]).astype(f32)
    counts = jnp.pad(counts, (0, D - 2))[None] * 0.5
    mine = jnp.where(section == 0, packs[0], packs[1])
    theirs = jnp.where(section == 0, packs[1], packs[0])
    shared = [cross_post_grad, cross_bias_grad.reshape(1, D), counts]
    small_rows = packs[0].shape[0]
    total = jnp.concatenate([mine] + shared, axis=0) + swap(
        jnp.concatenate([theirs] + shared, axis=0), "section"
    )
    distance = 1
    while distance < dp_count:
        total = total + swap(total, "dp", distance)
        distance *= 2
    unit_rows = units // D
    at = 0
    att_bias_grad = total[0:2].reshape(1, 2, 2, width)
    at = 2
    att_post_grad = total[at : at + 6].reshape(1, 2, 3, D)
    at += 6
    feed_bias_grad = total[at : at + 2 * unit_rows].reshape(1, 2, units)
    at += 2 * unit_rows
    feed_post_grad = total[at : at + 6].reshape(1, 2, 3, D)
    at += 6
    squares = total[at : at + 2].reshape(-1, 128)[:8, 0]
    at = small_rows
    cross_post_total = total[at : at + 3]
    cross_bias_total = total[at + 3].reshape(2, width)
    valid_counts = total[at + 4, :2]
    scales = jnp.sqrt(squares / (jnp.repeat(valid_counts, 4) * D))[None]

    outputs = (
        unflat(left["results"][0]),
        unflat(left["results"][1]),
        unflat(state_grad[spans[0]]),
        unflat(state_grad[spans[1]]),
        cross_bias_total,
        cross_post_total,
        att_bias_grad,
        att_post_grad,
        feed_bias_grad,
        feed_post_grad,
        scales,
    )
    late_words = [
        lax.ppermute(value, "section", [(0, 1)]) for value in (feed1_share, late1_share[:chunk])
    ]
    layer0_share, late_words, outputs = behind((layer0_share, late_words, outputs), (late1_share,))
    late_regions = lax.ppermute(layer0_share, "section", [(1, 0)])
    feed_in_grad, feed_out_grad, att_in_grad, att_out_grad, cross_in_grad, cross_out_grad = (
        placed_gradients(
            meta,
            (layer0_share, late_regions),
            (*late_words, feed1_share, late1_share),
            chunk,
            width,
            units,
        )
    )
    feed_in_grad = feed_in_grad[None]
    feed_out_grad = feed_out_grad.transpose(0, 2, 1)[None]
    att_in_grad = att_in_grad.transpose(0, 2, 1, 3)[None]
    att_out_grad = att_out_grad.transpose(0, 2, 1)[None]
    cross_in_grad = cross_in_grad.transpose(1, 0, 2)
    cross_out_grad = cross_out_grad.T
    return (
        *outputs[:4],
        cross_in_grad,
        outputs[4],
        cross_out_grad,
        outputs[5],
        att_in_grad,
        outputs[6],
        att_out_grad,
        outputs[7],
        feed_in_grad,
        outputs[8],
        feed_out_grad,
        outputs[9],
        outputs[10],
    )


def solution(mesh):
    placed = (
        P(None, "dp", None, None),
        P(None, "dp", None, None),
        P(None, "dp"),
        P(None, "dp"),
        P(None, "dp", None, None),
        P(None, "dp", None, None),
        P(None, None, "mp"),
        P(None, "mp"),
        P("mp", None),
        P(),
        P("section", None, None, None, "mp"),
        P("section", None, None, "mp"),
        P("section", None, "mp", None),
        P("section", None, None, None),
        P("section", None, None, "mp"),
        P("section", None, "mp"),
        P("section", None, "mp", None),
        P("section", None, None, None),
    )
    return jax.shard_map(
        on_device,
        mesh=mesh,
        in_specs=placed,
        out_specs=(
            P("section", "dp", None, None),
            P("section", "dp", None, None),
            P("section", "dp", None, None),
            P("section", "dp", None, None),
            P(("section", "dp"), None, "mp"),
            P(None, "mp"),
            P("mp", ("section", "dp")),
            P(),
            P("section", None, "dp", None, "mp"),
            P("section", None, None, "mp"),
            P("section", None, "mp", "dp"),
            P("section", None, None, None),
            P("section", None, "dp", "mp"),
            P("section", None, "mp"),
            P("section", None, "mp", "dp"),
            P("section", None, None, None),
            P("section", None),
        ),
        check_vma=False,
    )
```

```python
from functools import partial

import jax
import jax.numpy as jnp
from jax import lax
from jax.experimental import pallas as pl
from jax.experimental.pallas import tpu as pltpu
from jax.sharding import PartitionSpec as P

D = 768
HALF = D // 2
HEAD_DIM = 64
PAIR = 2 * HEAD_DIM
WORDS = 20
REGIONS = 36
EPS = 1e-06
SCALE = HEAD_DIM**-0.5
COST_SCALE = 0.5
ORDER = (0, 1)
bf16 = jnp.bfloat16
f32 = jnp.float32

ROW_ATT_BIAS, ROW_ATT_POST, ROW_FEED_BIAS, ROW_FEED_POST, SMALL_ROWS = 0, 1, 4, 6, 16


def mm(a, b):
    return jnp.dot(a, b, preferred_element_type=f32)


def mm_nt(a, b):
    return lax.dot_general(a, b, (((1,), (1,)), ((), ())), preferred_element_type=f32)


def mm_tn(a, b):
    return lax.dot_general(a, b, (((0,), (0,)), ((), ())), preferred_element_type=f32)


def norm_of(value, gain, shift):
    centred = value - jnp.mean(value, axis=-1, keepdims=True)
    spread = jnp.mean(centred * centred, axis=-1, keepdims=True)
    rstd = lax.rsqrt(spread + EPS)
    unit = centred * rstd
    return unit, rstd, unit * gain + shift


def norm_back(unit, rstd, gain, incoming):
    scaled = incoming * gain
    mean = jnp.mean(scaled, axis=-1, keepdims=True)
    along = jnp.mean(scaled * unit, axis=-1, keepdims=True)
    return (scaled - mean - unit * along) * rstd


def summed(own, other):
    return own[...].astype(f32) + other[...].astype(f32)


def column_sum(value):
    return jnp.sum(value, axis=0, keepdims=True)


def square_sum(value, valid):
    rows = jnp.sum(value * value, axis=-1, keepdims=True) * valid
    return jnp.broadcast_to(jnp.sum(rows, axis=0, keepdims=True), (1, 128))


def lengths_of(meta, side, batch, item):
    result = jnp.zeros_like(item)
    for i in range(batch):
        result = jnp.where(item == i, meta[1 + side * batch + i], result)
    return result


def row_valid(meta, side, batch, rows):
    index = lax.broadcasted_iota(jnp.int32, (rows, 1), 0)
    length = lengths_of(meta, side, batch, lax.rem(index, batch))
    return (lax.div(index, batch) < length).astype(f32)


def pair_valid(meta, side, batch, rows, keys):
    index = lax.broadcasted_iota(jnp.int32, (1, keys), 1)
    item = lax.rem(index, batch)
    length = lengths_of(meta, side, batch, item)
    item = jnp.where(lax.div(index, batch) < length, item, -1)
    row_item = lax.rem(lax.broadcasted_iota(jnp.int32, (rows, 1), 0), batch)
    return jnp.broadcast_to(row_item, (rows, keys)) == jnp.broadcast_to(item, (rows, keys))


def head_lanes(head):
    lane = lax.broadcasted_iota(jnp.int32, (1, PAIR), 1)
    return (lane // HEAD_DIM) == head


def attend(query, keys, values, valid, probs_ref, context_ref):
    for pair in range(query.shape[1] // PAIR):
        lanes = slice(pair * PAIR, (pair + 1) * PAIR)
        contexts = []
        for head in range(2):
            chosen = query[:, lanes] * head_lanes(head).astype(bf16)
            scores = mm_nt(chosen, keys[:, lanes]) * SCALE
            scores = jnp.where(valid, scores, -1e9)
            shifted = jnp.exp(scores - jnp.max(scores, axis=-1, keepdims=True))
            total = jnp.sum(shifted, axis=-1, keepdims=True)
            probs = (shifted * (1.0 / total)).astype(bf16)
            probs_ref[2 * pair + head] = probs
            contexts.append(mm(probs, values[:, lanes]))
        context_ref[:, lanes] = jnp.where(head_lanes(0), contexts[0], contexts[1]).astype(bf16)


def attend_back(query, keys, values, probs_ref, grad_context, emit):
    first = head_lanes(0)
    for pair in range(query.shape[1] // PAIR):
        lanes = slice(pair * PAIR, (pair + 1) * PAIR)
        grads = ([], [], [])
        for head in range(2):
            probs = probs_ref[2 * pair + head]
            chosen = grad_context[:, lanes] * head_lanes(head).astype(bf16)
            grad_probs = mm_nt(chosen, values[:, lanes])
            wide = probs.astype(f32)
            product = wide * grad_probs
            grad_scores = product - wide * jnp.sum(product, axis=-1, keepdims=True)
            grad_scores = grad_scores.astype(bf16)
            grads[0].append(mm(grad_scores, keys[:, lanes]) * SCALE)
            grads[1].append(mm_tn(grad_scores, query[:, lanes]) * SCALE)
            grads[2].append(mm_tn(probs, grad_context[:, lanes]))
        for kind in range(3):
            emit(kind, lanes, jnp.where(first, grads[kind][0], grads[kind][1]).astype(bf16))


def small_of(meta, layer, side, own, other):
    return jnp.where(meta[0] == layer, own[side], other[side])


class Fetched:
    def __init__(self, copy, buffer):
        self.copy, self.buffer, self.waited = copy, buffer, False
        self.shape, self.dtype = buffer.shape, buffer.dtype

    def wait(self):
        if not self.waited:
            self.copy.wait()
            self.waited = True
        return self.buffer

    def __getitem__(self, index):
        return self.wait()[index]


class Weights:
    def __init__(self, meta, layer, pairs, buffers, sems):
        self.copies = []
        mine = meta[0] == layer
        at = 0
        for (own, other, pieces), buffer in zip(pairs, buffers):
            copies = []
            for piece in pieces:
                copy = pltpu.make_async_copy(own.at[piece], buffer.at[piece], sems.at[at])
                if other is None:
                    copy.start()
                else:
                    second = pltpu.make_async_copy(
                        other.at[piece], buffer.at[piece], sems.at[at]
                    )
                    pl.when(mine)(copy.start)
                    pl.when(jnp.logical_not(mine))(second.start)
                copies.append(Fetched(copy, buffer))
                at += 1
            self.copies.append(copies)

    def get(self, slot, piece=None):
        copies = self.copies[slot]
        for copy in copies if piece is None else (copies[piece],):
            copy.wait()
        return copies[0].buffer


class Held:
    def __init__(self, *refs):
        self.refs = refs

    def get(self, slot, piece=None):
        return self.refs[slot]


def weight_inputs(entry, leave, kinds="wwww"):
    if len(entry) == 1:
        return [(entry[0], "v"), (leave[0], "v")]
    return list(zip(entry + leave, kinds))


def pass_on(meta, layer, offered, taken, sems):
    copies = []
    for i, target in enumerate(taken):
        own = pltpu.make_async_copy(offered[2 * i].at[0], target, sems.at[i])
        other = pltpu.make_async_copy(offered[2 * i + 1].at[0], target, sems.at[i])
        pl.when(meta[0] == layer)(own.start)
        pl.when(meta[0] != layer)(other.start)
        copies.append(own)
    return copies


def items_of(meta, source, raw, rows_ref, sem, batch):
    copy = pltpu.make_async_copy(source.at[meta[0]], raw, sem)
    copy.start()
    copy.wait()
    for slot in range(raw.shape[0]):
        rows_ref[slot * batch : (slot + 1) * batch] = raw[slot].astype(f32)


def maps(own, other, side, pieces=((),)):
    if other is None:
        return own, None, pieces
    return own.at[0, side], other.at[0, side], pieces


ENTRY = ((0,), (1,), (2,))


def column_pieces(size, count):
    return tuple(
        (slice(None), slice(i * size // count, (i + 1) * size // count)) for i in range(count)
    )


def row_pieces(size, count):
    return tuple((slice(i * size // count, (i + 1) * size // count),) for i in range(count))


def call(body, ins, outs, scratch=(), cost=0.0, name=None, ties=(), mib=14):
    spaces = {
        "s": pltpu.SMEM, "v": pltpu.VMEM, "w": pltpu.HBM, "h": pltpu.HBM, "a": pl.ANY, "f": pl.ANY
    }
    ties = [tie if isinstance(tie, tuple) else (tie, "w") for tie in ties]
    extra = [(i, out[5]) for i, out in enumerate(outs) if len(out) > 3 and out[5] is not None]
    aliases = {len(ins) + at: i for at, (i, _) in enumerate(extra)}
    ins = list(ins) + [(array, "w") for _, array in extra]
    places = [out[3:5] if len(out) > 3 else None for out in outs]
    fetched = [i for i, (_, kind) in enumerate(ins) if kind in "hf"]
    written = [i for i, out in enumerate(outs) if out[2] == "h"]
    n_ins, n_ties, n_outs, n_scratch = len(ins), len(ties), len(outs), len(scratch)

    def whole(*refs):
        given = list(refs[:n_ins])
        results = list(refs[n_ins + n_ties : n_ins + n_ties + n_outs])
        rest = refs[n_ins + n_ties + n_outs :]
        own, rest = rest[:n_scratch], rest[n_scratch:]
        buffers, rest = rest[: len(fetched)], rest[len(fetched) :]
        staged, rest = rest[: len(written)], rest[len(written) :]
        sems = rest[0] if rest else None
        for slot, i in enumerate(fetched):
            copy = pltpu.make_async_copy(given[i], buffers[slot], sems.at[slot])
            copy.start()
            given[i] = Fetched(copy, buffers[slot])
        leaving = {}
        for slot, i in enumerate(written):
            target = results[i]
            if places[i] is not None:
                target = target.at[pl.ds(places[i][1], staged[slot].shape[0])]
            copy = pltpu.make_async_copy(staged[slot], target, sems.at[len(fetched) + slot])
            leaving[id(staged[slot])] = copy
            results[i] = staged[slot]
        started = []

        def flush(*done):
            for ref in done:
                copy = leaving.pop(id(ref), None)
                if copy is not None:
                    copy.start()
                    started.append(copy)

        body(flush, *given[: n_ins - len(extra)], *results, *own)
        flush(*[staged[slot] for slot in range(len(written))])
        for copy in started:
            copy.wait()
        for item in given:
            if isinstance(item, Fetched):
                item.wait()

    arrays = [
        pltpu.with_memory_space_constraint(array, spaces[kind]) if kind in "vwh" else array
        for array, kind in [*ins, *ties]
    ]
    own_scratch = list(scratch)
    own_scratch += [pltpu.VMEM(arrays[i].shape, arrays[i].dtype) for i in fetched]
    own_scratch += [pltpu.VMEM(outs[i][0], outs[i][1]) for i in written]
    if fetched or written:
        own_scratch.append(pltpu.SemaphoreType.DMA((len(fetched) + len(written),)))
    return pl.pallas_call(
        whole,
        out_shape=[
            spaces[out[2]]((out[3], *out[0][1:]) if len(out) > 3 else out[0], out[1]) for out in outs
        ],
        in_specs=[pl.BlockSpec(memory_space=spaces[kind]) for _, kind in [*ins, *ties]],
        out_specs=[pl.BlockSpec(memory_space=spaces[out[2]]) for out in outs],
        input_output_aliases=aliases,
        scratch_shapes=own_scratch,
        compiler_params=pltpu.CompilerParams(vmem_limit_bytes=mib * 1024 * 1024),
        cost_estimate=pl.CostEstimate(
            flops=int(cost * COST_SCALE * 1.15e9), bytes_accessed=0, transcendentals=0
        ),
        name=name,
    )(*arrays)


def spans_of(rows):
    return slice(0, rows[0]), slice(rows[0], rows[0] + rows[1])


def select_rows(value, chooser, own_ref, pack_ref):
    moved = mm(value, chooser[...]).astype(bf16)
    own_ref[...] = moved[:, :HALF]
    pack_ref[:, :HALF] = moved[:, HALF:]


def project(low, weights, bias_q, bias_v, qkv_ref):
    qkv_ref[0] = (mm(low, weights.get(0, 0)[0]) + bias_q).astype(bf16)
    qkv_ref[1] = mm(low, weights.get(0, 1)[1]).astype(bf16)
    qkv_ref[2] = (mm(low, weights.get(0, 2)[2]) + bias_v).astype(bf16)


def self_forward(
    side, layer, batch, meta, state, prior, small, chooser, att_in, att_out, place, ties=(), later=()
):
    rows = state.shape[1] * batch if prior is None else state.shape[0]
    width = att_in[0].shape[-1]
    first = prior is None
    held, n_maps = len(att_in) == 1, len(att_in + att_out)

    def body(flush, meta, state, *refs):
        refs = list(refs)
        if not first:
            own, other, post = refs[:3]
            refs = refs[3:]
        small = small_of(meta, layer, side, refs[0], refs[1])
        chooser, refs = refs[2], refs[3:]
        given, refs = refs[:n_maps], refs[n_maps:]
        offered, refs = refs[: 2 * len(later)], refs[2 * len(later) :]
        qkv, probs, selected, pack, part, squares = refs[:6]
        refs = refs[6:]
        if not first:
            mixed_ref, unit_ref, rstd_ref = refs[:3]
            taken, refs = refs[3 : 3 + len(later)], refs[3 + len(later) :]
            passing = pass_on(meta, layer, offered, taken, refs[-1]) if later else []
        else:
            low_ref, refs = refs[0], refs[1:]
            raw, rows_ref, raw_sem = refs[-3:]
            refs = refs[:-3]
        if held:
            weights = Held(given[0].at[side], given[1].at[side])
        else:
            in_buffer, out_buffer, sems = refs
            weights = Weights(
                meta,
                layer,
                (maps(*given[:2], side, ENTRY), maps(*given[2:], side)),
                (in_buffer, out_buffer),
                sems,
            )
        valid = row_valid(meta, side, batch, rows)
        if first:
            items_of(meta, state, raw, rows_ref, raw_sem, batch)
            squares[...] = square_sum(rows_ref[...], valid)
            low = rows_ref[...].astype(bf16)
            low_ref[...] = low
        else:
            branch = summed(own, other) + post[0:1]
            squares[...] = square_sum(branch, valid)
            unit, rstd, mixed = norm_of(state[...].astype(f32) + branch, post[1:2], post[2:3])
            unit_ref[...] = unit
            rstd_ref[...] = rstd
            mixed_ref[...] = mixed
            low = mixed.astype(bf16)
        select_rows(low, chooser, selected, pack)
        flush(selected)
        biases = small[ROW_ATT_BIAS : ROW_ATT_BIAS + 1]
        project(low, weights, biases[:, :width], biases[:, width : 2 * width], qkv)
        context = pack.at[:, HALF:]
        attend(
            qkv[0], qkv[1], qkv[2], pair_valid(meta, side, batch, rows, rows), probs, context
        )
        flush(qkv, probs, pack)
        part[...] = mm(context[...], weights.get(1)[...]).astype(bf16)
        if not first:
            for copy in passing:
                copy.wait()

    ins = [(meta, "s"), (state, "w" if first else "v")]
    if not first:
        ins += list(zip(prior, "vvv"))
    ins += [(item, "v") for item in (*small, chooser)]
    ins += weight_inputs(att_in, att_out, "wawa")
    ins += [(item, "w") for pair in later for item in pair]
    outs = [
        ((3, rows, width), bf16, "h"),
        ((width // HEAD_DIM, rows, rows), bf16, "h"),
        ((rows, HALF), bf16, "h"),
        ((rows, HALF + width), bf16, "h", *place),
        ((rows, D), bf16, "v"),
        ((1, 128), f32, "h"),
    ]
    if not first:
        outs += [((rows, D), f32, "v"), ((rows, D), f32, "h"), ((rows, 1), f32, "h")]
        outs += [(pair[0].shape[1:], bf16, "v") for pair in later]
    else:
        outs.append(((rows, D), bf16, "v"))
    scratch = [
        pltpu.VMEM((3, D, width), bf16),
        pltpu.VMEM((width, D), bf16),
        pltpu.SemaphoreType.DMA((6,)),
    ]
    scratch = [] if held else scratch
    if first:
        scratch += [
            pltpu.VMEM(state.shape[1:], bf16),
            pltpu.VMEM((rows, D), f32),
            pltpu.SemaphoreType.DMA,
        ]
    if later:
        scratch.append(pltpu.SemaphoreType.DMA((len(later),)))
    return call(body, ins, outs, scratch, 4.0, f"self_forward_{layer}_{side}", ties, 12)


def hand_over(low_ref, kept, sent, sems):
    copies = []
    for slot, target in enumerate((kept, sent)):
        copies.append(
            pltpu.make_async_copy(low_ref, target.at[:, pl.ds(0, D)], sems.at[slot])
        )
        copies[-1].start()
    return copies


def hand_halves(meta, batch, wide_ref, kept, sent, sems):
    count = wide_ref.shape[1] // 2
    copies = []
    for half in (0, 1):
        source = wide_ref.at[:, pl.ds(half * count, count)]
        to_kept, to_sent = (
            pltpu.make_async_copy(source, target.at[:, pl.ds(D, count)], sems.at[2 + half])
            for target in (kept, sent)
        )
        mine = meta[1 + 2 * batch] == half
        pl.when(mine)(to_kept.start)
        pl.when(jnp.logical_not(mine))(to_sent.start)
        copies.append(to_kept)
    return copies


def hand_scratch(rows, units):
    return [
        pltpu.VMEM((rows, D), bf16),
        pltpu.VMEM((rows, units), bf16),
        pltpu.SemaphoreType.DMA((4,)),
    ]


def feed_forward(
    side, layer, batch, meta, residual, own, other, small, chooser, feed_in, feed_out, place, ties=()
):
    rows = residual.shape[0]
    units = feed_in[0].shape[-1]
    step = units // 4

    held, n_maps = len(feed_in) == 1, len(feed_in + feed_out)

    def body(flush, meta, residual, own, other, small_own, small_other, *refs):
        small = small_of(meta, layer, side, small_own, small_other)
        if not held:
            chooser, refs = refs[0], refs[1:]
        given, refs = refs[:n_maps], refs[n_maps:]
        settled_ref, unit_ref, rstd_ref, selected, pack, slope, part, squares = refs[:8]
        if held:
            weights = Held(given[0].at[side], given[1].at[side])
            low_ref, active_ref, sems = refs[8:]
        else:
            in_buffer, out_buffer, sems = refs[8:]
            weights = Weights(
                meta,
                layer,
                (
                    maps(*given[:2], side, column_pieces(units, 4)),
                    maps(*given[2:], side, row_pieces(units, 2)),
                ),
                (in_buffer, out_buffer),
                sems,
            )
        post = small[ROW_ATT_POST : ROW_ATT_POST + 3]
        branch = summed(own, other) + post[0:1]
        squares[...] = square_sum(branch, row_valid(meta, side, batch, rows))
        unit, rstd, settled = norm_of(residual[...].astype(f32) + branch, post[1:2], post[2:3])
        unit_ref[...] = unit
        rstd_ref[...] = rstd
        settled_ref[...] = settled
        low = settled.astype(bf16)
        if held:
            low_ref[...] = low
            copies = hand_over(low_ref, selected, pack, sems)
            flush(unit_ref, rstd_ref)
        else:
            select_rows(low, chooser, selected, pack)
            active_ref = pack.at[:, HALF:]
            flush(unit_ref, rstd_ref, selected)
        for i in range(units // step):
            first = weights.get(0, i)
            columns = slice(i * step, (i + 1) * step)
            row = ROW_FEED_BIAS + (i * step) // D
            place = (i * step) % D
            hidden = mm(low, first[:, columns]) + small[row : row + 1, place : place + step]
            below = 0.5 + 0.5 * lax.erf(hidden * (0.5**0.5))
            density = jnp.exp(hidden * hidden * -0.5) * 0.3989422804014327
            active_ref[:, columns] = (hidden * below).astype(bf16)
            slope[:, columns] = (below + hidden * density).astype(bf16)
        flush(pack, slope)
        if held:
            copies += hand_halves(meta, batch, active_ref, selected, pack, sems)
        part[...] = mm(active_ref[...], weights.get(1)[...]).astype(bf16)
        if held:
            for copy in copies:
                copy.wait()

    ins = [(meta, "s"), (residual, "v"), (own, "v"), (other, "v")]
    ins += [(item, "v") for item in ((*small,) if held else (*small, chooser))]
    ins += weight_inputs(feed_in, feed_out, "wawa")
    outs = [
        ((rows, D), f32, "v"),
        ((rows, D), f32, "h"),
        ((rows, 1), f32, "h"),
        *(
            [((rows, D + units // 2), bf16, "w")] * 2
            if held
            else [((rows, HALF), bf16, "h"), ((rows, HALF + units), bf16, "h", *place)]
        ),
        ((rows, units), bf16, "h"),
        ((rows, D), bf16, "v"),
        ((1, 128), f32, "h"),
    ]
    scratch = [
        pltpu.VMEM((D, units), bf16),
        pltpu.VMEM((units, D), bf16),
        pltpu.SemaphoreType.DMA((6,)),
    ]
    if held:
        scratch = hand_scratch(rows, units)
    cost = 12.0 if held and side == ORDER[-1] else 4.3
    return call(body, ins, outs, scratch, cost, f"feed_forward_{layer}_{side}", ties, 12 if held else 14)


def cross_forward(
    batch, meta, streams, smalls, chooser, cross_in, cross_bias, cross_out, later, ties=()
):
    rows = [stream[0].shape[0] for stream in streams]
    spans = spans_of(rows)
    width = cross_out.shape[0]
    heads = width // HEAD_DIM

    def body(flush, meta, *refs):
        given = (refs[0:3], refs[3:6])
        small = [small_of(meta, 0, side, refs[6], refs[7]) for side in (0, 1)]
        chooser, in_ref, bias, out_ref = refs[8:12]
        offered, refs = refs[12 : 12 + 2 * len(later)], refs[:12] + refs[12 + 2 * len(later) :]
        taken, refs = refs[29 : 29 + len(later)], refs[:29] + refs[29 + len(later) :]
        all_pack = refs[28]
        outs = [refs[12:20], refs[20:28]]
        for side in (0, 1):
            outs[side] = outs[side][:5] + (all_pack.at[spans[side]],) + outs[side][5:]
        in_buffer, out_buffer, sems, later_sems = refs[29:]
        weights = Weights(
            meta,
            0,
            (maps(in_ref, None, 0, ENTRY), maps(out_ref, None, 0)),
            (in_buffer, out_buffer),
            sems,
        )
        passing = pass_on(meta, 1, offered, taken, later_sems)
        lows = []
        for side in (0, 1):
            settled, own, other = given[side]
            state, unit_ref, rstd_ref, squares, selected, pack, qkv, probs, part = outs[side]
            post = small[side][ROW_FEED_POST : ROW_FEED_POST + 3]
            branch = summed(own, other) + post[0:1]
            unit, rstd, result = norm_of(settled[...] + branch, post[1:2], post[2:3])
            unit_ref[...] = unit
            rstd_ref[...] = rstd
            low = result.astype(bf16)
            state[...] = low
            valid = row_valid(meta, side, batch, rows[side])
            squares[0:1] = square_sum(branch, valid)
            squares[1:2] = square_sum(low.astype(f32), valid)
            select_rows(low, chooser, selected, pack)
            flush(unit_ref, rstd_ref, selected)
            lows.append(low)
        for side in (0, 1):
            project(lows[side], weights, bias[0:1], bias[1:2], outs[side][6])
        leave = weights.get(1)
        for side in (0, 1):
            pack, qkv, probs, part = outs[side][5:]
            there = outs[1 - side][6]
            valid = pair_valid(meta, 1 - side, batch, rows[side], rows[1 - side])
            context = pack.at[:, HALF:]
            attend(qkv[0], there[1], there[2], valid, probs, context)
            flush(qkv, probs)
            part[...] = mm(context[...], leave[...]).astype(bf16)
        for copy in passing:
            copy.wait()

    ins = [(meta, "s")] + [pair for stream in streams for pair in zip(stream, "vvv")]
    ins += [(item, "v") for item in smalls]
    ins += [(chooser, "v"), (cross_in, "w"), (cross_bias, "v"), (cross_out, "w")]
    ins += [(item, "w") for pair in later for item in pair]
    outs = []
    for side in (0, 1):
        here, there = rows[side], rows[1 - side]
        outs += [
            ((here, D), bf16, "v"),
            ((here, D), f32, "h"),
            ((here, 1), f32, "h"),
            ((2, 128), f32, "h"),
            ((here, HALF), bf16, "h"),
            ((3, here, width), bf16, "h"),
            ((heads, here, there), bf16, "h"),
            ((here, D), bf16, "v"),
        ]
    outs.append(((sum(rows), HALF + width), bf16, "h"))
    outs += [(pair[0].shape[1:], bf16, "v") for pair in later]
    scratch = [
        pltpu.VMEM((3, D, width), bf16),
        pltpu.VMEM((width, D), bf16),
        pltpu.SemaphoreType.DMA((6,)),
        pltpu.SemaphoreType.DMA((len(later),)),
    ]
    result = call(body, ins, outs, scratch, 6.8, "cross_forward", ties)
    return result[:8], result[8:16], result[16], result[17:]


class Layout:
    def __init__(self, sides, rows, given):
        self.sides, self.total, self.spans = sides, sum(rows), spans_of(rows)
        self.single = len(sides) == 1
        self.side = sides[0]
        self.count = rows[self.side] if self.single else self.total
        self.given = given

    def here(self, side):
        return slice(0, self.count) if self.single else self.spans[side]

    def index(self, side):
        return 0 if self.single else side

    def rows(self, width, dtype, at):
        if not self.single:
            return (self.total, width), dtype, "h"
        given = self.given[at] if self.given else None
        return (self.count, width), dtype, "h", self.total, self.spans[self.side].start, given

    def each(self, shape, at):
        if not self.single:
            return (2, *shape), f32, "h"
        given = self.given[at] if self.given else None
        return (1, *shape), f32, "h", 2, self.side, given


def feed_backward(
    layer, sides, rows, batch, meta, tops, joint, small, chooser, slopes, feed_in, feed_out, ties=(),
    given=None,
):
    last = joint is None
    layout = Layout(sides, rows, given)
    units = slopes[0].shape[1]
    step = units // 4
    n_top = len(tops[0])
    n = len(sides)
    held, n_maps = len(feed_in) == 1, len(feed_in + feed_out)

    def body(flush, meta, *refs):
        tops = {}
        for side in sides:
            tops[side], refs = refs[:n_top], refs[n_top:]
        if not last:
            joint, refs = refs[:3], refs[3:]
        small = {side: small_of(meta, layer, side, refs[0], refs[1]) for side in sides}
        refs = refs[2:]
        if not held:
            chooser, refs = refs[0], refs[1:]
        slopes, refs = dict(zip(sides, refs[:n])), refs[n:]
        given, refs = refs[:n_maps], refs[n_maps:]
        grad_all, selected_all, pack_all, part_all, post_all, bias_all = refs[:6]
        if last:
            squares_all, results = refs[6], dict(zip(sides, refs[7 : 7 + n]))
            low_ref, hidden_ref, hand_sems, raw, rows_ref, raw_sem = refs[-6:]
        weights = {}
        for i, side in enumerate(sides):
            if held:
                weights[side] = Held(given[1].at[side], given[0].at[side])
                continue
            in_buffer, out_buffer, sems = refs[-3:]
            weights[side] = Weights(
                meta,
                layer,
                (
                    maps(*given[2:], side, row_pieces(units, 4)),
                    maps(*given[:2], side, column_pieces(units, 2)),
                ),
                (out_buffer.at[i], in_buffer.at[i]),
                sems.at[i],
            )
        lows = {}
        for side in sides:
            here, at = layout.here(side), layout.index(side)
            post = small[side][ROW_FEED_POST : ROW_FEED_POST + 3]
            if last:
                settled, own, other, cotangent = tops[side]
                branch = summed(own, other) + post[0:1]
                unit, rstd, result = norm_of(settled[...] + branch, post[1:2], post[2:3])
                low = result.astype(bf16)
                results[side][...] = low
                valid = row_valid(meta, side, batch, rows[side])
                squares_all[at, 0:1] = square_sum(branch, valid)
                squares_all[at, 1:2] = square_sum(low.astype(f32), valid)
                items_of(meta, cotangent, raw, rows_ref, raw_sem, batch)
                incoming = rows_ref[...] * valid
            else:
                unit_ref, rstd_ref = tops[side]
                unit, rstd = unit_ref[...], rstd_ref[...]
                incoming = (joint[0][here] + summed_rows(joint[1], joint[2], here)).astype(bf16)
                incoming = incoming.astype(f32)
            grad = norm_back(unit, rstd, post[1:2], incoming)
            grad_all[here] = grad
            low = grad.astype(bf16)
            post_all[at, 0:1] = column_sum(low.astype(f32))
            post_all[at, 1:2] = column_sum(incoming * unit)
            post_all[at, 2:3] = column_sum(incoming)
            lows[side] = low
        flush(grad_all, post_all)
        if held:
            low_ref[...] = lows[sides[0]]
            copies = hand_over(low_ref, selected_all, pack_all, hand_sems)
        else:
            hidden_ref = pack_all.at[:, HALF:]
        for side in sides:
            here, at = layout.here(side), layout.index(side)
            for i in range(units // step):
                columns = slice(i * step, (i + 1) * step)
                active = mm_nt(lows[side], weights[side].get(0, i)[columns, :])
                hidden = (active * slopes[side][:, columns].astype(f32)).astype(bf16)
                hidden_ref[here, columns] = hidden
                bias_all[at, :, columns] = column_sum(hidden.astype(f32))
            if not held:
                select_rows(lows[side], chooser, selected_all.at[here], pack_all.at[here])
        flush(pack_all, selected_all)
        if held:
            copies += hand_halves(meta, batch, hidden_ref, selected_all, pack_all, hand_sems)
        for side in sides:
            here = layout.here(side)
            part_all[here] = mm_nt(hidden_ref[here], weights[side].get(1)[...]).astype(bf16)
        if held:
            for copy in copies:
                copy.wait()

    ins = [(meta, "s")] + [pair for top in tops for pair in zip(top, "vvvw" if last else "vv")]
    if not last:
        ins += [(item, "v") for item in joint]
    ins += [(item, "v") for item in ((*small, *slopes) if held else (*small, chooser, *slopes))]
    ins += weight_inputs(feed_in, feed_out)
    count = layout.count
    outs = [
        ((count, D), f32, "v" if last else "h"),
        *(
            [((count, D + units // 2), bf16, "w")] * 2
            if held
            else [layout.rows(HALF, bf16, 1), ((count, HALF + units), bf16, "h")]
        ),
        ((count, D), bf16, "v" if last else "h"),
        layout.each((3, D), 4),
        layout.each((1, units), 5),
    ]
    if last:
        outs += [layout.each((2, 128), 6)] + [((rows[side], D), bf16, "h") for side in sides]
    scratch = [
        pltpu.VMEM((n, D, units), bf16),
        pltpu.VMEM((n, units, D), bf16),
        pltpu.SemaphoreType.DMA((n, 6)),
    ]
    if last:
        side = sides[0]
        scratch = hand_scratch(rows[side], units) + [
            pltpu.VMEM(tops[0][3].shape[1:], bf16),
            pltpu.VMEM((rows[side], D), f32),
            pltpu.SemaphoreType.DMA,
        ]
    name = f"feed_backward_{layer}_" + "".join(map(str, sides))
    cost = 12.0 if sides == ORDER[:1] else 11.0 * count / layout.total
    return call(body, ins, outs, scratch, cost, name, ties, 12 if held else 24)


def summed_rows(own, other, here):
    return own[here].astype(f32) + other[here].astype(f32)


def back_through_norm(top, grad_in, branch, gain, grad_ref, post_ref):
    unit_ref, rstd_ref = top
    incoming = grad_in + branch
    unit = unit_ref[...]
    grad = norm_back(unit, rstd_ref[...], gain, incoming)
    grad_ref[...] = grad
    low = grad.astype(bf16)
    post_ref[0:1] = column_sum(low.astype(f32))
    post_ref[1:2] = column_sum(incoming * unit)
    post_ref[2:3] = column_sum(incoming)
    return low


def emit_into(pack, width):
    def emit(kind, lanes, value):
        start = HALF + kind * width + lanes.start
        pack[:, start : start + PAIR] = value

    return emit


def back_to_input(pack, weights, slot, width):
    grads = [pack[:, HALF + j * width : HALF + (j + 1) * width] for j in range(3)]
    total = mm_nt(grads[0], weights.get(slot, 0)[0])
    total += mm_nt(grads[1], weights.get(slot, 1)[1])
    total += mm_nt(grads[2], weights.get(slot, 2)[2])
    return total.astype(bf16)


def self_backward(
    layer, sides, rows, meta, tops, joint, small, chooser, qkvs, probs, att_in, att_out, ties=(),
    given=None,
):
    layout = Layout(sides, rows, given)
    width = qkvs[0].shape[2]
    n = len(sides)
    held, n_maps = len(att_in) == 1, len(att_in + att_out)

    def body(flush, meta, *refs):
        tops = {side: refs[2 * i : 2 * i + 2] for i, side in enumerate(sides)}
        joint, refs = refs[2 * n : 2 * n + 3], refs[2 * n + 3 :]
        small = {side: small_of(meta, layer, side, refs[0], refs[1]) for side in sides}
        chooser, refs = refs[2], refs[3:]
        qkvs, probs, refs = dict(zip(sides, refs[:n])), dict(zip(sides, refs[n : 2 * n])), refs[2 * n :]
        given, refs = refs[:n_maps], refs[n_maps:]
        grad_all, selected_all, pack_all, part_all, post_all, bias_all = refs[:6]
        weights = {}
        for i, side in enumerate(sides):
            if held:
                weights[side] = Held(given[1].at[side], given[0].at[side])
                continue
            in_buffer, out_buffer, sems = refs[6:]
            weights[side] = Weights(
                meta,
                layer,
                (maps(*given[2:], side), maps(*given[:2], side, ENTRY)),
                (out_buffer.at[i], in_buffer.at[i]),
                sems.at[i],
            )
        for side in sides:
            here, at = layout.here(side), layout.index(side)
            pack = pack_all.at[here]
            gain = small[side][ROW_ATT_POST + 1 : ROW_ATT_POST + 2]
            low = back_through_norm(
                tops[side],
                joint[0][here],
                summed_rows(joint[1], joint[2], here),
                gain,
                grad_all.at[here],
                post_all.at[at],
            )
            context = mm_nt(low, weights[side].get(0)[...]).astype(bf16)
            qkv = qkvs[side]
            attend_back(qkv[0], qkv[1], qkv[2], probs[side], context, emit_into(pack, width))
            bias_all[at, 0:1] = column_sum(pack[:, HALF : HALF + width].astype(f32))
            bias_all[at, 1:2] = column_sum(pack[:, HALF + 2 * width :].astype(f32))
            select_rows(low, chooser, selected_all.at[here], pack)
        flush(pack_all, selected_all, grad_all, post_all, bias_all)
        for side in sides:
            here = layout.here(side)
            part_all[here] = back_to_input(pack_all.at[here], weights[side], 1, width)

    near = "v" if layer == 1 else "h"
    ins = [(meta, "s")] + [(item, near) for top in tops for item in top]
    ins += [*zip(joint, "vvv" if layer == 1 else "hhf")] + [(item, near) for item in small]
    ins += [(item, near) for item in (chooser, *qkvs, *probs)]
    ins += weight_inputs(att_in, att_out)
    outs = [
        ((layout.count, D), f32, "h"),
        layout.rows(HALF, bf16, 1),
        layout.rows(HALF + 3 * width, bf16, 2),
        ((layout.count, D), bf16, "h"),
        layout.each((3, D), 4),
        layout.each((2, width), 5),
    ]
    scratch = [
        pltpu.VMEM((n, 3, D, width), bf16),
        pltpu.VMEM((n, width, D), bf16),
        pltpu.SemaphoreType.DMA((n, 6)),
    ]
    scratch = [] if held else scratch
    name = f"self_backward_{layer}_" + "".join(map(str, sides))
    cost = 12.0 * layout.count / layout.total
    return call(body, ins, outs, scratch, cost, name, ties, 12 if held else 18)


def cross_backward(meta, tops, grads, owns, others, post, chooser, qkvs, probs, cross_in, cross_out, ties=()):
    rows = [qkv.shape[1] for qkv in qkvs]
    width = cross_out.shape[0]
    spans, total = spans_of(rows), sum(rows)

    def body(flush, meta, *refs):
        tops, grads, owns, others = (refs[:2], refs[2:4]), refs[4:6], refs[6:8], refs[8:10]
        post, chooser, qkvs, probs = refs[10], refs[11], refs[12:14], refs[14:16]
        in_ref, out_ref = refs[16:18]
        grad_all, selected_all, pack_all, part_all, post_out, bias_out = refs[18:24]
        in_buffer, out_buffer, post_each, sems = refs[24:]
        weights = Weights(
            meta,
            0,
            (maps(out_ref, None, 0), maps(in_ref, None, 0, ENTRY)),
            (out_buffer, in_buffer),
            sems,
        )
        packs = [pack_all.at[here] for here in spans]
        lows = []
        for side in (0, 1):
            here = spans[side]
            low = back_through_norm(
                tops[side],
                grads[side][...],
                summed(owns[side], others[side]),
                post[1:2],
                grad_all.at[here],
                post_each.at[side],
            )
            lows.append(low)
        post_out[...] = post_each[0] + post_each[1]
        leave = weights.get(0)
        for side in (0, 1):
            context = mm_nt(lows[side], leave[...]).astype(bf16)
            to_here, to_there = emit_into(packs[side], width), emit_into(packs[1 - side], width)

            def emit(kind, lanes, value):
                (to_here if kind == 0 else to_there)(kind, lanes, value)

            attend_back(
                qkvs[side][0], qkvs[1 - side][1], qkvs[1 - side][2], probs[side], context, emit
            )
        for side in (0, 1):
            select_rows(lows[side], chooser, selected_all.at[spans[side]], packs[side])
        bias_out[0:1] = column_sum(pack_all[:, HALF : HALF + width].astype(f32))
        bias_out[1:2] = column_sum(pack_all[:, HALF + 2 * width :].astype(f32))
        flush(pack_all, selected_all)
        part_all[...] = back_to_input(pack_all, weights, 1, width)

    ins = [(meta, "s")] + [(item, "h") for top in tops for item in top]
    ins += [(item, "h") for item in (*grads, *owns)] + [(item, "f") for item in others]
    ins += [(item, "h") for item in (post, chooser, *qkvs, *probs)]
    ins += [(cross_in, "w"), (cross_out, "w")]
    outs = [
        ((total, D), f32, "v"),
        ((total, HALF), bf16, "h"),
        ((total, HALF + 3 * width), bf16, "h"),
        ((total, D), bf16, "v"),
        ((3, D), f32, "h"),
        ((2, width), f32, "h"),
    ]
    scratch = [
        pltpu.VMEM((3, D, width), bf16),
        pltpu.VMEM((width, D), bf16),
        pltpu.VMEM((2, 3, D), f32),
        pltpu.SemaphoreType.DMA((6,)),
    ]
    return call(body, ins, outs, scratch, 10.0, "cross_backward", ties, 16)


class Block:
    def __init__(self, in_selected, in_packs, in_gots, out_selected, out_packs, out_gots):
        self.parts = [*in_selected, *in_packs, *in_gots, out_selected, *out_packs, *out_gots]
        self.counts = (len(in_packs), len(out_packs))
        self.lead = HALF
        self.kinds = "w" * len(self.parts)
        self.sizes = (out_packs[0].shape[1] - HALF, in_packs[0].shape[1] - HALF)
        self.rows = [array.shape[0] for array in in_selected]

    def buffers(self):
        return [
            pltpu.VMEM((2 * rows, HALF + size), bf16)
            for rows in self.rows
            for size in (self.sizes[1], self.sizes[0])
        ]

    def fetch(self, refs, buffers, sems, at):
        spans = spans_of(self.rows)
        in_selected, rest = refs[:2], refs[2:]
        n_in, n_out = self.counts
        pack, got, rest = rest[:n_in], rest[n_in : 2 * n_in], rest[2 * n_in :]
        out_selected, out_pack, out_got = rest[0], rest[1 : 1 + n_out], rest[1 + n_out :]

        def rows_of(items, side):
            return items[0].at[spans[side]] if len(items) == 1 else items[side]

        result = []
        for side in (0, 1):
            count = self.rows[side]
            per_side = []
            for kind, (selected, own, other) in enumerate(
                (
                    (in_selected[side], rows_of(pack, side), rows_of(got, side)),
                    (out_selected.at[spans[side]], rows_of(out_pack, side), rows_of(out_got, side)),
                )
            ):
                buffer = buffers[2 * side + kind]
                size = buffer.shape[1] - HALF
                mine = slice(0, count)
                copies = [
                    pltpu.make_async_copy(
                        selected, buffer.at[mine, pl.ds(0, HALF)], sems.at[at]
                    ),
                    pltpu.make_async_copy(
                        own.at[:, pl.ds(HALF, size)], buffer.at[mine, pl.ds(HALF, size)], sems.at[at + 1]
                    ),
                    pltpu.make_async_copy(
                        other, buffer.at[slice(count, 2 * count)], sems.at[at + 2]
                    ),
                ]
                at += 3
                for copy in copies:
                    copy.start()
                per_side.append((buffer, copies))
            result.append(per_side)
        return result, at


class Halves:
    def __init__(self, in_kept, in_gots, out_kept, out_gots):
        self.parts = [*in_kept, *in_gots, *out_kept, *out_gots]
        self.kinds = "w" * len(self.parts)
        self.lead = D
        self.sizes = (out_kept[0].shape[1] - D, in_kept[0].shape[1] - D)
        self.rows = [array.shape[0] for array in in_kept]

    def buffers(self):
        return [
            pltpu.VMEM((2 * rows, D + size), bf16)
            for rows in self.rows
            for size in (self.sizes[1], self.sizes[0])
        ]

    def fetch(self, refs, buffers, sems, at):
        result = []
        for side in (0, 1):
            count = self.rows[side]
            per_side = []
            for kind in (0, 1):
                buffer = buffers[2 * side + kind]
                copies = []
                for part in (0, 1):
                    target = buffer.at[slice(part * count, (part + 1) * count)]
                    source = refs[4 * kind + 2 * part + side]
                    copies.append(pltpu.make_async_copy(source, target, sems.at[at]))
                    copies[-1].start()
                    at += 1
                per_side.append((buffer, copies))
            result.append(per_side)
        return result, at


def chunk_order(groups):
    return [(s, z) for z in range(groups) for s in ((0, 1) if z % 2 == 0 else (1, 0))]


def places_chunks(groups):
    return (D // (2 * groups) // 2) % 16 == 0


def gradients(meta, blocks, cross, groups, name, ties=(), mode="ring"):
    lead = blocks[0].lead
    chunk = lead // groups
    half = chunk // 2
    size = chunk + half if cross else chunk
    order = chunk_order(groups)
    aligned = places_chunks(groups)
    width = sum(sum(block.sizes) for block in blocks)
    every = blocks + ([cross] if cross else [])
    n_in = sum(len(block.parts) for block in every)
    pair = mode == "split"
    n_out = 2 if pair else 1 if aligned else 3 if cross else 2
    n_sems = 12 * len(every) + 4 * len(every)

    def body(flush, meta, *refs):
        inputs, outputs, rest = refs[:n_in], refs[n_in : n_in + n_out], list(refs[n_in + n_out :])
        if cross:
            cross_stage = rest.pop()
        stage, sems = rest.pop(), rest.pop()
        at = 0
        fetched = []
        for block in every:
            taken, inputs = inputs[: len(block.parts)], inputs[len(block.parts) :]
            own, rest = rest[:4], rest[4:]
            copies, at = block.fetch(taken, own, sems, at)
            fetched.append(copies)
        waited, leaving = set(), []

        def leave(source, side, columns, at):
            if pair and not cross:
                kept, sent = (
                    pltpu.make_async_copy(source, target.at[:, columns], sems.at[at])
                    for target in outputs
                )
                pl.when(meta[0] == side)(kept.start)
                pl.when(meta[0] != side)(sent.start)
                leaving.append(kept)
                return
            if not aligned:
                copy = pltpu.make_async_copy(source, outputs[side].at[:, columns], sems.at[at])
                copy.start()
                leaving.append(copy)
                return
            if mode == "ring":
                for k, (s, z) in enumerate(order):
                    if side == 2:
                        start, count, place = (s * groups + z) * half, half, k * size + chunk
                    elif s == side:
                        start, count, place = z * chunk, chunk, k * size
                    else:
                        continue
                    copy = pltpu.make_async_copy(
                        source.at[pl.ds(start, count)],
                        outputs[0].at[pl.ds(place, count), columns],
                        sems.at[at],
                    )
                    copy.start()
                    leaving.append(copy)
                return
            for section in (0, 1) if side == 2 else (side,):
                for z in range(groups):
                    if side == 2:
                        start, count, place = (section * groups + z) * half, half, z * size + chunk
                    else:
                        start, count, place = z * chunk, chunk, z * size
                    kept, sent = (
                        pltpu.make_async_copy(
                            source.at[pl.ds(start, count)],
                            target.at[pl.ds(place, count), columns],
                            sems.at[at],
                        )
                        for target in outputs
                    )
                    pl.when(meta[0] == section)(kept.start)
                    pl.when(meta[0] != section)(sent.start)
                    leaving.append(kept)

        def ready(item):
            buffer, copies = item
            if id(buffer) not in waited:
                waited.add(id(buffer))
                for copy in copies:
                    copy.wait()
            return buffer

        base = 0
        for block, copies in zip(blocks, fetched):
            for side in (0, 1):
                start = base
                for left, right in ((0, 1), (1, 0)):
                    left, right = ready(copies[side][left]), ready(copies[side][right])
                    turned = left[:, :lead].T
                    span = right.shape[1] - lead
                    for step in range(0, span, HALF):
                        value = mm(turned, right[:, lead + step : lead + step + HALF])
                        stage[side, :, start + step : start + step + HALF] = value.astype(bf16)
                    columns = pl.ds(start, span)
                    leave(stage.at[side, :, columns], side, columns, at)
                    at += 1
                    start += span
            base += sum(block.sizes)
        if cross:
            copies = fetched[-1]
            start = 0
            for left, right in ((0, 1), (1, 0)):
                lefts = [ready(copies[side][left])[:, :HALF].T for side in (0, 1)]
                rights = [ready(copies[side][right]) for side in (0, 1)]
                span = rights[0].shape[1] - HALF
                for step in range(0, span, HALF):
                    columns = slice(HALF + step, HALF + step + HALF)
                    value = mm(lefts[0], rights[0][:, columns]) + mm(lefts[1], rights[1][:, columns])
                    cross_stage[:, start + step : start + step + HALF] = value.astype(bf16)
                columns = pl.ds(start, span)
                leave(cross_stage.at[:, columns], 2, columns, at)
                at += 1
                start += span
        for copy in leaving:
            copy.wait()

    ins = [(meta, "s")] + [pair for block in every for pair in zip(block.parts, block.kinds)]
    if pair:
        outs = [((groups * size, width), bf16, "w")] * 2
    elif aligned:
        outs = [((2 * groups * size, width), bf16, "w")]
    else:
        outs = [((lead, width), bf16, "w")] * n_out
    scratch = [buffer for block in every for buffer in block.buffers()]
    if cross:
        scratch += [
            pltpu.SemaphoreType.DMA((n_sems,)),
            pltpu.VMEM((2, lead, width), bf16),
            pltpu.VMEM((HALF, sum(cross.sizes)), bf16),
        ]
    else:
        scratch += [pltpu.SemaphoreType.DMA((n_sems,)), pltpu.VMEM((2, lead, width), bf16)]
    result = call(body, ins, outs, scratch, 6.0, name, ties, 20)
    if pair:
        return result
    if aligned:
        return result[0]
    chunks = [result[side].reshape(groups, chunk, width) for side in (0, 1)]
    pieces = [chunks[s][z] for s, z in order]
    if cross:
        extra = result[2].reshape(2, groups, half, width)
        pieces = [jnp.concatenate([one, extra[s, z]]) for one, (s, z) in zip(pieces, order)]
    return jnp.concatenate(pieces)


def placed_gradients(meta, first, second, chunk, width, units):
    def body(flush, meta, *refs):
        layers, last = (refs[:4], refs[4:8]), refs[7]
        feed_in, feed_out, att_in, att_out, cross_in, cross_out = refs[8:]
        for item in refs[:8]:
            item.wait()

        def store(layer):
            for side in (0, 1):
                feed, late = layers[layer][2 * side : 2 * side + 2]
                feed_in[side] = feed[:, :units].astype(f32)
                feed_out[side] = feed[:, units:].astype(f32)
                for j in range(3):
                    att_in[side, j] = late[:chunk, j * width : (j + 1) * width].astype(f32)
                att_out[side] = late[:chunk, 3 * width :].astype(f32)

        pl.when(meta[0] == 0)(partial(store, 0))
        pl.when(meta[0] != 0)(partial(store, 1))
        for j in range(3):
            cross_in[j] = last[chunk:, j * width : (j + 1) * width].astype(f32)
        cross_out[...] = last[chunk:, 3 * width :].astype(f32)

    ins = [(meta, "s")] + [(item, "f") for item in (*first, *second)]
    half = chunk // 2
    outs = [
        ((2, chunk, units), f32, "h"),
        ((2, chunk, units), f32, "h"),
        ((2, 3, chunk, width), f32, "h"),
        ((2, chunk, width), f32, "h"),
        ((3, half, width), f32, "h"),
        ((half, width), f32, "h"),
    ]
    return call(body, ins, outs, (), 4.0, "placed_gradients")


def small_shape(width, units):
    n_feed = 2 * units // D
    sizes = (2 * 2 * width // D, 6, n_feed, 6, 2, 3, 2 * width // D, 1)
    starts = [sum(sizes[:i]) for i in range(len(sizes))]
    return starts, sum(sizes)


def finished(meta, batch, rows, results, state_grad, layers, cross_post, cross_bias, ties):
    spans = spans_of(rows)
    width, units = cross_bias.shape[1], layers[0][2].shape[2]
    starts, total = small_shape(width, units)
    flat = [
        [*layer[:4], *layer[4], *layer[5], *layer[6]] for layer in layers
    ]
    counts = [len(layer) for layer in flat]

    def body(flush, meta, *refs):
        results, (grad, own, other), refs = refs[:2], refs[2:5], refs[5:]
        first, second, refs = refs[: counts[0]], refs[counts[0] : sum(counts)], refs[sum(counts) :]
        cross_post, cross_bias, refs = refs[0], refs[1], refs[2:]
        outs, mine, theirs, packs = refs[:4], refs[4], refs[5], refs[6]
        for k, layer in enumerate((first, second)):
            att_bias, att_post, feed_bias, feed_post, *squares = layer
            for side in (0, 1):
                for j in (0, 1):
                    place = (2 * side + j) * width
                    row, lane = starts[0] + place // D, place % D
                    packs[k, row : row + 1, lane : lane + width] = att_bias[side, j : j + 1]
                for start, post in ((starts[1], att_post), (starts[3], feed_post)):
                    packs[k, start + 3 * side : start + 3 * side + 3] = post[side]
                for j in range(units // D):
                    row = starts[2] + side * (units // D) + j
                    packs[k, row : row + 1] = feed_bias[side, :, j * D : (j + 1) * D]
            lead, middle, tails = squares[:2], squares[2:4], squares[4:]
            packs[k, starts[4] : starts[5]] = jnp.zeros((2, D), f32)
            for side in (0, 1):
                tail = tails[side] if len(tails) == 2 else tails[0].wait().at[side]
                terms = (lead[side][0:1], middle[side][0:1], tail[0:1], tail[1:2])
                for j, term in enumerate(terms):
                    at = 4 * side + j
                    row, lane = starts[4] + at // 6, at % 6 * 128
                    packs[k, row : row + 1, lane : lane + 128] = term
            packs[k, starts[5] : starts[6]] = cross_post[...]
            for j in (0, 1):
                row, lane = starts[6] + j * width // D, j * width % D
                packs[k, row : row + 1, lane : lane + width] = cross_bias[j : j + 1]
            lane = lax.broadcasted_iota(jnp.int32, (1, D), 1)
            count = jnp.zeros((1, D), f32)
            for side in (0, 1):
                for i in range(batch):
                    length = meta[1 + side * batch + i].astype(f32)
                    count += jnp.where(lane == side, length, 0.0)
            packs[k, starts[7] : starts[7] + 1] = count
        mine[...] = packs[meta[0]]
        theirs[...] = packs[1 - meta[0]]
        flush(mine, theirs)
        for side in (0, 1):
            here = spans[side]
            whole = results[side][...].astype(f32)
            back = (grad[here] + summed_rows(own, other, here)).astype(bf16).astype(f32)
            for slot in range(rows[side] // batch):
                these = slice(slot * batch, (slot + 1) * batch)
                outs[side][slot] = whole[these].astype(bf16)
                outs[2 + side][slot] = back[these].astype(bf16)

    ins = [(meta, "s")] + [(item, "f") for item in results] + list(zip(state_grad, "fff"))
    ins += [(item, "f") for layer in flat for item in layer]
    ins += [(cross_post, "f"), (cross_bias, "f")]
    outs = [((count // batch, batch, D), bf16, "h") for count in (*rows, *rows)]
    outs += [((total, D), f32, "h")] * 2
    scratch = [pltpu.VMEM((2, total, D), f32)]
    return call(body, ins, outs, scratch, 4.0, "finished", ties)


def unpacked(sums, width, units):
    starts, _ = small_shape(width, units)

    def body(flush, sums, att_bias, att_post, feed_bias, feed_post, cross_bias, cross_post, scales):
        for side in (0, 1):
            for j in (0, 1):
                place = (2 * side + j) * width
                row, lane = starts[0] + place // D, place % D
                att_bias[0, side, j : j + 1] = sums[row : row + 1, lane : lane + width]
            for start, post in ((starts[1], att_post), (starts[3], feed_post)):
                for j in range(3):
                    row = start + 3 * side + j
                    post[0, j, side : side + 1] = sums[row : row + 1]
            for j in range(units // D):
                row = starts[2] + side * (units // D) + j
                feed_bias[0, side : side + 1, j * D : (j + 1) * D] = sums[row : row + 1]
        cross_post[...] = sums[starts[5] : starts[6]]
        for j in (0, 1):
            row, lane = starts[6] + j * width // D, j * width % D
            cross_bias[j : j + 1] = sums[row : row + 1, lane : lane + width]
        counts = sums[starts[7] : starts[7] + 1]
        lane = lax.broadcasted_iota(jnp.int32, (1, 8), 1)
        result = jnp.zeros((1, 8), f32)
        for at in range(8):
            row, place = starts[4] + at // 6, at % 6 * 128
            square = sums[row : row + 1, place : place + 1]
            scale = jnp.sqrt(square / (counts[:, at // 4 : at // 4 + 1] * D))
            result = jnp.where(lane == at, scale, result)
        scales[...] = result

    outs = [
        ((1, 2, 2, width), f32, "h"),
        ((1, 3, 2, D), f32, "h"),
        ((1, 2, units), f32, "h"),
        ((1, 3, 2, D), f32, "h"),
        ((2, width), f32, "h"),
        ((3, D), f32, "h"),
        ((1, 8), f32, "h"),
    ]
    return call(body, [(sums, "f")], outs, (), 2.0, "unpacked")


def prepared(ids, lengths, att_bias, att_post, feed_bias, feed_post):
    batch = lengths[0].shape[1]
    n_feed = feed_bias.shape[2] // D
    n_ids = ids.shape[0]

    def body(flush, ids, words, regions, att_bias, att_post, feed_bias, feed_post, small, meta):
        meta[0] = ids[0]
        for i in range(1, n_ids):
            meta[2 * batch + i] = ids[i]
        for side, counts in enumerate((words, regions)):
            for i in range(batch):
                meta[1 + side * batch + i] = counts[ids[0], i]
        half = att_bias.shape[3]
        for side in (0, 1):
            for j in (0, 1):
                small[side, ROW_ATT_BIAS : ROW_ATT_BIAS + 1, j * half : (j + 1) * half] = att_bias[
                    0, side, j : j + 1
                ]
            for j in range(3):
                for row, post in ((ROW_ATT_POST, att_post), (ROW_FEED_POST, feed_post)):
                    small[side, row + j : row + j + 1] = post[0, j, side : side + 1]
            for j in range(n_feed):
                row = ROW_FEED_BIAS + j
                small[side, row : row + 1] = feed_bias[0, side : side + 1, j * D : (j + 1) * D]
            end = ROW_FEED_POST + 3
            small[side, end:] = jnp.zeros((SMALL_ROWS - end, D), f32)

    ins = [(ids, "s"), (lengths[0], "s"), (lengths[1], "s")]
    ins += [(item, "h") for item in (att_bias, att_post, feed_bias, feed_post)]
    outs = [((2, SMALL_ROWS, D), f32, "h"), ((n_ids + 2 * batch,), jnp.int32, "s")]
    return call(body, ins, outs, (), 1.0, "prepared")


def swap(value, axis, distance=1):
    count = lax.axis_size(axis)
    return lax.ppermute(value, axis, [(i, i ^ distance) for i in range(count)])


def total_of(parts):
    return sum(part.astype(f32) for part in parts).astype(bf16)


class Halving:
    def __init__(self, parts, groups):
        self.parts = [part.reshape(groups, -1, part.shape[1]) for part in parts]
        self.position, self.distance, self.groups = lax.axis_index("dp") // 2, 2, groups

    def half(self, bit):
        split = [part.reshape(-1, 2, *part.shape[1:]) for part in self.parts]
        return [lax.dynamic_index_in_dim(part, bit, 1, keepdims=False) for part in split]

    def send(self, *after):
        self.parts = behind(self.parts, after)
        bit = self.position % 2
        sent = total_of(self.half(1 - bit))
        self.parts = self.half(bit) + [swap(sent, "dp", self.distance)]
        self.position, self.distance = self.position // 2, 2 * self.distance
        self.groups //= 2
        return sent

    def finish(self, *after):
        while self.groups > 1:
            self.send()
        return total_of([part[0] for part in behind(self.parts, after)])


def behind(values, after):
    return lax.optimization_barrier((values, after))[0] if after else values


def on_device(
    word_state,
    region_state,
    word_lengths,
    region_counts,
    word_cotangent,
    region_cotangent,
    cross_in,
    cross_bias,
    cross_out,
    cross_post,
    attention_in,
    attention_bias,
    attention_out,
    attention_post,
    feed_in,
    feed_bias,
    feed_out,
    feed_post,
):
    section = lax.axis_index("section")
    dp_count = lax.axis_size("dp")
    groups = dp_count // 2
    place = lax.axis_index("dp") % 2
    batch = word_state.shape[1]
    width = cross_out.shape[0]
    units = feed_in.shape[-1]
    both = (0, 1)
    chains = [[s * dp_count + 2 * z + y for s, z in chunk_order(groups)] for y in both]

    def unflat(value):
        return value.reshape(-1, batch, D).transpose(1, 0, 2)[None]

    def chooser_of(pieces, per_section):
        column = jnp.arange(D)
        half = column // HALF
        inner = column % HALF
        side = jnp.where(half == 0, place, 1 - place)
        size = D // pieces
        if per_section:
            block = inner // (HALF // 2)
            inner = inner % (HALF // 2)
            feature = size * (dp_count * block + 2 * (inner // size) + side) + inner % size
        else:
            feature = size * (2 * (inner // size) + side) + inner % size
        return (jnp.arange(D)[:, None] == feature[None, :]).astype(bf16)

    chooser = chooser_of(dp_count, False)
    cross_chooser = chooser_of(2 * dp_count, True)

    ids = jnp.stack([section, place]).astype(jnp.int32)
    small_own, meta = prepared(
        ids,
        (word_lengths, region_counts),
        attention_bias,
        attention_post.transpose(0, 2, 1, 3),
        feed_bias,
        feed_post.transpose(0, 2, 1, 3),
    )
    small = (small_own, swap(small_own, "section"))
    att_in_own = attention_in.transpose(0, 1, 3, 2, 4)
    att_in = (att_in_own, swap(att_in_own, "section"))
    att_out = (attention_out, swap(attention_out, "section"))
    states = [value.transpose(0, 2, 1, 3) for value in (word_state, region_state)]
    feed_in_later, feed_out_later, *_ = lax.optimization_barrier(
        (feed_in, feed_out, att_in[1], att_out[1], small[1], chooser, cross_chooser)
    )
    ff_in = (feed_in, swap(feed_in_later, "section"))
    ff_out = (feed_out, swap(feed_out_later, "section"))
    cross_entry = cross_in.transpose(1, 0, 2)

    cotangents = [value.transpose(0, 2, 1, 3) for value in (word_cotangent, region_cotangent)]
    rows = [state.shape[1] * batch for state in states]
    total_rows = sum(rows)

    def in_order(step, pack_index, tie=None, joined=True, order=(1, 0)):
        results = [None, None]
        given = None
        for side in order:
            ties = () if tie is None else (tie,)
            place = (total_rows, rows[0] * side, given) if joined else ()
            results[side] = step(side, place, ties)
            tie, given = results[side][pack_index + 2], results[side][pack_index]
        return results

    def over_mp(results, index):
        return [swap(results[side][index], "mp") for side in both]

    self0 = in_order(
        lambda side, place, ties: self_forward(
            side, 0, batch, meta, states[side], None, small, chooser, att_in, att_out,
            place, ties,
        ),
        3,
    )
    got = over_mp(self0, 4)
    feed0 = in_order(
        lambda side, place, ties: feed_forward(
            side, 0, batch, meta, self0[side][6], self0[side][4], got[side], small, chooser,
            ff_in, ff_out, place, ties,
        ),
        4,
        self0[0][5],
    )
    got = over_mp(feed0, 6)
    self0_there = swap(self0[0][3], "dp")
    cross_w, cross_r, cross_pack, held = cross_forward(
        batch,
        meta,
        [(feed0[side][0], feed0[side][6], got[side]) for side in both],
        small,
        cross_chooser,
        cross_entry,
        cross_bias,
        cross_out,
        (att_in, att_out, ff_in),
    )
    att_in1, att_out1, ff_in1 = [(item,) for item in held]
    cross = (cross_w, cross_r)
    got = over_mp(cross, 7)
    feed0_there = swap(feed0[0][4], "dp")
    self1 = in_order(
        lambda side, place, ties: self_forward(
            side, 1, batch, meta, cross[side][0], (cross[side][7], got[side], cross_post),
            small, chooser, att_in1, att_out1, place, ties + ((self0_there, "a"),),
            (ff_out,) if side == ORDER[0] else (),
        ),
        3,
        None,
        True,
        ORDER,
    )
    ff_out1 = (self1[ORDER[0]][9],)
    got = over_mp(self1, 4)
    cross_there = swap(cross_pack, "dp")
    feed1 = in_order(
        lambda side, place, ties: feed_forward(
            side, 1, batch, meta, self1[side][6], self1[side][4], got[side], small, chooser,
            ff_in1, ff_out1, place, ties + (((feed0_there, "a"),) if side == ORDER[0] else ()),
        ),
        4,
        self1[ORDER[-1]][5],
        False,
        ORDER,
    )
    got = over_mp(feed1, 6)
    self1_there = swap(self1[ORDER[-1]][3], "dp")
    feed1_there = [swap(feed1[side][4], "dp") for side in both]

    def over_sections_and_groups(value):
        return lax.psum_scatter(
            value, ("section", "dp"), scatter_dimension=0, axis_index_groups=chains, tiled=True
        )

    def over_groups(value):
        pairs = [[2 * z + y for z in range(groups)] for y in both]
        return lax.psum_scatter(
            value, "dp", scatter_dimension=0, axis_index_groups=pairs, tiled=True
        )

    given, back_feed1 = None, [None, None]
    for side in ORDER:
        given = feed_backward(
            1,
            (side,),
            rows,
            batch,
            meta,
            [(feed1[side][0], feed1[side][6], got[side], cotangents[side])],
            None,
            small,
            chooser,
            [feed1[side][5]],
            ff_in1,
            ff_out1,
            ((feed1_there[side], "a"), (cross_there, "a")) if side == ORDER[0] else (),
            given,
        )
        back_feed1[side] = given
    got = over_mp(back_feed1, 3)
    back_feed1_there = [swap(back_feed1[side][2], "dp") for side in both]

    given, back_self1 = None, [None, None]
    for side in ORDER:
        given = self_backward(
            1,
            (side,),
            rows,
            meta,
            [feed1[side][1:3]],
            (back_feed1[side][0], back_feed1[side][3], got[side]),
            small,
            chooser,
            [self1[side][0]],
            [self1[side][1]],
            att_in1,
            att_out1,
            (
                ((feed1_there[ORDER[-1]], "a"), (back_feed1_there[ORDER[0]], "a"))
                if side == ORDER[0]
                else ()
            ),
            given,
        )
        back_self1[side] = given
    got = over_mp(back_self1, 3)
    feed1_grads = gradients(
        meta,
        [
            Halves(
                [feed1[side][3] for side in both],
                feed1_there,
                [back_feed1[side][1] for side in both],
                back_feed1_there,
            )
        ],
        None,
        groups,
        "feed_gradients_1",
        (back_self1[ORDER[-1]][5],),
    )
    feed1_pair = over_sections_and_groups(feed1_grads).reshape(2, D // dp_count, -1)
    back_self1_there = swap(back_self1[ORDER[-1]][2], "dp")
    back_cross = cross_backward(
        meta,
        [self1[side][7:9] for side in both],
        [back_self1[side][0] for side in both],
        [back_self1[side][3] for side in both],
        got,
        cross_post,
        cross_chooser,
        [cross[side][5] for side in both],
        [cross[side][6] for side in both],
        cross_entry,
        cross_out,
        (feed1_grads,),
    )
    cross_post_grad, cross_bias_grad = back_cross[4:6]
    got = swap(back_cross[3], "mp")
    back_cross_there = swap(back_cross[2], "dp")
    back_feed0 = feed_backward(
        0,
        (1, 0),
        rows,
        batch,
        meta,
        [cross[side][1:3] for side in (1, 0)],
        (back_cross[0], back_cross[3], got),
        small,
        chooser,
        [feed0[side][5] for side in (1, 0)],
        ff_in,
        ff_out,
        ((back_self1_there, "a"),),
    )
    got = swap(back_feed0[3], "mp")
    back_feed0_there = swap(back_feed0[2], "dp")
    late1_grads = gradients(
        meta,
        [
            Block(
                [self1[side][2] for side in both],
                [self1[ORDER[-1]][3]],
                [self1_there],
                back_self1[ORDER[-1]][1],
                [back_self1[ORDER[-1]][2]],
                [back_self1_there],
            )
        ],
        Block(
            [cross[side][4] for side in both],
            [cross_pack],
            [cross_there],
            back_cross[1],
            [back_cross[2]],
            [back_cross_there],
        ),
        groups,
        "late_gradients_1",
        (back_feed0[5],),
    )
    late1_share = over_sections_and_groups(late1_grads)
    back_self0 = self_backward(
        0,
        (1, 0),
        rows,
        meta,
        [feed0[side][1:3] for side in (1, 0)],
        (back_feed0[0], back_feed0[3], got),
        small,
        chooser,
        [self0[side][0] for side in (1, 0)],
        [self0[side][1] for side in (1, 0)],
        att_in,
        att_out,
        (late1_grads,),
    )
    got = swap(back_self0[3], "mp")
    back_self0_there = swap(back_self0[2], "dp")
    feed0_grads = gradients(
        meta,
        [
            Block(
                [feed0[side][3] for side in both],
                [feed0[0][4]],
                [feed0_there],
                back_feed0[1],
                [back_feed0[2]],
                [back_feed0_there],
            )
        ],
        None,
        groups,
        "feed_gradients_0",
        (back_self0[5], feed1_pair),
        "split",
    )
    feed0_total = total_of([feed0_grads[0], swap(feed0_grads[1], "section")])
    self0_grads = gradients(
        meta,
        [
            Block(
                [self0[side][2] for side in both],
                [self0[0][3]],
                [self0_there],
                back_self0[1],
                [back_self0[2]],
                [back_self0_there],
            )
        ],
        None,
        groups,
        "self_gradients_0",
        (feed0_total,),
        "split",
    )
    feed0_share = over_groups(feed0_total)
    self0_parts = [self0_grads[0], swap(self0_grads[1], "section")]
    if groups & (groups - 1) == 0:
        halving = Halving(self0_parts, groups)
        self0_sent = halving.send() if groups > 1 else self0_parts[0]
    else:
        halving = None
        self0_sent = total_of(self0_parts)
    chunk = D // dp_count
    word_full, region_full, word_back, region_back, mine, theirs = finished(
        meta,
        batch,
        rows,
        [back_feed1[side][7] for side in both],
        (back_self0[0], back_self0[3], got),
        [
            (
                back_self0[5],
                back_self0[4],
                back_feed0[5],
                back_feed0[4],
                [self0[side][5] for side in both],
                [feed0[side][7] for side in both],
                [cross[side][3] for side in both],
            ),
            (
                back_self1[ORDER[-1]][5],
                back_self1[ORDER[-1]][4],
                back_feed1[ORDER[-1]][5],
                back_feed1[ORDER[-1]][4],
                [self1[side][5] for side in both],
                [feed1[side][7] for side in both],
                [back_feed1[ORDER[-1]][6]],
            ),
        ],
        cross_post_grad,
        cross_bias_grad,
        (self0_sent,),
    )
    total = mine + swap(theirs, "section")
    distance = 1
    while 2 * distance < dp_count:
        total, distance = total + swap(total, "dp", distance), 2 * distance
    last_sent = halving.send(total) if halving and groups > 2 else total
    feed1_pair, late1_share = behind((feed1_pair, late1_share), (last_sent,))
    feed1_own = lax.dynamic_index_in_dim(feed1_pair, place, 0, keepdims=False)
    feed1_other = swap(lax.dynamic_index_in_dim(feed1_pair, 1 - place, 0, keepdims=False), "dp")
    halves = (
        jnp.where(place == 0, feed1_own, feed1_other),
        jnp.where(place == 0, feed1_other, feed1_own),
    )
    count = units // 2
    feed1_share = jnp.concatenate(
        [half[:, j * count : (j + 1) * count] for j in both for half in halves], axis=1
    )
    late_words = [
        lax.ppermute(value, "section", [(0, 1)]) for value in (feed1_share, late1_share[:chunk])
    ]
    self0_share = halving.finish(late_words) if halving else over_groups(self0_sent)
    self_regions = lax.ppermute(self0_share, "section", [(1, 0)])
    total = behind(total, (self0_share,))
    last_total = swap(total, "dp", distance)
    feed0_share, late_words, self_regions = behind(
        (feed0_share, late_words, self_regions), (late1_share,)
    )
    feed_regions = lax.ppermute(feed0_share, "section", [(1, 0)])
    feed_in_grad, feed_out_grad, att_in_grad, att_out_grad, cross_in_grad, cross_out_grad = (
        placed_gradients(
            meta,
            (feed0_share, self0_share, feed_regions, self_regions),
            (*late_words, feed1_share, late1_share),
            chunk,
            width,
            units,
        )
    )
    outputs = unpacked(total + behind(last_total, (att_out_grad,)), width, units)
    feed_in_grad = feed_in_grad[None]
    feed_out_grad = feed_out_grad.transpose(0, 2, 1)[None]
    att_in_grad = att_in_grad.transpose(0, 2, 1, 3)[None]
    att_out_grad = att_out_grad.transpose(0, 2, 1)[None]
    cross_in_grad = cross_in_grad.transpose(1, 0, 2)
    cross_out_grad = cross_out_grad.T
    att_bias_grad, att_post_grad, feed_bias_grad, feed_post_grad, cross_bias_grad, cross_post_grad = (
        outputs[:6]
    )
    return (
        word_full.transpose(1, 0, 2)[None],
        region_full.transpose(1, 0, 2)[None],
        word_back.transpose(1, 0, 2)[None],
        region_back.transpose(1, 0, 2)[None],
        cross_in_grad,
        cross_bias_grad,
        cross_out_grad,
        cross_post_grad,
        att_in_grad,
        att_bias_grad,
        att_out_grad,
        att_post_grad.transpose(0, 2, 1, 3),
        feed_in_grad,
        feed_bias_grad,
        feed_out_grad,
        feed_post_grad.transpose(0, 2, 1, 3),
        outputs[6],
    )


def solution(mesh):
    placed = (
        P(None, "dp", None, None),
        P(None, "dp", None, None),
        P(None, "dp"),
        P(None, "dp"),
        P(None, "dp", None, None),
        P(None, "dp", None, None),
        P(None, None, "mp"),
        P(None, "mp"),
        P("mp", None),
        P(),
        P("section", None, None, None, "mp"),
        P("section", None, None, "mp"),
        P("section", None, "mp", None),
        P("section", None, None, None),
        P("section", None, None, "mp"),
        P("section", None, "mp"),
        P("section", None, "mp", None),
        P("section", None, None, None),
    )
    return jax.shard_map(
        on_device,
        mesh=mesh,
        in_specs=placed,
        out_specs=(
            P("section", "dp", None, None),
            P("section", "dp", None, None),
            P("section", "dp", None, None),
            P("section", "dp", None, None),
            P(("section", "dp"), None, "mp"),
            P(None, "mp"),
            P("mp", ("section", "dp")),
            P(),
            P("section", None, "dp", None, "mp"),
            P("section", None, None, "mp"),
            P("section", None, "mp", "dp"),
            P("section", None, None, None),
            P("section", None, "dp", "mp"),
            P("section", None, "mp"),
            P("section", None, "mp", "dp"),
            P("section", None, None, None),
            P("section", None),
        ),
        check_vma=False,
    )
```

```python
from functools import partial

import jax
import jax.numpy as jnp
from jax import lax
from jax.experimental import pallas as pl
from jax.experimental.pallas import tpu as pltpu
from jax.sharding import PartitionSpec as P

D = 768
HALF = D // 2
HEAD_DIM = 64
PAIR = 2 * HEAD_DIM
WORDS = 20
REGIONS = 36
EPS = 1e-06
SCALE = HEAD_DIM**-0.5
COST_SCALE = 0.5
ORDER = (0, 1)
bf16 = jnp.bfloat16
f32 = jnp.float32

ROW_ATT_BIAS, ROW_ATT_POST, ROW_FEED_BIAS, ROW_FEED_POST, SMALL_ROWS = 0, 1, 4, 6, 16


def mm(a, b):
    return jnp.dot(a, b, preferred_element_type=f32)


def mm_nt(a, b):
    return lax.dot_general(a, b, (((1,), (1,)), ((), ())), preferred_element_type=f32)


def mm_tn(a, b):
    return lax.dot_general(a, b, (((0,), (0,)), ((), ())), preferred_element_type=f32)


def norm_of(value, gain, shift):
    centred = value - jnp.mean(value, axis=-1, keepdims=True)
    spread = jnp.mean(centred * centred, axis=-1, keepdims=True)
    rstd = lax.rsqrt(spread + EPS)
    unit = centred * rstd
    return unit, rstd, unit * gain + shift


def norm_back(unit, rstd, gain, incoming):
    scaled = incoming * gain
    mean = jnp.mean(scaled, axis=-1, keepdims=True)
    along = jnp.mean(scaled * unit, axis=-1, keepdims=True)
    return (scaled - mean - unit * along) * rstd


def summed(own, other):
    return own[...].astype(f32) + other[...].astype(f32)


def column_sum(value):
    return jnp.sum(value, axis=0, keepdims=True)


def square_sum(value, valid):
    rows = jnp.sum(value * value, axis=-1, keepdims=True) * valid
    return jnp.broadcast_to(jnp.sum(rows, axis=0, keepdims=True), (1, 128))


def lengths_of(meta, side, batch, item):
    result = jnp.zeros_like(item)
    for i in range(batch):
        result = jnp.where(item == i, meta[1 + side * batch + i], result)
    return result


def row_valid(meta, side, batch, rows):
    index = lax.broadcasted_iota(jnp.int32, (rows, 1), 0)
    length = lengths_of(meta, side, batch, lax.rem(index, batch))
    return (lax.div(index, batch) < length).astype(f32)


def pair_valid(meta, side, batch, rows, keys):
    index = lax.broadcasted_iota(jnp.int32, (1, keys), 1)
    item = lax.rem(index, batch)
    length = lengths_of(meta, side, batch, item)
    item = jnp.where(lax.div(index, batch) < length, item, -1)
    row_item = lax.rem(lax.broadcasted_iota(jnp.int32, (rows, 1), 0), batch)
    return jnp.broadcast_to(row_item, (rows, keys)) == jnp.broadcast_to(item, (rows, keys))


def head_lanes(head):
    lane = lax.broadcasted_iota(jnp.int32, (1, PAIR), 1)
    return (lane // HEAD_DIM) == head


def attend(query, keys, values, valid, probs_ref, context_ref):
    for pair in range(query.shape[1] // PAIR):
        lanes = slice(pair * PAIR, (pair + 1) * PAIR)
        contexts = []
        for head in range(2):
            chosen = query[:, lanes] * head_lanes(head).astype(bf16)
            scores = mm_nt(chosen, keys[:, lanes]) * SCALE
            scores = jnp.where(valid, scores, -1e9)
            shifted = jnp.exp(scores - jnp.max(scores, axis=-1, keepdims=True))
            total = jnp.sum(shifted, axis=-1, keepdims=True)
            probs = (shifted * (1.0 / total)).astype(bf16)
            probs_ref[2 * pair + head] = probs
            contexts.append(mm(probs, values[:, lanes]))
        context_ref[:, lanes] = jnp.where(head_lanes(0), contexts[0], contexts[1]).astype(bf16)


def attend_back(query, keys, values, probs_ref, grad_context, emit):
    first = head_lanes(0)
    for pair in range(query.shape[1] // PAIR):
        lanes = slice(pair * PAIR, (pair + 1) * PAIR)
        grads = ([], [], [])
        for head in range(2):
            probs = probs_ref[2 * pair + head]
            chosen = grad_context[:, lanes] * head_lanes(head).astype(bf16)
            grad_probs = mm_nt(chosen, values[:, lanes])
            wide = probs.astype(f32)
            product = wide * grad_probs
            grad_scores = product - wide * jnp.sum(product, axis=-1, keepdims=True)
            grad_scores = grad_scores.astype(bf16)
            grads[0].append(mm(grad_scores, keys[:, lanes]) * SCALE)
            grads[1].append(mm_tn(grad_scores, query[:, lanes]) * SCALE)
            grads[2].append(mm_tn(probs, grad_context[:, lanes]))
        for kind in range(3):
            emit(kind, lanes, jnp.where(first, grads[kind][0], grads[kind][1]).astype(bf16))


def small_of(meta, layer, side, own, other):
    return jnp.where(meta[0] == layer, own[side], other[side])


class Fetched:
    def __init__(self, copy, buffer):
        self.copy, self.buffer, self.waited = copy, buffer, False
        self.shape, self.dtype = buffer.shape, buffer.dtype

    def wait(self):
        if not self.waited:
            self.copy.wait()
            self.waited = True
        return self.buffer

    def __getitem__(self, index):
        return self.wait()[index]


class Weights:
    def __init__(self, meta, layer, pairs, buffers, sems):
        self.copies = []
        mine = meta[0] == layer
        at = 0
        for (own, other, pieces), buffer in zip(pairs, buffers):
            copies = []
            for piece in pieces:
                copy = pltpu.make_async_copy(own.at[piece], buffer.at[piece], sems.at[at])
                if other is None:
                    copy.start()
                else:
                    second = pltpu.make_async_copy(
                        other.at[piece], buffer.at[piece], sems.at[at]
                    )
                    pl.when(mine)(copy.start)
                    pl.when(jnp.logical_not(mine))(second.start)
                copies.append(Fetched(copy, buffer))
                at += 1
            self.copies.append(copies)

    def get(self, slot, piece=None):
        copies = self.copies[slot]
        for copy in copies if piece is None else (copies[piece],):
            copy.wait()
        return copies[0].buffer


class Held:
    def __init__(self, *refs):
        self.refs = refs

    def get(self, slot, piece=None):
        return self.refs[slot]


def weight_inputs(entry, leave, kinds="wwww"):
    if len(entry) == 1:
        return [(entry[0], "v"), (leave[0], "v")]
    return list(zip(entry + leave, kinds))


def pass_on(meta, layer, offered, taken, sems):
    copies = []
    for i, target in enumerate(taken):
        own = pltpu.make_async_copy(offered[2 * i].at[0], target, sems.at[i])
        other = pltpu.make_async_copy(offered[2 * i + 1].at[0], target, sems.at[i])
        pl.when(meta[0] == layer)(own.start)
        pl.when(meta[0] != layer)(other.start)
        copies.append(own)
    return copies


def items_of(meta, source, raw, rows_ref, sem, batch):
    copy = pltpu.make_async_copy(source.at[meta[0]], raw, sem)
    copy.start()
    copy.wait()
    for slot in range(raw.shape[0]):
        rows_ref[slot * batch : (slot + 1) * batch] = raw[slot].astype(f32)


def maps(own, other, side, pieces=((),)):
    if other is None:
        return own, None, pieces
    return own.at[0, side], other.at[0, side], pieces


ENTRY = ((0,), (1,), (2,))


def column_pieces(size, count):
    return tuple(
        (slice(None), slice(i * size // count, (i + 1) * size // count)) for i in range(count)
    )


def row_pieces(size, count):
    return tuple((slice(i * size // count, (i + 1) * size // count),) for i in range(count))


def call(body, ins, outs, scratch=(), cost=0.0, name=None, ties=(), mib=14):
    spaces = {
        "s": pltpu.SMEM, "v": pltpu.VMEM, "w": pltpu.HBM, "h": pltpu.HBM, "a": pl.ANY, "f": pl.ANY
    }
    ties = [tie if isinstance(tie, tuple) else (tie, "w") for tie in ties]
    extra = [(i, out[5]) for i, out in enumerate(outs) if len(out) > 3 and out[5] is not None]
    aliases = {len(ins) + at: i for at, (i, _) in enumerate(extra)}
    ins = list(ins) + [(array, "w") for _, array in extra]
    places = [out[3:5] if len(out) > 3 else None for out in outs]
    fetched = [i for i, (_, kind) in enumerate(ins) if kind in "hf"]
    written = [i for i, out in enumerate(outs) if out[2] == "h"]
    n_ins, n_ties, n_outs, n_scratch = len(ins), len(ties), len(outs), len(scratch)

    def whole(*refs):
        given = list(refs[:n_ins])
        results = list(refs[n_ins + n_ties : n_ins + n_ties + n_outs])
        rest = refs[n_ins + n_ties + n_outs :]
        own, rest = rest[:n_scratch], rest[n_scratch:]
        buffers, rest = rest[: len(fetched)], rest[len(fetched) :]
        staged, rest = rest[: len(written)], rest[len(written) :]
        sems = rest[0] if rest else None
        for slot, i in enumerate(fetched):
            copy = pltpu.make_async_copy(given[i], buffers[slot], sems.at[slot])
            copy.start()
            given[i] = Fetched(copy, buffers[slot])
        leaving = {}
        for slot, i in enumerate(written):
            target = results[i]
            if places[i] is not None:
                target = target.at[pl.ds(places[i][1], staged[slot].shape[0])]
            copy = pltpu.make_async_copy(staged[slot], target, sems.at[len(fetched) + slot])
            leaving[id(staged[slot])] = copy
            results[i] = staged[slot]
        started = []

        def flush(*done):
            for ref in done:
                copy = leaving.pop(id(ref), None)
                if copy is not None:
                    copy.start()
                    started.append(copy)

        body(flush, *given[: n_ins - len(extra)], *results, *own)
        flush(*[staged[slot] for slot in range(len(written))])
        for copy in started:
            copy.wait()
        for item in given:
            if isinstance(item, Fetched):
                item.wait()

    arrays = [
        pltpu.with_memory_space_constraint(array, spaces[kind]) if kind in "vwh" else array
        for array, kind in [*ins, *ties]
    ]
    own_scratch = list(scratch)
    own_scratch += [pltpu.VMEM(arrays[i].shape, arrays[i].dtype) for i in fetched]
    own_scratch += [pltpu.VMEM(outs[i][0], outs[i][1]) for i in written]
    if fetched or written:
        own_scratch.append(pltpu.SemaphoreType.DMA((len(fetched) + len(written),)))
    return pl.pallas_call(
        whole,
        out_shape=[
            spaces[out[2]]((out[3], *out[0][1:]) if len(out) > 3 else out[0], out[1]) for out in outs
        ],
        in_specs=[pl.BlockSpec(memory_space=spaces[kind]) for _, kind in [*ins, *ties]],
        out_specs=[pl.BlockSpec(memory_space=spaces[out[2]]) for out in outs],
        input_output_aliases=aliases,
        scratch_shapes=own_scratch,
        compiler_params=pltpu.CompilerParams(vmem_limit_bytes=mib * 1024 * 1024),
        cost_estimate=pl.CostEstimate(
            flops=int(cost * COST_SCALE * 1.15e9), bytes_accessed=0, transcendentals=0
        ),
        name=name,
    )(*arrays)


def spans_of(rows):
    return slice(0, rows[0]), slice(rows[0], rows[0] + rows[1])


def select_rows(value, chooser, own_ref, pack_ref):
    moved = mm(value, chooser[...]).astype(bf16)
    own_ref[...] = moved[:, :HALF]
    pack_ref[:, :HALF] = moved[:, HALF:]


def project(low, weights, bias_q, bias_v, qkv_ref):
    qkv_ref[0] = (mm(low, weights.get(0, 0)[0]) + bias_q).astype(bf16)
    qkv_ref[1] = mm(low, weights.get(0, 1)[1]).astype(bf16)
    qkv_ref[2] = (mm(low, weights.get(0, 2)[2]) + bias_v).astype(bf16)


def self_forward(
    side, layer, batch, meta, state, prior, small, chooser, att_in, att_out, place, ties=(), later=()
):
    rows = state.shape[1] * batch if prior is None else state.shape[0]
    width = att_in[0].shape[-1]
    first = prior is None
    held, n_maps = len(att_in) == 1, len(att_in + att_out)

    def body(flush, meta, state, *refs):
        refs = list(refs)
        if not first:
            own, other, post = refs[:3]
            refs = refs[3:]
        small = small_of(meta, layer, side, refs[0], refs[1])
        chooser, refs = refs[2], refs[3:]
        given, refs = refs[:n_maps], refs[n_maps:]
        offered, refs = refs[: 2 * len(later)], refs[2 * len(later) :]
        qkv, probs, selected, pack, part, squares = refs[:6]
        refs = refs[6:]
        if not first:
            mixed_ref, unit_ref, rstd_ref = refs[:3]
            taken, refs = refs[3 : 3 + len(later)], refs[3 + len(later) :]
            passing = pass_on(meta, layer, offered, taken, refs[-1]) if later else []
        else:
            low_ref, refs = refs[0], refs[1:]
            raw, rows_ref, raw_sem = refs[-3:]
            refs = refs[:-3]
        if held:
            weights = Held(given[0].at[side], given[1].at[side])
        else:
            in_buffer, out_buffer, sems = refs
            weights = Weights(
                meta,
                layer,
                (maps(*given[:2], side, ENTRY), maps(*given[2:], side)),
                (in_buffer, out_buffer),
                sems,
            )
        valid = row_valid(meta, side, batch, rows)
        if first:
            items_of(meta, state, raw, rows_ref, raw_sem, batch)
            squares[...] = square_sum(rows_ref[...], valid)
            low = rows_ref[...].astype(bf16)
            low_ref[...] = low
        else:
            branch = summed(own, other) + post[0:1]
            squares[...] = square_sum(branch, valid)
            unit, rstd, mixed = norm_of(state[...].astype(f32) + branch, post[1:2], post[2:3])
            unit_ref[...] = unit
            rstd_ref[...] = rstd
            mixed_ref[...] = mixed
            low = mixed.astype(bf16)
        select_rows(low, chooser, selected, pack)
        flush(selected)
        biases = small[ROW_ATT_BIAS : ROW_ATT_BIAS + 1]
        project(low, weights, biases[:, :width], biases[:, width : 2 * width], qkv)
        context = pack.at[:, HALF:]
        attend(
            qkv[0], qkv[1], qkv[2], pair_valid(meta, side, batch, rows, rows), probs, context
        )
        flush(qkv, probs, pack)
        part[...] = mm(context[...], weights.get(1)[...]).astype(bf16)
        if not first:
            for copy in passing:
                copy.wait()

    ins = [(meta, "s"), (state, "w" if first else "v")]
    if not first:
        ins += list(zip(prior, "vvv"))
    ins += [(item, "v") for item in (*small, chooser)]
    ins += weight_inputs(att_in, att_out, "wawa")
    ins += [(item, "w") for pair in later for item in pair]
    outs = [
        ((3, rows, width), bf16, "h"),
        ((width // HEAD_DIM, rows, rows), bf16, "h"),
        ((rows, HALF), bf16, "h"),
        ((rows, HALF + width), bf16, "h", *place),
        ((rows, D), bf16, "v"),
        ((1, 128), f32, "h"),
    ]
    if not first:
        outs += [((rows, D), f32, "v"), ((rows, D), f32, "h"), ((rows, 1), f32, "h")]
        outs += [(pair[0].shape[1:], bf16, "v") for pair in later]
    else:
        outs.append(((rows, D), bf16, "v"))
    scratch = [
        pltpu.VMEM((3, D, width), bf16),
        pltpu.VMEM((width, D), bf16),
        pltpu.SemaphoreType.DMA((6,)),
    ]
    scratch = [] if held else scratch
    if first:
        scratch += [
            pltpu.VMEM(state.shape[1:], bf16),
            pltpu.VMEM((rows, D), f32),
            pltpu.SemaphoreType.DMA,
        ]
    if later:
        scratch.append(pltpu.SemaphoreType.DMA((len(later),)))
    return call(body, ins, outs, scratch, 4.0, f"self_forward_{layer}_{side}", ties, 12)


def hand_over(low_ref, kept, sent, sems):
    copies = []
    for slot, target in enumerate((kept, sent)):
        copies.append(
            pltpu.make_async_copy(low_ref, target.at[:, pl.ds(0, D)], sems.at[slot])
        )
        copies[-1].start()
    return copies


def hand_halves(meta, batch, wide_ref, kept, sent, sems):
    count = wide_ref.shape[1] // 2
    copies = []
    for half in (0, 1):
        source = wide_ref.at[:, pl.ds(half * count, count)]
        to_kept, to_sent = (
            pltpu.make_async_copy(source, target.at[:, pl.ds(D, count)], sems.at[2 + half])
            for target in (kept, sent)
        )
        mine = meta[1 + 2 * batch] == half
        pl.when(mine)(to_kept.start)
        pl.when(jnp.logical_not(mine))(to_sent.start)
        copies.append(to_kept)
    return copies


def hand_scratch(rows, units):
    return [
        pltpu.VMEM((rows, D), bf16),
        pltpu.VMEM((rows, units), bf16),
        pltpu.SemaphoreType.DMA((4,)),
    ]


def feed_forward(
    side, layer, batch, meta, residual, own, other, small, chooser, feed_in, feed_out, place, ties=()
):
    rows = residual.shape[0]
    units = feed_in[0].shape[-1]
    step = units // 4

    held, n_maps = len(feed_in) == 1, len(feed_in + feed_out)

    def body(flush, meta, residual, own, other, small_own, small_other, *refs):
        small = small_of(meta, layer, side, small_own, small_other)
        if not held:
            chooser, refs = refs[0], refs[1:]
        given, refs = refs[:n_maps], refs[n_maps:]
        settled_ref, unit_ref, rstd_ref, selected, pack, slope, part, squares = refs[:8]
        if held:
            weights = Held(given[0].at[side], given[1].at[side])
            low_ref, active_ref, sems = refs[8:]
        else:
            in_buffer, out_buffer, sems = refs[8:]
            weights = Weights(
                meta,
                layer,
                (
                    maps(*given[:2], side, column_pieces(units, 4)),
                    maps(*given[2:], side, row_pieces(units, 2)),
                ),
                (in_buffer, out_buffer),
                sems,
            )
        post = small[ROW_ATT_POST : ROW_ATT_POST + 3]
        branch = summed(own, other) + post[0:1]
        squares[...] = square_sum(branch, row_valid(meta, side, batch, rows))
        unit, rstd, settled = norm_of(residual[...].astype(f32) + branch, post[1:2], post[2:3])
        unit_ref[...] = unit
        rstd_ref[...] = rstd
        settled_ref[...] = settled
        low = settled.astype(bf16)
        if held:
            low_ref[...] = low
            copies = hand_over(low_ref, selected, pack, sems)
            flush(unit_ref, rstd_ref)
        else:
            select_rows(low, chooser, selected, pack)
            active_ref = pack.at[:, HALF:]
            flush(unit_ref, rstd_ref, selected)
        for i in range(units // step):
            first = weights.get(0, i)
            columns = slice(i * step, (i + 1) * step)
            row = ROW_FEED_BIAS + (i * step) // D
            place = (i * step) % D
            hidden = mm(low, first[:, columns]) + small[row : row + 1, place : place + step]
            below = 0.5 + 0.5 * lax.erf(hidden * (0.5**0.5))
            density = jnp.exp(hidden * hidden * -0.5) * 0.3989422804014327
            active_ref[:, columns] = (hidden * below).astype(bf16)
            slope[:, columns] = (below + hidden * density).astype(bf16)
        flush(pack, slope)
        if held:
            copies += hand_halves(meta, batch, active_ref, selected, pack, sems)
        part[...] = mm(active_ref[...], weights.get(1)[...]).astype(bf16)
        if held:
            for copy in copies:
                copy.wait()

    ins = [(meta, "s"), (residual, "v"), (own, "v"), (other, "v")]
    ins += [(item, "v") for item in ((*small,) if held else (*small, chooser))]
    ins += weight_inputs(feed_in, feed_out, "wawa")
    outs = [
        ((rows, D), f32, "v"),
        ((rows, D), f32, "h"),
        ((rows, 1), f32, "h"),
        *(
            [((rows, D + units // 2), bf16, "w")] * 2
            if held
            else [((rows, HALF), bf16, "h"), ((rows, HALF + units), bf16, "h", *place)]
        ),
        ((rows, units), bf16, "h"),
        ((rows, D), bf16, "v"),
        ((1, 128), f32, "h"),
    ]
    scratch = [
        pltpu.VMEM((D, units), bf16),
        pltpu.VMEM((units, D), bf16),
        pltpu.SemaphoreType.DMA((6,)),
    ]
    if held:
        scratch = hand_scratch(rows, units)
    cost = 12.0 if held and side == ORDER[-1] else 4.3
    return call(body, ins, outs, scratch, cost, f"feed_forward_{layer}_{side}", ties, 12 if held else 14)


def cross_forward(
    batch, meta, streams, smalls, chooser, cross_in, cross_bias, cross_out, later, ties=()
):
    rows = [stream[0].shape[0] for stream in streams]
    spans = spans_of(rows)
    width = cross_out.shape[0]
    heads = width // HEAD_DIM

    def body(flush, meta, *refs):
        given = (refs[0:3], refs[3:6])
        small = [small_of(meta, 0, side, refs[6], refs[7]) for side in (0, 1)]
        chooser, in_ref, bias, out_ref = refs[8:12]
        offered, refs = refs[12 : 12 + 2 * len(later)], refs[:12] + refs[12 + 2 * len(later) :]
        taken, refs = refs[29 : 29 + len(later)], refs[:29] + refs[29 + len(later) :]
        all_pack = refs[28]
        outs = [refs[12:20], refs[20:28]]
        for side in (0, 1):
            outs[side] = outs[side][:5] + (all_pack.at[spans[side]],) + outs[side][5:]
        in_buffer, out_buffer, sems, later_sems = refs[29:]
        weights = Weights(
            meta,
            0,
            (maps(in_ref, None, 0, ENTRY), maps(out_ref, None, 0)),
            (in_buffer, out_buffer),
            sems,
        )
        passing = pass_on(meta, 1, offered, taken, later_sems)
        lows = []
        for side in (0, 1):
            settled, own, other = given[side]
            state, unit_ref, rstd_ref, squares, selected, pack, qkv, probs, part = outs[side]
            post = small[side][ROW_FEED_POST : ROW_FEED_POST + 3]
            branch = summed(own, other) + post[0:1]
            unit, rstd, result = norm_of(settled[...] + branch, post[1:2], post[2:3])
            unit_ref[...] = unit
            rstd_ref[...] = rstd
            low = result.astype(bf16)
            state[...] = low
            valid = row_valid(meta, side, batch, rows[side])
            squares[0:1] = square_sum(branch, valid)
            squares[1:2] = square_sum(low.astype(f32), valid)
            select_rows(low, chooser, selected, pack)
            flush(unit_ref, rstd_ref, selected)
            lows.append(low)
        for side in (0, 1):
            project(lows[side], weights, bias[0:1], bias[1:2], outs[side][6])
        leave = weights.get(1)
        for side in (0, 1):
            pack, qkv, probs, part = outs[side][5:]
            there = outs[1 - side][6]
            valid = pair_valid(meta, 1 - side, batch, rows[side], rows[1 - side])
            context = pack.at[:, HALF:]
            attend(qkv[0], there[1], there[2], valid, probs, context)
            flush(qkv, probs)
            part[...] = mm(context[...], leave[...]).astype(bf16)
        for copy in passing:
            copy.wait()

    ins = [(meta, "s")] + [pair for stream in streams for pair in zip(stream, "vvv")]
    ins += [(item, "v") for item in smalls]
    ins += [(chooser, "v"), (cross_in, "w"), (cross_bias, "v"), (cross_out, "w")]
    ins += [(item, "w") for pair in later for item in pair]
    outs = []
    for side in (0, 1):
        here, there = rows[side], rows[1 - side]
        outs += [
            ((here, D), bf16, "v"),
            ((here, D), f32, "h"),
            ((here, 1), f32, "h"),
            ((2, 128), f32, "h"),
            ((here, HALF), bf16, "h"),
            ((3, here, width), bf16, "h"),
            ((heads, here, there), bf16, "h"),
            ((here, D), bf16, "v"),
        ]
    outs.append(((sum(rows), HALF + width), bf16, "h"))
    outs += [(pair[0].shape[1:], bf16, "v") for pair in later]
    scratch = [
        pltpu.VMEM((3, D, width), bf16),
        pltpu.VMEM((width, D), bf16),
        pltpu.SemaphoreType.DMA((6,)),
        pltpu.SemaphoreType.DMA((len(later),)),
    ]
    result = call(body, ins, outs, scratch, 6.8, "cross_forward", ties)
    return result[:8], result[8:16], result[16], result[17:]


class Layout:
    def __init__(self, sides, rows, given):
        self.sides, self.total, self.spans = sides, sum(rows), spans_of(rows)
        self.single = len(sides) == 1
        self.side = sides[0]
        self.count = rows[self.side] if self.single else self.total
        self.given = given

    def here(self, side):
        return slice(0, self.count) if self.single else self.spans[side]

    def index(self, side):
        return 0 if self.single else side

    def rows(self, width, dtype, at):
        if not self.single:
            return (self.total, width), dtype, "h"
        given = self.given[at] if self.given else None
        return (self.count, width), dtype, "h", self.total, self.spans[self.side].start, given

    def each(self, shape, at):
        if not self.single:
            return (2, *shape), f32, "h"
        given = self.given[at] if self.given else None
        return (1, *shape), f32, "h", 2, self.side, given


def feed_backward(
    layer, sides, rows, batch, meta, tops, joint, small, chooser, slopes, feed_in, feed_out, ties=(),
    given=None,
):
    last = joint is None
    layout = Layout(sides, rows, given)
    units = slopes[0].shape[1]
    step = units // 4
    n_top = len(tops[0])
    n = len(sides)
    held, n_maps = len(feed_in) == 1, len(feed_in + feed_out)

    def body(flush, meta, *refs):
        tops = {}
        for side in sides:
            tops[side], refs = refs[:n_top], refs[n_top:]
        if not last:
            joint, refs = refs[:3], refs[3:]
        small = {side: small_of(meta, layer, side, refs[0], refs[1]) for side in sides}
        refs = refs[2:]
        if not held:
            chooser, refs = refs[0], refs[1:]
        slopes, refs = dict(zip(sides, refs[:n])), refs[n:]
        given, refs = refs[:n_maps], refs[n_maps:]
        grad_all, selected_all, pack_all, part_all, post_all, bias_all = refs[:6]
        if last:
            squares_all, results = refs[6], dict(zip(sides, refs[7 : 7 + n]))
            low_ref, hidden_ref, hand_sems, raw, rows_ref, raw_sem = refs[-6:]
        weights = {}
        for i, side in enumerate(sides):
            if held:
                weights[side] = Held(given[1].at[side], given[0].at[side])
                continue
            in_buffer, out_buffer, sems = refs[-3:]
            weights[side] = Weights(
                meta,
                layer,
                (
                    maps(*given[2:], side, row_pieces(units, 4)),
                    maps(*given[:2], side, column_pieces(units, 2)),
                ),
                (out_buffer.at[i], in_buffer.at[i]),
                sems.at[i],
            )
        lows = {}
        for side in sides:
            here, at = layout.here(side), layout.index(side)
            post = small[side][ROW_FEED_POST : ROW_FEED_POST + 3]
            if last:
                settled, own, other, cotangent = tops[side]
                branch = summed(own, other) + post[0:1]
                unit, rstd, result = norm_of(settled[...] + branch, post[1:2], post[2:3])
                low = result.astype(bf16)
                results[side][...] = low
                valid = row_valid(meta, side, batch, rows[side])
                squares_all[at, 0:1] = square_sum(branch, valid)
                squares_all[at, 1:2] = square_sum(low.astype(f32), valid)
                items_of(meta, cotangent, raw, rows_ref, raw_sem, batch)
                incoming = rows_ref[...] * valid
            else:
                unit_ref, rstd_ref = tops[side]
                unit, rstd = unit_ref[...], rstd_ref[...]
                incoming = (joint[0][here] + summed_rows(joint[1], joint[2], here)).astype(bf16)
                incoming = incoming.astype(f32)
            grad = norm_back(unit, rstd, post[1:2], incoming)
            grad_all[here] = grad
            low = grad.astype(bf16)
            post_all[at, 0:1] = column_sum(low.astype(f32))
            post_all[at, 1:2] = column_sum(incoming * unit)
            post_all[at, 2:3] = column_sum(incoming)
            lows[side] = low
        flush(grad_all, post_all)
        if held:
            low_ref[...] = lows[sides[0]]
            copies = hand_over(low_ref, selected_all, pack_all, hand_sems)
        else:
            hidden_ref = pack_all.at[:, HALF:]
        for side in sides:
            here, at = layout.here(side), layout.index(side)
            for i in range(units // step):
                columns = slice(i * step, (i + 1) * step)
                active = mm_nt(lows[side], weights[side].get(0, i)[columns, :])
                hidden = (active * slopes[side][:, columns].astype(f32)).astype(bf16)
                hidden_ref[here, columns] = hidden
                bias_all[at, :, columns] = column_sum(hidden.astype(f32))
            if not held:
                select_rows(lows[side], chooser, selected_all.at[here], pack_all.at[here])
        flush(pack_all, selected_all)
        if held:
            copies += hand_halves(meta, batch, hidden_ref, selected_all, pack_all, hand_sems)
        for side in sides:
            here = layout.here(side)
            part_all[here] = mm_nt(hidden_ref[here], weights[side].get(1)[...]).astype(bf16)
        if held:
            for copy in copies:
                copy.wait()

    ins = [(meta, "s")] + [pair for top in tops for pair in zip(top, "vvvw" if last else "vv")]
    if not last:
        ins += [(item, "v") for item in joint]
    ins += [(item, "v") for item in ((*small, *slopes) if held else (*small, chooser, *slopes))]
    ins += weight_inputs(feed_in, feed_out)
    count = layout.count
    outs = [
        ((count, D), f32, "v" if last else "h"),
        *(
            [((count, D + units // 2), bf16, "w")] * 2
            if held
            else [layout.rows(HALF, bf16, 1), ((count, HALF + units), bf16, "h")]
        ),
        ((count, D), bf16, "v" if last else "h"),
        layout.each((3, D), 4),
        layout.each((1, units), 5),
    ]
    if last:
        outs += [layout.each((2, 128), 6)] + [((rows[side], D), bf16, "h") for side in sides]
    scratch = [
        pltpu.VMEM((n, D, units), bf16),
        pltpu.VMEM((n, units, D), bf16),
        pltpu.SemaphoreType.DMA((n, 6)),
    ]
    if last:
        side = sides[0]
        scratch = hand_scratch(rows[side], units) + [
            pltpu.VMEM(tops[0][3].shape[1:], bf16),
            pltpu.VMEM((rows[side], D), f32),
            pltpu.SemaphoreType.DMA,
        ]
    name = f"feed_backward_{layer}_" + "".join(map(str, sides))
    cost = 12.0 if sides == ORDER[:1] else 11.0 * count / layout.total
    return call(body, ins, outs, scratch, cost, name, ties, 12 if held else 24)


def summed_rows(own, other, here):
    return own[here].astype(f32) + other[here].astype(f32)


def back_through_norm(top, grad_in, branch, gain, grad_ref, post_ref):
    unit_ref, rstd_ref = top
    incoming = grad_in + branch
    unit = unit_ref[...]
    grad = norm_back(unit, rstd_ref[...], gain, incoming)
    grad_ref[...] = grad
    low = grad.astype(bf16)
    post_ref[0:1] = column_sum(low.astype(f32))
    post_ref[1:2] = column_sum(incoming * unit)
    post_ref[2:3] = column_sum(incoming)
    return low


def emit_into(pack, width):
    def emit(kind, lanes, value):
        start = HALF + kind * width + lanes.start
        pack[:, start : start + PAIR] = value

    return emit


def back_to_input(pack, weights, slot, width):
    grads = [pack[:, HALF + j * width : HALF + (j + 1) * width] for j in range(3)]
    total = mm_nt(grads[0], weights.get(slot, 0)[0])
    total += mm_nt(grads[1], weights.get(slot, 1)[1])
    total += mm_nt(grads[2], weights.get(slot, 2)[2])
    return total.astype(bf16)


def self_backward(
    layer, sides, rows, meta, tops, joint, small, chooser, qkvs, probs, att_in, att_out, ties=(),
    given=None,
):
    layout = Layout(sides, rows, given)
    width = qkvs[0].shape[2]
    n = len(sides)
    held, n_maps = len(att_in) == 1, len(att_in + att_out)

    def body(flush, meta, *refs):
        tops = {side: refs[2 * i : 2 * i + 2] for i, side in enumerate(sides)}
        joint, refs = refs[2 * n : 2 * n + 3], refs[2 * n + 3 :]
        small = {side: small_of(meta, layer, side, refs[0], refs[1]) for side in sides}
        chooser, refs = refs[2], refs[3:]
        qkvs, probs, refs = dict(zip(sides, refs[:n])), dict(zip(sides, refs[n : 2 * n])), refs[2 * n :]
        given, refs = refs[:n_maps], refs[n_maps:]
        grad_all, selected_all, pack_all, part_all, post_all, bias_all = refs[:6]
        weights = {}
        for i, side in enumerate(sides):
            if held:
                weights[side] = Held(given[1].at[side], given[0].at[side])
                continue
            in_buffer, out_buffer, sems = refs[6:]
            weights[side] = Weights(
                meta,
                layer,
                (maps(*given[2:], side), maps(*given[:2], side, ENTRY)),
                (out_buffer.at[i], in_buffer.at[i]),
                sems.at[i],
            )
        for side in sides:
            here, at = layout.here(side), layout.index(side)
            pack = pack_all.at[here]
            gain = small[side][ROW_ATT_POST + 1 : ROW_ATT_POST + 2]
            low = back_through_norm(
                tops[side],
                joint[0][here],
                summed_rows(joint[1], joint[2], here),
                gain,
                grad_all.at[here],
                post_all.at[at],
            )
            context = mm_nt(low, weights[side].get(0)[...]).astype(bf16)
            qkv = qkvs[side]
            attend_back(qkv[0], qkv[1], qkv[2], probs[side], context, emit_into(pack, width))
            bias_all[at, 0:1] = column_sum(pack[:, HALF : HALF + width].astype(f32))
            bias_all[at, 1:2] = column_sum(pack[:, HALF + 2 * width :].astype(f32))
            select_rows(low, chooser, selected_all.at[here], pack)
        flush(pack_all, selected_all, grad_all, post_all, bias_all)
        for side in sides:
            here = layout.here(side)
            part_all[here] = back_to_input(pack_all.at[here], weights[side], 1, width)

    near = "v" if layer == 1 else "h"
    ins = [(meta, "s")] + [(item, near) for top in tops for item in top]
    ins += [*zip(joint, "vvv" if layer == 1 else "hhf")] + [(item, near) for item in small]
    ins += [(item, near) for item in (chooser, *qkvs, *probs)]
    ins += weight_inputs(att_in, att_out)
    outs = [
        ((layout.count, D), f32, "h"),
        layout.rows(HALF, bf16, 1),
        layout.rows(HALF + 3 * width, bf16, 2),
        ((layout.count, D), bf16, "h"),
        layout.each((3, D), 4),
        layout.each((2, width), 5),
    ]
    scratch = [
        pltpu.VMEM((n, 3, D, width), bf16),
        pltpu.VMEM((n, width, D), bf16),
        pltpu.SemaphoreType.DMA((n, 6)),
    ]
    scratch = [] if held else scratch
    name = f"self_backward_{layer}_" + "".join(map(str, sides))
    cost = 12.0 * layout.count / layout.total
    return call(body, ins, outs, scratch, cost, name, ties, 12 if held else 18)


def cross_backward(meta, tops, grads, owns, others, post, chooser, qkvs, probs, cross_in, cross_out, ties=()):
    rows = [qkv.shape[1] for qkv in qkvs]
    width = cross_out.shape[0]
    spans, total = spans_of(rows), sum(rows)

    def body(flush, meta, *refs):
        tops, grads, owns, others = (refs[:2], refs[2:4]), refs[4:6], refs[6:8], refs[8:10]
        post, chooser, qkvs, probs = refs[10], refs[11], refs[12:14], refs[14:16]
        in_ref, out_ref = refs[16:18]
        grad_all, selected_all, pack_all, part_all, post_out, bias_out = refs[18:24]
        in_buffer, out_buffer, post_each, sems = refs[24:]
        weights = Weights(
            meta,
            0,
            (maps(out_ref, None, 0), maps(in_ref, None, 0, ENTRY)),
            (out_buffer, in_buffer),
            sems,
        )
        packs = [pack_all.at[here] for here in spans]
        lows = []
        for side in (0, 1):
            here = spans[side]
            low = back_through_norm(
                tops[side],
                grads[side][...],
                summed(owns[side], others[side]),
                post[1:2],
                grad_all.at[here],
                post_each.at[side],
            )
            lows.append(low)
        post_out[...] = post_each[0] + post_each[1]
        leave = weights.get(0)
        for side in (0, 1):
            context = mm_nt(lows[side], leave[...]).astype(bf16)
            to_here, to_there = emit_into(packs[side], width), emit_into(packs[1 - side], width)

            def emit(kind, lanes, value):
                (to_here if kind == 0 else to_there)(kind, lanes, value)

            attend_back(
                qkvs[side][0], qkvs[1 - side][1], qkvs[1 - side][2], probs[side], context, emit
            )
        for side in (0, 1):
            select_rows(lows[side], chooser, selected_all.at[spans[side]], packs[side])
        bias_out[0:1] = column_sum(pack_all[:, HALF : HALF + width].astype(f32))
        bias_out[1:2] = column_sum(pack_all[:, HALF + 2 * width :].astype(f32))
        flush(pack_all, selected_all)
        part_all[...] = back_to_input(pack_all, weights, 1, width)

    ins = [(meta, "s")] + [(item, "h") for top in tops for item in top]
    ins += [(item, "h") for item in (*grads, *owns)] + [(item, "f") for item in others]
    ins += [(item, "h") for item in (post, chooser, *qkvs, *probs)]
    ins += [(cross_in, "w"), (cross_out, "w")]
    outs = [
        ((total, D), f32, "v"),
        ((total, HALF), bf16, "h"),
        ((total, HALF + 3 * width), bf16, "h"),
        ((total, D), bf16, "v"),
        ((3, D), f32, "h"),
        ((2, width), f32, "h"),
    ]
    scratch = [
        pltpu.VMEM((3, D, width), bf16),
        pltpu.VMEM((width, D), bf16),
        pltpu.VMEM((2, 3, D), f32),
        pltpu.SemaphoreType.DMA((6,)),
    ]
    return call(body, ins, outs, scratch, 10.0, "cross_backward", ties, 16)


class Block:
    def __init__(self, in_selected, in_packs, in_gots, out_selected, out_packs, out_gots):
        self.parts = [*in_selected, *in_packs, *in_gots, out_selected, *out_packs, *out_gots]
        self.counts = (len(in_packs), len(out_packs))
        self.lead = HALF
        self.kinds = "w" * len(self.parts)
        self.sizes = (out_packs[0].shape[1] - HALF, in_packs[0].shape[1] - HALF)
        self.rows = [array.shape[0] for array in in_selected]

    def buffers(self):
        return [
            pltpu.VMEM((2 * rows, HALF + size), bf16)
            for rows in self.rows
            for size in (self.sizes[1], self.sizes[0])
        ]

    def fetch(self, refs, buffers, sems, at):
        spans = spans_of(self.rows)
        in_selected, rest = refs[:2], refs[2:]
        n_in, n_out = self.counts
        pack, got, rest = rest[:n_in], rest[n_in : 2 * n_in], rest[2 * n_in :]
        out_selected, out_pack, out_got = rest[0], rest[1 : 1 + n_out], rest[1 + n_out :]

        def rows_of(items, side):
            return items[0].at[spans[side]] if len(items) == 1 else items[side]

        result = []
        for side in (0, 1):
            count = self.rows[side]
            per_side = []
            for kind, (selected, own, other) in enumerate(
                (
                    (in_selected[side], rows_of(pack, side), rows_of(got, side)),
                    (out_selected.at[spans[side]], rows_of(out_pack, side), rows_of(out_got, side)),
                )
            ):
                buffer = buffers[2 * side + kind]
                size = buffer.shape[1] - HALF
                mine = slice(0, count)
                copies = [
                    pltpu.make_async_copy(
                        selected, buffer.at[mine, pl.ds(0, HALF)], sems.at[at]
                    ),
                    pltpu.make_async_copy(
                        own.at[:, pl.ds(HALF, size)], buffer.at[mine, pl.ds(HALF, size)], sems.at[at + 1]
                    ),
                    pltpu.make_async_copy(
                        other, buffer.at[slice(count, 2 * count)], sems.at[at + 2]
                    ),
                ]
                at += 3
                for copy in copies:
                    copy.start()
                per_side.append((buffer, copies))
            result.append(per_side)
        return result, at


class Halves:
    def __init__(self, in_kept, in_gots, out_kept, out_gots):
        self.parts = [*in_kept, *in_gots, *out_kept, *out_gots]
        self.kinds = "w" * len(self.parts)
        self.lead = D
        self.sizes = (out_kept[0].shape[1] - D, in_kept[0].shape[1] - D)
        self.rows = [array.shape[0] for array in in_kept]

    def buffers(self):
        return [
            pltpu.VMEM((2 * rows, D + size), bf16)
            for rows in self.rows
            for size in (self.sizes[1], self.sizes[0])
        ]

    def fetch(self, refs, buffers, sems, at):
        result = []
        for side in (0, 1):
            count = self.rows[side]
            per_side = []
            for kind in (0, 1):
                buffer = buffers[2 * side + kind]
                copies = []
                for part in (0, 1):
                    target = buffer.at[slice(part * count, (part + 1) * count)]
                    source = refs[4 * kind + 2 * part + side]
                    copies.append(pltpu.make_async_copy(source, target, sems.at[at]))
                    copies[-1].start()
                    at += 1
                per_side.append((buffer, copies))
            result.append(per_side)
        return result, at


def chunk_order(groups):
    return [(s, z) for z in range(groups) for s in ((0, 1) if z % 2 == 0 else (1, 0))]


def places_chunks(groups):
    return (D // (2 * groups) // 2) % 16 == 0


def gradients(meta, blocks, cross, groups, name, ties=(), mode="ring"):
    lead = blocks[0].lead
    chunk = lead // groups
    half = chunk // 2
    size = chunk + half if cross else chunk
    order = chunk_order(groups)
    aligned = places_chunks(groups)
    width = sum(sum(block.sizes) for block in blocks)
    every = blocks + ([cross] if cross else [])
    n_in = sum(len(block.parts) for block in every)
    pair = mode == "split"
    n_out = 2 if pair else 1 if aligned else 3 if cross else 2
    n_sems = 12 * len(every) + 4 * len(every)

    def body(flush, meta, *refs):
        inputs, outputs, rest = refs[:n_in], refs[n_in : n_in + n_out], list(refs[n_in + n_out :])
        if cross:
            cross_stage = rest.pop()
        stage, sems = rest.pop(), rest.pop()
        at = 0
        fetched = []
        for block in every:
            taken, inputs = inputs[: len(block.parts)], inputs[len(block.parts) :]
            own, rest = rest[:4], rest[4:]
            copies, at = block.fetch(taken, own, sems, at)
            fetched.append(copies)
        waited, leaving = set(), []

        def leave(source, side, columns, at):
            if pair and not cross:
                kept, sent = (
                    pltpu.make_async_copy(source, target.at[:, columns], sems.at[at])
                    for target in outputs
                )
                pl.when(meta[0] == side)(kept.start)
                pl.when(meta[0] != side)(sent.start)
                leaving.append(kept)
                return
            if not aligned:
                copy = pltpu.make_async_copy(source, outputs[side].at[:, columns], sems.at[at])
                copy.start()
                leaving.append(copy)
                return
            if mode == "ring":
                for k, (s, z) in enumerate(order):
                    if side == 2:
                        start, count, place = (s * groups + z) * half, half, k * size + chunk
                    elif s == side:
                        start, count, place = z * chunk, chunk, k * size
                    else:
                        continue
                    copy = pltpu.make_async_copy(
                        source.at[pl.ds(start, count)],
                        outputs[0].at[pl.ds(place, count), columns],
                        sems.at[at],
                    )
                    copy.start()
                    leaving.append(copy)
                return
            for section in (0, 1) if side == 2 else (side,):
                for z in range(groups):
                    if side == 2:
                        start, count, place = (section * groups + z) * half, half, z * size + chunk
                    else:
                        start, count, place = z * chunk, chunk, z * size
                    kept, sent = (
                        pltpu.make_async_copy(
                            source.at[pl.ds(start, count)],
                            target.at[pl.ds(place, count), columns],
                            sems.at[at],
                        )
                        for target in outputs
                    )
                    pl.when(meta[0] == section)(kept.start)
                    pl.when(meta[0] != section)(sent.start)
                    leaving.append(kept)

        def ready(item):
            buffer, copies = item
            if id(buffer) not in waited:
                waited.add(id(buffer))
                for copy in copies:
                    copy.wait()
            return buffer

        base = 0
        for block, copies in zip(blocks, fetched):
            for side in (0, 1):
                start = base
                for left, right in ((0, 1), (1, 0)):
                    left, right = ready(copies[side][left]), ready(copies[side][right])
                    turned = left[:, :lead].T
                    span = right.shape[1] - lead
                    for step in range(0, span, HALF):
                        value = mm(turned, right[:, lead + step : lead + step + HALF])
                        stage[side, :, start + step : start + step + HALF] = value.astype(bf16)
                    columns = pl.ds(start, span)
                    leave(stage.at[side, :, columns], side, columns, at)
                    at += 1
                    start += span
            base += sum(block.sizes)
        if cross:
            copies = fetched[-1]
            start = 0
            for left, right in ((0, 1), (1, 0)):
                lefts = [ready(copies[side][left])[:, :HALF].T for side in (0, 1)]
                rights = [ready(copies[side][right]) for side in (0, 1)]
                span = rights[0].shape[1] - HALF
                for step in range(0, span, HALF):
                    columns = slice(HALF + step, HALF + step + HALF)
                    value = mm(lefts[0], rights[0][:, columns]) + mm(lefts[1], rights[1][:, columns])
                    cross_stage[:, start + step : start + step + HALF] = value.astype(bf16)
                columns = pl.ds(start, span)
                leave(cross_stage.at[:, columns], 2, columns, at)
                at += 1
                start += span
        for copy in leaving:
            copy.wait()

    ins = [(meta, "s")] + [pair for block in every for pair in zip(block.parts, block.kinds)]
    if pair:
        outs = [((groups * size, width), bf16, "w")] * 2
    elif aligned:
        outs = [((2 * groups * size, width), bf16, "w")]
    else:
        outs = [((lead, width), bf16, "w")] * n_out
    scratch = [buffer for block in every for buffer in block.buffers()]
    if cross:
        scratch += [
            pltpu.SemaphoreType.DMA((n_sems,)),
            pltpu.VMEM((2, lead, width), bf16),
            pltpu.VMEM((HALF, sum(cross.sizes)), bf16),
        ]
    else:
        scratch += [pltpu.SemaphoreType.DMA((n_sems,)), pltpu.VMEM((2, lead, width), bf16)]
    result = call(body, ins, outs, scratch, 6.0, name, ties, 20)
    if pair:
        return result
    if aligned:
        return result[0]
    chunks = [result[side].reshape(groups, chunk, width) for side in (0, 1)]
    pieces = [chunks[s][z] for s, z in order]
    if cross:
        extra = result[2].reshape(2, groups, half, width)
        pieces = [jnp.concatenate([one, extra[s, z]]) for one, (s, z) in zip(pieces, order)]
    return jnp.concatenate(pieces)


def placed_gradients(meta, first, second, chunk, width, units):
    def body(flush, meta, *refs):
        layers, last = (refs[:4], refs[4:8]), refs[7]
        feed_in, feed_out, att_in, att_out, cross_in, cross_out = refs[8:]
        for item in refs[:8]:
            item.wait()

        def store(layer):
            for side in (0, 1):
                feed, late = layers[layer][2 * side : 2 * side + 2]
                feed_in[side] = feed[:, :units].astype(f32)
                feed_out[side] = feed[:, units:].astype(f32)
                for j in range(3):
                    att_in[side, j] = late[:chunk, j * width : (j + 1) * width].astype(f32)
                att_out[side] = late[:chunk, 3 * width :].astype(f32)

        pl.when(meta[0] == 0)(partial(store, 0))
        pl.when(meta[0] != 0)(partial(store, 1))
        for j in range(3):
            cross_in[j] = last[chunk:, j * width : (j + 1) * width].astype(f32)
        cross_out[...] = last[chunk:, 3 * width :].astype(f32)

    ins = [(meta, "s")] + list(zip((*first, *second), "hfffffff"))
    half = chunk // 2
    outs = [
        ((2, chunk, units), f32, "h"),
        ((2, chunk, units), f32, "h"),
        ((2, 3, chunk, width), f32, "h"),
        ((2, chunk, width), f32, "h"),
        ((3, half, width), f32, "h"),
        ((half, width), f32, "h"),
    ]
    return call(body, ins, outs, (), 4.0, "placed_gradients")


def small_shape(width, units):
    n_feed = 2 * units // D
    sizes = (2 * 2 * width // D, 6, n_feed, 6, 2, 3, 2 * width // D, 1)
    starts = [sum(sizes[:i]) for i in range(len(sizes))]
    return starts, -(-sum(sizes) * D // (4 * width)) * 4 * width // D


def finished(meta, batch, rows, results, state_grad, layers, cross_post, cross_bias, ties):
    spans = spans_of(rows)
    width, units = cross_bias.shape[1], layers[0][2].shape[2]
    starts, total = small_shape(width, units)
    flat = [
        [*layer[:4], *layer[4], *layer[5], *layer[6]] for layer in layers
    ]
    counts = [len(layer) for layer in flat]

    def body(flush, meta, *refs):
        results, (grad, own, other), refs = refs[:2], refs[2:5], refs[5:]
        first, second, refs = refs[: counts[0]], refs[counts[0] : sum(counts)], refs[sum(counts) :]
        cross_post, cross_bias, refs = refs[0], refs[1], refs[2:]
        outs, mine, theirs, packs = refs[:4], refs[4], refs[5], refs[6]
        for k, layer in enumerate((first, second)):
            att_bias, att_post, feed_bias, feed_post, *squares = layer
            for side in (0, 1):
                for j in (0, 1):
                    place = (2 * side + j) * width
                    row, lane = starts[0] + place // D, place % D
                    packs[k, row : row + 1, lane : lane + width] = att_bias[side, j : j + 1]
                for start, post in ((starts[1], att_post), (starts[3], feed_post)):
                    packs[k, start + 3 * side : start + 3 * side + 3] = post[side]
                for j in range(units // D):
                    row = starts[2] + side * (units // D) + j
                    packs[k, row : row + 1] = feed_bias[side, :, j * D : (j + 1) * D]
            lead, middle, tails = squares[:2], squares[2:4], squares[4:]
            packs[k, starts[4] : starts[5]] = jnp.zeros((2, D), f32)
            for side in (0, 1):
                tail = tails[side] if len(tails) == 2 else tails[0].wait().at[side]
                terms = (lead[side][0:1], middle[side][0:1], tail[0:1], tail[1:2])
                for j, term in enumerate(terms):
                    at = 4 * side + j
                    row, lane = starts[4] + at // 6, at % 6 * 128
                    packs[k, row : row + 1, lane : lane + 128] = term
            packs[k, starts[5] : starts[6]] = cross_post[...]
            for j in (0, 1):
                row, lane = starts[6] + j * width // D, j * width % D
                packs[k, row : row + 1, lane : lane + width] = cross_bias[j : j + 1]
            lane = lax.broadcasted_iota(jnp.int32, (1, D), 1)
            count = jnp.zeros((1, D), f32)
            for side in (0, 1):
                for i in range(batch):
                    length = meta[1 + side * batch + i].astype(f32)
                    count += jnp.where(lane == side, length, 0.0)
            packs[k, starts[7] : starts[7] + 1] = count
            if total > starts[7] + 1:
                packs[k, starts[7] + 1 :] = jnp.zeros((total - starts[7] - 1, D), f32)
        mine[...] = packs[meta[0]]
        theirs[...] = packs[1 - meta[0]]
        flush(mine, theirs)
        for side in (0, 1):
            here = spans[side]
            whole = results[side][...].astype(f32)
            back = (grad[here] + summed_rows(own, other, here)).astype(bf16).astype(f32)
            for slot in range(rows[side] // batch):
                these = slice(slot * batch, (slot + 1) * batch)
                outs[side][slot] = whole[these].astype(bf16)
                outs[2 + side][slot] = back[these].astype(bf16)

    ins = [(meta, "s")] + [(item, "f") for item in results] + list(zip(state_grad, "fff"))
    ins += [(item, "f") for layer in flat for item in layer]
    ins += [(cross_post, "f"), (cross_bias, "f")]
    outs = [((count // batch, batch, D), bf16, "h") for count in (*rows, *rows)]
    outs += [((total, D), f32, "h")] * 2
    scratch = [pltpu.VMEM((2, total, D), f32)]
    return call(body, ins, outs, scratch, 4.0, "finished", ties)


def unpacked(sums, width, units):
    starts, _ = small_shape(width, units)

    def body(flush, sums, att_bias, att_post, feed_bias, feed_post, cross_bias, cross_post, scales):
        for side in (0, 1):
            for j in (0, 1):
                place = (2 * side + j) * width
                row, lane = starts[0] + place // D, place % D
                att_bias[0, side, j : j + 1] = sums[row : row + 1, lane : lane + width]
            for start, post in ((starts[1], att_post), (starts[3], feed_post)):
                for j in range(3):
                    row = start + 3 * side + j
                    post[0, j, side : side + 1] = sums[row : row + 1]
            for j in range(units // D):
                row = starts[2] + side * (units // D) + j
                feed_bias[0, side : side + 1, j * D : (j + 1) * D] = sums[row : row + 1]
        cross_post[...] = sums[starts[5] : starts[6]]
        for j in (0, 1):
            row, lane = starts[6] + j * width // D, j * width % D
            cross_bias[j : j + 1] = sums[row : row + 1, lane : lane + width]
        counts = sums[starts[7] : starts[7] + 1]
        lane = lax.broadcasted_iota(jnp.int32, (1, 8), 1)
        result = jnp.zeros((1, 8), f32)
        for at in range(8):
            row, place = starts[4] + at // 6, at % 6 * 128
            square = sums[row : row + 1, place : place + 1]
            scale = jnp.sqrt(square / (counts[:, at // 4 : at // 4 + 1] * D))
            result = jnp.where(lane == at, scale, result)
        scales[...] = result

    outs = [
        ((1, 2, 2, width), f32, "h"),
        ((1, 3, 2, D), f32, "h"),
        ((1, 2, units), f32, "h"),
        ((1, 3, 2, D), f32, "h"),
        ((2, width), f32, "h"),
        ((3, D), f32, "h"),
        ((1, 8), f32, "h"),
    ]
    return call(body, [(sums, "f")], outs, (), 2.0, "unpacked")


def prepared(ids, lengths, att_bias, att_post, feed_bias, feed_post):
    batch = lengths[0].shape[1]
    n_feed = feed_bias.shape[2] // D
    n_ids = ids.shape[0]

    def body(flush, ids, words, regions, att_bias, att_post, feed_bias, feed_post, small, meta):
        meta[0] = ids[0]
        for i in range(1, n_ids):
            meta[2 * batch + i] = ids[i]
        for side, counts in enumerate((words, regions)):
            for i in range(batch):
                meta[1 + side * batch + i] = counts[ids[0], i]
        half = att_bias.shape[3]
        for side in (0, 1):
            for j in (0, 1):
                small[side, ROW_ATT_BIAS : ROW_ATT_BIAS + 1, j * half : (j + 1) * half] = att_bias[
                    0, side, j : j + 1
                ]
            for j in range(3):
                for row, post in ((ROW_ATT_POST, att_post), (ROW_FEED_POST, feed_post)):
                    small[side, row + j : row + j + 1] = post[0, j, side : side + 1]
            for j in range(n_feed):
                row = ROW_FEED_BIAS + j
                small[side, row : row + 1] = feed_bias[0, side : side + 1, j * D : (j + 1) * D]
            end = ROW_FEED_POST + 3
            small[side, end:] = jnp.zeros((SMALL_ROWS - end, D), f32)

    ins = [(ids, "s"), (lengths[0], "s"), (lengths[1], "s")]
    ins += [(item, "h") for item in (att_bias, att_post, feed_bias, feed_post)]
    outs = [((2, SMALL_ROWS, D), f32, "h"), ((n_ids + 2 * batch,), jnp.int32, "s")]
    return call(body, ins, outs, (), 1.0, "prepared")


def swap(value, axis, distance=1):
    count = lax.axis_size(axis)
    return lax.ppermute(value, axis, [(i, i ^ distance) for i in range(count)])


def total_of(parts):
    return sum(part.astype(f32) for part in parts).astype(bf16)


class Halving:
    def __init__(self, parts, groups):
        self.parts = [part.reshape(groups, -1, part.shape[1]) for part in parts]
        self.position, self.distance, self.groups = lax.axis_index("dp") // 2, 2, groups

    def half(self, bit):
        split = [part.reshape(-1, 2, *part.shape[1:]) for part in self.parts]
        return [lax.dynamic_index_in_dim(part, bit, 1, keepdims=False) for part in split]

    def send(self, *after, extra=None):
        self.parts = behind(self.parts, after)
        bit = self.position % 2
        chunks = total_of(self.half(1 - bit))
        payload = chunks.reshape(-1, chunks.shape[-1])
        count = payload.shape[0]
        if extra is not None:
            low = extra.astype(bf16).reshape(-1, payload.shape[1])
            payload = jnp.concatenate([payload, low])
        got = swap(payload, "dp", self.distance)
        self.parts = self.half(bit) + [got[:count].reshape(chunks.shape)]
        self.position, self.distance = self.position // 2, 2 * self.distance
        self.groups //= 2
        if extra is None:
            return payload
        return payload, (low.astype(f32) + got[count:].astype(f32)).reshape(extra.shape)

    def finish(self, *after):
        while self.groups > 1:
            self.send()
        return total_of([part[0] for part in behind(self.parts, after)])


def behind(values, after):
    return lax.optimization_barrier((values, after))[0] if after else values


def on_device(
    word_state,
    region_state,
    word_lengths,
    region_counts,
    word_cotangent,
    region_cotangent,
    cross_in,
    cross_bias,
    cross_out,
    cross_post,
    attention_in,
    attention_bias,
    attention_out,
    attention_post,
    feed_in,
    feed_bias,
    feed_out,
    feed_post,
):
    section = lax.axis_index("section")
    dp_count = lax.axis_size("dp")
    groups = dp_count // 2
    place = lax.axis_index("dp") % 2
    batch = word_state.shape[1]
    width = cross_out.shape[0]
    units = feed_in.shape[-1]
    both = (0, 1)
    chains = [[s * dp_count + 2 * z + y for s, z in chunk_order(groups)] for y in both]

    def unflat(value):
        return value.reshape(-1, batch, D).transpose(1, 0, 2)[None]

    def chooser_of(pieces, per_section):
        column = jnp.arange(D)
        half = column // HALF
        inner = column % HALF
        side = jnp.where(half == 0, place, 1 - place)
        size = D // pieces
        if per_section:
            block = inner // (HALF // 2)
            inner = inner % (HALF // 2)
            feature = size * (dp_count * block + 2 * (inner // size) + side) + inner % size
        else:
            feature = size * (2 * (inner // size) + side) + inner % size
        return (jnp.arange(D)[:, None] == feature[None, :]).astype(bf16)

    chooser = chooser_of(dp_count, False)
    cross_chooser = chooser_of(2 * dp_count, True)

    ids = jnp.stack([section, place]).astype(jnp.int32)
    small_own, meta = prepared(
        ids,
        (word_lengths, region_counts),
        attention_bias,
        attention_post.transpose(0, 2, 1, 3),
        feed_bias,
        feed_post.transpose(0, 2, 1, 3),
    )
    small = (small_own, swap(small_own, "section"))
    att_in_own = attention_in.transpose(0, 1, 3, 2, 4)
    att_in = (att_in_own, swap(att_in_own, "section"))
    att_out = (attention_out, swap(attention_out, "section"))
    states = [value.transpose(0, 2, 1, 3) for value in (word_state, region_state)]
    feed_in_later, feed_out_later, *_ = lax.optimization_barrier(
        (feed_in, feed_out, att_in[1], att_out[1], small[1], chooser, cross_chooser)
    )
    ff_in = (feed_in, swap(feed_in_later, "section"))
    ff_out = (feed_out, swap(feed_out_later, "section"))
    cross_entry = cross_in.transpose(1, 0, 2)

    cotangents = [value.transpose(0, 2, 1, 3) for value in (word_cotangent, region_cotangent)]
    rows = [state.shape[1] * batch for state in states]
    total_rows = sum(rows)

    def in_order(step, pack_index, tie=None, joined=True, order=(1, 0)):
        results = [None, None]
        given = None
        for side in order:
            ties = () if tie is None else (tie,)
            place = (total_rows, rows[0] * side, given) if joined else ()
            results[side] = step(side, place, ties)
            tie, given = results[side][pack_index + 2], results[side][pack_index]
        return results

    def over_mp(results, index):
        return [swap(results[side][index], "mp") for side in both]

    self0 = in_order(
        lambda side, place, ties: self_forward(
            side, 0, batch, meta, states[side], None, small, chooser, att_in, att_out,
            place, ties,
        ),
        3,
    )
    got = over_mp(self0, 4)
    feed0 = in_order(
        lambda side, place, ties: feed_forward(
            side, 0, batch, meta, self0[side][6], self0[side][4], got[side], small, chooser,
            ff_in, ff_out, place, ties,
        ),
        4,
        self0[0][5],
    )
    got = over_mp(feed0, 6)
    self0_there = swap(self0[0][3], "dp")
    cross_w, cross_r, cross_pack, held = cross_forward(
        batch,
        meta,
        [(feed0[side][0], feed0[side][6], got[side]) for side in both],
        small,
        cross_chooser,
        cross_entry,
        cross_bias,
        cross_out,
        (att_in, att_out, ff_in),
    )
    att_in1, att_out1, ff_in1 = [(item,) for item in held]
    cross = (cross_w, cross_r)
    got = over_mp(cross, 7)
    feed0_there = swap(feed0[0][4], "dp")
    self1 = in_order(
        lambda side, place, ties: self_forward(
            side, 1, batch, meta, cross[side][0], (cross[side][7], got[side], cross_post),
            small, chooser, att_in1, att_out1, place, ties + ((self0_there, "a"),),
            (ff_out,) if side == ORDER[0] else (),
        ),
        3,
        None,
        True,
        ORDER,
    )
    ff_out1 = (self1[ORDER[0]][9],)
    got = over_mp(self1, 4)
    cross_there = swap(cross_pack, "dp")
    feed1 = in_order(
        lambda side, place, ties: feed_forward(
            side, 1, batch, meta, self1[side][6], self1[side][4], got[side], small, chooser,
            ff_in1, ff_out1, place, ties + (((feed0_there, "a"),) if side == ORDER[0] else ()),
        ),
        4,
        self1[ORDER[-1]][5],
        False,
        ORDER,
    )
    got = over_mp(feed1, 6)
    self1_there = swap(self1[ORDER[-1]][3], "dp")
    feed1_there = [swap(feed1[side][4], "dp") for side in both]

    def over_sections_and_groups(value):
        return lax.psum_scatter(
            value, ("section", "dp"), scatter_dimension=0, axis_index_groups=chains, tiled=True
        )

    def over_groups(value):
        pairs = [[2 * z + y for z in range(groups)] for y in both]
        return lax.psum_scatter(
            value, "dp", scatter_dimension=0, axis_index_groups=pairs, tiled=True
        )

    given, back_feed1 = None, [None, None]
    for side in ORDER:
        given = feed_backward(
            1,
            (side,),
            rows,
            batch,
            meta,
            [(feed1[side][0], feed1[side][6], got[side], cotangents[side])],
            None,
            small,
            chooser,
            [feed1[side][5]],
            ff_in1,
            ff_out1,
            ((feed1_there[side], "a"), (cross_there, "a")) if side == ORDER[0] else (),
            given,
        )
        back_feed1[side] = given
    got = over_mp(back_feed1, 3)
    back_feed1_there = [swap(back_feed1[side][2], "dp") for side in both]

    given, back_self1 = None, [None, None]
    for side in ORDER:
        given = self_backward(
            1,
            (side,),
            rows,
            meta,
            [feed1[side][1:3]],
            (back_feed1[side][0], back_feed1[side][3], got[side]),
            small,
            chooser,
            [self1[side][0]],
            [self1[side][1]],
            att_in1,
            att_out1,
            (
                ((feed1_there[ORDER[-1]], "a"), (back_feed1_there[ORDER[0]], "a"))
                if side == ORDER[0]
                else ()
            ),
            given,
        )
        back_self1[side] = given
    got = over_mp(back_self1, 3)
    feed1_grads = gradients(
        meta,
        [
            Halves(
                [feed1[side][3] for side in both],
                feed1_there,
                [back_feed1[side][1] for side in both],
                back_feed1_there,
            )
        ],
        None,
        groups,
        "feed_gradients_1",
        (back_self1[ORDER[-1]][5],),
    )
    feed1_pair = over_sections_and_groups(feed1_grads).reshape(2, D // dp_count, -1)
    back_self1_there = swap(back_self1[ORDER[-1]][2], "dp")
    back_cross = cross_backward(
        meta,
        [self1[side][7:9] for side in both],
        [back_self1[side][0] for side in both],
        [back_self1[side][3] for side in both],
        got,
        cross_post,
        cross_chooser,
        [cross[side][5] for side in both],
        [cross[side][6] for side in both],
        cross_entry,
        cross_out,
        (feed1_grads,),
    )
    cross_post_grad, cross_bias_grad = back_cross[4:6]
    got = swap(back_cross[3], "mp")
    back_cross_there = swap(back_cross[2], "dp")
    back_feed0 = feed_backward(
        0,
        (1, 0),
        rows,
        batch,
        meta,
        [cross[side][1:3] for side in (1, 0)],
        (back_cross[0], back_cross[3], got),
        small,
        chooser,
        [feed0[side][5] for side in (1, 0)],
        ff_in,
        ff_out,
        ((back_self1_there, "a"),),
    )
    got = swap(back_feed0[3], "mp")
    back_feed0_there = swap(back_feed0[2], "dp")
    late1_grads = gradients(
        meta,
        [
            Block(
                [self1[side][2] for side in both],
                [self1[ORDER[-1]][3]],
                [self1_there],
                back_self1[ORDER[-1]][1],
                [back_self1[ORDER[-1]][2]],
                [back_self1_there],
            )
        ],
        Block(
            [cross[side][4] for side in both],
            [cross_pack],
            [cross_there],
            back_cross[1],
            [back_cross[2]],
            [back_cross_there],
        ),
        groups,
        "late_gradients_1",
        (back_feed0[5],),
    )
    late1_share = over_sections_and_groups(late1_grads)
    back_self0 = self_backward(
        0,
        (1, 0),
        rows,
        meta,
        [feed0[side][1:3] for side in (1, 0)],
        (back_feed0[0], back_feed0[3], got),
        small,
        chooser,
        [self0[side][0] for side in (1, 0)],
        [self0[side][1] for side in (1, 0)],
        att_in,
        att_out,
        (late1_grads,),
    )
    got = swap(back_self0[3], "mp")
    back_self0_there = swap(back_self0[2], "dp")
    feed0_grads = gradients(
        meta,
        [
            Block(
                [feed0[side][3] for side in both],
                [feed0[0][4]],
                [feed0_there],
                back_feed0[1],
                [back_feed0[2]],
                [back_feed0_there],
            )
        ],
        None,
        groups,
        "feed_gradients_0",
        (back_self0[5], feed1_pair),
        "split",
    )
    feed0_total = total_of([feed0_grads[0], swap(feed0_grads[1], "section")])
    self0_grads = gradients(
        meta,
        [
            Block(
                [self0[side][2] for side in both],
                [self0[0][3]],
                [self0_there],
                back_self0[1],
                [back_self0[2]],
                [back_self0_there],
            )
        ],
        None,
        groups,
        "self_gradients_0",
        (feed0_total,),
        "split",
    )
    feed0_share = over_groups(feed0_total)
    self0_parts = [self0_grads[0], swap(self0_grads[1], "section")]
    if groups & (groups - 1) == 0:
        halving = Halving(self0_parts, groups)
        self0_sent = halving.send() if groups > 1 else self0_parts[0]
    else:
        halving = None
        self0_sent = total_of(self0_parts)
    chunk = D // dp_count
    word_full, region_full, word_back, region_back, mine, theirs = finished(
        meta,
        batch,
        rows,
        [back_feed1[side][7] for side in both],
        (back_self0[0], back_self0[3], got),
        [
            (
                back_self0[5],
                back_self0[4],
                back_feed0[5],
                back_feed0[4],
                [self0[side][5] for side in both],
                [feed0[side][7] for side in both],
                [cross[side][3] for side in both],
            ),
            (
                back_self1[ORDER[-1]][5],
                back_self1[ORDER[-1]][4],
                back_feed1[ORDER[-1]][5],
                back_feed1[ORDER[-1]][4],
                [self1[side][5] for side in both],
                [feed1[side][7] for side in both],
                [back_feed1[ORDER[-1]][6]],
            ),
        ],
        cross_post_grad,
        cross_bias_grad,
        (self0_sent,),
    )
    total = mine + swap(theirs, "section")
    distance = 1
    while 2 * distance < dp_count:
        total, distance = total + swap(total, "dp", distance), 2 * distance
    if halving and groups > 2:
        while halving.groups > 2:
            halving.send(total)
        last_sent, total = halving.send(total, extra=total)
    else:
        last_sent, total = total, total + swap(total, "dp", distance)
    feed1_pair, late1_share = behind((feed1_pair, late1_share), (last_sent,))
    feed1_own = lax.dynamic_index_in_dim(feed1_pair, place, 0, keepdims=False)
    feed1_other = swap(lax.dynamic_index_in_dim(feed1_pair, 1 - place, 0, keepdims=False), "dp")
    halves = (
        jnp.where(place == 0, feed1_own, feed1_other),
        jnp.where(place == 0, feed1_other, feed1_own),
    )
    count = units // 2
    feed1_share = jnp.concatenate(
        [half[:, j * count : (j + 1) * count] for j in both for half in halves], axis=1
    )
    late_words = [
        lax.ppermute(value, "section", [(0, 1)]) for value in (feed1_share, late1_share[:chunk])
    ]
    self0_share = halving.finish(late_words) if halving else over_groups(self0_sent)
    self_regions = lax.ppermute(self0_share, "section", [(1, 0)])
    feed_regions = lax.ppermute(feed0_share, "section", [(1, 0)])
    feed_in_grad, feed_out_grad, att_in_grad, att_out_grad, cross_in_grad, cross_out_grad = (
        placed_gradients(
            meta,
            (feed0_share, self0_share, feed_regions, self_regions),
            (*late_words, feed1_share, late1_share),
            chunk,
            width,
            units,
        )
    )
    outputs = unpacked(total, width, units)
    feed_in_grad = feed_in_grad[None]
    feed_out_grad = feed_out_grad.transpose(0, 2, 1)[None]
    att_in_grad = att_in_grad.transpose(0, 2, 1, 3)[None]
    att_out_grad = att_out_grad.transpose(0, 2, 1)[None]
    cross_in_grad = cross_in_grad.transpose(1, 0, 2)
    cross_out_grad = cross_out_grad.T
    att_bias_grad, att_post_grad, feed_bias_grad, feed_post_grad, cross_bias_grad, cross_post_grad = (
        outputs[:6]
    )
    return (
        word_full.transpose(1, 0, 2)[None],
        region_full.transpose(1, 0, 2)[None],
        word_back.transpose(1, 0, 2)[None],
        region_back.transpose(1, 0, 2)[None],
        cross_in_grad,
        cross_bias_grad,
        cross_out_grad,
        cross_post_grad,
        att_in_grad,
        att_bias_grad,
        att_out_grad,
        att_post_grad.transpose(0, 2, 1, 3),
        feed_in_grad,
        feed_bias_grad,
        feed_out_grad,
        feed_post_grad.transpose(0, 2, 1, 3),
        outputs[6],
    )


def solution(mesh):
    placed = (
        P(None, "dp", None, None),
        P(None, "dp", None, None),
        P(None, "dp"),
        P(None, "dp"),
        P(None, "dp", None, None),
        P(None, "dp", None, None),
        P(None, None, "mp"),
        P(None, "mp"),
        P("mp", None),
        P(),
        P("section", None, None, None, "mp"),
        P("section", None, None, "mp"),
        P("section", None, "mp", None),
        P("section", None, None, None),
        P("section", None, None, "mp"),
        P("section", None, "mp"),
        P("section", None, "mp", None),
        P("section", None, None, None),
    )
    return jax.shard_map(
        on_device,
        mesh=mesh,
        in_specs=placed,
        out_specs=(
            P("section", "dp", None, None),
            P("section", "dp", None, None),
            P("section", "dp", None, None),
            P("section", "dp", None, None),
            P(("section", "dp"), None, "mp"),
            P(None, "mp"),
            P("mp", ("section", "dp")),
            P(),
            P("section", None, "dp", None, "mp"),
            P("section", None, None, "mp"),
            P("section", None, "mp", "dp"),
            P("section", None, None, None),
            P("section", None, "dp", "mp"),
            P("section", None, "mp"),
            P("section", None, "mp", "dp"),
            P("section", None, None, None),
            P("section", None),
        ),
        check_vma=False,
    )
```

```python
from functools import partial

import jax
import jax.numpy as jnp
from jax import lax
from jax.experimental import pallas as pl
from jax.experimental.pallas import tpu as pltpu
from jax.sharding import PartitionSpec as P

D = 768
HALF = D // 2
HEAD_DIM = 64
PAIR = 2 * HEAD_DIM
WORDS = 20
REGIONS = 36
EPS = 1e-06
SCALE = HEAD_DIM**-0.5
COST_SCALE = 0.5
ORDER = (0, 1)
bf16 = jnp.bfloat16
f32 = jnp.float32

ROW_ATT_BIAS, ROW_ATT_POST, ROW_FEED_BIAS, ROW_FEED_POST, SMALL_ROWS = 0, 1, 4, 6, 16


def mm(a, b):
    return jnp.dot(a, b, preferred_element_type=f32)


def mm_nt(a, b):
    return lax.dot_general(a, b, (((1,), (1,)), ((), ())), preferred_element_type=f32)


def mm_tn(a, b):
    return lax.dot_general(a, b, (((0,), (0,)), ((), ())), preferred_element_type=f32)


def norm_of(value, gain, shift):
    centred = value - jnp.mean(value, axis=-1, keepdims=True)
    spread = jnp.mean(centred * centred, axis=-1, keepdims=True)
    rstd = lax.rsqrt(spread + EPS)
    unit = centred * rstd
    return unit, rstd, unit * gain + shift


def norm_back(unit, rstd, gain, incoming):
    scaled = incoming * gain
    mean = jnp.mean(scaled, axis=-1, keepdims=True)
    along = jnp.mean(scaled * unit, axis=-1, keepdims=True)
    return (scaled - mean - unit * along) * rstd


def summed(own, other):
    return own[...].astype(f32) + other[...].astype(f32)


def column_sum(value):
    return jnp.sum(value, axis=0, keepdims=True)


def square_sum(value, valid):
    rows = jnp.sum(value * value, axis=-1, keepdims=True) * valid
    return jnp.broadcast_to(jnp.sum(rows, axis=0, keepdims=True), (1, 128))


def lengths_of(meta, side, batch, item):
    result = jnp.zeros_like(item)
    for i in range(batch):
        result = jnp.where(item == i, meta[1 + side * batch + i], result)
    return result


def row_valid(meta, side, batch, rows):
    index = lax.broadcasted_iota(jnp.int32, (rows, 1), 0)
    length = lengths_of(meta, side, batch, lax.rem(index, batch))
    return (lax.div(index, batch) < length).astype(f32)


def pair_valid(meta, side, batch, rows, keys):
    index = lax.broadcasted_iota(jnp.int32, (1, keys), 1)
    item = lax.rem(index, batch)
    length = lengths_of(meta, side, batch, item)
    item = jnp.where(lax.div(index, batch) < length, item, -1)
    row_item = lax.rem(lax.broadcasted_iota(jnp.int32, (rows, 1), 0), batch)
    return jnp.broadcast_to(row_item, (rows, keys)) == jnp.broadcast_to(item, (rows, keys))


def head_lanes(head):
    lane = lax.broadcasted_iota(jnp.int32, (1, PAIR), 1)
    return (lane // HEAD_DIM) == head


def attend(query, keys, values, valid, probs_ref, context_ref):
    for pair in range(query.shape[1] // PAIR):
        lanes = slice(pair * PAIR, (pair + 1) * PAIR)
        contexts = []
        for head in range(2):
            chosen = query[:, lanes] * head_lanes(head).astype(bf16)
            scores = mm_nt(chosen, keys[:, lanes]) * SCALE
            scores = jnp.where(valid, scores, -1e9)
            shifted = jnp.exp(scores - jnp.max(scores, axis=-1, keepdims=True))
            total = jnp.sum(shifted, axis=-1, keepdims=True)
            probs = (shifted * (1.0 / total)).astype(bf16)
            probs_ref[2 * pair + head] = probs
            contexts.append(mm(probs, values[:, lanes]))
        context_ref[:, lanes] = jnp.where(head_lanes(0), contexts[0], contexts[1]).astype(bf16)


def attend_back(query, keys, values, probs_ref, grad_context, emit):
    first = head_lanes(0)
    for pair in range(query.shape[1] // PAIR):
        lanes = slice(pair * PAIR, (pair + 1) * PAIR)
        grads = ([], [], [])
        for head in range(2):
            probs = probs_ref[2 * pair + head]
            chosen = grad_context[:, lanes] * head_lanes(head).astype(bf16)
            grad_probs = mm_nt(chosen, values[:, lanes])
            wide = probs.astype(f32)
            product = wide * grad_probs
            grad_scores = product - wide * jnp.sum(product, axis=-1, keepdims=True)
            grad_scores = grad_scores.astype(bf16)
            grads[0].append(mm(grad_scores, keys[:, lanes]) * SCALE)
            grads[1].append(mm_tn(grad_scores, query[:, lanes]) * SCALE)
            grads[2].append(mm_tn(probs, grad_context[:, lanes]))
        for kind in range(3):
            emit(kind, lanes, jnp.where(first, grads[kind][0], grads[kind][1]).astype(bf16))


def small_of(meta, layer, side, own, other):
    return jnp.where(meta[0] == layer, own[side], other[side])


class Fetched:
    def __init__(self, copy, buffer):
        self.copy, self.buffer, self.waited = copy, buffer, False
        self.shape, self.dtype = buffer.shape, buffer.dtype

    def wait(self):
        if not self.waited:
            self.copy.wait()
            self.waited = True
        return self.buffer

    def __getitem__(self, index):
        return self.wait()[index]


class Weights:
    def __init__(self, meta, layer, pairs, buffers, sems):
        self.copies = []
        mine = meta[0] == layer
        at = 0
        for (own, other, pieces), buffer in zip(pairs, buffers):
            copies = []
            for piece in pieces:
                copy = pltpu.make_async_copy(own.at[piece], buffer.at[piece], sems.at[at])
                if other is None:
                    copy.start()
                else:
                    second = pltpu.make_async_copy(
                        other.at[piece], buffer.at[piece], sems.at[at]
                    )
                    pl.when(mine)(copy.start)
                    pl.when(jnp.logical_not(mine))(second.start)
                copies.append(Fetched(copy, buffer))
                at += 1
            self.copies.append(copies)

    def get(self, slot, piece=None):
        copies = self.copies[slot]
        for copy in copies if piece is None else (copies[piece],):
            copy.wait()
        return copies[0].buffer


class Held:
    def __init__(self, *refs):
        self.refs = refs

    def get(self, slot, piece=None):
        return self.refs[slot]


def weight_inputs(entry, leave, kinds="wwww"):
    if len(entry) == 1:
        return [(entry[0], "v"), (leave[0], "v")]
    return list(zip(entry + leave, kinds))


def pass_on(meta, layer, offered, taken, sems):
    copies = []
    for i, target in enumerate(taken):
        own = pltpu.make_async_copy(offered[2 * i].at[0], target, sems.at[i])
        other = pltpu.make_async_copy(offered[2 * i + 1].at[0], target, sems.at[i])
        pl.when(meta[0] == layer)(own.start)
        pl.when(meta[0] != layer)(other.start)
        copies.append(own)
    return copies


def items_of(meta, source, raw, rows_ref, sem, batch):
    copy = pltpu.make_async_copy(source.at[meta[0]], raw, sem)
    copy.start()
    copy.wait()
    for slot in range(raw.shape[0]):
        rows_ref[slot * batch : (slot + 1) * batch] = raw[slot].astype(f32)


def maps(own, other, side, pieces=((),)):
    if other is None:
        return own, None, pieces
    return own.at[0, side], other.at[0, side], pieces


ENTRY = ((0,), (1,), (2,))


def column_pieces(size, count):
    return tuple(
        (slice(None), slice(i * size // count, (i + 1) * size // count)) for i in range(count)
    )


def row_pieces(size, count):
    return tuple((slice(i * size // count, (i + 1) * size // count),) for i in range(count))


def call(body, ins, outs, scratch=(), cost=0.0, name=None, ties=(), mib=14):
    spaces = {
        "s": pltpu.SMEM, "v": pltpu.VMEM, "w": pltpu.HBM, "h": pltpu.HBM, "a": pl.ANY, "f": pl.ANY
    }
    ties = [tie if isinstance(tie, tuple) else (tie, "w") for tie in ties]
    extra = [(i, out[5]) for i, out in enumerate(outs) if len(out) > 3 and out[5] is not None]
    aliases = {len(ins) + at: i for at, (i, _) in enumerate(extra)}
    ins = list(ins) + [(array, "w") for _, array in extra]
    places = [out[3:5] if len(out) > 3 else None for out in outs]
    fetched = [i for i, (_, kind) in enumerate(ins) if kind in "hf"]
    written = [i for i, out in enumerate(outs) if out[2] == "h"]
    n_ins, n_ties, n_outs, n_scratch = len(ins), len(ties), len(outs), len(scratch)

    def whole(*refs):
        given = list(refs[:n_ins])
        results = list(refs[n_ins + n_ties : n_ins + n_ties + n_outs])
        rest = refs[n_ins + n_ties + n_outs :]
        own, rest = rest[:n_scratch], rest[n_scratch:]
        buffers, rest = rest[: len(fetched)], rest[len(fetched) :]
        staged, rest = rest[: len(written)], rest[len(written) :]
        sems = rest[0] if rest else None
        for slot, i in enumerate(fetched):
            copy = pltpu.make_async_copy(given[i], buffers[slot], sems.at[slot])
            copy.start()
            given[i] = Fetched(copy, buffers[slot])
        leaving = {}
        for slot, i in enumerate(written):
            target = results[i]
            if places[i] is not None:
                target = target.at[pl.ds(places[i][1], staged[slot].shape[0])]
            copy = pltpu.make_async_copy(staged[slot], target, sems.at[len(fetched) + slot])
            leaving[id(staged[slot])] = copy
            results[i] = staged[slot]
        started = []

        def flush(*done):
            for ref in done:
                copy = leaving.pop(id(ref), None)
                if copy is not None:
                    copy.start()
                    started.append(copy)

        body(flush, *given[: n_ins - len(extra)], *results, *own)
        flush(*[staged[slot] for slot in range(len(written))])
        for copy in started:
            copy.wait()
        for item in given:
            if isinstance(item, Fetched):
                item.wait()

    arrays = [
        pltpu.with_memory_space_constraint(array, spaces[kind]) if kind in "vwh" else array
        for array, kind in [*ins, *ties]
    ]
    own_scratch = list(scratch)
    own_scratch += [pltpu.VMEM(arrays[i].shape, arrays[i].dtype) for i in fetched]
    own_scratch += [pltpu.VMEM(outs[i][0], outs[i][1]) for i in written]
    if fetched or written:
        own_scratch.append(pltpu.SemaphoreType.DMA((len(fetched) + len(written),)))
    return pl.pallas_call(
        whole,
        out_shape=[
            spaces[out[2]]((out[3], *out[0][1:]) if len(out) > 3 else out[0], out[1]) for out in outs
        ],
        in_specs=[pl.BlockSpec(memory_space=spaces[kind]) for _, kind in [*ins, *ties]],
        out_specs=[pl.BlockSpec(memory_space=spaces[out[2]]) for out in outs],
        input_output_aliases=aliases,
        scratch_shapes=own_scratch,
        compiler_params=pltpu.CompilerParams(vmem_limit_bytes=mib * 1024 * 1024),
        cost_estimate=pl.CostEstimate(
            flops=int(cost * COST_SCALE * 1.15e9), bytes_accessed=0, transcendentals=0
        ),
        name=name,
    )(*arrays)


def spans_of(rows):
    return slice(0, rows[0]), slice(rows[0], rows[0] + rows[1])


def select_rows(value, chooser, own_ref, pack_ref):
    moved = mm(value, chooser[...]).astype(bf16)
    own_ref[...] = moved[:, :HALF]
    pack_ref[:, :HALF] = moved[:, HALF:]


def project(low, weights, bias_q, bias_v, qkv_ref):
    qkv_ref[0] = (mm(low, weights.get(0, 0)[0]) + bias_q).astype(bf16)
    qkv_ref[1] = mm(low, weights.get(0, 1)[1]).astype(bf16)
    qkv_ref[2] = (mm(low, weights.get(0, 2)[2]) + bias_v).astype(bf16)


def self_forward(
    side, layer, batch, meta, state, prior, small, chooser, att_in, att_out, place, ties=(), later=()
):
    rows = state.shape[1] * batch if prior is None else state.shape[0]
    width = att_in[0].shape[-1]
    first = prior is None
    held, n_maps = len(att_in) == 1, len(att_in + att_out)

    def body(flush, meta, state, *refs):
        refs = list(refs)
        if not first:
            own, other, post = refs[:3]
            refs = refs[3:]
        small = small_of(meta, layer, side, refs[0], refs[1])
        chooser, refs = refs[2], refs[3:]
        given, refs = refs[:n_maps], refs[n_maps:]
        offered, refs = refs[: 2 * len(later)], refs[2 * len(later) :]
        qkv, probs, selected, pack, part, squares = refs[:6]
        refs = refs[6:]
        if not first:
            mixed_ref, unit_ref, rstd_ref = refs[:3]
            taken, refs = refs[3 : 3 + len(later)], refs[3 + len(later) :]
            passing = pass_on(meta, layer, offered, taken, refs[-1]) if later else []
        else:
            low_ref, refs = refs[0], refs[1:]
            raw, rows_ref, raw_sem = refs[-3:]
            refs = refs[:-3]
        if held:
            weights = Held(given[0].at[side], given[1].at[side])
        else:
            in_buffer, out_buffer, sems = refs
            weights = Weights(
                meta,
                layer,
                (maps(*given[:2], side, ENTRY), maps(*given[2:], side)),
                (in_buffer, out_buffer),
                sems,
            )
        valid = row_valid(meta, side, batch, rows)
        if first:
            items_of(meta, state, raw, rows_ref, raw_sem, batch)
            squares[...] = square_sum(rows_ref[...], valid)
            low = rows_ref[...].astype(bf16)
            low_ref[...] = low
        else:
            branch = summed(own, other) + post[0:1]
            squares[...] = square_sum(branch, valid)
            unit, rstd, mixed = norm_of(state[...].astype(f32) + branch, post[1:2], post[2:3])
            unit_ref[...] = unit
            rstd_ref[...] = rstd
            mixed_ref[...] = mixed
            low = mixed.astype(bf16)
        select_rows(low, chooser, selected, pack)
        flush(selected)
        biases = small[ROW_ATT_BIAS : ROW_ATT_BIAS + 1]
        project(low, weights, biases[:, :width], biases[:, width : 2 * width], qkv)
        context = pack.at[:, HALF:]
        attend(
            qkv[0], qkv[1], qkv[2], pair_valid(meta, side, batch, rows, rows), probs, context
        )
        flush(qkv, probs, pack)
        part[...] = mm(context[...], weights.get(1)[...]).astype(bf16)
        if not first:
            for copy in passing:
                copy.wait()

    ins = [(meta, "s"), (state, "w" if first else "v")]
    if not first:
        ins += list(zip(prior, "vvv"))
    ins += [(item, "v") for item in (*small, chooser)]
    ins += weight_inputs(att_in, att_out, "wawa")
    ins += [(item, "w") for pair in later for item in pair]
    outs = [
        ((3, rows, width), bf16, "h"),
        ((width // HEAD_DIM, rows, rows), bf16, "h"),
        ((rows, HALF), bf16, "h"),
        ((rows, HALF + width), bf16, "h", *place),
        ((rows, D), bf16, "v"),
        ((1, 128), f32, "h"),
    ]
    if not first:
        outs += [((rows, D), f32, "v"), ((rows, D), f32, "h"), ((rows, 1), f32, "h")]
        outs += [(pair[0].shape[1:], bf16, "v") for pair in later]
    else:
        outs.append(((rows, D), bf16, "v"))
    scratch = [
        pltpu.VMEM((3, D, width), bf16),
        pltpu.VMEM((width, D), bf16),
        pltpu.SemaphoreType.DMA((6,)),
    ]
    scratch = [] if held else scratch
    if first:
        scratch += [
            pltpu.VMEM(state.shape[1:], bf16),
            pltpu.VMEM((rows, D), f32),
            pltpu.SemaphoreType.DMA,
        ]
    if later:
        scratch.append(pltpu.SemaphoreType.DMA((len(later),)))
    return call(body, ins, outs, scratch, 4.0, f"self_forward_{layer}_{side}", ties, 12)


def hand_over(low_ref, kept, sent, sems):
    copies = []
    for slot, target in enumerate((kept, sent)):
        copies.append(
            pltpu.make_async_copy(low_ref, target.at[:, pl.ds(0, D)], sems.at[slot])
        )
        copies[-1].start()
    return copies


def hand_halves(meta, batch, wide_ref, kept, sent, sems):
    count = wide_ref.shape[1] // 2
    copies = []
    for half in (0, 1):
        source = wide_ref.at[:, pl.ds(half * count, count)]
        to_kept, to_sent = (
            pltpu.make_async_copy(source, target.at[:, pl.ds(D, count)], sems.at[2 + half])
            for target in (kept, sent)
        )
        mine = meta[1 + 2 * batch] == half
        pl.when(mine)(to_kept.start)
        pl.when(jnp.logical_not(mine))(to_sent.start)
        copies.append(to_kept)
    return copies


def hand_scratch(rows, units):
    return [
        pltpu.VMEM((rows, D), bf16),
        pltpu.VMEM((rows, units), bf16),
        pltpu.SemaphoreType.DMA((4,)),
    ]


def feed_forward(
    side, layer, batch, meta, residual, own, other, small, chooser, feed_in, feed_out, place, ties=()
):
    rows = residual.shape[0]
    units = feed_in[0].shape[-1]
    step = units // 4

    held, n_maps = len(feed_in) == 1, len(feed_in + feed_out)

    def body(flush, meta, residual, own, other, small_own, small_other, *refs):
        small = small_of(meta, layer, side, small_own, small_other)
        if not held:
            chooser, refs = refs[0], refs[1:]
        given, refs = refs[:n_maps], refs[n_maps:]
        settled_ref, unit_ref, rstd_ref, selected, pack, slope, part, squares = refs[:8]
        if held:
            weights = Held(given[0].at[side], given[1].at[side])
            low_ref, active_ref, sems = refs[8:]
        else:
            in_buffer, out_buffer, sems = refs[8:]
            weights = Weights(
                meta,
                layer,
                (
                    maps(*given[:2], side, column_pieces(units, 4)),
                    maps(*given[2:], side, row_pieces(units, 2)),
                ),
                (in_buffer, out_buffer),
                sems,
            )
        post = small[ROW_ATT_POST : ROW_ATT_POST + 3]
        branch = summed(own, other) + post[0:1]
        squares[...] = square_sum(branch, row_valid(meta, side, batch, rows))
        unit, rstd, settled = norm_of(residual[...].astype(f32) + branch, post[1:2], post[2:3])
        unit_ref[...] = unit
        rstd_ref[...] = rstd
        settled_ref[...] = settled
        low = settled.astype(bf16)
        if held:
            low_ref[...] = low
            copies = hand_over(low_ref, selected, pack, sems)
            flush(unit_ref, rstd_ref)
        else:
            select_rows(low, chooser, selected, pack)
            active_ref = pack.at[:, HALF:]
            flush(unit_ref, rstd_ref, selected)
        for i in range(units // step):
            first = weights.get(0, i)
            columns = slice(i * step, (i + 1) * step)
            row = ROW_FEED_BIAS + (i * step) // D
            place = (i * step) % D
            hidden = mm(low, first[:, columns]) + small[row : row + 1, place : place + step]
            below = 0.5 + 0.5 * lax.erf(hidden * (0.5**0.5))
            density = jnp.exp(hidden * hidden * -0.5) * 0.3989422804014327
            active_ref[:, columns] = (hidden * below).astype(bf16)
            slope[:, columns] = (below + hidden * density).astype(bf16)
        flush(pack, slope)
        if held:
            copies += hand_halves(meta, batch, active_ref, selected, pack, sems)
        part[...] = mm(active_ref[...], weights.get(1)[...]).astype(bf16)
        if held:
            for copy in copies:
                copy.wait()

    ins = [(meta, "s"), (residual, "v"), (own, "v"), (other, "v")]
    ins += [(item, "v") for item in ((*small,) if held else (*small, chooser))]
    ins += weight_inputs(feed_in, feed_out, "wawa")
    outs = [
        ((rows, D), f32, "v"),
        ((rows, D), f32, "h"),
        ((rows, 1), f32, "h"),
        *(
            [((rows, D + units // 2), bf16, "w")] * 2
            if held
            else [((rows, HALF), bf16, "h"), ((rows, HALF + units), bf16, "h", *place)]
        ),
        ((rows, units), bf16, "h"),
        ((rows, D), bf16, "v"),
        ((1, 128), f32, "h"),
    ]
    scratch = [
        pltpu.VMEM((D, units), bf16),
        pltpu.VMEM((units, D), bf16),
        pltpu.SemaphoreType.DMA((6,)),
    ]
    if held:
        scratch = hand_scratch(rows, units)
    cost = 12.0 if held and side == ORDER[-1] else 4.3
    return call(body, ins, outs, scratch, cost, f"feed_forward_{layer}_{side}", ties, 12 if held else 14)


def cross_forward(
    batch, meta, streams, smalls, chooser, cross_in, cross_bias, cross_out, later, ties=()
):
    rows = [stream[0].shape[0] for stream in streams]
    spans = spans_of(rows)
    width = cross_out.shape[0]
    heads = width // HEAD_DIM

    def body(flush, meta, *refs):
        given = (refs[0:3], refs[3:6])
        small = [small_of(meta, 0, side, refs[6], refs[7]) for side in (0, 1)]
        chooser, in_ref, bias, out_ref = refs[8:12]
        offered, refs = refs[12 : 12 + 2 * len(later)], refs[:12] + refs[12 + 2 * len(later) :]
        taken, refs = refs[29 : 29 + len(later)], refs[:29] + refs[29 + len(later) :]
        all_pack = refs[28]
        outs = [refs[12:20], refs[20:28]]
        for side in (0, 1):
            outs[side] = outs[side][:5] + (all_pack.at[spans[side]],) + outs[side][5:]
        in_buffer, out_buffer, sems, later_sems = refs[29:]
        weights = Weights(
            meta,
            0,
            (maps(in_ref, None, 0, ENTRY), maps(out_ref, None, 0)),
            (in_buffer, out_buffer),
            sems,
        )
        passing = pass_on(meta, 1, offered, taken, later_sems)
        lows = []
        for side in (0, 1):
            settled, own, other = given[side]
            state, unit_ref, rstd_ref, squares, selected, pack, qkv, probs, part = outs[side]
            post = small[side][ROW_FEED_POST : ROW_FEED_POST + 3]
            branch = summed(own, other) + post[0:1]
            unit, rstd, result = norm_of(settled[...] + branch, post[1:2], post[2:3])
            unit_ref[...] = unit
            rstd_ref[...] = rstd
            low = result.astype(bf16)
            state[...] = low
            valid = row_valid(meta, side, batch, rows[side])
            squares[0:1] = square_sum(branch, valid)
            squares[1:2] = square_sum(low.astype(f32), valid)
            select_rows(low, chooser, selected, pack)
            flush(unit_ref, rstd_ref, selected)
            lows.append(low)
        for side in (0, 1):
            project(lows[side], weights, bias[0:1], bias[1:2], outs[side][6])
        leave = weights.get(1)
        for side in (0, 1):
            pack, qkv, probs, part = outs[side][5:]
            there = outs[1 - side][6]
            valid = pair_valid(meta, 1 - side, batch, rows[side], rows[1 - side])
            context = pack.at[:, HALF:]
            attend(qkv[0], there[1], there[2], valid, probs, context)
            flush(qkv, probs)
            part[...] = mm(context[...], leave[...]).astype(bf16)
        for copy in passing:
            copy.wait()

    ins = [(meta, "s")] + [pair for stream in streams for pair in zip(stream, "vvv")]
    ins += [(item, "v") for item in smalls]
    ins += [(chooser, "v"), (cross_in, "w"), (cross_bias, "v"), (cross_out, "w")]
    ins += [(item, "w") for pair in later for item in pair]
    outs = []
    for side in (0, 1):
        here, there = rows[side], rows[1 - side]
        outs += [
            ((here, D), bf16, "v"),
            ((here, D), f32, "h"),
            ((here, 1), f32, "h"),
            ((2, 128), f32, "h"),
            ((here, HALF), bf16, "h"),
            ((3, here, width), bf16, "h"),
            ((heads, here, there), bf16, "h"),
            ((here, D), bf16, "v"),
        ]
    outs.append(((sum(rows), HALF + width), bf16, "h"))
    outs += [(pair[0].shape[1:], bf16, "v") for pair in later]
    scratch = [
        pltpu.VMEM((3, D, width), bf16),
        pltpu.VMEM((width, D), bf16),
        pltpu.SemaphoreType.DMA((6,)),
        pltpu.SemaphoreType.DMA((len(later),)),
    ]
    result = call(body, ins, outs, scratch, 6.8, "cross_forward", ties)
    return result[:8], result[8:16], result[16], result[17:]


class Layout:
    def __init__(self, sides, rows, given):
        self.sides, self.total, self.spans = sides, sum(rows), spans_of(rows)
        self.single = len(sides) == 1
        self.side = sides[0]
        self.count = rows[self.side] if self.single else self.total
        self.given = given

    def here(self, side):
        return slice(0, self.count) if self.single else self.spans[side]

    def index(self, side):
        return 0 if self.single else side

    def rows(self, width, dtype, at):
        if not self.single:
            return (self.total, width), dtype, "h"
        given = self.given[at] if self.given else None
        return (self.count, width), dtype, "h", self.total, self.spans[self.side].start, given

    def each(self, shape, at):
        if not self.single:
            return (2, *shape), f32, "h"
        given = self.given[at] if self.given else None
        return (1, *shape), f32, "h", 2, self.side, given


def feed_backward(
    layer, sides, rows, batch, meta, tops, joint, small, chooser, slopes, feed_in, feed_out, ties=(),
    given=None,
):
    last = joint is None
    layout = Layout(sides, rows, given)
    units = slopes[0].shape[1]
    step = units // 4
    n_top = len(tops[0])
    n = len(sides)
    held, n_maps = len(feed_in) == 1, len(feed_in + feed_out)

    def body(flush, meta, *refs):
        tops = {}
        for side in sides:
            tops[side], refs = refs[:n_top], refs[n_top:]
        if not last:
            joint, refs = refs[:3], refs[3:]
        small = {side: small_of(meta, layer, side, refs[0], refs[1]) for side in sides}
        refs = refs[2:]
        if not held:
            chooser, refs = refs[0], refs[1:]
        slopes, refs = dict(zip(sides, refs[:n])), refs[n:]
        given, refs = refs[:n_maps], refs[n_maps:]
        grad_all, selected_all, pack_all, part_all, post_all, bias_all = refs[:6]
        if last:
            squares_all, results = refs[6], dict(zip(sides, refs[7 : 7 + n]))
            low_ref, hidden_ref, hand_sems, raw, rows_ref, raw_sem = refs[-6:]
        weights = {}
        for i, side in enumerate(sides):
            if held:
                weights[side] = Held(given[1].at[side], given[0].at[side])
                continue
            in_buffer, out_buffer, sems = refs[-3:]
            weights[side] = Weights(
                meta,
                layer,
                (
                    maps(*given[2:], side, row_pieces(units, 4)),
                    maps(*given[:2], side, column_pieces(units, 2)),
                ),
                (out_buffer.at[i], in_buffer.at[i]),
                sems.at[i],
            )
        lows = {}
        for side in sides:
            here, at = layout.here(side), layout.index(side)
            post = small[side][ROW_FEED_POST : ROW_FEED_POST + 3]
            if last:
                settled, own, other, cotangent = tops[side]
                branch = summed(own, other) + post[0:1]
                unit, rstd, result = norm_of(settled[...] + branch, post[1:2], post[2:3])
                low = result.astype(bf16)
                results[side][...] = low
                valid = row_valid(meta, side, batch, rows[side])
                squares_all[at, 0:1] = square_sum(branch, valid)
                squares_all[at, 1:2] = square_sum(low.astype(f32), valid)
                items_of(meta, cotangent, raw, rows_ref, raw_sem, batch)
                incoming = rows_ref[...] * valid
            else:
                unit_ref, rstd_ref = tops[side]
                unit, rstd = unit_ref[...], rstd_ref[...]
                incoming = (joint[0][here] + summed_rows(joint[1], joint[2], here)).astype(bf16)
                incoming = incoming.astype(f32)
            grad = norm_back(unit, rstd, post[1:2], incoming)
            grad_all[here] = grad
            low = grad.astype(bf16)
            post_all[at, 0:1] = column_sum(low.astype(f32))
            post_all[at, 1:2] = column_sum(incoming * unit)
            post_all[at, 2:3] = column_sum(incoming)
            lows[side] = low
        flush(grad_all, post_all)
        if held:
            low_ref[...] = lows[sides[0]]
            copies = hand_over(low_ref, selected_all, pack_all, hand_sems)
        else:
            hidden_ref = pack_all.at[:, HALF:]
        for side in sides:
            here, at = layout.here(side), layout.index(side)
            for i in range(units // step):
                columns = slice(i * step, (i + 1) * step)
                active = mm_nt(lows[side], weights[side].get(0, i)[columns, :])
                hidden = (active * slopes[side][:, columns].astype(f32)).astype(bf16)
                hidden_ref[here, columns] = hidden
                bias_all[at, :, columns] = column_sum(hidden.astype(f32))
            if not held:
                select_rows(lows[side], chooser, selected_all.at[here], pack_all.at[here])
        flush(pack_all, selected_all)
        if held:
            copies += hand_halves(meta, batch, hidden_ref, selected_all, pack_all, hand_sems)
        for side in sides:
            here = layout.here(side)
            part_all[here] = mm_nt(hidden_ref[here], weights[side].get(1)[...]).astype(bf16)
        if held:
            for copy in copies:
                copy.wait()

    ins = [(meta, "s")] + [pair for top in tops for pair in zip(top, "vvvw" if last else "vv")]
    if not last:
        ins += [(item, "v") for item in joint]
    ins += [(item, "v") for item in ((*small, *slopes) if held else (*small, chooser, *slopes))]
    ins += weight_inputs(feed_in, feed_out)
    count = layout.count
    outs = [
        ((count, D), f32, "v" if last else "h"),
        *(
            [((count, D + units // 2), bf16, "w")] * 2
            if held
            else [layout.rows(HALF, bf16, 1), ((count, HALF + units), bf16, "h")]
        ),
        ((count, D), bf16, "v" if last else "h"),
        layout.each((3, D), 4),
        layout.each((1, units), 5),
    ]
    if last:
        outs += [layout.each((2, 128), 6)] + [((rows[side], D), bf16, "h") for side in sides]
    scratch = [
        pltpu.VMEM((n, D, units), bf16),
        pltpu.VMEM((n, units, D), bf16),
        pltpu.SemaphoreType.DMA((n, 6)),
    ]
    if last:
        side = sides[0]
        scratch = hand_scratch(rows[side], units) + [
            pltpu.VMEM(tops[0][3].shape[1:], bf16),
            pltpu.VMEM((rows[side], D), f32),
            pltpu.SemaphoreType.DMA,
        ]
    name = f"feed_backward_{layer}_" + "".join(map(str, sides))
    cost = 12.0 if sides == ORDER[:1] else 11.0 * count / layout.total
    return call(body, ins, outs, scratch, cost, name, ties, 12 if held else 24)


def summed_rows(own, other, here):
    return own[here].astype(f32) + other[here].astype(f32)


def back_through_norm(top, grad_in, branch, gain, grad_ref, post_ref):
    unit_ref, rstd_ref = top
    incoming = grad_in + branch
    unit = unit_ref[...]
    grad = norm_back(unit, rstd_ref[...], gain, incoming)
    grad_ref[...] = grad
    low = grad.astype(bf16)
    post_ref[0:1] = column_sum(low.astype(f32))
    post_ref[1:2] = column_sum(incoming * unit)
    post_ref[2:3] = column_sum(incoming)
    return low


def emit_into(pack, width):
    def emit(kind, lanes, value):
        start = HALF + kind * width + lanes.start
        pack[:, start : start + PAIR] = value

    return emit


def back_to_input(pack, weights, slot, width):
    grads = [pack[:, HALF + j * width : HALF + (j + 1) * width] for j in range(3)]
    total = mm_nt(grads[0], weights.get(slot, 0)[0])
    total += mm_nt(grads[1], weights.get(slot, 1)[1])
    total += mm_nt(grads[2], weights.get(slot, 2)[2])
    return total.astype(bf16)


def self_backward(
    layer, sides, rows, meta, tops, joint, small, chooser, qkvs, probs, att_in, att_out, ties=(),
    given=None,
):
    layout = Layout(sides, rows, given)
    width = qkvs[0].shape[2]
    n = len(sides)
    held, n_maps = len(att_in) == 1, len(att_in + att_out)

    def body(flush, meta, *refs):
        tops = {side: refs[2 * i : 2 * i + 2] for i, side in enumerate(sides)}
        joint, refs = refs[2 * n : 2 * n + 3], refs[2 * n + 3 :]
        small = {side: small_of(meta, layer, side, refs[0], refs[1]) for side in sides}
        chooser, refs = refs[2], refs[3:]
        qkvs, probs, refs = dict(zip(sides, refs[:n])), dict(zip(sides, refs[n : 2 * n])), refs[2 * n :]
        given, refs = refs[:n_maps], refs[n_maps:]
        grad_all, selected_all, pack_all, part_all, post_all, bias_all = refs[:6]
        weights = {}
        for i, side in enumerate(sides):
            if held:
                weights[side] = Held(given[1].at[side], given[0].at[side])
                continue
            in_buffer, out_buffer, sems = refs[6:]
            weights[side] = Weights(
                meta,
                layer,
                (maps(*given[2:], side), maps(*given[:2], side, ENTRY)),
                (out_buffer.at[i], in_buffer.at[i]),
                sems.at[i],
            )
        for side in sides:
            here, at = layout.here(side), layout.index(side)
            pack = pack_all.at[here]
            gain = small[side][ROW_ATT_POST + 1 : ROW_ATT_POST + 2]
            low = back_through_norm(
                tops[side],
                joint[0][here],
                summed_rows(joint[1], joint[2], here),
                gain,
                grad_all.at[here],
                post_all.at[at],
            )
            context = mm_nt(low, weights[side].get(0)[...]).astype(bf16)
            qkv = qkvs[side]
            attend_back(qkv[0], qkv[1], qkv[2], probs[side], context, emit_into(pack, width))
            bias_all[at, 0:1] = column_sum(pack[:, HALF : HALF + width].astype(f32))
            bias_all[at, 1:2] = column_sum(pack[:, HALF + 2 * width :].astype(f32))
            select_rows(low, chooser, selected_all.at[here], pack)
        flush(pack_all, selected_all, grad_all, post_all, bias_all)
        for side in sides:
            here = layout.here(side)
            part_all[here] = back_to_input(pack_all.at[here], weights[side], 1, width)

    near = "v" if layer == 1 else "h"
    ins = [(meta, "s")] + [(item, near) for top in tops for item in top]
    ins += [*zip(joint, "vvv" if layer == 1 else "hhf")] + [(item, near) for item in small]
    ins += [(item, near) for item in (chooser, *qkvs, *probs)]
    ins += weight_inputs(att_in, att_out)
    outs = [
        ((layout.count, D), f32, "h"),
        layout.rows(HALF, bf16, 1),
        layout.rows(HALF + 3 * width, bf16, 2),
        ((layout.count, D), bf16, "h"),
        layout.each((3, D), 4),
        layout.each((2, width), 5),
    ]
    scratch = [
        pltpu.VMEM((n, 3, D, width), bf16),
        pltpu.VMEM((n, width, D), bf16),
        pltpu.SemaphoreType.DMA((n, 6)),
    ]
    scratch = [] if held else scratch
    name = f"self_backward_{layer}_" + "".join(map(str, sides))
    cost = 12.0 * layout.count / layout.total
    return call(body, ins, outs, scratch, cost, name, ties, 12 if held else 18)


def cross_backward(meta, tops, grads, owns, others, post, chooser, qkvs, probs, cross_in, cross_out, ties=()):
    rows = [qkv.shape[1] for qkv in qkvs]
    width = cross_out.shape[0]
    spans, total = spans_of(rows), sum(rows)

    def body(flush, meta, *refs):
        tops, grads, owns, others = (refs[:2], refs[2:4]), refs[4:6], refs[6:8], refs[8:10]
        post, chooser, qkvs, probs = refs[10], refs[11], refs[12:14], refs[14:16]
        in_ref, out_ref = refs[16:18]
        grad_all, selected_all, pack_all, part_all, post_out, bias_out = refs[18:24]
        in_buffer, out_buffer, post_each, sems = refs[24:]
        weights = Weights(
            meta,
            0,
            (maps(out_ref, None, 0), maps(in_ref, None, 0, ENTRY)),
            (out_buffer, in_buffer),
            sems,
        )
        packs = [pack_all.at[here] for here in spans]
        lows = []
        for side in (0, 1):
            here = spans[side]
            low = back_through_norm(
                tops[side],
                grads[side][...],
                summed(owns[side], others[side]),
                post[1:2],
                grad_all.at[here],
                post_each.at[side],
            )
            lows.append(low)
        post_out[...] = post_each[0] + post_each[1]
        leave = weights.get(0)
        for side in (0, 1):
            context = mm_nt(lows[side], leave[...]).astype(bf16)
            to_here, to_there = emit_into(packs[side], width), emit_into(packs[1 - side], width)

            def emit(kind, lanes, value):
                (to_here if kind == 0 else to_there)(kind, lanes, value)

            attend_back(
                qkvs[side][0], qkvs[1 - side][1], qkvs[1 - side][2], probs[side], context, emit
            )
        for side in (0, 1):
            select_rows(lows[side], chooser, selected_all.at[spans[side]], packs[side])
        bias_out[0:1] = column_sum(pack_all[:, HALF : HALF + width].astype(f32))
        bias_out[1:2] = column_sum(pack_all[:, HALF + 2 * width :].astype(f32))
        flush(pack_all, selected_all)
        part_all[...] = back_to_input(pack_all, weights, 1, width)

    ins = [(meta, "s")] + [(item, "h") for top in tops for item in top]
    ins += [(item, "h") for item in (*grads, *owns)] + [(item, "f") for item in others]
    ins += [(item, "h") for item in (post, chooser, *qkvs, *probs)]
    ins += [(cross_in, "w"), (cross_out, "w")]
    outs = [
        ((total, D), f32, "v"),
        ((total, HALF), bf16, "h"),
        ((total, HALF + 3 * width), bf16, "h"),
        ((total, D), bf16, "v"),
        ((3, D), f32, "h"),
        ((2, width), f32, "h"),
    ]
    scratch = [
        pltpu.VMEM((3, D, width), bf16),
        pltpu.VMEM((width, D), bf16),
        pltpu.VMEM((2, 3, D), f32),
        pltpu.SemaphoreType.DMA((6,)),
    ]
    return call(body, ins, outs, scratch, 10.0, "cross_backward", ties, 16)


class Block:
    def __init__(self, in_selected, in_packs, in_gots, out_selected, out_packs, out_gots):
        self.parts = [*in_selected, *in_packs, *in_gots, out_selected, *out_packs, *out_gots]
        self.counts = (len(in_packs), len(out_packs))
        self.lead = HALF
        self.kinds = "w" * len(self.parts)
        self.sizes = (out_packs[0].shape[1] - HALF, in_packs[0].shape[1] - HALF)
        self.rows = [array.shape[0] for array in in_selected]

    def buffers(self):
        return [
            pltpu.VMEM((2 * rows, HALF + size), bf16)
            for rows in self.rows
            for size in (self.sizes[1], self.sizes[0])
        ]

    def fetch(self, refs, buffers, sems, at):
        spans = spans_of(self.rows)
        in_selected, rest = refs[:2], refs[2:]
        n_in, n_out = self.counts
        pack, got, rest = rest[:n_in], rest[n_in : 2 * n_in], rest[2 * n_in :]
        out_selected, out_pack, out_got = rest[0], rest[1 : 1 + n_out], rest[1 + n_out :]

        def rows_of(items, side):
            return items[0].at[spans[side]] if len(items) == 1 else items[side]

        result = []
        for side in (0, 1):
            count = self.rows[side]
            per_side = []
            for kind, (selected, own, other) in enumerate(
                (
                    (in_selected[side], rows_of(pack, side), rows_of(got, side)),
                    (out_selected.at[spans[side]], rows_of(out_pack, side), rows_of(out_got, side)),
                )
            ):
                buffer = buffers[2 * side + kind]
                size = buffer.shape[1] - HALF
                mine = slice(0, count)
                copies = [
                    pltpu.make_async_copy(
                        selected, buffer.at[mine, pl.ds(0, HALF)], sems.at[at]
                    ),
                    pltpu.make_async_copy(
                        own.at[:, pl.ds(HALF, size)], buffer.at[mine, pl.ds(HALF, size)], sems.at[at + 1]
                    ),
                    pltpu.make_async_copy(
                        other, buffer.at[slice(count, 2 * count)], sems.at[at + 2]
                    ),
                ]
                at += 3
                for copy in copies:
                    copy.start()
                per_side.append((buffer, copies))
            result.append(per_side)
        return result, at


class Halves:
    def __init__(self, in_kept, in_gots, out_kept, out_gots):
        self.parts = [*in_kept, *in_gots, *out_kept, *out_gots]
        self.kinds = "wwwwwwaa"
        self.lead = D
        self.sizes = (out_kept[0].shape[1] - D, in_kept[0].shape[1] - D)
        self.rows = [array.shape[0] for array in in_kept]

    def buffers(self):
        return [
            pltpu.VMEM((2 * rows, D + size), bf16)
            for rows in self.rows
            for size in (self.sizes[1], self.sizes[0])
        ]

    def fetch(self, refs, buffers, sems, at):
        result = []
        for side in (0, 1):
            count = self.rows[side]
            per_side = []
            for kind in (0, 1):
                buffer = buffers[2 * side + kind]
                copies = []
                for part in (0, 1):
                    target = buffer.at[slice(part * count, (part + 1) * count)]
                    source = refs[4 * kind + 2 * part + side]
                    copies.append(pltpu.make_async_copy(source, target, sems.at[at]))
                    copies[-1].start()
                    at += 1
                per_side.append((buffer, copies))
            result.append(per_side)
        return result, at


def chunk_order(groups):
    return [(s, z) for z in range(groups) for s in ((0, 1) if z % 2 == 0 else (1, 0))]


def places_chunks(groups):
    return (D // (2 * groups) // 2) % 16 == 0


def gradients(meta, blocks, cross, groups, name, ties=(), mode="ring"):
    lead = blocks[0].lead
    chunk = lead // groups
    half = chunk // 2
    size = chunk + half if cross else chunk
    order = chunk_order(groups)
    aligned = places_chunks(groups)
    width = sum(sum(block.sizes) for block in blocks)
    every = blocks + ([cross] if cross else [])
    n_in = sum(len(block.parts) for block in every)
    pair = mode == "split"
    n_out = 2 if pair else 1 if aligned else 3 if cross else 2
    n_sems = 12 * len(every) + 4 * len(every)

    def body(flush, meta, *refs):
        inputs, outputs, rest = refs[:n_in], refs[n_in : n_in + n_out], list(refs[n_in + n_out :])
        if cross:
            cross_stage = rest.pop()
        stage, sems = rest.pop(), rest.pop()
        at = 0
        fetched = []
        for block in every:
            taken, inputs = inputs[: len(block.parts)], inputs[len(block.parts) :]
            own, rest = rest[:4], rest[4:]
            copies, at = block.fetch(taken, own, sems, at)
            fetched.append(copies)
        waited, leaving = set(), []

        def leave(source, side, columns, at):
            if pair and not cross:
                kept, sent = (
                    pltpu.make_async_copy(source, target.at[:, columns], sems.at[at])
                    for target in outputs
                )
                pl.when(meta[0] == side)(kept.start)
                pl.when(meta[0] != side)(sent.start)
                leaving.append(kept)
                return
            if not aligned:
                copy = pltpu.make_async_copy(source, outputs[side].at[:, columns], sems.at[at])
                copy.start()
                leaving.append(copy)
                return
            if mode == "ring":
                for k, (s, z) in enumerate(order):
                    if side == 2:
                        start, count, place = (s * groups + z) * half, half, k * size + chunk
                    elif s == side:
                        start, count, place = z * chunk, chunk, k * size
                    else:
                        continue
                    copy = pltpu.make_async_copy(
                        source.at[pl.ds(start, count)],
                        outputs[0].at[pl.ds(place, count), columns],
                        sems.at[at],
                    )
                    copy.start()
                    leaving.append(copy)
                return
            for section in (0, 1) if side == 2 else (side,):
                for z in range(groups):
                    if side == 2:
                        start, count, place = (section * groups + z) * half, half, z * size + chunk
                    else:
                        start, count, place = z * chunk, chunk, z * size
                    kept, sent = (
                        pltpu.make_async_copy(
                            source.at[pl.ds(start, count)],
                            target.at[pl.ds(place, count), columns],
                            sems.at[at],
                        )
                        for target in outputs
                    )
                    pl.when(meta[0] == section)(kept.start)
                    pl.when(meta[0] != section)(sent.start)
                    leaving.append(kept)

        def ready(item):
            buffer, copies = item
            if id(buffer) not in waited:
                waited.add(id(buffer))
                for copy in copies:
                    copy.wait()
            return buffer

        base = 0
        for block, copies in zip(blocks, fetched):
            for side in (0, 1):
                start = base
                for left, right in ((0, 1), (1, 0)):
                    left, right = ready(copies[side][left]), ready(copies[side][right])
                    turned = left[:, :lead].T
                    span = right.shape[1] - lead
                    for step in range(0, span, HALF):
                        value = mm(turned, right[:, lead + step : lead + step + HALF])
                        stage[side, :, start + step : start + step + HALF] = value.astype(bf16)
                    columns = pl.ds(start, span)
                    leave(stage.at[side, :, columns], side, columns, at)
                    at += 1
                    start += span
            base += sum(block.sizes)
        if cross:
            copies = fetched[-1]
            start = 0
            for left, right in ((0, 1), (1, 0)):
                lefts = [ready(copies[side][left])[:, :HALF].T for side in (0, 1)]
                rights = [ready(copies[side][right]) for side in (0, 1)]
                span = rights[0].shape[1] - HALF
                for step in range(0, span, HALF):
                    columns = slice(HALF + step, HALF + step + HALF)
                    value = mm(lefts[0], rights[0][:, columns]) + mm(lefts[1], rights[1][:, columns])
                    cross_stage[:, start + step : start + step + HALF] = value.astype(bf16)
                columns = pl.ds(start, span)
                leave(cross_stage.at[:, columns], 2, columns, at)
                at += 1
                start += span
        for copy in leaving:
            copy.wait()

    ins = [(meta, "s")] + [pair for block in every for pair in zip(block.parts, block.kinds)]
    if pair:
        outs = [((groups * size, width), bf16, "w")] * 2
    elif aligned:
        outs = [((2 * groups * size, width), bf16, "w")]
    else:
        outs = [((lead, width), bf16, "w")] * n_out
    scratch = [buffer for block in every for buffer in block.buffers()]
    if cross:
        scratch += [
            pltpu.SemaphoreType.DMA((n_sems,)),
            pltpu.VMEM((2, lead, width), bf16),
            pltpu.VMEM((HALF, sum(cross.sizes)), bf16),
        ]
    else:
        scratch += [pltpu.SemaphoreType.DMA((n_sems,)), pltpu.VMEM((2, lead, width), bf16)]
    result = call(body, ins, outs, scratch, 6.0, name, ties, 20)
    if pair:
        return result
    if aligned:
        return result[0]
    chunks = [result[side].reshape(groups, chunk, width) for side in (0, 1)]
    pieces = [chunks[s][z] for s, z in order]
    if cross:
        extra = result[2].reshape(2, groups, half, width)
        pieces = [jnp.concatenate([one, extra[s, z]]) for one, (s, z) in zip(pieces, order)]
    return jnp.concatenate(pieces)


def placed_gradients(meta, first, second, chunk, width, units):
    def body(flush, meta, *refs):
        layers, last = (refs[:4], refs[4:8]), refs[7]
        feed_in, feed_out, att_in, att_out, cross_in, cross_out = refs[8:]
        for j in range(3):
            cross_in[j] = last[chunk:, j * width : (j + 1) * width].astype(f32)
        cross_out[...] = last[chunk:, 3 * width :].astype(f32)
        flush(cross_in, cross_out)
        for item in refs[:8]:
            item.wait()

        def store_rest(layer):
            for side in (0, 1):
                late = layers[layer][2 * side + 1]
                for j in range(3):
                    att_in[side, j] = late[:chunk, j * width : (j + 1) * width].astype(f32)
                att_out[side] = late[:chunk, 3 * width :].astype(f32)

        def store_feed(layer):
            for side in (0, 1):
                feed = layers[layer][2 * side]
                feed_in[side] = feed[:, :units].astype(f32)
                feed_out[side] = feed[:, units:].astype(f32)

        pl.when(meta[0] == 0)(partial(store_rest, 0))
        pl.when(meta[0] != 0)(partial(store_rest, 1))
        flush(att_in, att_out)
        pl.when(meta[0] == 0)(partial(store_feed, 0))
        pl.when(meta[0] != 0)(partial(store_feed, 1))

    ins = [(meta, "s")] + list(zip((*first, *second), "hfffffff"))
    half = chunk // 2
    outs = [
        ((2, chunk, units), f32, "h"),
        ((2, chunk, units), f32, "h"),
        ((2, 3, chunk, width), f32, "h"),
        ((2, chunk, width), f32, "h"),
        ((3, half, width), f32, "h"),
        ((half, width), f32, "h"),
    ]
    return call(body, ins, outs, (), 4.0, "placed_gradients")


def small_shape(width, units):
    n_feed = 2 * units // D
    sizes = (2 * 2 * width // D, 6, n_feed, 6, 2, 3, 2 * width // D, 1)
    starts = [sum(sizes[:i]) for i in range(len(sizes))]
    return starts, -(-sum(sizes) * D // (4 * width)) * 4 * width // D


def finished(meta, batch, rows, results, state_grad, layers, cross_post, cross_bias, ties):
    spans = spans_of(rows)
    width, units = cross_bias.shape[1], layers[0][2].shape[2]
    starts, total = small_shape(width, units)
    flat = [
        [*layer[:4], *layer[4], *layer[5], *layer[6]] for layer in layers
    ]
    counts = [len(layer) for layer in flat]

    def body(flush, meta, *refs):
        results, (grad, own, other), refs = refs[:2], refs[2:5], refs[5:]
        first, second, refs = refs[: counts[0]], refs[counts[0] : sum(counts)], refs[sum(counts) :]
        cross_post, cross_bias, refs = refs[0], refs[1], refs[2:]
        outs, mine, theirs, packs = refs[:4], refs[4], refs[5], refs[6]
        for k, layer in enumerate((first, second)):
            att_bias, att_post, feed_bias, feed_post, *squares = layer
            for side in (0, 1):
                for j in (0, 1):
                    place = (2 * side + j) * width
                    row, lane = starts[0] + place // D, place % D
                    packs[k, row : row + 1, lane : lane + width] = att_bias[side, j : j + 1]
                for start, post in ((starts[1], att_post), (starts[3], feed_post)):
                    packs[k, start + 3 * side : start + 3 * side + 3] = post[side]
                for j in range(units // D):
                    row = starts[2] + side * (units // D) + j
                    packs[k, row : row + 1] = feed_bias[side, :, j * D : (j + 1) * D]
            lead, middle, tails = squares[:2], squares[2:4], squares[4:]
            packs[k, starts[4] : starts[5]] = jnp.zeros((2, D), f32)
            for side in (0, 1):
                tail = tails[side] if len(tails) == 2 else tails[0].wait().at[side]
                terms = (lead[side][0:1], middle[side][0:1], tail[0:1], tail[1:2])
                for j, term in enumerate(terms):
                    at = 4 * side + j
                    row, lane = starts[4] + at // 6, at % 6 * 128
                    packs[k, row : row + 1, lane : lane + 128] = term
            packs[k, starts[5] : starts[6]] = cross_post[...]
            for j in (0, 1):
                row, lane = starts[6] + j * width // D, j * width % D
                packs[k, row : row + 1, lane : lane + width] = cross_bias[j : j + 1]
            lane = lax.broadcasted_iota(jnp.int32, (1, D), 1)
            count = jnp.zeros((1, D), f32)
            for side in (0, 1):
                for i in range(batch):
                    length = meta[1 + side * batch + i].astype(f32)
                    count += jnp.where(lane == side, length, 0.0)
            packs[k, starts[7] : starts[7] + 1] = count
            if total > starts[7] + 1:
                packs[k, starts[7] + 1 :] = jnp.zeros((total - starts[7] - 1, D), f32)
        mine[...] = packs[meta[0]]
        theirs[...] = packs[1 - meta[0]]
        flush(mine, theirs)
        for side in (0, 1):
            here = spans[side]
            whole = results[side][...].astype(f32)
            back = (grad[here] + summed_rows(own, other, here)).astype(bf16).astype(f32)
            for slot in range(rows[side] // batch):
                these = slice(slot * batch, (slot + 1) * batch)
                outs[side][slot] = whole[these].astype(bf16)
                outs[2 + side][slot] = back[these].astype(bf16)

    ins = [(meta, "s")] + [(item, "f") for item in results] + list(zip(state_grad, "fff"))
    ins += [(item, "f") for layer in flat for item in layer]
    ins += [(cross_post, "f"), (cross_bias, "f")]
    outs = [((count // batch, batch, D), bf16, "h") for count in (*rows, *rows)]
    outs += [((total, D), f32, "h")] * 2
    scratch = [pltpu.VMEM((2, total, D), f32)]
    return call(body, ins, outs, scratch, 4.0, "finished", ties)


def unpacked(sums, width, units):
    starts, _ = small_shape(width, units)

    def body(flush, sums, att_bias, att_post, feed_bias, feed_post, cross_bias, cross_post, scales):
        for side in (0, 1):
            for j in (0, 1):
                place = (2 * side + j) * width
                row, lane = starts[0] + place // D, place % D
                att_bias[0, side, j : j + 1] = sums[row : row + 1, lane : lane + width]
            for start, post in ((starts[1], att_post), (starts[3], feed_post)):
                for j in range(3):
                    row = start + 3 * side + j
                    post[0, j, side : side + 1] = sums[row : row + 1]
            for j in range(units // D):
                row = starts[2] + side * (units // D) + j
                feed_bias[0, side : side + 1, j * D : (j + 1) * D] = sums[row : row + 1]
        cross_post[...] = sums[starts[5] : starts[6]]
        for j in (0, 1):
            row, lane = starts[6] + j * width // D, j * width % D
            cross_bias[j : j + 1] = sums[row : row + 1, lane : lane + width]
        counts = sums[starts[7] : starts[7] + 1]
        lane = lax.broadcasted_iota(jnp.int32, (1, 8), 1)
        result = jnp.zeros((1, 8), f32)
        for at in range(8):
            row, place = starts[4] + at // 6, at % 6 * 128
            square = sums[row : row + 1, place : place + 1]
            scale = jnp.sqrt(square / (counts[:, at // 4 : at // 4 + 1] * D))
            result = jnp.where(lane == at, scale, result)
        scales[...] = result

    outs = [
        ((1, 2, 2, width), f32, "h"),
        ((1, 3, 2, D), f32, "h"),
        ((1, 2, units), f32, "h"),
        ((1, 3, 2, D), f32, "h"),
        ((2, width), f32, "h"),
        ((3, D), f32, "h"),
        ((1, 8), f32, "h"),
    ]
    return call(body, [(sums, "f")], outs, (), 2.0, "unpacked")


def prepared(ids, lengths, att_bias, att_post, feed_bias, feed_post):
    batch = lengths[0].shape[1]
    n_feed = feed_bias.shape[2] // D
    n_ids = ids.shape[0]

    def body(flush, ids, words, regions, att_bias, att_post, feed_bias, feed_post, small, meta):
        meta[0] = ids[0]
        for i in range(1, n_ids):
            meta[2 * batch + i] = ids[i]
        for side, counts in enumerate((words, regions)):
            for i in range(batch):
                meta[1 + side * batch + i] = counts[ids[0], i]
        half = att_bias.shape[3]
        for side in (0, 1):
            for j in (0, 1):
                small[side, ROW_ATT_BIAS : ROW_ATT_BIAS + 1, j * half : (j + 1) * half] = att_bias[
                    0, side, j : j + 1
                ]
            for j in range(3):
                for row, post in ((ROW_ATT_POST, att_post), (ROW_FEED_POST, feed_post)):
                    small[side, row + j : row + j + 1] = post[0, j, side : side + 1]
            for j in range(n_feed):
                row = ROW_FEED_BIAS + j
                small[side, row : row + 1] = feed_bias[0, side : side + 1, j * D : (j + 1) * D]
            end = ROW_FEED_POST + 3
            small[side, end:] = jnp.zeros((SMALL_ROWS - end, D), f32)

    ins = [(ids, "s"), (lengths[0], "s"), (lengths[1], "s")]
    ins += [(item, "h") for item in (att_bias, att_post, feed_bias, feed_post)]
    outs = [((2, SMALL_ROWS, D), f32, "h"), ((n_ids + 2 * batch,), jnp.int32, "s")]
    return call(body, ins, outs, (), 1.0, "prepared")


def swap(value, axis, distance=1):
    count = lax.axis_size(axis)
    return lax.ppermute(value, axis, [(i, i ^ distance) for i in range(count)])


def total_of(parts):
    return sum(part.astype(f32) for part in parts).astype(bf16)


class Halving:
    def __init__(self, parts, groups):
        self.parts = [part.reshape(groups, -1, part.shape[1]) for part in parts]
        self.position, self.distance, self.groups = lax.axis_index("dp") // 2, 2, groups

    def half(self, bit):
        split = [part.reshape(-1, 2, *part.shape[1:]) for part in self.parts]
        return [lax.dynamic_index_in_dim(part, bit, 1, keepdims=False) for part in split]

    def send(self, *after, extra=None):
        self.parts = behind(self.parts, after)
        bit = self.position % 2
        chunks = total_of(self.half(1 - bit))
        payload = chunks.reshape(-1, chunks.shape[-1])
        count = payload.shape[0]
        if extra is not None:
            low = extra.astype(bf16).reshape(-1, payload.shape[1])
            payload = jnp.concatenate([payload, low])
        got = swap(payload, "dp", self.distance)
        self.parts = self.half(bit) + [got[:count].reshape(chunks.shape)]
        self.position, self.distance = self.position // 2, 2 * self.distance
        self.groups //= 2
        if extra is None:
            return payload
        return payload, (low.astype(f32) + got[count:].astype(f32)).reshape(extra.shape)

    def finish(self, *after):
        while self.groups > 1:
            self.send()
        return total_of([part[0] for part in behind(self.parts, after)])


def behind(values, after):
    return lax.optimization_barrier((values, after))[0] if after else values


def on_device(
    word_state,
    region_state,
    word_lengths,
    region_counts,
    word_cotangent,
    region_cotangent,
    cross_in,
    cross_bias,
    cross_out,
    cross_post,
    attention_in,
    attention_bias,
    attention_out,
    attention_post,
    feed_in,
    feed_bias,
    feed_out,
    feed_post,
):
    section = lax.axis_index("section")
    dp_count = lax.axis_size("dp")
    groups = dp_count // 2
    place = lax.axis_index("dp") % 2
    batch = word_state.shape[1]
    width = cross_out.shape[0]
    units = feed_in.shape[-1]
    both = (0, 1)
    chains = [[s * dp_count + 2 * z + y for s, z in chunk_order(groups)] for y in both]

    def unflat(value):
        return value.reshape(-1, batch, D).transpose(1, 0, 2)[None]

    def chooser_of(pieces, per_section):
        column = jnp.arange(D)
        half = column // HALF
        inner = column % HALF
        side = jnp.where(half == 0, place, 1 - place)
        size = D // pieces
        if per_section:
            block = inner // (HALF // 2)
            inner = inner % (HALF // 2)
            feature = size * (dp_count * block + 2 * (inner // size) + side) + inner % size
        else:
            feature = size * (2 * (inner // size) + side) + inner % size
        return (jnp.arange(D)[:, None] == feature[None, :]).astype(bf16)

    chooser = chooser_of(dp_count, False)
    cross_chooser = chooser_of(2 * dp_count, True)

    ids = jnp.stack([section, place]).astype(jnp.int32)
    small_own, meta = prepared(
        ids,
        (word_lengths, region_counts),
        attention_bias,
        attention_post.transpose(0, 2, 1, 3),
        feed_bias,
        feed_post.transpose(0, 2, 1, 3),
    )
    small = (small_own, swap(small_own, "section"))
    att_in_own = attention_in.transpose(0, 1, 3, 2, 4)
    att_in = (att_in_own, swap(att_in_own, "section"))
    att_out = (attention_out, swap(attention_out, "section"))
    states = [value.transpose(0, 2, 1, 3) for value in (word_state, region_state)]
    feed_in_later, feed_out_later, *_ = lax.optimization_barrier(
        (feed_in, feed_out, att_in[1], att_out[1], small[1], chooser, cross_chooser)
    )
    ff_in = (feed_in, swap(feed_in_later, "section"))
    ff_out = (feed_out, swap(feed_out_later, "section"))
    cross_entry = cross_in.transpose(1, 0, 2)

    cotangents = [value.transpose(0, 2, 1, 3) for value in (word_cotangent, region_cotangent)]
    rows = [state.shape[1] * batch for state in states]
    total_rows = sum(rows)

    def in_order(step, pack_index, tie=None, joined=True, order=(1, 0)):
        results = [None, None]
        given = None
        for side in order:
            ties = () if tie is None else (tie,)
            place = (total_rows, rows[0] * side, given) if joined else ()
            results[side] = step(side, place, ties)
            tie, given = results[side][pack_index + 2], results[side][pack_index]
        return results

    def over_mp(results, index):
        return [swap(results[side][index], "mp") for side in both]

    self0 = in_order(
        lambda side, place, ties: self_forward(
            side, 0, batch, meta, states[side], None, small, chooser, att_in, att_out,
            place, ties,
        ),
        3,
    )
    got = over_mp(self0, 4)
    feed0 = in_order(
        lambda side, place, ties: feed_forward(
            side, 0, batch, meta, self0[side][6], self0[side][4], got[side], small, chooser,
            ff_in, ff_out, place, ties,
        ),
        4,
        self0[0][5],
    )
    got = over_mp(feed0, 6)
    self0_there = swap(self0[0][3], "dp")
    cross_w, cross_r, cross_pack, held = cross_forward(
        batch,
        meta,
        [(feed0[side][0], feed0[side][6], got[side]) for side in both],
        small,
        cross_chooser,
        cross_entry,
        cross_bias,
        cross_out,
        (att_in, att_out, ff_in),
    )
    att_in1, att_out1, ff_in1 = [(item,) for item in held]
    cross = (cross_w, cross_r)
    got = over_mp(cross, 7)
    feed0_there = swap(feed0[0][4], "dp")
    self1 = in_order(
        lambda side, place, ties: self_forward(
            side, 1, batch, meta, cross[side][0], (cross[side][7], got[side], cross_post),
            small, chooser, att_in1, att_out1, place, ties + ((self0_there, "a"),),
            (ff_out,) if side == ORDER[0] else (),
        ),
        3,
        None,
        True,
        ORDER,
    )
    ff_out1 = (self1[ORDER[0]][9],)
    got = over_mp(self1, 4)
    cross_there = swap(cross_pack, "dp")
    feed1 = in_order(
        lambda side, place, ties: feed_forward(
            side, 1, batch, meta, self1[side][6], self1[side][4], got[side], small, chooser,
            ff_in1, ff_out1, place, ties + (((feed0_there, "a"),) if side == ORDER[0] else ()),
        ),
        4,
        self1[ORDER[-1]][5],
        False,
        ORDER,
    )
    got = over_mp(feed1, 6)
    self1_there = swap(self1[ORDER[-1]][3], "dp")
    feed1_there = [swap(feed1[side][4], "dp") for side in both]

    def over_sections_and_groups(value):
        return lax.psum_scatter(
            value, ("section", "dp"), scatter_dimension=0, axis_index_groups=chains, tiled=True
        )

    def over_groups(value):
        pairs = [[2 * z + y for z in range(groups)] for y in both]
        return lax.psum_scatter(
            value, "dp", scatter_dimension=0, axis_index_groups=pairs, tiled=True
        )

    given, back_feed1 = None, [None, None]
    for side in ORDER:
        given = feed_backward(
            1,
            (side,),
            rows,
            batch,
            meta,
            [(feed1[side][0], feed1[side][6], got[side], cotangents[side])],
            None,
            small,
            chooser,
            [feed1[side][5]],
            ff_in1,
            ff_out1,
            ((feed1_there[side], "a"), (cross_there, "a")) if side == ORDER[0] else (),
            given,
        )
        back_feed1[side] = given
    got = over_mp(back_feed1, 3)
    back_feed1_there = [swap(back_feed1[side][2], "dp") for side in both]

    given, back_self1 = None, [None, None]
    for side in ORDER:
        given = self_backward(
            1,
            (side,),
            rows,
            meta,
            [feed1[side][1:3]],
            (back_feed1[side][0], back_feed1[side][3], got[side]),
            small,
            chooser,
            [self1[side][0]],
            [self1[side][1]],
            att_in1,
            att_out1,
            (
                ((feed1_there[ORDER[-1]], "a"), (back_feed1_there[ORDER[0]], "a"))
                if side == ORDER[0]
                else ()
            ),
            given,
        )
        back_self1[side] = given
    got = over_mp(back_self1, 3)
    feed1_grads = gradients(
        meta,
        [
            Halves(
                [feed1[side][3] for side in both],
                feed1_there,
                [back_feed1[side][1] for side in both],
                back_feed1_there,
            )
        ],
        None,
        groups,
        "feed_gradients_1",
        (back_self1[ORDER[-1]][5],),
    )
    feed1_pair = over_sections_and_groups(feed1_grads).reshape(2, D // dp_count, -1)
    back_self1_there = swap(back_self1[ORDER[-1]][2], "dp")
    back_cross = cross_backward(
        meta,
        [self1[side][7:9] for side in both],
        [back_self1[side][0] for side in both],
        [back_self1[side][3] for side in both],
        got,
        cross_post,
        cross_chooser,
        [cross[side][5] for side in both],
        [cross[side][6] for side in both],
        cross_entry,
        cross_out,
        (feed1_grads,),
    )
    cross_post_grad, cross_bias_grad = back_cross[4:6]
    got = swap(back_cross[3], "mp")
    back_cross_there = swap(back_cross[2], "dp")
    back_feed0 = feed_backward(
        0,
        (1, 0),
        rows,
        batch,
        meta,
        [cross[side][1:3] for side in (1, 0)],
        (back_cross[0], back_cross[3], got),
        small,
        chooser,
        [feed0[side][5] for side in (1, 0)],
        ff_in,
        ff_out,
        ((back_self1_there, "a"),),
    )
    got = swap(back_feed0[3], "mp")
    back_feed0_there = swap(back_feed0[2], "dp")
    late1_grads = gradients(
        meta,
        [
            Block(
                [self1[side][2] for side in both],
                [self1[ORDER[-1]][3]],
                [self1_there],
                back_self1[ORDER[-1]][1],
                [back_self1[ORDER[-1]][2]],
                [back_self1_there],
            )
        ],
        Block(
            [cross[side][4] for side in both],
            [cross_pack],
            [cross_there],
            back_cross[1],
            [back_cross[2]],
            [back_cross_there],
        ),
        groups,
        "late_gradients_1",
        (back_feed0[5],),
    )
    late1_share = over_sections_and_groups(late1_grads)
    back_self0 = self_backward(
        0,
        (1, 0),
        rows,
        meta,
        [feed0[side][1:3] for side in (1, 0)],
        (back_feed0[0], back_feed0[3], got),
        small,
        chooser,
        [self0[side][0] for side in (1, 0)],
        [self0[side][1] for side in (1, 0)],
        att_in,
        att_out,
        (late1_grads,),
    )
    got = swap(back_self0[3], "mp")
    back_self0_there = swap(back_self0[2], "dp")
    feed0_grads = gradients(
        meta,
        [
            Block(
                [feed0[side][3] for side in both],
                [feed0[0][4]],
                [feed0_there],
                back_feed0[1],
                [back_feed0[2]],
                [back_feed0_there],
            )
        ],
        None,
        groups,
        "feed_gradients_0",
        (back_self0[5], feed1_pair),
        "split",
    )
    feed0_total = total_of([feed0_grads[0], swap(feed0_grads[1], "section")])
    self0_grads = gradients(
        meta,
        [
            Block(
                [self0[side][2] for side in both],
                [self0[0][3]],
                [self0_there],
                back_self0[1],
                [back_self0[2]],
                [back_self0_there],
            )
        ],
        None,
        groups,
        "self_gradients_0",
        (feed0_total,),
        "split",
    )
    feed0_share = over_groups(feed0_total)
    self0_parts = [self0_grads[0], swap(self0_grads[1], "section")]
    if groups & (groups - 1) == 0:
        halving = Halving(self0_parts, groups)
        self0_sent = halving.send() if groups > 1 else self0_parts[0]
    else:
        halving = None
        self0_sent = total_of(self0_parts)
    chunk = D // dp_count
    word_full, region_full, word_back, region_back, mine, theirs = finished(
        meta,
        batch,
        rows,
        [back_feed1[side][7] for side in both],
        (back_self0[0], back_self0[3], got),
        [
            (
                back_self0[5],
                back_self0[4],
                back_feed0[5],
                back_feed0[4],
                [self0[side][5] for side in both],
                [feed0[side][7] for side in both],
                [cross[side][3] for side in both],
            ),
            (
                back_self1[ORDER[-1]][5],
                back_self1[ORDER[-1]][4],
                back_feed1[ORDER[-1]][5],
                back_feed1[ORDER[-1]][4],
                [self1[side][5] for side in both],
                [feed1[side][7] for side in both],
                [back_feed1[ORDER[-1]][6]],
            ),
        ],
        cross_post_grad,
        cross_bias_grad,
        (self0_sent,),
    )
    total = mine + swap(theirs, "section")
    distance = 1
    while 2 * distance < dp_count:
        total, distance = total + swap(total, "dp", distance), 2 * distance
    if halving and groups > 2:
        while halving.groups > 2:
            halving.send(total)
        last_sent, total = halving.send(total, extra=total)
    else:
        last_sent, total = total, total + swap(total, "dp", distance)
    feed1_pair, late1_share = behind((feed1_pair, late1_share), (last_sent,))
    feed1_own = lax.dynamic_index_in_dim(feed1_pair, place, 0, keepdims=False)
    feed1_other = swap(lax.dynamic_index_in_dim(feed1_pair, 1 - place, 0, keepdims=False), "dp")
    halves = (
        jnp.where(place == 0, feed1_own, feed1_other),
        jnp.where(place == 0, feed1_other, feed1_own),
    )
    count = units // 2
    feed1_share = jnp.concatenate(
        [half[:, j * count : (j + 1) * count] for j in both for half in halves], axis=1
    )
    late_words = [
        lax.ppermute(value, "section", [(0, 1)]) for value in (feed1_share, late1_share[:chunk])
    ]
    self0_share = halving.finish(late_words) if halving else over_groups(self0_sent)
    self_regions = lax.ppermute(self0_share, "section", [(1, 0)])
    feed_regions = lax.ppermute(feed0_share, "section", [(1, 0)])
    feed_in_grad, feed_out_grad, att_in_grad, att_out_grad, cross_in_grad, cross_out_grad = (
        placed_gradients(
            meta,
            (feed0_share, self0_share, feed_regions, self_regions),
            (*late_words, feed1_share, late1_share),
            chunk,
            width,
            units,
        )
    )
    outputs = unpacked(total, width, units)
    feed_in_grad = feed_in_grad[None]
    feed_out_grad = feed_out_grad.transpose(0, 2, 1)[None]
    att_in_grad = att_in_grad.transpose(0, 2, 1, 3)[None]
    att_out_grad = att_out_grad.transpose(0, 2, 1)[None]
    cross_in_grad = cross_in_grad.transpose(1, 0, 2)
    cross_out_grad = cross_out_grad.T
    att_bias_grad, att_post_grad, feed_bias_grad, feed_post_grad, cross_bias_grad, cross_post_grad = (
        outputs[:6]
    )
    return (
        word_full.transpose(1, 0, 2)[None],
        region_full.transpose(1, 0, 2)[None],
        word_back.transpose(1, 0, 2)[None],
        region_back.transpose(1, 0, 2)[None],
        cross_in_grad,
        cross_bias_grad,
        cross_out_grad,
        cross_post_grad,
        att_in_grad,
        att_bias_grad,
        att_out_grad,
        att_post_grad.transpose(0, 2, 1, 3),
        feed_in_grad,
        feed_bias_grad,
        feed_out_grad,
        feed_post_grad.transpose(0, 2, 1, 3),
        outputs[6],
    )


def solution(mesh):
    placed = (
        P(None, "dp", None, None),
        P(None, "dp", None, None),
        P(None, "dp"),
        P(None, "dp"),
        P(None, "dp", None, None),
        P(None, "dp", None, None),
        P(None, None, "mp"),
        P(None, "mp"),
        P("mp", None),
        P(),
        P("section", None, None, None, "mp"),
        P("section", None, None, "mp"),
        P("section", None, "mp", None),
        P("section", None, None, None),
        P("section", None, None, "mp"),
        P("section", None, "mp"),
        P("section", None, "mp", None),
        P("section", None, None, None),
    )
    return jax.shard_map(
        on_device,
        mesh=mesh,
        in_specs=placed,
        out_specs=(
            P("section", "dp", None, None),
            P("section", "dp", None, None),
            P("section", "dp", None, None),
            P("section", "dp", None, None),
            P(("section", "dp"), None, "mp"),
            P(None, "mp"),
            P("mp", ("section", "dp")),
            P(),
            P("section", None, "dp", None, "mp"),
            P("section", None, None, "mp"),
            P("section", None, "mp", "dp"),
            P("section", None, None, None),
            P("section", None, "dp", "mp"),
            P("section", None, "mp"),
            P("section", None, "mp", "dp"),
            P("section", None, None, None),
            P("section", None),
        ),
        check_vma=False,
    )
```
